32 devices in a mesh: dp: 8 (over y, x, core), tensor: 4 (over z).
Axes of the slice: x: 2, y: 2, z: 4, core: 2. Of those that a mesh axis runs over, the one named last changes fastest.
Arguments:
- block_input: bfloat16 [16, 2048, 768], P('dp', 'tensor'), may hold values from -6 to 6
- norm_gain: float32 [768], replicated, may hold values from 0.5 to 1.5
- input_gate_inner_weight: bfloat16 [768, 2, 1536], P('dp', None, 'tensor'), may hold values from -0.21875 to 0.21875
- input_shared_weight: bfloat16 [768, 256], P('dp'), may hold values from -0.21875 to 0.21875
- input_delta_weight: bfloat16 [768, 24], P('dp', 'tensor'), may hold values from -0.21875 to 0.21875
- conv_inner: bfloat16 [4, 1536], P(None, 'tensor'), may hold values from -3 to 3
- shift_inner: bfloat16 [1536], P('tensor'), may hold values from -3 to 3
- conv_shared: bfloat16 [4, 256], replicated, may hold values from -3 to 3
- shift_shared: bfloat16 [256], replicated, may hold values from -3 to 3
- decay_log: float32 [24], P('tensor'), may hold values from 0 to 2.77
- delta_bias: float32 [24], P('tensor'), may hold values from -6.9 to -2.3
- skip_gain: float32 [24], P('tensor'), may hold values from 0.5 to 1.5
- gated_gain: float32 [1536], P('tensor'), may hold values from 0.5 to 1.5
- output_projection_weight: bfloat16 [1536, 768], P('tensor', 'dp'), may hold values from -0.15625 to 0.15625
- cotangent: bfloat16 [16, 2048, 768], P('dp', 'tensor'), may hold values from -6 to 6
Outputs:
- block_output: bfloat16 [16, 2048, 768], P('dp', 'tensor')
- input_grad: bfloat16 [16, 2048, 768], P('dp', 'tensor')
- norm_gain_grad: float32 [768], replicated
- gate_inner_grad: float32 [768, 2, 1536], P('dp', None, 'tensor')
- shared_bc_grad: float32 [768, 256], P('dp')
- delta_grad: float32 [768, 24], P('dp', 'tensor')
- conv_inner_grad: float32 [4, 1536], P(None, 'tensor')
- shift_inner_grad: float32 [1536], P('tensor')
- conv_shared_grad: float32 [4, 256], replicated
- shift_shared_grad: float32 [256], replicated
- decay_log_grad: float32 [24], P('tensor')
- delta_bias_grad: float32 [24], P('tensor')
- bypass_factor_sensitivity: float32 [24], P('tensor')
- gated_gain_grad: float32 [1536], P('tensor')
- out_weight_grad: float32 [1536, 768], P('tensor', 'dp')
The draws below stay inside these ranges and needn't reach their ends.
All inputs are finite; a program needn't handle non-finite values.
Results may differ from the reference program's by a relative error of at most 0.0095.
Values may be sent and summed in bfloat16 or wider, within the bound.
A program may use at most 320 MiB of HBM per device.

```python
from functools import partial
import jax
import jax.numpy as jnp
from jax import lax

D = 768
DI = 1536
P_SIZE = 64
N = 128
K = 4
SPAN = 256
SEQ_LEN = 2048
S_DEV = 2
H = 24
SEQS = 16


def raised(values, own_key, source, target, parts, factor):
    owner, partner = [(jnp.arange(values.shape[axis_at]) // (values.shape[axis_at] // parts)).reshape([-1 if axis == axis_at else 1 for axis in range(values.ndim)]) for axis_at in (source, target)]
    chosen = jax.random.permutation(own_key, parts)[partner]
    strong = (owner == chosen) | (owner == (partner + parts // 2) % parts)
    return jnp.where(strong, factor * values, values)


def levels(own_key, shape, pieces, low, top_value):
    def one(position, blocks):
        heights = jax.random.uniform(jax.random.fold_in(jax.random.fold_in(own_key, 6), position), (blocks,), jnp.float32, low / len(pieces), top_value / len(pieces))
        return jnp.repeat(jnp.exp(heights), shape[position] // blocks).reshape((-1,) + (1,) * (len(shape) - position - 1))

    loudness = one(*pieces[0])
    for cut in pieces[1:]:
        loudness = loudness * one(*cut)
    return loudness


def centred(stream_key, dims, scale, reach, pieces=(), kind=jnp.bfloat16):
    entries = jax.random.normal(stream_key, dims, jnp.float32) * scale
    if len(pieces) > 0:
        entries = levels(stream_key, dims, pieces, -0.22, 0.18) * entries
    return jnp.clip(entries, min=-reach, max=reach).astype(kind)


def noise_with(key, shape, deviation, most, cuts, heavy, kind=jnp.bfloat16):
    values = deviation * jax.random.normal(key, shape, jnp.float32)
    if cuts:
        values = values * levels(key, shape, cuts, -0.22, 0.18)
    return jnp.clip(raised(values, jax.random.fold_in(key, 3), *heavy), -most, most).astype(kind)


def setup_inputs(seed: int = 0) -> dict:
    streams_of = jax.random.split(jax.random.key(seed), 16)
    block_input = noise_with(streams_of[0], (SEQS, SEQ_LEN, D), 1.0, 6.0, ((0, 8), (1, 4)), (0, 2, 8, 2.0))
    norm_gain = jnp.clip(1.0 + 0.1 * jax.random.normal(streams_of[1], (D,), jnp.float32), 0.5, 1.5)
    input_gate_inner_weight = centred(streams_of[2], (D, 2, DI), D ** -0.5, 0.21875, ((0, 8), (2, 4)))
    input_shared_weight = centred(streams_of[3], (D, 2 * N), D ** -0.5, 0.21875, ((0, 8),))
    input_delta_weight = centred(streams_of[4], (D, H), D ** -0.5, 0.21875, ((0, 8), (1, 4)))
    conv_inner = centred(streams_of[5], (K, DI), 0.5, 3.0, ((1, 4),))
    shift_inner = centred(streams_of[6], (DI,), 0.5, 3.0, ((0, 4),))
    conv_shared = centred(streams_of[7], (K, 2 * N), 0.5, 3.0)
    shift_shared = centred(streams_of[8], (2 * N,), 0.5, 3.0)
    decay_log = jnp.clip(2.77 * jax.random.uniform(streams_of[9], (H,), jnp.float32) ** levels(streams_of[9], (H,), ((0, 4),), -0.2, 0.2), 0.0, 2.77)
    delta_bias = jnp.clip(-6.9 + 4.6000001430511475 * jax.random.uniform(streams_of[10], (H,), jnp.float32) ** levels(streams_of[10], (H,), ((0, 4),), -0.2, 0.2), -6.9, -2.3)
    skip_gain = jnp.clip(0.5 + 1.0 * jax.random.uniform(streams_of[11], (H,), jnp.float32) ** levels(streams_of[11], (H,), ((0, 4),), -0.2, 0.2), 0.5, 1.5)
    gated_gain = jnp.clip(1.0 + 0.1 * jax.random.normal(streams_of[12], (DI,), jnp.float32), 0.5, 1.5)
    output_projection_weight = centred(streams_of[13], (DI, D), DI ** -0.5, 0.15625, ((0, 4), (1, 8)))
    cotangent = noise_with(streams_of[14], (SEQS, SEQ_LEN, D), 1.0, 6.0, ((0, 8), (1, 4)), (0, 2, 8, 2.0))
    return {"block_input": block_input, "norm_gain": norm_gain, "input_gate_inner_weight": input_gate_inner_weight, "input_shared_weight": input_shared_weight, "input_delta_weight": input_delta_weight, "conv_inner": conv_inner, "shift_inner": shift_inner, "conv_shared": conv_shared, "shift_shared": shift_shared, "decay_log": decay_log, "delta_bias": delta_bias, "skip_gain": skip_gain, "gated_gain": gated_gain, "output_projection_weight": output_projection_weight, "cotangent": cotangent}


EPSILON = 1e-05
TOP_PRECISION = lax.Precision.HIGHEST

@jax.custom_vjp
def low(v):
    return lax.optimization_barrier(v.astype(jnp.bfloat16)).astype(jnp.float32)

@jax.custom_vjp
def low_precision_pullback(v):
    return v

def low_keep(v):
    return (low(v), None)

def low_pass(kept, grad):
    return (grad,)

def back_keep(v):
    return (v, None)

def back_low(kept, grad):
    return (low(grad),)
low.defvjp(low_keep, low_pass)
low_precision_pullback.defvjp(back_keep, back_low)

def causal_conv(values, kernel, offset):
    taps = kernel.shape[0]
    seq_length = values.shape[1]
    padded = jnp.pad(values, ((0, 0), (taps - 1, 0), (0, 0)))
    running = offset + jnp.zeros_like(values)
    for tap_index in range(taps):
        running = running + padded[:, tap_index:tap_index + seq_length, :] * kernel[tap_index]
    return running

def scan_heads(inner_act, delta, decay_log, b_values, c_values, skip_gain, block, head_dim):
    seq_length = inner_act.shape[0]
    head_count = delta.shape[1]
    block_count = seq_length // block
    decay_rate = -jnp.exp(decay_log)
    blocked_x = inner_act.reshape(block_count, block, head_count, head_dim)
    blocked_dt = delta.reshape(block_count, block, head_count)
    blocked_b = b_values.reshape(block_count, block, -1)
    readout_matrix_tiles = c_values.reshape(block_count, block, -1)
    log_decay = jnp.cumsum(blocked_dt * decay_rate, axis=1)
    mixing = jnp.einsum('ctn,csn->cts', readout_matrix_tiles, blocked_b, precision=TOP_PRECISION)
    spread = log_decay[:, :, None, :] - log_decay[:, None, :, :]
    lower = (jnp.arange(block)[:, None] >= jnp.arange(block)[None, :])[None, :, :, None]
    decay_mat = jnp.where(lower, jnp.exp(jnp.where(lower, spread, 0.0)), 0.0)
    scores = mixing[:, :, :, None] * decay_mat * blocked_dt[:, None, :, :]
    intra_segment_term = jnp.einsum('ctsh,cshp->cthp', scores, blocked_x, precision=TOP_PRECISION)
    to_end = jnp.exp(log_decay[:, -1:, :] - log_decay) * blocked_dt
    fresh_states = jnp.einsum('csn,csh,cshp->chnp', blocked_b, to_end, blocked_x, precision=TOP_PRECISION)
    block_decay = jnp.exp(log_decay[:, -1, :])

    def advance(carried, scan_item):
        factor, fresh = scan_item
        return (factor[:, None, None] * carried + fresh, carried)
    initial = jnp.zeros(fresh_states.shape[1:], fresh_states.dtype)
    final_state, entering = lax.scan(advance, initial, (block_decay, fresh_states))
    across = jnp.einsum('ctn,chnp->cthp', readout_matrix_tiles, entering, precision=TOP_PRECISION) * jnp.exp(log_decay)[..., None]
    result = intra_segment_term + across + skip_gain[None, None, :, None] * blocked_x
    return result.reshape(seq_length, head_count * head_dim)

def forward(block_inputs_rows, norm_gain, input_gate_inner_weight, input_shared_weight, input_delta_weight, conv_inner, shift_inner, conv_shared, shift_shared, decay_log, delta_bias, skip_gain, gated_gain, output_projection_weight):
    inv_root = lax.rsqrt(lax.optimization_barrier(jnp.mean(block_inputs_rows * block_inputs_rows, axis=-1, keepdims=True)) + EPSILON)
    rescaled_token_vectors = low(block_inputs_rows * inv_root * norm_gain)
    model_channel_count = input_gate_inner_weight.shape[0]
    inner_channel_count = input_gate_inner_weight.shape[2]
    projected_output_rows = low_precision_pullback(jnp.einsum('kaf,ft->kat', rescaled_token_vectors, input_gate_inner_weight.reshape(model_channel_count, 2 * inner_channel_count), precision=TOP_PRECISION))
    gate_raw = projected_output_rows[..., :inner_channel_count]
    inner_raw = projected_output_rows[..., inner_channel_count:]
    shared_before_activation = low_precision_pullback(jnp.einsum('kaf,ft->kat', rescaled_token_vectors, input_shared_weight, precision=TOP_PRECISION))
    delta_before_softplus = low_precision_pullback(jnp.einsum('jct,ti->jci', rescaled_token_vectors, input_delta_weight, precision=TOP_PRECISION))
    inner_act = low(jax.nn.silu(causal_conv(inner_raw, conv_inner, shift_inner)))
    shared_act = low(jax.nn.silu(causal_conv(shared_before_activation, conv_shared, shift_shared)))
    state_dim = input_shared_weight.shape[1] // 2
    delta = jax.nn.softplus(delta_before_softplus + delta_bias)
    scanner = partial(scan_heads, block=SPAN, head_dim=P_SIZE)
    mixed = jax.vmap(scanner, in_axes=(0, 0, None, 0, 0, None))(inner_act, delta, decay_log, shared_act[..., :state_dim], shared_act[..., state_dim:], skip_gain)
    gated = mixed * jax.nn.silu(gate_raw)
    inv_gate = lax.rsqrt(lax.optimization_barrier(jnp.mean(gated * gated, axis=-1, keepdims=True)) + EPSILON)
    mixer_output_rows = low(gated * inv_gate * gated_gain)
    return block_inputs_rows + jnp.einsum('gue,ea->gua', mixer_output_rows, output_projection_weight, precision=TOP_PRECISION)

def reference(block_input, norm_gain, input_gate_inner_weight, input_shared_weight, input_delta_weight, conv_inner, shift_inner, conv_shared, shift_shared, decay_log, delta_bias, skip_gain, gated_gain, output_projection_weight, cotangent):
    weights = tuple((weight_arg.astype(jnp.float32) for weight_arg in (norm_gain, input_gate_inner_weight, input_shared_weight, input_delta_weight, conv_inner, shift_inner, conv_shared, shift_shared, decay_log, delta_bias, skip_gain, gated_gain, output_projection_weight)))
    group_count = block_input.shape[0] // S_DEV
    block_inputs_rows = block_input.astype(jnp.float32).reshape(group_count, S_DEV, SEQ_LEN, D)
    cotangents = cotangent.astype(jnp.float32).reshape(group_count, S_DEV, SEQ_LEN, D)

    def one_group(totals, batch_item):
        batch_in, batch_cot = batch_item
        result, pullback = jax.vjp(forward, batch_in, *weights)
        gradients = pullback(batch_cot)
        summed = tuple((total + grad_term for total, grad_term in zip(totals, gradients[1:])))
        return (summed, (result.astype(jnp.bfloat16), gradients[0].astype(jnp.bfloat16)))
    leading_prefix_totals = tuple((jnp.zeros_like(weight_arg) for weight_arg in weights))
    totals, outputs = lax.scan(one_group, leading_prefix_totals, (block_inputs_rows, cotangents))
    block_output = outputs[0].reshape(block_input.shape)
    input_grad = outputs[1].reshape(block_input.shape)
    return (block_output, input_grad, totals[0], totals[1], totals[2], totals[3], totals[4], totals[5], totals[6], totals[7], totals[8], totals[9], totals[10], totals[11], totals[12])
```

```python
import functools

import jax
import jax.numpy as jnp
from jax import lax
from jax.experimental import pallas as pl
from jax.experimental.pallas import tpu as pltpu
from jax.sharding import PartitionSpec as P

P_SIZE = 64
SPAN = 256
HALF = SPAN // 2
EPSILON = 1e-05
LOG2E = 1.4426950408889634
F32 = jnp.float32
BF16 = jnp.bfloat16
VMEM_LIMIT = 60 * 1024 * 1024
WIDE = 512


def dot(a, b):
    return jnp.dot(a, b, preferred_element_type=F32)


def dot_nt(a, b):
    return lax.dot_general(a, b, (((1,), (1,)), ((), ())), preferred_element_type=F32)


def dot_tn(a, b):
    return lax.dot_general(a, b, (((0,), (0,)), ((), ())), preferred_element_type=F32)


def sigmoid(v):
    return 0.5 * jnp.tanh(0.5 * v) + 0.5


def split2(v):
    hi = v.astype(BF16)
    return hi, (v - hi.astype(F32)).astype(BF16)


def lanes_of(shape):
    return lax.broadcasted_iota(jnp.int32, shape, len(shape) - 1)


def packed(v, heads):
    v = jnp.where(lanes_of(v.shape) < heads, v, 0.0)
    hi = v.astype(BF16).astype(F32)
    low = (v - hi).astype(BF16).astype(F32)
    return (hi + pltpu.roll(low, 32, 1)).astype(BF16)


def spread_heads(pk, sel):
    return dot(pk, sel)


def gather_heads(v, selt):
    hi, low = split2(v)
    return dot(hi, selt) + dot(low, selt)


def cumulate(tri, v, heads):
    v = jnp.where(lanes_of(v.shape) < heads, v, 0.0)
    p0 = v.astype(BF16).astype(F32)
    r = v - p0
    p1 = r.astype(BF16).astype(F32)
    p2 = r - p1
    pk = (p0 + pltpu.roll(p1, 32, 1) + pltpu.roll(p2, 64, 1)).astype(BF16)
    s = dot(tri, pk)
    n = s.shape[1]
    s = s + pltpu.roll(s, n - 32, 1) + pltpu.roll(s, n - 64, 1)
    return jnp.where(lanes_of(v.shape) < heads, s, 0.0)


def block_rows(b, size):
    return pl.ds(pl.multiple_of(b * size, size), size)


def front_kernel(
    heads,
    x_ref, xh_ref, gain_ref, wi_ref, wsd_ref, ti_ref, ts_ref, dpar_ref, sel_ref, tri_ref,
    h_ref, rawi_ref, raws_ref, xs_ref, bc_ref, draw_ref, acs_ref, bs_ref, fresh_ref, dec_ref,
    hh_ref, w_ref,
):
    seqs, ext, di = rawi_ref.shape
    span = ext - 16
    per = span // SPAN
    state = bc_ref.shape[1] // 2
    sh = raws_ref.shape[2]

    def norm(v):
        v = v.astype(F32)
        return (v * lax.rsqrt(jnp.mean(v * v, axis=-1, keepdims=True) + EPSILON) * gain_ref[...]).astype(BF16)

    hh_ref[...] = norm(xh_ref[...])
    for s in range(seqs):
        rawi_ref[s, 0:16, :] = dot(hh_ref[16 * s : 16 * s + 16, :], wi_ref[...])
        raws_ref[s, 0:16, :] = dot(hh_ref[16 * s : 16 * s + 16, :], wsd_ref[:, :sh])

    def seq_step(s, carry):
        def norm_step(b, c):
            rows = block_rows(s * per + b, SPAN)
            h_ref[rows, :] = norm(x_ref[rows, :])
            return c

        lax.fori_loop(0, per, norm_step, 0)
        rows = block_rows(s, span)
        for c0 in range(0, di, WIDE):
            rawi_ref[s, 16:ext, c0 : c0 + WIDE] = dot(h_ref[rows, :], wi_ref[:, c0 : c0 + WIDE])
        sd = dot(h_ref[rows, :], wsd_ref[...])
        raws_ref[s, 16:ext, :] = sd[:, :sh]
        draw_ref[rows, :] = sd[:, sh:] + dpar_ref[0:1, :]

        def conv(raw, par, out, cols):
            def step(r, c):
                r0 = pl.multiple_of(r * 128, 128)
                v = raw[s, pl.ds(r0, 144), cols]
                acc = par[4:5, cols] + par[0:1, cols] * v[13:141]
                for k in range(1, 4):
                    acc = acc + par[k : k + 1, cols] * v[13 + k : 141 + k]
                out[pl.ds(pl.multiple_of(s * span + r0, 128), 128), cols] = (acc * sigmoid(acc)).astype(BF16)
                return c

            lax.fori_loop(0, span // 128, step, 0)

        for c0 in range(0, di, 256):
            conv(rawi_ref, ti_ref, xs_ref, slice(c0, c0 + 256))
        for c0 in range(0, sh, 256):
            conv(raws_ref, ts_ref, bc_ref, slice(c0, c0 + 256))

        def block_step(j, c):
            b = s * per + j
            rows = block_rows(b, SPAN)
            x = draw_ref[rows, :]
            e = jnp.log1p(jnp.exp(-jnp.abs(x)))
            dt = jnp.maximum(x, 0.0) + e
            lg = jnp.where(x < -20.0, x * LOG2E, jnp.log2(jnp.maximum(dt, 1e-30)))
            acs = cumulate(tri_ref[...], dt * dpar_ref[1:2, :], heads)
            bs = acs - lg
            acs_ref[rows, :] = acs
            bs_ref[rows, :] = bs
            end = acs[SPAN - 1 : SPAN, :]
            w_ref[...] = packed(jnp.exp2(end - bs), heads)
            bt = bc_ref[rows, :state].astype(F32).T.astype(BF16)
            dk = packed(jnp.broadcast_to(jnp.exp2(end), (8, 128)), heads)
            for c0 in range(0, di, WIDE):
                cols = slice(c0, c0 + WIDE)
                w = spread_heads(w_ref[...], sel_ref[:, cols])
                wx = (w * xs_ref[rows, cols].astype(F32)).astype(BF16)
                fresh_ref[b, :, cols] = dot(bt, wx)
                dec_ref[b, :, cols] = spread_heads(dk, sel_ref[:, cols])
            return c

        lax.fori_loop(0, per, block_step, 0)
        return carry

    lax.fori_loop(0, seqs, seq_step, 0)


def mid_kernel(
    heads,
    x_ref, c_ref, h_ref, wg_ref, wo_ref, ggain_ref, skip_ref, xs_ref, bc_ref, acs_ref, bs_ref,
    sin_ref, fresh_ref, dec_ref, sel_ref, selt_ref,
    out_ref, yn_ref, dgate_ref, dy_ref, rr_ref, vv_ref, gg_ref, sk_ref, go_ref,
    y_ref, gate_ref, q_ref, g_ref, acst_ref, bst_ref, ea_ref,
):
    tokens, di = xs_ref.shape
    seqs = sin_ref.shape[0]
    blocks = tokens // SPAN
    per = blocks // seqs
    state = bc_ref.shape[1] // 2
    lower = lax.broadcasted_iota(jnp.int32, (HALF, HALF), 0) >= lax.broadcasted_iota(jnp.int32, (HALF, HALF), 1)
    first = lanes_of((HALF, 128)) < P_SIZE
    gg_ref[...] = jnp.zeros_like(gg_ref)
    sk_ref[...] = jnp.zeros_like(sk_ref)

    def block_step(b, carry):
        rows = block_rows(b, SPAN)
        s = b // per
        j = b - s * per
        acst_ref[...] = acs_ref[rows, :].T
        bst_ref[...] = bs_ref[rows, :].T
        ea_ref[...] = packed(jnp.exp2(acs_ref[rows, :]), heads)
        bb = bc_ref[rows, :state]
        cc = bc_ref[rows, state:]
        g00 = dot_nt(cc[:HALF], bb[:HALF])
        g10 = dot_nt(cc[HALF:], bb[:HALF])
        g11 = dot_nt(cc[HALF:], bb[HALF:])
        for p in range(di // 128):
            cols = slice(128 * p, 128 * p + 128)
            xp = xs_ref[rows, cols]
            y0, y1 = [], []
            for h in (2 * p, 2 * p + 1):
                a0 = acs_ref[block_rows(2 * b, HALF), h : h + 1]
                a1 = acs_ref[block_rows(2 * b + 1, HALF), h : h + 1]
                r0 = bst_ref[h : h + 1, :HALF]
                r1 = bst_ref[h : h + 1, HALF:]
                m00 = jnp.where(lower, jnp.exp2(a0 - r0) * g00, 0.0).astype(BF16)
                m10 = (jnp.exp2(a1 - r0) * g10).astype(BF16)
                m11 = jnp.where(lower, jnp.exp2(a1 - r1) * g11, 0.0).astype(BF16)
                y0.append(dot(m00, xp[:HALF]))
                y1.append(dot(jnp.concatenate([m10, m11], axis=1), xp))
            y_ref[0:HALF, cols] = jnp.where(first, y0[0], y0[1])
            y_ref[HALF:SPAN, cols] = jnp.where(first, y1[0], y1[1])

        ss = jnp.zeros((SPAN, 1), F32)
        for c0 in range(0, di, WIDE):
            cols = slice(c0, c0 + WIDE)
            prev = sin_ref[s, :, cols].astype(F32)
            later = dec_ref[s * per, 0:1, cols] * prev + fresh_ref[s * per, :, cols]
            s_in = jnp.where(j == 0, prev, later).astype(BF16)
            ea = spread_heads(ea_ref[...], sel_ref[:, cols])
            ynos = y_ref[:, cols] + ea * dot(cc, s_in)
            y_ref[:, cols] = ynos
            y = ynos + skip_ref[0:1, cols] * xs_ref[rows, cols].astype(F32)
            gate = dot(h_ref[rows, :], wg_ref[:, cols])
            gate_ref[:, cols] = gate
            g = y * (gate * sigmoid(gate))
            g_ref[:, cols] = g
            ss = ss + jnp.sum(g * g, axis=-1, keepdims=True)
        r2 = lax.rsqrt(ss / di + EPSILON)
        qg = jnp.zeros((SPAN, 1), F32)
        for c0 in range(0, di, WIDE):
            cols = slice(c0, c0 + WIDE)
            g = g_ref[:, cols]
            gain = ggain_ref[0:1, cols]
            yn_ref[rows, cols] = (g * r2 * gain).astype(BF16)
            dyn = dot(c_ref[rows, :], wo_ref[:, cols])
            gg_ref[0:1, cols] += jnp.sum(dyn * (g * r2), axis=0, keepdims=True)
            q = dyn * gain
            q_ref[:, cols] = q
            qg = qg + jnp.sum(q * g, axis=-1, keepdims=True)
        out_ref[rows, :] = (x_ref[rows, :].astype(F32) + dot_nt(yn_ref[rows, :], wo_ref[...])).astype(BF16)
        coef = r2 * r2 * r2 * (qg / di)
        rr = jnp.zeros((SPAN, 128), F32)
        dk = jnp.zeros((SPAN, 128), F32)
        ct = cc.astype(F32).T.astype(BF16)
        for c0 in range(0, di, WIDE):
            cols = slice(c0, c0 + WIDE)
            xf = xs_ref[rows, cols].astype(F32)
            ynos = y_ref[:, cols]
            y = ynos + skip_ref[0:1, cols] * xf
            gate = gate_ref[:, cols]
            sg = sigmoid(gate)
            dg = r2 * q_ref[:, cols] - coef * g_ref[:, cols]
            dgate_ref[rows, cols] = (dg * y * (sg * (1.0 + gate * (1.0 - sg)))).astype(BF16)
            dyb = (dg * (gate * sg)).astype(BF16)
            dy_ref[rows, cols] = dyb
            dy = dyb.astype(F32)
            rr = rr + gather_heads(dy * ynos, selt_ref[cols, :])
            dk = dk + gather_heads(dy * xf, selt_ref[cols, :])
            ea = spread_heads(ea_ref[...], sel_ref[:, cols])
            vv_ref[b, :, cols] = dot(ct, (ea * dy).astype(BF16))
        rr_ref[rows, :] = rr
        sk_ref[0:1, :] += jnp.sum(dk, axis=0, keepdims=True)
        return carry

    lax.fori_loop(0, blocks, block_step, 0)
    for c0 in range(0, di, WIDE):
        cols = slice(c0, c0 + WIDE)
        go_ref[:, cols] = dot_tn(c_ref[...], yn_ref[:, cols]).astype(BF16)


def back_kernel(
    heads,
    xs_ref, bc_ref, draw_ref, acs_ref, bs_ref, sin_ref, fresh_ref, dec_ref, ds_ref, vv_ref, dy_ref, rr_ref,
    rawi_ref, raws_ref, ti_ref, ts_ref, dpar_ref, skip_ref, sel_ref, selt_ref, tri_ref, triu_ref,
    dpi_ref, dps_ref, dd_ref, small_ref, tgi_ref, tgs_ref,
    acst_ref, ea_ref, w_ref, dg_ref, dx_ref, dbc_ref,
):
    tokens, di = xs_ref.shape
    seqs, ext, _ = rawi_ref.shape
    span = ext - 16
    blocks = tokens // SPAN
    per = blocks // seqs
    state = bc_ref.shape[1] // 2
    sh = 2 * state
    upper = lax.broadcasted_iota(jnp.int32, (HALF, HALF), 0) <= lax.broadcasted_iota(jnp.int32, (HALF, HALF), 1)
    first = lanes_of((HALF, 128)) < P_SIZE
    first_all = lanes_of((SPAN, 128)) < P_SIZE
    small_ref[...] = jnp.zeros_like(small_ref)
    tgi_ref[...] = jnp.zeros_like(tgi_ref)
    tgs_ref[...] = jnp.zeros_like(tgs_ref)

    def block_step(b, carry):
        rows = block_rows(b, SPAN)
        s = b // per
        j = b - s * per
        acst_ref[...] = acs_ref[rows, :].T
        acs = acs_ref[rows, :]
        bs = bs_ref[rows, :]
        end = acs[SPAN - 1 : SPAN, :]
        ea_ref[...] = packed(jnp.exp2(acs), heads)
        w_ref[...] = packed(jnp.exp2(end - bs), heads)
        bb = bc_ref[rows, :state]
        cc = bc_ref[rows, state:]
        g00 = dot_nt(bb[:HALF], cc[:HALF])
        g01 = dot_nt(bb[:HALF], cc[HALF:])
        g11 = dot_nt(bb[HALF:], cc[HALF:])
        dg_ref[...] = jnp.zeros_like(dg_ref)
        for p in range(di // 128):
            cols = slice(128 * p, 128 * p + 128)
            xp = xs_ref[rows, cols]
            dyp = dy_ref[rows, cols]
            d0, d1 = [], []
            for i, h in enumerate((2 * p, 2 * p + 1)):
                keep = first_all if i == 0 else jnp.logical_not(first_all)
                xm = jnp.where(keep, xp, jnp.zeros_like(xp))
                b0 = bs_ref[block_rows(2 * b, HALF), h : h + 1]
                b1 = bs_ref[block_rows(2 * b + 1, HALF), h : h + 1]
                r0 = acst_ref[h : h + 1, :HALF]
                r1 = acst_ref[h : h + 1, HALF:]
                e00 = jnp.where(upper, jnp.exp2(r0 - b0), 0.0)
                e01 = jnp.exp2(r1 - b0)
                e11 = jnp.where(upper, jnp.exp2(r1 - b1), 0.0)
                m0 = jnp.concatenate([(e00 * g00).astype(BF16), (e01 * g01).astype(BF16)], axis=1)
                m1 = (e11 * g11).astype(BF16)
                d0.append(dot(m0, dyp))
                d1.append(dot(m1, dyp[HALF:]))
                dm0 = dot_nt(xm[:HALF], dyp)
                dm1 = dot_nt(xm[HALF:], dyp[HALF:])
                dg_ref[0] += dm0[:, :HALF] * e00
                dg_ref[1] += dm0[:, HALF:] * e01
                dg_ref[2] += dm1 * e11
            dx_ref[0:HALF, cols] = jnp.where(first, d0[0], d0[1])
            dx_ref[HALF:SPAN, cols] = jnp.where(first, d1[0], d1[1])

        dg00 = dg_ref[0]
        dg01 = dg_ref[1]
        dg11 = dg_ref[2]
        db0 = dot(jnp.concatenate([dg00, dg01], axis=1).astype(BF16), cc)
        db1 = dot(dg11.astype(BF16), cc[HALF:])
        dc0 = dot(dg00.T.astype(BF16), bb[:HALF])
        dc1 = dot(jnp.concatenate([dg01.T, dg11.T], axis=1).astype(BF16), bb)
        db = jnp.concatenate([db0, db1], axis=0)
        dc = jnp.concatenate([dc0, dc1], axis=0)
        rr = rr_ref[rows, :]
        pin = jnp.zeros((SPAN, 128), F32)
        pst = jnp.zeros((SPAN, 128), F32)
        endsum = jnp.zeros((8, 128), F32)
        for c0 in range(0, di, WIDE):
            cols = slice(c0, c0 + WIDE)
            prev = sin_ref[s, :, cols].astype(F32)
            later = dec_ref[s * per, 0:1, cols] * prev + fresh_ref[s * per, :, cols]
            s_in = jnp.where(j == 0, prev, later).astype(BF16)
            dlast = ds_ref[s, :, cols].astype(F32)
            dprev = dec_ref[s * per + per - 1, 0:1, cols] * dlast + vv_ref[s * per + per - 1, :, cols]
            ds = jnp.where(j == per - 1, dlast, dprev).astype(BF16)
            w = spread_heads(w_ref[...], sel_ref[:, cols])
            ea = spread_heads(ea_ref[...], sel_ref[:, cols])
            xf = xs_ref[rows, cols].astype(F32)
            dyf = dy_ref[rows, cols].astype(F32)
            dxs = w * dot(bb, ds)
            dxi = dx_ref[:, cols]
            pin = pin + gather_heads(dxi * xf, selt_ref[cols, :])
            pst = pst + gather_heads(dxs * xf, selt_ref[cols, :])
            both = jnp.sum(ds.astype(F32) * s_in.astype(F32), axis=0, keepdims=True) * dec_ref[b, 0:1, cols]
            endsum = endsum + gather_heads(jnp.broadcast_to(both, (8, WIDE)), selt_ref[cols, :])
            dc = dc + dot_nt((ea * dyf).astype(BF16), s_in)
            db = db + dot_nt((w * xf).astype(BF16), ds)
            dx_ref[:, cols] = dxi + dxs + skip_ref[0:1, cols] * dyf
        dbc_ref[:, :state] = db
        dbc_ref[:, state:] = dc
        pp = pin + pst
        da = cumulate(triu_ref[...], rr - pp, heads) + (endsum[0:1, :] + jnp.sum(pst, axis=0, keepdims=True))
        x = draw_ref[rows, :]
        sg = 1.0 / (1.0 + jnp.exp(-x))
        dt = jnp.maximum(x, 0.0) + jnp.log1p(jnp.exp(-jnp.abs(x)))
        ratio = jnp.where(x < -20.0, 1.0, sg / jnp.maximum(dt, 1e-30))
        ak = dpar_ref[2:3, :]
        dd = da * ak * sg + pp * ratio
        dd_ref[rows, :] = dd.astype(BF16)
        small_ref[0:1, :] += jnp.sum(da * dt * ak, axis=0, keepdims=True)
        small_ref[1:2, :] += jnp.sum(dd, axis=0, keepdims=True)

        def conv_back(raw, par, dact, dpre, tg, cols):
            def step(r, c):
                r0 = pl.multiple_of(r * HALF, HALF)
                v = raw[s, pl.ds(pl.multiple_of(j * SPAN + r0, HALF), HALF + 16), cols]
                sh_v = [v[13 + k : 13 + k + HALF] for k in range(4)]
                pre = par[4:5, cols] + par[0:1, cols] * sh_v[0]
                for k in range(1, 4):
                    pre = pre + par[k : k + 1, cols] * sh_v[k]
                sg = sigmoid(pre)
                dp = dact[pl.ds(r0, HALF), cols] * (sg * (1.0 + pre * (1.0 - sg)))
                dpre[pl.ds(pl.multiple_of(b * SPAN + r0, HALF), HALF), cols] = dp
                for k in range(4):
                    tg[k : k + 1, cols] += jnp.sum(dp * sh_v[k], axis=0, keepdims=True)
                tg[4:5, cols] += jnp.sum(dp, axis=0, keepdims=True)
                return c

            lax.fori_loop(0, SPAN // HALF, step, 0)

        for c0 in range(0, di, 256):
            conv_back(rawi_ref, ti_ref, dx_ref, dpi_ref, tgi_ref, slice(c0, c0 + 256))
        for c0 in range(0, sh, 256):
            conv_back(raws_ref, ts_ref, dbc_ref, dps_ref, tgs_ref, slice(c0, c0 + 256))
        return carry

    lax.fori_loop(0, blocks, block_step, 0)


def last_kernel(
    x_ref, c_ref, gain_ref, h_ref, dpi_ref, dps_ref, hi_ref, hs_ref, dd_ref, dgate_ref, ti_ref, ts_ref,
    wi_ref, wg_ref, wsd_ref,
    ig_ref, gi_ref, gg_ref, gsd_ref, ng_ref,
    din_ref, dsd_ref,
):
    tokens, di = dgate_ref.shape
    seqs = hi_ref.shape[0]
    span = tokens // seqs
    sh = dps_ref.shape[1]
    ng_ref[...] = jnp.zeros_like(ng_ref)
    dsd_ref[:, sh:] = dd_ref[...]

    def conv_t(dpre, halo, par, out, cols):
        for s in range(seqs):
            for r0 in range(0, span, HALF):
                base = s * span + r0
                v = dpre[base : base + HALF, cols]
                if r0 + HALF < span:
                    nxt = dpre[base + HALF : base + HALF + 8, cols]
                else:
                    nxt = halo[s, :, cols]
                v = jnp.concatenate([v, nxt], axis=0)
                acc = par[3:4, cols] * v[0:HALF]
                for k in range(3):
                    acc = acc + par[k : k + 1, cols] * v[3 - k : 3 - k + HALF]
                out[base : base + HALF, cols] = acc.astype(BF16)

    for c0 in range(0, di, 256):
        conv_t(dpi_ref, hi_ref, ti_ref, din_ref, slice(c0, c0 + 256))
    for c0 in range(0, sh, 256):
        conv_t(dps_ref, hs_ref, ts_ref, dsd_ref, slice(c0, c0 + 256))

    for c0 in range(0, di, WIDE):
        cols = slice(c0, c0 + WIDE)
        gi_ref[:, cols] = dot_tn(h_ref[...], din_ref[:, cols]).astype(BF16)
        gg_ref[:, cols] = dot_tn(h_ref[...], dgate_ref[:, cols]).astype(BF16)
    gsd_ref[...] = dot_tn(h_ref[...], dsd_ref[...]).astype(BF16)

    def step(b, carry):
        rows = block_rows(b, SPAN)
        dh = dot_nt(dgate_ref[rows, :], wg_ref[...])
        dh = dh + dot_nt(din_ref[rows, :], wi_ref[...])
        dh = dh + dot_nt(dsd_ref[rows, :], wsd_ref[...])
        u = x_ref[rows, :].astype(F32)
        r1 = lax.rsqrt(jnp.mean(u * u, axis=-1, keepdims=True) + EPSILON)
        ng_ref[0:1, :] += jnp.sum(dh * u * r1, axis=0, keepdims=True)
        e = dh * gain_ref[...]
        m = jnp.mean(e * u, axis=-1, keepdims=True)
        ig_ref[rows, :] = (c_ref[rows, :].astype(F32) + r1 * e - u * (r1 * r1 * r1 * m)).astype(BF16)
        return carry

    lax.fori_loop(0, tokens // SPAN, step, 0)


def call(kernel, outs, scratch, *args, name):
    return pl.pallas_call(
        kernel,
        out_shape=[jax.ShapeDtypeStruct(s, d) for s, d in outs],
        in_specs=[pl.BlockSpec(memory_space=pltpu.VMEM)] * len(args),
        out_specs=[pl.BlockSpec(memory_space=pltpu.VMEM)] * len(outs),
        scratch_shapes=[pltpu.VMEM(s, d) for s, d in scratch],
        compiler_params=pltpu.CompilerParams(vmem_limit_bytes=VMEM_LIMIT),
        name=name,
    )(*args)


def shifted(v, axis, by):
    n = lax.axis_size(axis)
    return lax.ppermute(v, axis, [(i, i + by) for i in range(n) if 0 <= i + by < n])


def local(
    block_input, norm_gain, input_gate_inner_weight, input_shared_weight, input_delta_weight, conv_inner, shift_inner,
    conv_shared, shift_shared, decay_log, delta_bias, skip_gain, gated_gain, output_projection_weight, cotangent,
):
    nt = lax.axis_size("tensor")
    nd = lax.axis_size("dp")
    both = ("tensor", "dp")
    me = lax.axis_index("tensor")
    seqs, span, dim = block_input.shape
    tokens = seqs * span
    blocks = tokens // SPAN
    rows, _, dcol = input_gate_inner_weight.shape
    di = dcol * nt
    sh = input_shared_weight.shape[1]
    state = sh // 2
    hloc = input_delta_weight.shape[1]
    heads = hloc * nt

    delta_w = lax.dynamic_update_slice(jnp.zeros((rows, 128), BF16), input_delta_weight, (0, me * hloc))
    pack = jnp.concatenate(
        [input_gate_inner_weight[:, 1], input_gate_inner_weight[:, 0], output_projection_weight.T, delta_w], axis=1
    )
    full = lax.all_gather(pack, both, axis=0).reshape(nt, dim, 3 * dcol + 128)
    wi, wg, wo = (full[:, :, dcol * k : dcol * (k + 1)].transpose(1, 0, 2).reshape(dim, di) for k in range(3))
    wd = jnp.sum(full[:, :, 3 * dcol :].astype(F32), axis=0).astype(BF16)
    ws = lax.all_gather(input_shared_weight, "dp", axis=0, tiled=True)
    wsd = jnp.concatenate([ws, wd], axis=1)
    chan = jnp.concatenate([conv_inner.astype(F32), shift_inner.astype(F32)[None], gated_gain[None]], axis=0)
    head = jnp.stack([decay_log, delta_bias, skip_gain])
    par = jnp.concatenate([chan, jnp.pad(head, ((0, 3), (0, dcol - hloc)))], axis=0)
    par = lax.all_gather(par, "tensor", axis=0)
    chan = par[:, :6].transpose(1, 0, 2).reshape(6, di)
    head = par[:, 6:9, :hloc].transpose(1, 0, 2).reshape(3, heads)
    ti = jnp.pad(chan[:5], ((0, 3), (0, 0)))
    ts = jnp.pad(jnp.concatenate([conv_shared.astype(F32), shift_shared.astype(F32)[None]], axis=0), ((0, 3), (0, 0)))
    ak = -jnp.exp(head[0])
    dpar = jnp.pad(jnp.stack([head[1], ak * LOG2E, ak]), ((0, 5), (0, 128 - heads)))
    ggain = chan[5:6]
    skip = jnp.repeat(head[2], P_SIZE)[None]
    gain = norm_gain[None]

    lane = jnp.arange(128)
    owner = jnp.arange(di) // P_SIZE
    sel = ((lane[:, None] % 32 == owner[None]) & (lane[:, None] < 64)).astype(BF16)
    selt = (lane[None] == owner[:, None]).astype(BF16)
    at = jnp.arange(SPAN)
    tri = (at[:, None] >= at[None]).astype(BF16)
    triu = tri.T

    x = block_input.reshape(tokens, dim)
    c = cotangent.reshape(tokens, dim)
    xh = shifted(block_input[:, span - 16 :], "tensor", 1).reshape(seqs * 16, dim)

    h, rawi, raws, xs, bc, draw, acs, bs, fresh, dec = call(
        functools.partial(front_kernel, heads),
        [((tokens, dim), BF16), ((seqs, span + 16, di), F32), ((seqs, span + 16, sh), F32), ((tokens, di), BF16),
         ((tokens, sh), BF16), ((tokens, 128), F32), ((tokens, 128), F32), ((tokens, 128), F32),
         ((blocks, state, di), F32), ((blocks, 8, di), F32)],
        [((seqs * 16, dim), BF16), ((SPAN, 128), BF16)],
        x, xh, gain, wi, wsd, ti, ts, dpar, sel, tri, name="front",
    )

    fr = fresh.reshape(seqs, blocks // seqs, state, di)
    de = dec.reshape(seqs, blocks // seqs, 8, di)[:, :, 0:1]
    whole, mine = de[:, 0], fr[:, 0]
    for j in range(1, blocks // seqs):
        mine = de[:, j] * mine + fr[:, j]
        whole = de[:, j] * whole
    sin = jnp.zeros((seqs, state, di), BF16)
    for _ in range(nt - 1):
        sin = shifted((mine + whole * sin.astype(F32)).astype(BF16), "tensor", 1)

    out, yn, dgate, dy, rr, vv, ggg, skg, go = call(
        functools.partial(mid_kernel, heads),
        [((tokens, dim), BF16), ((tokens, di), BF16), ((tokens, di), BF16), ((tokens, di), BF16), ((tokens, 128), F32),
         ((blocks, state, di), F32), ((8, di), F32), ((8, 128), F32), ((dim, di), BF16)],
        [((SPAN, di), F32)] * 4 + [((128, SPAN), F32)] * 2 + [((SPAN, 128), BF16)],
        x, c, h, wg, wo, ggain, skip, xs, bc, acs, bs, sin, fresh, dec, sel, selt, name="mid",
    )

    vr = vv.reshape(seqs, blocks // seqs, state, di)
    mine = vr[:, blocks // seqs - 1]
    for j in range(blocks // seqs - 2, -1, -1):
        mine = de[:, j] * mine + vr[:, j]
    ds = jnp.zeros((seqs, state, di), BF16)
    for _ in range(nt - 1):
        ds = shifted((mine + whole * ds.astype(F32)).astype(BF16), "tensor", -1)

    dpi, dps, dd, small, tgi, tgs = call(
        functools.partial(back_kernel, heads),
        [((tokens, di), F32), ((tokens, sh), F32), ((tokens, 128), BF16), ((8, 128), F32), ((8, di), F32), ((8, sh), F32)],
        [((128, SPAN), F32), ((SPAN, 128), BF16), ((SPAN, 128), BF16), ((3, HALF, HALF), F32), ((SPAN, di), F32),
         ((SPAN, sh), F32)],
        xs, bc, draw, acs, bs, sin, fresh, dec, ds, vv, dy, rr, rawi, raws, ti, ts, dpar, skip, sel, selt, tri, triu,
        name="back",
    )

    hi = shifted(dpi.reshape(seqs, span, di)[:, :8], "tensor", -1)
    hs = shifted(dps.reshape(seqs, span, sh)[:, :8], "tensor", -1)
    ig, gi, gg, gsd, ng = call(
        last_kernel,
        [((tokens, dim), BF16), ((dim, di), BF16), ((dim, di), BF16), ((dim, sh + 128), BF16), ((8, dim), F32)],
        [((tokens, di), BF16), ((tokens, sh + 128), BF16)],
        x, c, gain, h, dpi, dps, hi, hs, dd, dgate, ti, ts, wi, wg, wsd, name="last",
    )

    parts = [g.reshape(dim, nt, dcol).transpose(1, 0, 2) for g in (gg, gi, go)]
    big = jnp.concatenate(parts, axis=2).reshape(nt * nd, rows, 3 * dcol)
    mine = lax.psum_scatter(big, both, scatter_dimension=0).astype(F32)
    gate_inner_grad = mine[:, : 2 * dcol].reshape(rows, 2, dcol)
    out_weight_grad = mine[:, 2 * dcol :].T
    gsd = lax.psum_scatter(gsd.reshape(nd, rows, sh + 128).astype(F32), "dp", scatter_dimension=0)
    gsd = lax.psum(gsd, "tensor")
    tgi, ggg, tgs, ng, small, skg = lax.psum((tgi, ggg, tgs, ng, small, skg), both)
    cut = lambda v: lax.dynamic_slice_in_dim(v, me * dcol, dcol, axis=-1)
    hcut = lambda v: lax.dynamic_slice_in_dim(v, me * hloc, hloc, axis=-1)
    return (
        out.reshape(block_input.shape),
        ig.reshape(block_input.shape),
        ng[0],
        gate_inner_grad,
        gsd[:, :sh],
        hcut(gsd[:, sh:]),
        cut(tgi[:4]),
        cut(tgi[4]),
        tgs[:4],
        tgs[4],
        hcut(small[0]),
        hcut(small[1]),
        hcut(skg[0]),
        cut(ggg[0]),
        out_weight_grad,
    )


def solution(mesh):
    placed = (
        P("dp", "tensor", None), P(), P("dp", None, "tensor"), P("dp", None), P("dp", "tensor"), P(None, "tensor"),
        P("tensor"), P(), P(), P("tensor"), P("tensor"), P("tensor"), P("tensor"), P("tensor", "dp"),
        P("dp", "tensor", None),
    )
    return jax.shard_map(
        local,
        mesh=mesh,
        in_specs=placed,
        out_specs=(
            P("dp", "tensor", None), P("dp", "tensor", None), P(), P("dp", None, "tensor"), P("dp", None),
            P("dp", "tensor"), P(None, "tensor"), P("tensor"), P(), P(), P("tensor"), P("tensor"), P("tensor"),
            P("tensor"), P("tensor", "dp"),
        ),
        check_vma=False,
    )
```

```python
import functools

import jax
import jax.numpy as jnp
from jax import lax
from jax.experimental import pallas as pl
from jax.experimental.pallas import tpu as pltpu
from jax.sharding import PartitionSpec as P

P_SIZE = 64
SPAN = 256
HALF = SPAN // 2
EPSILON = 1e-05
LOG2E = 1.4426950408889634
F32 = jnp.float32
BF16 = jnp.bfloat16
VMEM_LIMIT = 60 * 1024 * 1024
WIDE = 512


def dot(a, b):
    return jnp.dot(a, b, preferred_element_type=F32)


def dot_nt(a, b):
    return lax.dot_general(a, b, (((1,), (1,)), ((), ())), preferred_element_type=F32)


def dot_tn(a, b):
    return lax.dot_general(a, b, (((0,), (0,)), ((), ())), preferred_element_type=F32)


def sigmoid(v):
    return 0.5 * jnp.tanh(0.5 * v) + 0.5


def split2(v):
    hi = v.astype(BF16)
    return hi, (v - hi.astype(F32)).astype(BF16)


def lanes_of(shape):
    return lax.broadcasted_iota(jnp.int32, shape, len(shape) - 1)


def packed(v, heads):
    v = jnp.where(lanes_of(v.shape) < heads, v, 0.0)
    hi = v.astype(BF16).astype(F32)
    low = (v - hi).astype(BF16).astype(F32)
    return (hi + pltpu.roll(low, 32, 1)).astype(BF16)


def spread_heads(pk, sel):
    return dot(pk, sel)


def gather_heads(v, selt):
    hi, low = split2(v)
    return dot(hi, selt) + dot(low, selt)


def cumulate(tri, v, heads):
    v = jnp.where(lanes_of(v.shape) < heads, v, 0.0)
    p0 = v.astype(BF16).astype(F32)
    r = v - p0
    p1 = r.astype(BF16).astype(F32)
    p2 = r - p1
    pk = (p0 + pltpu.roll(p1, 32, 1) + pltpu.roll(p2, 64, 1)).astype(BF16)
    s = dot(tri, pk)
    n = s.shape[1]
    s = s + pltpu.roll(s, n - 32, 1) + pltpu.roll(s, n - 64, 1)
    return jnp.where(lanes_of(v.shape) < heads, s, 0.0)


def block_rows(b, size):
    return pl.ds(pl.multiple_of(b * size, size), size)


def front_kernel(
    heads, nt,
    x_ref, xh_ref, gain_ref, w1_ref, ws_ref, ti_ref, ts_ref, dpar_ref, sel_ref, tri_ref,
    h_ref, rawi_ref, raws_ref, xs_ref, bc_ref, draw_ref, acs_ref, bs_ref, fresh_ref, dec_ref,
    hh_ref, w_ref,
):
    seqs, ext, di = rawi_ref.shape
    span = ext - 16
    per = span // SPAN
    state = bc_ref.shape[1] // 2
    sh = raws_ref.shape[2]

    def norm(v):
        v = v.astype(F32)
        return (v * lax.rsqrt(jnp.mean(v * v, axis=-1, keepdims=True) + EPSILON) * gain_ref[...]).astype(BF16)

    hh_ref[...] = norm(xh_ref[...])
    part = w1_ref.shape[1] // nt
    for s in range(seqs):
        rows = slice(16 * s, 16 * s + 16)
        for t in range(nt):
            own = dot(hh_ref[rows, :], w1_ref[:, part * t : part * (t + 1) - 128])
            rawi_ref[s, 0:16, (part - 128) * t : (part - 128) * (t + 1)] = own
        raws_ref[s, 0:16, :] = dot(hh_ref[rows, :], ws_ref[...])

    def seq_step(s, carry):
        def norm_step(b, c):
            rows = block_rows(s * per + b, SPAN)
            h_ref[rows, :] = norm(x_ref[rows, :])
            return c

        lax.fori_loop(0, per, norm_step, 0)
        rows = block_rows(s, span)
        part = w1_ref.shape[1] // nt
        draw = dpar_ref[0:1, :]
        for t in range(nt):
            both = dot(h_ref[rows, :], w1_ref[:, part * t : part * (t + 1)])
            rawi_ref[s, 16:ext, (part - 128) * t : (part - 128) * (t + 1)] = both[:, : part - 128]
            draw = draw + both[:, part - 128 :]
        draw_ref[rows, :] = draw
        raws_ref[s, 16:ext, :] = dot(h_ref[rows, :], ws_ref[...])

        def conv(raw, par, out, cols):
            def step(r, c):
                r0 = pl.multiple_of(r * 128, 128)
                v = raw[s, pl.ds(r0, 144), cols]
                acc = par[4:5, cols] + par[0:1, cols] * v[13:141]
                for k in range(1, 4):
                    acc = acc + par[k : k + 1, cols] * v[13 + k : 141 + k]
                out[pl.ds(pl.multiple_of(s * span + r0, 128), 128), cols] = (acc * sigmoid(acc)).astype(BF16)
                return c

            lax.fori_loop(0, span // 128, step, 0)

        for c0 in range(0, di, 256):
            conv(rawi_ref, ti_ref, xs_ref, slice(c0, c0 + 256))
        for c0 in range(0, sh, 256):
            conv(raws_ref, ts_ref, bc_ref, slice(c0, c0 + 256))

        def block_step(j, c):
            b = s * per + j
            rows = block_rows(b, SPAN)
            x = draw_ref[rows, :]
            e = jnp.log1p(jnp.exp(-jnp.abs(x)))
            dt = jnp.maximum(x, 0.0) + e
            lg = jnp.where(x < -20.0, x * LOG2E, jnp.log2(jnp.maximum(dt, 1e-30)))
            acs = cumulate(tri_ref[...], dt * dpar_ref[1:2, :], heads)
            bs = acs - lg
            acs_ref[rows, :] = acs
            bs_ref[rows, :] = bs
            end = acs[SPAN - 1 : SPAN, :]
            w_ref[...] = packed(jnp.exp2(end - bs), heads)
            bt = bc_ref[rows, :state].astype(F32).T.astype(BF16)
            dk = packed(jnp.broadcast_to(jnp.exp2(end), (8, 128)), heads)
            for c0 in range(0, di, WIDE):
                cols = slice(c0, c0 + WIDE)
                w = spread_heads(w_ref[...], sel_ref[:, cols])
                wx = (w * xs_ref[rows, cols].astype(F32)).astype(BF16)
                fresh_ref[b, :, cols] = dot(bt, wx)
                dec_ref[b, :, cols] = spread_heads(dk, sel_ref[:, cols])
            return c

        lax.fori_loop(0, per, block_step, 0)
        return carry

    lax.fori_loop(0, seqs, seq_step, 0)


def mid_kernel(
    heads,
    x_ref, c_ref, h_ref, wg_ref, wo_ref, ggain_ref, skip_ref, xs_ref, bc_ref, acs_ref, bs_ref,
    sin_ref, fresh_ref, dec_ref, sel_ref, selt_ref,
    out_ref, yn_ref, dgate_ref, dy_ref, rr_ref, vv_ref, gg_ref, sk_ref, go_ref,
    y_ref, gate_ref, q_ref, g_ref, acst_ref, bst_ref, ea_ref,
):
    tokens, di = xs_ref.shape
    seqs = sin_ref.shape[0]
    blocks = tokens // SPAN
    per = blocks // seqs
    state = bc_ref.shape[1] // 2
    lower = lax.broadcasted_iota(jnp.int32, (HALF, HALF), 0) >= lax.broadcasted_iota(jnp.int32, (HALF, HALF), 1)
    first = lanes_of((HALF, 128)) < P_SIZE
    gg_ref[...] = jnp.zeros_like(gg_ref)
    sk_ref[...] = jnp.zeros_like(sk_ref)

    def block_step(b, carry):
        rows = block_rows(b, SPAN)
        s = b // per
        j = b - s * per
        acst_ref[...] = acs_ref[rows, :].T
        bst_ref[...] = bs_ref[rows, :].T
        ea_ref[...] = packed(jnp.exp2(acs_ref[rows, :]), heads)
        bb = bc_ref[rows, :state]
        cc = bc_ref[rows, state:]
        g00 = dot_nt(cc[:HALF], bb[:HALF])
        g10 = dot_nt(cc[HALF:], bb[:HALF])
        g11 = dot_nt(cc[HALF:], bb[HALF:])
        for p in range(di // 128):
            cols = slice(128 * p, 128 * p + 128)
            xp = xs_ref[rows, cols]
            y0, y1 = [], []
            for h in (2 * p, 2 * p + 1):
                a0 = acs_ref[block_rows(2 * b, HALF), h : h + 1]
                a1 = acs_ref[block_rows(2 * b + 1, HALF), h : h + 1]
                r0 = bst_ref[h : h + 1, :HALF]
                r1 = bst_ref[h : h + 1, HALF:]
                m00 = jnp.where(lower, jnp.exp2(a0 - r0) * g00, 0.0).astype(BF16)
                m10 = (jnp.exp2(a1 - r0) * g10).astype(BF16)
                m11 = jnp.where(lower, jnp.exp2(a1 - r1) * g11, 0.0).astype(BF16)
                y0.append(dot(m00, xp[:HALF]))
                y1.append(dot(jnp.concatenate([m10, m11], axis=1), xp))
            y_ref[0:HALF, cols] = jnp.where(first, y0[0], y0[1])
            y_ref[HALF:SPAN, cols] = jnp.where(first, y1[0], y1[1])

        ss = jnp.zeros((SPAN, 1), F32)
        for c0 in range(0, di, WIDE):
            cols = slice(c0, c0 + WIDE)
            prev = sin_ref[s, :, cols].astype(F32)
            later = dec_ref[s * per, 0:1, cols] * prev + fresh_ref[s * per, :, cols]
            s_in = jnp.where(j == 0, prev, later).astype(BF16)
            ea = spread_heads(ea_ref[...], sel_ref[:, cols])
            ynos = y_ref[:, cols] + ea * dot(cc, s_in)
            y_ref[:, cols] = ynos
            y = ynos + skip_ref[0:1, cols] * xs_ref[rows, cols].astype(F32)
            gate = dot(h_ref[rows, :], wg_ref[:, cols])
            gate_ref[:, cols] = gate
            g = y * (gate * sigmoid(gate))
            g_ref[:, cols] = g
            ss = ss + jnp.sum(g * g, axis=-1, keepdims=True)
        r2 = lax.rsqrt(ss / di + EPSILON)
        qg = jnp.zeros((SPAN, 1), F32)
        for c0 in range(0, di, WIDE):
            cols = slice(c0, c0 + WIDE)
            g = g_ref[:, cols]
            gain = ggain_ref[0:1, cols]
            yn_ref[rows, cols] = (g * r2 * gain).astype(BF16)
            dyn = dot(c_ref[rows, :], wo_ref[:, cols])
            gg_ref[0:1, cols] += jnp.sum(dyn * (g * r2), axis=0, keepdims=True)
            q = dyn * gain
            q_ref[:, cols] = q
            qg = qg + jnp.sum(q * g, axis=-1, keepdims=True)
        out_ref[rows, :] = (x_ref[rows, :].astype(F32) + dot_nt(yn_ref[rows, :], wo_ref[...])).astype(BF16)
        coef = r2 * r2 * r2 * (qg / di)
        rr = jnp.zeros((SPAN, 128), F32)
        dk = jnp.zeros((SPAN, 128), F32)
        ct = cc.astype(F32).T.astype(BF16)
        for c0 in range(0, di, WIDE):
            cols = slice(c0, c0 + WIDE)
            xf = xs_ref[rows, cols].astype(F32)
            ynos = y_ref[:, cols]
            y = ynos + skip_ref[0:1, cols] * xf
            gate = gate_ref[:, cols]
            sg = sigmoid(gate)
            dg = r2 * q_ref[:, cols] - coef * g_ref[:, cols]
            dgate_ref[rows, cols] = (dg * y * (sg * (1.0 + gate * (1.0 - sg)))).astype(BF16)
            dyb = (dg * (gate * sg)).astype(BF16)
            dy_ref[rows, cols] = dyb
            dy = dyb.astype(F32)
            rr = rr + gather_heads(dy * ynos, selt_ref[cols, :])
            dk = dk + gather_heads(dy * xf, selt_ref[cols, :])
            ea = spread_heads(ea_ref[...], sel_ref[:, cols])
            vv_ref[b, :, cols] = dot(ct, (ea * dy).astype(BF16))
        rr_ref[rows, :] = rr
        sk_ref[0:1, :] += jnp.sum(dk, axis=0, keepdims=True)
        return carry

    lax.fori_loop(0, blocks, block_step, 0)
    for c0 in range(0, di, WIDE):
        cols = slice(c0, c0 + WIDE)
        go_ref[:, cols] = dot_tn(c_ref[...], yn_ref[:, cols]).astype(BF16)


def back_kernel(
    heads,
    xs_ref, bc_ref, draw_ref, acs_ref, bs_ref, sin_ref, fresh_ref, dec_ref, ds_ref, vv_ref, dy_ref, rr_ref,
    rawi_ref, raws_ref, ti_ref, ts_ref, dpar_ref, skip_ref, sel_ref, selt_ref, tri_ref, triu_ref,
    dpi_ref, dps_ref, dd_ref, small_ref, tgi_ref, tgs_ref,
    acst_ref, ea_ref, w_ref, dg_ref, dx_ref, dbc_ref,
):
    tokens, di = xs_ref.shape
    seqs, ext, _ = rawi_ref.shape
    span = ext - 16
    blocks = tokens // SPAN
    per = blocks // seqs
    state = bc_ref.shape[1] // 2
    sh = 2 * state
    upper = lax.broadcasted_iota(jnp.int32, (HALF, HALF), 0) <= lax.broadcasted_iota(jnp.int32, (HALF, HALF), 1)
    first = lanes_of((HALF, 128)) < P_SIZE
    first_all = lanes_of((SPAN, 128)) < P_SIZE
    small_ref[...] = jnp.zeros_like(small_ref)
    tgi_ref[...] = jnp.zeros_like(tgi_ref)
    tgs_ref[...] = jnp.zeros_like(tgs_ref)

    def block_step(b, carry):
        rows = block_rows(b, SPAN)
        s = b // per
        j = b - s * per
        acst_ref[...] = acs_ref[rows, :].T
        acs = acs_ref[rows, :]
        bs = bs_ref[rows, :]
        end = acs[SPAN - 1 : SPAN, :]
        ea_ref[...] = packed(jnp.exp2(acs), heads)
        w_ref[...] = packed(jnp.exp2(end - bs), heads)
        bb = bc_ref[rows, :state]
        cc = bc_ref[rows, state:]
        g00 = dot_nt(bb[:HALF], cc[:HALF])
        g01 = dot_nt(bb[:HALF], cc[HALF:])
        g11 = dot_nt(bb[HALF:], cc[HALF:])
        dg_ref[...] = jnp.zeros_like(dg_ref)
        for p in range(di // 128):
            cols = slice(128 * p, 128 * p + 128)
            xp = xs_ref[rows, cols]
            dyp = dy_ref[rows, cols]
            d0, d1 = [], []
            for i, h in enumerate((2 * p, 2 * p + 1)):
                keep = first_all if i == 0 else jnp.logical_not(first_all)
                xm = jnp.where(keep, xp, jnp.zeros_like(xp))
                b0 = bs_ref[block_rows(2 * b, HALF), h : h + 1]
                b1 = bs_ref[block_rows(2 * b + 1, HALF), h : h + 1]
                r0 = acst_ref[h : h + 1, :HALF]
                r1 = acst_ref[h : h + 1, HALF:]
                e00 = jnp.where(upper, jnp.exp2(r0 - b0), 0.0)
                e01 = jnp.exp2(r1 - b0)
                e11 = jnp.where(upper, jnp.exp2(r1 - b1), 0.0)
                m0 = jnp.concatenate([(e00 * g00).astype(BF16), (e01 * g01).astype(BF16)], axis=1)
                m1 = (e11 * g11).astype(BF16)
                d0.append(dot(m0, dyp))
                d1.append(dot(m1, dyp[HALF:]))
                dm0 = dot_nt(xm[:HALF], dyp)
                dm1 = dot_nt(xm[HALF:], dyp[HALF:])
                dg_ref[0] += dm0[:, :HALF] * e00
                dg_ref[1] += dm0[:, HALF:] * e01
                dg_ref[2] += dm1 * e11
            dx_ref[0:HALF, cols] = jnp.where(first, d0[0], d0[1])
            dx_ref[HALF:SPAN, cols] = jnp.where(first, d1[0], d1[1])

        dg00 = dg_ref[0]
        dg01 = dg_ref[1]
        dg11 = dg_ref[2]
        db0 = dot(jnp.concatenate([dg00, dg01], axis=1).astype(BF16), cc)
        db1 = dot(dg11.astype(BF16), cc[HALF:])
        dc0 = dot(dg00.T.astype(BF16), bb[:HALF])
        dc1 = dot(jnp.concatenate([dg01.T, dg11.T], axis=1).astype(BF16), bb)
        db = jnp.concatenate([db0, db1], axis=0)
        dc = jnp.concatenate([dc0, dc1], axis=0)
        rr = rr_ref[rows, :]
        pin = jnp.zeros((SPAN, 128), F32)
        pst = jnp.zeros((SPAN, 128), F32)
        endsum = jnp.zeros((8, 128), F32)
        for c0 in range(0, di, WIDE):
            cols = slice(c0, c0 + WIDE)
            prev = sin_ref[s, :, cols].astype(F32)
            later = dec_ref[s * per, 0:1, cols] * prev + fresh_ref[s * per, :, cols]
            s_in = jnp.where(j == 0, prev, later).astype(BF16)
            dlast = ds_ref[s, :, cols].astype(F32)
            dprev = dec_ref[s * per + per - 1, 0:1, cols] * dlast + vv_ref[s * per + per - 1, :, cols]
            ds = jnp.where(j == per - 1, dlast, dprev).astype(BF16)
            w = spread_heads(w_ref[...], sel_ref[:, cols])
            ea = spread_heads(ea_ref[...], sel_ref[:, cols])
            xf = xs_ref[rows, cols].astype(F32)
            dyf = dy_ref[rows, cols].astype(F32)
            dxs = w * dot(bb, ds)
            dxi = dx_ref[:, cols]
            pin = pin + gather_heads(dxi * xf, selt_ref[cols, :])
            pst = pst + gather_heads(dxs * xf, selt_ref[cols, :])
            both = jnp.sum(ds.astype(F32) * s_in.astype(F32), axis=0, keepdims=True) * dec_ref[b, 0:1, cols]
            endsum = endsum + gather_heads(jnp.broadcast_to(both, (8, WIDE)), selt_ref[cols, :])
            dc = dc + dot_nt((ea * dyf).astype(BF16), s_in)
            db = db + dot_nt((w * xf).astype(BF16), ds)
            dx_ref[:, cols] = dxi + dxs + skip_ref[0:1, cols] * dyf
        dbc_ref[:, :state] = db
        dbc_ref[:, state:] = dc
        pp = pin + pst
        da = cumulate(triu_ref[...], rr - pp, heads) + (endsum[0:1, :] + jnp.sum(pst, axis=0, keepdims=True))
        x = draw_ref[rows, :]
        sg = 1.0 / (1.0 + jnp.exp(-x))
        dt = jnp.maximum(x, 0.0) + jnp.log1p(jnp.exp(-jnp.abs(x)))
        ratio = jnp.where(x < -20.0, 1.0, sg / jnp.maximum(dt, 1e-30))
        ak = dpar_ref[2:3, :]
        dd = da * ak * sg + pp * ratio
        dd_ref[rows, :] = dd.astype(BF16)
        small_ref[0:1, :] += jnp.sum(da * dt * ak, axis=0, keepdims=True)
        small_ref[1:2, :] += jnp.sum(dd, axis=0, keepdims=True)

        def conv_back(raw, par, dact, dpre, tg, cols):
            def step(r, c):
                r0 = pl.multiple_of(r * HALF, HALF)
                v = raw[s, pl.ds(pl.multiple_of(j * SPAN + r0, HALF), HALF + 16), cols]
                sh_v = [v[13 + k : 13 + k + HALF] for k in range(4)]
                pre = par[4:5, cols] + par[0:1, cols] * sh_v[0]
                for k in range(1, 4):
                    pre = pre + par[k : k + 1, cols] * sh_v[k]
                sg = sigmoid(pre)
                dp = dact[pl.ds(r0, HALF), cols] * (sg * (1.0 + pre * (1.0 - sg)))
                dpre[pl.ds(pl.multiple_of(b * SPAN + r0, HALF), HALF), cols] = dp
                for k in range(4):
                    tg[k : k + 1, cols] += jnp.sum(dp * sh_v[k], axis=0, keepdims=True)
                tg[4:5, cols] += jnp.sum(dp, axis=0, keepdims=True)
                return c

            lax.fori_loop(0, SPAN // HALF, step, 0)

        for c0 in range(0, di, 256):
            conv_back(rawi_ref, ti_ref, dx_ref, dpi_ref, tgi_ref, slice(c0, c0 + 256))
        for c0 in range(0, sh, 256):
            conv_back(raws_ref, ts_ref, dbc_ref, dps_ref, tgs_ref, slice(c0, c0 + 256))
        return carry

    lax.fori_loop(0, blocks, block_step, 0)


def last_kernel(
    nt,
    x_ref, c_ref, gain_ref, h_ref, dpi_ref, dps_ref, hi_ref, hs_ref, dd_ref, dgate_ref, ti_ref, ts_ref,
    w1_ref, w2_ref, ws_ref,
    ig_ref, g1_ref, g2_ref, ng_ref,
    din_ref,
):
    tokens, di = dgate_ref.shape
    seqs = hi_ref.shape[0]
    span = tokens // seqs
    sh = dps_ref.shape[1]
    part = w1_ref.shape[1] // nt
    inner = part * nt
    ng_ref[...] = jnp.zeros_like(ng_ref)
    for t in range(nt):
        din_ref[:, part * (t + 1) - 128 : part * (t + 1)] = dd_ref[...]

    def conv_t(dpre, halo, par, c0, to):
        cols = slice(c0, c0 + 128)
        for s in range(seqs):
            for r0 in range(0, span, HALF):
                base = s * span + r0
                v = dpre[base : base + HALF, cols]
                if r0 + HALF < span:
                    nxt = dpre[base + HALF : base + HALF + 8, cols]
                else:
                    nxt = halo[s, :, cols]
                v = jnp.concatenate([v, nxt], axis=0)
                acc = par[3:4, cols] * v[0:HALF]
                for k in range(3):
                    acc = acc + par[k : k + 1, cols] * v[3 - k : 3 - k + HALF]
                din_ref[base : base + HALF, to : to + 128] = acc.astype(BF16)

    for c0 in range(0, di, 128):
        t = c0 // (part - 128)
        conv_t(dpi_ref, hi_ref, ti_ref, c0, part * t + c0 - (part - 128) * t)
    for c0 in range(0, sh, 128):
        conv_t(dps_ref, hs_ref, ts_ref, c0, inner + c0)

    for c0 in range(0, inner, WIDE):
        g1_ref[:, c0 : c0 + WIDE] = dot_tn(h_ref[...], din_ref[:, c0 : c0 + WIDE]).astype(BF16)
    g1_ref[:, inner:] = dot_tn(h_ref[...], din_ref[:, inner:]).astype(BF16)
    for c0 in range(0, di, WIDE):
        g2_ref[:, c0 : c0 + WIDE] = dot_tn(h_ref[...], dgate_ref[:, c0 : c0 + WIDE]).astype(BF16)

    def step(b, carry):
        rows = block_rows(b, SPAN)
        dh = dot_nt(dgate_ref[rows, :], w2_ref[...])
        dh = dh + dot_nt(din_ref[rows, :inner], w1_ref[...])
        dh = dh + dot_nt(din_ref[rows, inner:], ws_ref[...])
        u = x_ref[rows, :].astype(F32)
        r1 = lax.rsqrt(jnp.mean(u * u, axis=-1, keepdims=True) + EPSILON)
        ng_ref[0:1, :] += jnp.sum(dh * u * r1, axis=0, keepdims=True)
        e = dh * gain_ref[...]
        m = jnp.mean(e * u, axis=-1, keepdims=True)
        ig_ref[rows, :] = (c_ref[rows, :].astype(F32) + r1 * e - u * (r1 * r1 * r1 * m)).astype(BF16)
        return carry

    lax.fori_loop(0, tokens // SPAN, step, 0)


MESH = pl.DeviceIdType.MESH


class Sends:
    def __init__(self, send, recv):
        self.send, self.recv, self.used, self.started = send, recv, 0, []

    def make(self, src, dst, to):
        k = self.used
        self.used += 1
        return pltpu.make_async_remote_copy(
            src_ref=src, dst_ref=dst, send_sem=self.send.at[k], recv_sem=self.recv.at[k],
            device_id=to, device_id_type=MESH,
        )

    def start(self, src, dst, to):
        copy = self.make(src, dst, to)
        copy.start()
        self.started.append(copy)
        return copy

    def finish(self):
        for copy in self.started:
            copy.wait_send()


def greet(others):
    barrier = pltpu.get_barrier_semaphore()
    for to in others:
        pl.semaphore_signal(barrier, inc=1, device_id=to, device_id_type=MESH)
    pl.semaphore_wait(barrier, len(others))


def place():
    z = lax.axis_index("tensor")
    d = lax.axis_index("dp")
    core = lax.rem(d, 2)
    x = lax.rem(d // 2, 2)
    y = d // 4
    return z, d, core, x, y


def xor_peer(core, x, y, k):
    c1 = 1 - core if k & 1 else core
    x1 = 1 - x if k & 2 else x
    y1 = 1 - y if k & 4 else y
    return y1 * 4 + x1 * 2 + c1


def dp_rows(d, size, part=None):
    if part is None:
        return pl.ds(pl.multiple_of(d * size, 16), size)
    return pl.ds(pl.multiple_of(d * size + part * (size // 2), 16), size // 2)


def columns(t, size):
    return pl.ds(pl.multiple_of(t * size, 128), size)


class Gather:
    MESSAGES = 13

    def __init__(self, sends, nt, shard, full, here):
        self.sends, self.nt, self.shard, self.full = sends, nt, shard, full
        self.z, self.d, self.core, self.x, self.y = here
        self.rows, self.width = shard.shape

    def to(self, k):
        return {"dp": xor_peer(self.core, self.x, self.y, k)}

    def ref(self, k, part=None):
        return self.full.at[dp_rows(xor_peer(self.core, self.x, self.y, k), self.rows, part), :]

    def begin(self, sem):
        mine = self.full.at[dp_rows(self.d, self.rows), columns(self.z, self.width)]
        self.local = pltpu.make_async_copy(self.shard, mine, sem)
        self.local.start()
        self.zs = []
        for dz in range(1, self.nt):
            to = {"tensor": lax.rem(self.z + dz, self.nt)}
            self.zs.append(self.sends.start(self.shard, mine, to))

    def column(self):
        self.local.wait()
        for copy in self.zs:
            copy.wait_recv()
        own_a, own_b = self.ref(0, 0), self.ref(0, 1)
        self.x0 = self.sends.start(own_a, own_a, self.to(2))
        self.y0 = self.sends.start(own_b, own_b, self.to(4))
        self.c = [self.sends.start(self.ref(0), self.ref(0), self.to(1))]
        self.y1 = self.sends.start(own_a, own_a, self.to(4))
        self.x1 = self.sends.start(own_b, own_b, self.to(2))

    def forward(self):
        self.x0.wait_recv()
        self.y2 = self.sends.start(self.ref(2, 0), self.ref(2, 0), self.to(4))
        self.y0.wait_recv()
        self.x2 = self.sends.start(self.ref(4, 1), self.ref(4, 1), self.to(2))
        self.x1.wait_recv()
        self.c.append(self.sends.start(self.ref(2), self.ref(2), self.to(1)))
        self.y1.wait_recv()
        self.c.append(self.sends.start(self.ref(4), self.ref(4), self.to(1)))

    def corner(self):
        self.y2.wait_recv()
        self.x2.wait_recv()
        self.c.append(self.sends.start(self.ref(6), self.ref(6), self.to(1)))

    def finish(self):
        for copy in self.c:
            copy.wait_recv()


def gather_kernel(
    nt, w1_ref, w2_ref, w3_ref, ws_ref, par_ref, xl_ref,
    f1_ref, f2_ref, f3_ref, fs_ref, fp_ref, xh_ref,
    send, recv, local,
):
    here = place()
    z, d, core, x, y = here
    sends = Sends(send, recv)
    others = [{"tensor": lax.rem(z + dz, nt)} for dz in range(1, nt)]
    others += [{"dp": xor_peer(core, x, y, k)} for k in range(1, 8)]
    greet(others)
    rows = ws_ref.shape[0]
    secs = [Gather(sends, nt, a, b, here) for a, b in ((w1_ref, f1_ref), (w2_ref, f2_ref), (w3_ref, f3_ref))]
    secs[0].begin(local.at[0])
    mine = fs_ref.at[dp_rows(d, rows), :]
    own = [pltpu.make_async_copy(ws_ref, mine, local.at[3]), pltpu.make_async_copy(par_ref, fp_ref.at[z], local.at[4])]
    for copy in own:
        copy.start()
    got = [sends.start(ws_ref, mine, {"dp": xor_peer(core, x, y, k)}) for k in range(1, 8)]
    got += [sends.start(par_ref, fp_ref.at[z], {"tensor": lax.rem(z + dz, nt)}) for dz in range(1, nt)]
    edge = sends.make(xl_ref, xh_ref, {"tensor": lax.rem(z + 1, nt)})

    @pl.when(z < nt - 1)
    def _():
        edge.start()

    for k in (1, 2):
        secs[k].begin(local.at[k])
    for sec in secs:
        sec.column()
        sec.forward()
    for sec in secs:
        sec.corner()
    for copy in own:
        copy.wait()
    for copy in got:
        copy.wait_recv()

    @pl.when(z > 0)
    def _():
        edge.wait_recv()

    @pl.when(z == 0)
    def _():
        xh_ref[...] = jnp.zeros_like(xh_ref)

    for sec in secs:
        sec.finish()
    sends.finish()

    @pl.when(z < nt - 1)
    def _():
        edge.wait_send()


def chain_kernel(nt, by, mine_ref, whole_ref, got_ref, out_ref, send, recv):
    z = lax.axis_index("tensor")
    seqs, _, di = got_ref.shape
    has_prev = z > 0 if by > 0 else z < nt - 1
    has_next = z < nt - 1 if by > 0 else z > 0
    prev = {"tensor": lax.rem(z - by + nt, nt)}
    nxt = {"tensor": lax.rem(z + by + nt, nt)}
    greet((prev, nxt))

    @pl.when(jnp.logical_not(has_prev))
    def _():
        got_ref[...] = jnp.zeros_like(got_ref)

    sends = Sends(send, recv)
    copies = []
    for s in range(seqs):
        for c0 in range(0, di, WIDE):
            cols = slice(c0, c0 + WIDE)
            copy = sends.make(out_ref.at[s, :, cols], got_ref.at[s, :, cols], nxt)
            copies.append(copy)

            @pl.when(has_prev)
            def _(copy=copy):
                copy.wait_recv()

            @pl.when(has_next)
            def _(copy=copy, s=s, cols=cols):
                out_ref[s, :, cols] = (
                    mine_ref[s, :, cols] + whole_ref[s, 0:1, cols] * got_ref[s, :, cols].astype(F32)
                ).astype(BF16)
                copy.start()

    for copy in copies:

        @pl.when(has_next)
        def _(copy=copy):
            copy.wait_send()


class Reduce:
    MESSAGES = 24

    @staticmethod
    def scratch(rows, width, nt, wz):
        half = rows // 2
        shapes = [(4, rows, width)] * 2 + [(2, half, width)] * 4 + [(half, width)] * 2 + [(rows, width), (nt, rows, wz)]
        return [pltpu.VMEM(s, BF16) for s in shapes]

    def __init__(self, sends, nt, g, bufs, cuts, here):
        self.sends, self.nt, self.g, self.cuts = sends, nt, g, cuts
        self.rc, self.p, self.ra, self.rb, self.qa, self.qb, self.ta, self.tb, self.f, self.rz = bufs
        self.z, self.d, self.core, self.x, self.y = here
        self.rows = self.p.shape[1]
        self.half = self.rows // 2

    def to(self, k):
        return {"dp": xor_peer(self.core, self.x, self.y, k)}

    def begin(self):
        self.got = []
        for q in range(4):
            src = self.g.at[dp_rows(2 * q + 1 - self.core, self.rows), :]
            self.got.append(self.sends.start(src, self.rc.at[q], self.to(1)))

    def first(self):
        h = self.half
        for q in range(4):
            self.got[q].wait_recv()
            own = self.g[dp_rows(2 * q + self.core, self.rows), :].astype(F32)
            self.p[q] = (own + self.rc[q].astype(F32)).astype(BF16)
        self.a = []
        self.b = []
        for i in range(2):
            src = self.p.at[2 * i + 1 - self.x, pl.ds(0, h), :]
            self.a.append(self.sends.start(src, self.ra.at[i], self.to(2)))
            src = self.p.at[2 * (1 - self.y) + i, pl.ds(h, h), :]
            self.b.append(self.sends.start(src, self.rb.at[i], self.to(4)))

    def second(self):
        h = self.half
        for i in range(2):
            self.a[i].wait_recv()
            own = self.p[2 * i + self.x, 0:h, :].astype(F32)
            self.qa[i] = (own + self.ra[i].astype(F32)).astype(BF16)
            self.b[i].wait_recv()
            own = self.p[2 * self.y + i, h:, :].astype(F32)
            self.qb[i] = (own + self.rb[i].astype(F32)).astype(BF16)
        self.a2 = self.sends.start(self.qa.at[1 - self.y], self.ta, self.to(4))
        self.b2 = self.sends.start(self.qb.at[1 - self.x], self.tb, self.to(2))

    def third(self):
        h = self.half
        self.a2.wait_recv()
        self.f[0:h, :] = (self.qa[self.y].astype(F32) + self.ta[...].astype(F32)).astype(BF16)
        self.b2.wait_recv()
        self.f[h:, :] = (self.qb[self.x].astype(F32) + self.tb[...].astype(F32)).astype(BF16)
        self.zs = []
        at = 0
        for first, size, by_t in self.cuts:
            dst = self.rz.at[self.z, :, pl.ds(at, size)]
            for dz in range(1, self.nt):
                t = lax.rem(self.z + dz, self.nt)
                src = self.f.at[:, columns(t, size) if by_t else pl.ds(first, size)]
                self.zs.append(self.sends.start(src, dst, {"tensor": t}))
            self.rz[self.z, :, at : at + size] = self.f[:, columns(self.z, size) if by_t else pl.ds(first, size)]
            at += size

    def last(self):
        for copy in self.zs:
            copy.wait_recv()
        total = self.rz[0].astype(F32)
        for t in range(1, self.nt):
            total = total + self.rz[t].astype(F32)
        return total


class SmallSum:
    MESSAGES = 6

    @staticmethod
    def scratch(shape, nt):
        return [pltpu.VMEM((3,) + shape, F32), pltpu.VMEM((3,) + shape, F32), pltpu.VMEM((nt,) + shape, F32)]

    def __init__(self, sends, nt, v, bufs, here):
        self.sends, self.nt, self.v = sends, nt, v
        self.own, self.got, self.rz = bufs
        self.z, self.d, self.core, self.x, self.y = here

    def begin(self):
        self.own[0] = self.v[...]
        self.copy = self.sends.start(self.own.at[0], self.got.at[0], {"dp": xor_peer(self.core, self.x, self.y, 1)})

    def step(self, k):
        self.copy.wait_recv()
        total = self.own[k - 1] + self.got[k - 1]
        if k < 3:
            self.own[k] = total
            self.copy = self.sends.start(
                self.own.at[k], self.got.at[k], {"dp": xor_peer(self.core, self.x, self.y, 2**k)}
            )
        else:
            self.rz[self.z] = total
            self.zs = [
                self.sends.start(self.rz.at[self.z], self.rz.at[self.z], {"tensor": lax.rem(self.z + dz, self.nt)})
                for dz in range(1, self.nt)
            ]

    def last(self):
        for copy in self.zs:
            copy.wait_recv()
        total = self.rz[0]
        for t in range(1, self.nt):
            total = total + self.rz[t]
        return total


def reduce_kernel(nt, cuts1, cuts, g1_ref, g2_ref, g3_ref, sm_ref, o1_ref, os_ref, o2_ref, o3_ref, om_ref, *rest):
    here = place()
    z, d, core, x, y = here
    send, recv = rest[-2:]
    sends = Sends(send, recv)
    others = [{"tensor": lax.rem(z + dz, nt)} for dz in range(1, nt)]
    others += [{"dp": xor_peer(core, x, y, k)} for k in (1, 2, 4)]
    greet(others)
    secs = [
        Reduce(sends, nt, g, rest[10 * i : 10 * i + 10], c, here)
        for i, (g, c) in enumerate(((g1_ref, cuts1), (g2_ref, cuts), (g3_ref, cuts)))
    ]
    small = SmallSum(sends, nt, sm_ref, rest[30:33], here)
    for sec in secs:
        sec.begin()
    small.begin()
    for sec in secs:
        sec.first()
    small.step(1)
    for sec in secs:
        sec.second()
    small.step(2)
    for sec in secs:
        sec.third()
    small.step(3)
    total = secs[0].last()
    width = o1_ref.shape[1]
    o1_ref[...] = total[:, :width]
    os_ref[...] = total[:, width:]
    o2_ref[...] = secs[1].last()
    o3_ref[...] = secs[2].last()
    om_ref[...] = small.last()
    sends.finish()


def call(kernel, outs, scratch, *args, name, collective_id=None):
    params = dict(vmem_limit_bytes=VMEM_LIMIT)
    if collective_id is not None:
        params.update(collective_id=collective_id, has_side_effects=True)
    return pl.pallas_call(
        kernel,
        out_shape=[jax.ShapeDtypeStruct(s, d) for s, d in outs],
        in_specs=[pl.BlockSpec(memory_space=pltpu.VMEM)] * len(args),
        out_specs=[pl.BlockSpec(memory_space=pltpu.VMEM)] * len(outs),
        scratch_shapes=[s if not isinstance(s, tuple) else pltpu.VMEM(*s) for s in scratch],
        compiler_params=pltpu.CompilerParams(**params),
        name=name,
    )(*args)


def semaphores(n):
    return [pltpu.SemaphoreType.DMA((n,)), pltpu.SemaphoreType.DMA((n,))]


def shifted(v, axis, by):
    n = lax.axis_size(axis)
    return lax.ppermute(v, axis, [(i, i + by) for i in range(n) if 0 <= i + by < n])


def gather_all(nt, nd, w1, w2, w3, ws, par, edge):
    rows = ws.shape[0]
    if nd == 8:
        full = lambda w: ((rows * nd, w.shape[1] * nt), BF16)
        return call(
            functools.partial(gather_kernel, nt),
            [full(w1), full(w2), full(w3), ((rows * nd, ws.shape[1]), BF16), ((nt, *par.shape), F32), (edge.shape, BF16)],
            semaphores(3 * Gather.MESSAGES + 7 + nt) + [pltpu.SemaphoreType.DMA((5,))],
            w1, w2, w3, ws, par, edge, name="gather", collective_id=0,
        )
    both = ("tensor", "dp")
    pack = lax.all_gather(jnp.concatenate([w1, w2, w3], axis=1), both, axis=0).reshape(nt, nd * rows, -1)
    out, at = [], 0
    for w in (w1, w2, w3):
        k = w.shape[1]
        out.append(pack[:, :, at : at + k].transpose(1, 0, 2).reshape(nd * rows, nt * k))
        at += k
    out.append(lax.all_gather(ws, "dp", axis=0, tiled=True))
    out.append(lax.all_gather(par, "tensor", axis=0))
    return (*out, shifted(edge, "tensor", 1))


def chain(nt, by, mine, whole):
    seqs, state, di = mine.shape
    return call(
        functools.partial(chain_kernel, nt, by),
        [(mine.shape, BF16)],
        [(mine.shape, BF16)] + semaphores(seqs * di // WIDE),
        mine, whole, name="states" if by > 0 else "states_back", collective_id=1 if by > 0 else 2,
    )[0]


def reduce_all(nt, nd, g1, g2, g3, sm, sh):
    dim = g1.shape[0]
    rows = dim // nd
    part = (g1.shape[1] - sh) // nt
    dcol = g2.shape[1] // nt
    if nd == 8:
        cuts1 = ((0, part, True), (part * nt, sh, False))
        cuts = ((0, dcol, True),)
        scratch = []
        for g, w in ((g1, part + sh), (g2, dcol), (g3, dcol)):
            scratch += Reduce.scratch(rows, g.shape[1], nt, w)
        scratch += SmallSum.scratch(sm.shape, nt)
        count = 3 * Reduce.MESSAGES + SmallSum.MESSAGES
        return call(
            functools.partial(reduce_kernel, nt, cuts1, cuts),
            [((rows, part), F32), ((rows, sh), F32), ((rows, dcol), F32), ((rows, dcol), F32), (sm.shape, F32)],
            scratch + semaphores(count),
            g1, g2, g3, sm, name="reduce", collective_id=3,
        )
    both = ("tensor", "dp")
    parts = [g[:, : nt * w].reshape(dim, nt, w).transpose(1, 0, 2) for g, w in ((g1, part), (g2, dcol), (g3, dcol))]
    big = jnp.concatenate(parts, axis=2).reshape(nt * nd, rows, -1)
    big = lax.psum_scatter(big, both, scatter_dimension=0).astype(F32)
    shared = g1[:, nt * part :].reshape(nd, rows, sh).astype(F32)
    shared = lax.psum(lax.psum_scatter(shared, "dp", scatter_dimension=0), "tensor")
    return big[:, :part], shared, big[:, part : part + dcol], big[:, part + dcol :], lax.psum(sm, both)


def local(
    block_input, norm_gain, input_gate_inner_weight, input_shared_weight, input_delta_weight, conv_inner, shift_inner,
    conv_shared, shift_shared, decay_log, delta_bias, skip_gain, gated_gain, output_projection_weight, cotangent,
):
    nt = lax.axis_size("tensor")
    nd = lax.axis_size("dp")
    me = lax.axis_index("tensor")
    seqs, span, dim = block_input.shape
    tokens = seqs * span
    blocks = tokens // SPAN
    rows, _, dcol = input_gate_inner_weight.shape
    di = dcol * nt
    sh = input_shared_weight.shape[1]
    state = sh // 2
    hloc = input_delta_weight.shape[1]
    heads = hloc * nt

    delta_w = lax.dynamic_update_slice(jnp.zeros((rows, 128), BF16), input_delta_weight, (0, me * hloc))
    w1 = jnp.concatenate([input_gate_inner_weight[:, 1], delta_w], axis=1)
    w2 = input_gate_inner_weight[:, 0]
    w3 = output_projection_weight.T
    head = jnp.stack([decay_log, delta_bias, skip_gain])
    par = jnp.concatenate([
        conv_inner.astype(F32), shift_inner.astype(F32)[None], gated_gain[None], jnp.zeros((2, dcol), F32),
        jnp.pad(head, ((0, 5), (0, dcol - hloc)))], axis=0)
    w1, w2, w3, ws, par, xh = gather_all(
        nt, nd, w1, w2, w3, input_shared_weight, par, block_input[:, span - 16 :].reshape(seqs * 16, dim)
    )
    chan = par[:, :8].transpose(1, 0, 2).reshape(8, di)
    head = par[:, 8:11, :hloc].transpose(1, 0, 2).reshape(3, heads)
    ti = chan
    ts = jnp.pad(jnp.concatenate([conv_shared.astype(F32), shift_shared.astype(F32)[None]], axis=0), ((0, 3), (0, 0)))
    ak = -jnp.exp(head[0])
    dpar = jnp.pad(jnp.stack([head[1], ak * LOG2E, ak]), ((0, 5), (0, 128 - heads)))
    ggain = chan[5:6]
    skip = jnp.repeat(head[2], P_SIZE)[None]
    gain = norm_gain[None]

    lane = jnp.arange(128)
    owner = jnp.arange(di) // P_SIZE
    sel = ((lane[:, None] % 32 == owner[None]) & (lane[:, None] < 64)).astype(BF16)
    selt = (lane[None] == owner[:, None]).astype(BF16)
    at = jnp.arange(SPAN)
    tri = (at[:, None] >= at[None]).astype(BF16)
    triu = tri.T

    x = block_input.reshape(tokens, dim)
    c = cotangent.reshape(tokens, dim)

    h, rawi, raws, xs, bc, draw, acs, bs, fresh, dec = call(
        functools.partial(front_kernel, heads, nt),
        [((tokens, dim), BF16), ((seqs, span + 16, di), F32), ((seqs, span + 16, sh), F32), ((tokens, di), BF16),
         ((tokens, sh), BF16), ((tokens, 128), F32), ((tokens, 128), F32), ((tokens, 128), F32),
         ((blocks, state, di), F32), ((blocks, 8, di), F32)],
        [((seqs * 16, dim), BF16), ((SPAN, 128), BF16)],
        x, xh, gain, w1, ws, ti, ts, dpar, sel, tri, name="front",
    )

    fr = fresh.reshape(seqs, blocks // seqs, state, di)
    de = dec.reshape(seqs, blocks // seqs, 8, di)
    whole, mine = de[:, 0], fr[:, 0]
    for j in range(1, blocks // seqs):
        mine = de[:, j, 0:1] * mine + fr[:, j]
        whole = de[:, j] * whole
    sin = chain(nt, 1, mine, whole)

    out, yn, dgate, dy, rr, vv, ggg, skg, g3 = call(
        functools.partial(mid_kernel, heads),
        [((tokens, dim), BF16), ((tokens, di), BF16), ((tokens, di), BF16), ((tokens, di), BF16), ((tokens, 128), F32),
         ((blocks, state, di), F32), ((8, di), F32), ((8, 128), F32), ((dim, di), BF16)],
        [((SPAN, di), F32)] * 4 + [((128, SPAN), F32)] * 2 + [((SPAN, 128), BF16)],
        x, c, h, w2, w3, ggain, skip, xs, bc, acs, bs, sin, fresh, dec, sel, selt, name="mid",
    )

    vr = vv.reshape(seqs, blocks // seqs, state, di)
    mine = vr[:, blocks // seqs - 1]
    for j in range(blocks // seqs - 2, -1, -1):
        mine = de[:, j, 0:1] * mine + vr[:, j]
    ds = chain(nt, -1, mine, whole)

    dpi, dps, dd, small, tgi, tgs = call(
        functools.partial(back_kernel, heads),
        [((tokens, di), F32), ((tokens, sh), F32), ((tokens, 128), BF16), ((8, 128), F32), ((8, di), F32), ((8, sh), F32)],
        [((128, SPAN), F32), ((SPAN, 128), BF16), ((SPAN, 128), BF16), ((3, HALF, HALF), F32), ((SPAN, di), F32),
         ((SPAN, sh), F32)],
        xs, bc, draw, acs, bs, sin, fresh, dec, ds, vv, dy, rr, rawi, raws, ti, ts, dpar, skip, sel, selt, tri, triu,
        name="back",
    )

    hi = shifted(dpi.reshape(seqs, span, di)[:, :8], "tensor", -1)
    hs = shifted(dps.reshape(seqs, span, sh)[:, :8], "tensor", -1)
    ig, g1, g2, ng = call(
        functools.partial(last_kernel, nt),
        [((tokens, dim), BF16), ((dim, w1.shape[1] + sh), BF16), ((dim, di), BF16), ((8, dim), F32)],
        [((tokens, w1.shape[1] + sh), BF16)],
        x, c, gain, h, dpi, dps, hi, hs, dd, dgate, ti, ts, w1, w2, ws, name="last",
    )

    sm = jnp.concatenate([
        tgi[:5].reshape(-1), ggg[0], ng[0], tgs[:5].reshape(-1), small[0], small[1], skg[0],
        jnp.zeros(8 * di - 6 * di - dim - 5 * sh - 3 * 128, F32)]).reshape(8, di)
    g1, gs, g2, g3, sm = reduce_all(nt, nd, g1, g2, g3, sm, sh)
    sm = sm.reshape(-1)
    cut = lambda k: lax.dynamic_slice_in_dim(sm, k * di + me * dcol, dcol)
    at = 6 * di
    ng = sm[at : at + dim]
    tgs = sm[at + dim : at + dim + 5 * sh].reshape(5, sh)
    at = at + dim + 5 * sh
    hcut = lambda k: lax.dynamic_slice_in_dim(sm, at + 128 * k + me * hloc, hloc)
    return (
        out.reshape(block_input.shape),
        ig.reshape(block_input.shape),
        ng,
        jnp.stack([g2, g1[:, :dcol]], axis=1),
        gs,
        lax.dynamic_slice_in_dim(g1[:, dcol:], me * hloc, hloc, axis=1),
        jnp.stack([cut(k) for k in range(4)]),
        cut(4),
        tgs[:4],
        tgs[4],
        hcut(0),
        hcut(1),
        hcut(2),
        cut(5),
        g3.T,
    )


def solution(mesh):
    placed = (
        P("dp", "tensor", None), P(), P("dp", None, "tensor"), P("dp", None), P("dp", "tensor"), P(None, "tensor"),
        P("tensor"), P(), P(), P("tensor"), P("tensor"), P("tensor"), P("tensor"), P("tensor", "dp"),
        P("dp", "tensor", None),
    )
    return jax.shard_map(
        local,
        mesh=mesh,
        in_specs=placed,
        out_specs=(
            P("dp", "tensor", None), P("dp", "tensor", None), P(), P("dp", None, "tensor"), P("dp", None),
            P("dp", "tensor"), P(None, "tensor"), P("tensor"), P(), P(), P("tensor"), P("tensor"), P("tensor"),
            P("tensor"), P("tensor", "dp"),
        ),
        check_vma=False,
    )
```

```python
import functools

import jax
import jax.numpy as jnp
from jax import lax
from jax.experimental import pallas as pl
from jax.experimental.pallas import tpu as pltpu
from jax.sharding import PartitionSpec as P

P_SIZE = 64
SPAN = 256
HALF = SPAN // 2
EPSILON = 1e-05
LOG2E = 1.4426950408889634
F32 = jnp.float32
BF16 = jnp.bfloat16
VMEM_LIMIT = 60 * 1024 * 1024
WIDE = 512


def dot(a, b):
    return jnp.dot(a, b, preferred_element_type=F32)


def dot_nt(a, b):
    return lax.dot_general(a, b, (((1,), (1,)), ((), ())), preferred_element_type=F32)


def dot_tn(a, b):
    return lax.dot_general(a, b, (((0,), (0,)), ((), ())), preferred_element_type=F32)


def sigmoid(v):
    return 0.5 * jnp.tanh(0.5 * v) + 0.5


def split2(v):
    hi = v.astype(BF16)
    return hi, (v - hi.astype(F32)).astype(BF16)


def lanes_of(shape):
    return lax.broadcasted_iota(jnp.int32, shape, len(shape) - 1)


def packed(v, heads):
    v = jnp.where(lanes_of(v.shape) < heads, v, 0.0)
    hi = v.astype(BF16).astype(F32)
    low = (v - hi).astype(BF16).astype(F32)
    return (hi + pltpu.roll(low, 32, 1)).astype(BF16)


def spread_heads(pk, sel):
    return dot(pk, sel)


def gather_heads(v, selt):
    hi, low = split2(v)
    return dot(hi, selt) + dot(low, selt)


def cumulate(tri, v, heads):
    v = jnp.where(lanes_of(v.shape) < heads, v, 0.0)
    p0 = v.astype(BF16).astype(F32)
    r = v - p0
    p1 = r.astype(BF16).astype(F32)
    p2 = r - p1
    pk = (p0 + pltpu.roll(p1, 32, 1) + pltpu.roll(p2, 64, 1)).astype(BF16)
    s = dot(tri, pk)
    n = s.shape[1]
    s = s + pltpu.roll(s, n - 32, 1) + pltpu.roll(s, n - 64, 1)
    return jnp.where(lanes_of(v.shape) < heads, s, 0.0)


def block_rows(b, size):
    return pl.ds(pl.multiple_of(b * size, size), size)


MESH = pl.DeviceIdType.MESH


class Sends:
    def __init__(self, send, recv):
        self.send, self.recv, self.used, self.started = send, recv, 0, []

    def make(self, src, dst, to):
        k = self.used
        self.used += 1
        return pltpu.make_async_remote_copy(
            src_ref=src, dst_ref=dst, send_sem=self.send.at[k], recv_sem=self.recv.at[k],
            device_id=to, device_id_type=MESH,
        )

    def start(self, src, dst, to):
        copy = self.make(src, dst, to)
        copy.start()
        self.started.append(copy)
        return copy

    def finish(self):
        for copy in self.started:
            copy.wait_send()


def greet(others):
    barrier = pltpu.get_barrier_semaphore()
    for to in others:
        pl.semaphore_signal(barrier, inc=1, device_id=to, device_id_type=MESH)
    pl.semaphore_wait(barrier, len(others))


def place():
    z = lax.axis_index("tensor")
    d = lax.axis_index("dp")
    core = lax.rem(d, 2)
    x = lax.rem(d // 2, 2)
    y = d // 4
    return z, d, core, x, y


def xor_peer(core, x, y, k):
    c1 = 1 - core if k & 1 else core
    x1 = 1 - x if k & 2 else x
    y1 = 1 - y if k & 4 else y
    return y1 * 4 + x1 * 2 + c1


def dp_rows(d, size, part=None):
    if part is None:
        return pl.ds(pl.multiple_of(d * size, 16), size)
    return pl.ds(pl.multiple_of(d * size + part * (size // 2), 16), size // 2)


def columns(t, size):
    return pl.ds(pl.multiple_of(t * size, 128), size)


def cut_at(base, size, by_t, t):
    return pl.ds(pl.multiple_of(base + t * size, 128), size) if by_t else pl.ds(base, size)


class Gather:
    MESSAGES = 13

    def __init__(self, sends, nt, shard, full, here):
        self.sends, self.nt, self.shard, self.full = sends, nt, shard, full
        self.z, self.d, self.core, self.x, self.y = here
        self.rows, self.width = shard.shape

    def to(self, k):
        return {"dp": xor_peer(self.core, self.x, self.y, k)}

    def ref(self, k, part=None):
        return self.full.at[dp_rows(xor_peer(self.core, self.x, self.y, k), self.rows, part), :]

    def begin(self, sem):
        mine = self.full.at[dp_rows(self.d, self.rows), columns(self.z, self.width)]
        self.local = pltpu.make_async_copy(self.shard, mine, sem)
        self.local.start()
        self.zs = []
        for dz in range(1, self.nt):
            to = {"tensor": lax.rem(self.z + dz, self.nt)}
            self.zs.append(self.sends.start(self.shard, mine, to))

    def column(self):
        self.local.wait()
        for copy in self.zs:
            copy.wait_recv()
        own_a, own_b = self.ref(0, 0), self.ref(0, 1)
        self.x0 = self.sends.start(own_a, own_a, self.to(2))
        self.y0 = self.sends.start(own_b, own_b, self.to(4))
        self.c = [self.sends.start(self.ref(0), self.ref(0), self.to(1))]
        self.y1 = self.sends.start(own_a, own_a, self.to(4))
        self.x1 = self.sends.start(own_b, own_b, self.to(2))

    def forward(self):
        self.x0.wait_recv()
        self.y2 = self.sends.start(self.ref(2, 0), self.ref(2, 0), self.to(4))
        self.y0.wait_recv()
        self.x2 = self.sends.start(self.ref(4, 1), self.ref(4, 1), self.to(2))
        self.x1.wait_recv()
        self.c.append(self.sends.start(self.ref(2), self.ref(2), self.to(1)))
        self.y1.wait_recv()
        self.c.append(self.sends.start(self.ref(4), self.ref(4), self.to(1)))

    def corner(self):
        self.y2.wait_recv()
        self.x2.wait_recv()
        self.c.append(self.sends.start(self.ref(6), self.ref(6), self.to(1)))

    def finish(self):
        for copy in self.c:
            copy.wait_recv()


def chain_kernel(nt, by, mine_ref, whole_ref, got_ref, out_ref, send, recv):
    z = lax.axis_index("tensor")
    seqs, _, di = got_ref.shape
    has_prev = z > 0 if by > 0 else z < nt - 1
    has_next = z < nt - 1 if by > 0 else z > 0
    prev = {"tensor": lax.rem(z - by + nt, nt)}
    nxt = {"tensor": lax.rem(z + by + nt, nt)}
    greet((prev, nxt))

    @pl.when(jnp.logical_not(has_prev))
    def _():
        got_ref[...] = jnp.zeros_like(got_ref)

    sends = Sends(send, recv)
    copies = []
    for s in range(seqs):
        for c0 in range(0, di, WIDE):
            cols = slice(c0, c0 + WIDE)
            copy = sends.make(out_ref.at[s, :, cols], got_ref.at[s, :, cols], nxt)
            copies.append(copy)

            @pl.when(has_prev)
            def _(copy=copy):
                copy.wait_recv()

            @pl.when(has_next)
            def _(copy=copy, s=s, cols=cols):
                out_ref[s, :, cols] = (
                    mine_ref[s, :, cols] + whole_ref[s, 0:1, cols] * got_ref[s, :, cols].astype(F32)
                ).astype(BF16)
                copy.start()

    for copy in copies:

        @pl.when(has_next)
        def _(copy=copy):
            copy.wait_send()


class Reduce:
    MESSAGES = 24

    @staticmethod
    def scratch(rows, width, nt, wz):
        half = rows // 2
        shapes = [(4, rows, width)] * 2 + [(2, half, width)] * 4 + [(half, width)] * 2 + [(rows, width), (nt, rows, wz)]
        return [pltpu.VMEM(s, BF16) for s in shapes]

    def __init__(self, sends, nt, g, bufs, cuts, here):
        self.sends, self.nt, self.g, self.cuts = sends, nt, g, cuts
        self.rc, self.p, self.ra, self.rb, self.qa, self.qb, self.ta, self.tb, self.f, self.rz = bufs
        self.z, self.d, self.core, self.x, self.y = here
        self.rows = self.p.shape[1]
        self.half = self.rows // 2

    def to(self, k):
        return {"dp": xor_peer(self.core, self.x, self.y, k)}

    def begin(self):
        self.got = []
        for q in range(4):
            src = self.g.at[dp_rows(2 * q + 1 - self.core, self.rows), :]
            self.got.append(self.sends.start(src, self.rc.at[q], self.to(1)))

    def first(self):
        h = self.half
        for q in range(4):
            self.got[q].wait_recv()
            own = self.g[dp_rows(2 * q + self.core, self.rows), :].astype(F32)
            self.p[q] = (own + self.rc[q].astype(F32)).astype(BF16)
        self.a = []
        self.b = []
        for i in range(2):
            src = self.p.at[2 * i + 1 - self.x, pl.ds(0, h), :]
            self.a.append(self.sends.start(src, self.ra.at[i], self.to(2)))
            src = self.p.at[2 * (1 - self.y) + i, pl.ds(h, h), :]
            self.b.append(self.sends.start(src, self.rb.at[i], self.to(4)))

    def second(self):
        h = self.half
        for i in range(2):
            self.a[i].wait_recv()
            own = self.p[2 * i + self.x, 0:h, :].astype(F32)
            self.qa[i] = (own + self.ra[i].astype(F32)).astype(BF16)
            self.b[i].wait_recv()
            own = self.p[2 * self.y + i, h:, :].astype(F32)
            self.qb[i] = (own + self.rb[i].astype(F32)).astype(BF16)
        self.a2 = self.sends.start(self.qa.at[1 - self.y], self.ta, self.to(4))
        self.b2 = self.sends.start(self.qb.at[1 - self.x], self.tb, self.to(2))

    def third(self):
        h = self.half
        self.a2.wait_recv()
        self.f[0:h, :] = (self.qa[self.y].astype(F32) + self.ta[...].astype(F32)).astype(BF16)
        self.b2.wait_recv()
        self.f[h:, :] = (self.qb[self.x].astype(F32) + self.tb[...].astype(F32)).astype(BF16)
        self.zs = []
        at = 0
        for base, size, by_t in self.cuts:
            dst = self.rz.at[self.z, :, pl.ds(at, size)]
            for dz in range(1, self.nt):
                t = lax.rem(self.z + dz, self.nt)
                src = self.f.at[:, cut_at(base, size, by_t, t)]
                self.zs.append(self.sends.start(src, dst, {"tensor": t}))
            self.rz[self.z, :, at : at + size] = self.f[:, cut_at(base, size, by_t, self.z)]
            at += size

    def last(self):
        for copy in self.zs:
            copy.wait_recv()
        total = self.rz[0].astype(F32)
        for t in range(1, self.nt):
            total = total + self.rz[t].astype(F32)
        return total


class SmallSum:
    MESSAGES = 6

    @staticmethod
    def scratch(shape, nt):
        return [pltpu.VMEM((3,) + shape, F32), pltpu.VMEM((3,) + shape, F32), pltpu.VMEM((nt,) + shape, F32)]

    def __init__(self, sends, nt, v, bufs, here):
        self.sends, self.nt, self.v = sends, nt, v
        self.own, self.got, self.rz = bufs
        self.z, self.d, self.core, self.x, self.y = here

    def begin(self):
        self.own[0] = self.v[...]
        self.copy = self.sends.start(self.own.at[0], self.got.at[0], {"dp": xor_peer(self.core, self.x, self.y, 1)})

    def step(self, k):
        self.copy.wait_recv()
        total = self.own[k - 1] + self.got[k - 1]
        if k < 3:
            self.own[k] = total
            self.copy = self.sends.start(
                self.own.at[k], self.got.at[k], {"dp": xor_peer(self.core, self.x, self.y, 2**k)}
            )
        else:
            self.rz[self.z] = total
            self.zs = [
                self.sends.start(self.rz.at[self.z], self.rz.at[self.z], {"tensor": lax.rem(self.z + dz, self.nt)})
                for dz in range(1, self.nt)
            ]

    def last(self):
        for copy in self.zs:
            copy.wait_recv()
        total = self.rz[0]
        for t in range(1, self.nt):
            total = total + self.rz[t]
        return total


def reduce_kernel(nt, cuts1, cuts, g1_ref, g2_ref, g3_ref, sm_ref, o1_ref, os_ref, o2_ref, o3_ref, om_ref, *rest):
    here = place()
    z, d, core, x, y = here
    send, recv = rest[-2:]
    sends = Sends(send, recv)
    others = [{"tensor": lax.rem(z + dz, nt)} for dz in range(1, nt)]
    others += [{"dp": xor_peer(core, x, y, k)} for k in (1, 2, 4)]
    greet(others)
    secs = [
        Reduce(sends, nt, g, rest[10 * i : 10 * i + 10], c, here)
        for i, (g, c) in enumerate(((g1_ref, cuts1), (g2_ref, cuts), (g3_ref, cuts)))
    ]
    small = SmallSum(sends, nt, sm_ref, rest[30:33], here)
    for sec in secs:
        sec.begin()
    small.begin()
    for sec in secs:
        sec.first()
    small.step(1)
    for sec in secs:
        sec.second()
    small.step(2)
    for sec in secs:
        sec.third()
    small.step(3)
    total = secs[0].last()
    width = o1_ref.shape[1]
    o1_ref[...] = total[:, :width]
    os_ref[...] = total[:, width:]
    o2_ref[...] = secs[1].last()
    o3_ref[...] = secs[2].last()
    om_ref[...] = small.last()
    sends.finish()


class Chain:
    def __init__(self, nt, by, mine, whole, got, out, send, recv):
        self.mine, self.whole, self.got, self.out, self.send, self.recv = mine, whole, got, out, send, recv
        z = lax.axis_index("tensor")
        self.seqs, _, di = got.shape
        self.per = di // WIDE
        self.pieces = self.seqs * self.per
        self.at = z if by > 0 else nt - 1 - z
        self.has_prev = self.at > 0
        self.has_next = self.at < nt - 1
        self.next = {"tensor": lax.rem(z + by + nt, nt)}
        self.begin_slot = 3 * self.at - 1

    def copy(self, k):
        s = k // self.per
        cols = pl.ds(pl.multiple_of((k - s * self.per) * WIDE, WIDE), WIDE)
        return pltpu.make_async_remote_copy(
            src_ref=self.out.at[s, :, cols], dst_ref=self.got.at[s, :, cols], send_sem=self.send.at[k],
            recv_sem=self.recv.at[k], device_id=self.next, device_id_type=MESH,
        )

    def pass_on(self, k, first):
        s = k // self.per
        cols = pl.ds(pl.multiple_of((k - s * self.per) * WIDE, WIDE), WIDE)
        v = self.mine[s, :, cols].astype(F32)
        if not first:
            v = v + self.whole[s, 0:1, cols] * self.got[s, :, cols].astype(F32)
        self.out[s, :, cols] = v.astype(BF16)
        self.copy(k).start()

    def begin(self):
        @pl.when(jnp.logical_not(self.has_prev))
        def _():
            self.got[...] = jnp.zeros_like(self.got)
            for k in range(self.pieces):
                self.pass_on(k, True)

    def step(self, k):
        self.copy(k).wait_recv()

        @pl.when(self.has_next)
        def _():
            self.pass_on(k, False)

    def slot(self, n):
        since = n - self.begin_slot

        @pl.when(self.has_prev & (since >= 0) & (lax.rem(since + 8, 2) == 0) & (since < 2 * self.pieces))
        def _():
            self.step(since // 2)

    def rest(self, slots, first, last):
        for k in range(first, last):

            @pl.when(self.has_prev & (self.begin_slot + 2 * k >= slots))
            def _(k=k):
                self.step(k)

    def finish(self):
        @pl.when(self.has_next)
        def _():
            for k in range(self.pieces):
                self.copy(k).wait_send()


class Moves:
    def __init__(self, sems):
        self.sems, self.used, self.open = sems, 0, []

    def start(self, src, dst):
        copy = pltpu.make_async_copy(src, dst, self.sems.at[self.used])
        self.used += 1
        copy.start()
        self.open.append(copy)
        return copy

    def finish(self, done=()):
        for copy in self.open:
            if all(copy is not other for other in done):
                copy.wait()


def heads_table(sel_ref, di):
    r = lax.broadcasted_iota(jnp.int32, (128, WIDE), 0)
    c = lax.broadcasted_iota(jnp.int32, (128, WIDE), 1)
    for c0 in range(0, di, WIDE):
        hit = ((r & 31) == ((c + c0) >> 6)) & (r < 64)
        sel_ref[:, c0 : c0 + WIDE] = jnp.where(hit, 1.0, 0.0).astype(BF16)


def heads_table_t(selt_ref, di):
    c = lax.broadcasted_iota(jnp.int32, (WIDE, 128), 0)
    r = lax.broadcasted_iota(jnp.int32, (WIDE, 128), 1)
    for c0 in range(0, di, WIDE):
        selt_ref[c0 : c0 + WIDE, :] = jnp.where(r == ((c + c0) >> 6), 1.0, 0.0).astype(BF16)


def ones_below(tri_ref, up):
    r = lax.broadcasted_iota(jnp.int32, (SPAN, SPAN), 0)
    c = lax.broadcasted_iota(jnp.int32, (SPAN, SPAN), 1)
    tri_ref[...] = jnp.where(r <= c if up else r >= c, 1.0, 0.0).astype(BF16)


def forward_kernel(heads, nt, nd, gathers, *refs):
    refs = list(refs)
    take = lambda n: [refs.pop(0) for _ in range(n)]
    x_hbm, c_hbm, gain_ref, ts_ref = take(4)
    if gathers:
        pack_ref, wo_ref, wsh_ref, par_ref, xl_ref = take(5)
    else:
        w1_hbm, w2_hbm, w3_hbm, ws_hbm, parf_ref, xhf_ref = take(6)
    (out_hbm, h_hbm, rawi_hbm, raws_hbm, xs_hbm, bc_hbm, w1_out, w2_out, ws_out, yn_hbm, dgate_hbm, dy_hbm) = take(12)
    (draw_ref, acs_ref, bs_ref, rr_ref, fresh_ref, vv_ref, mineb_ref, dec_ref, sin_ref, chan_ref, dpar_ref, skip_ref,
     gg_ref, sk_ref) = take(14)
    (x_ref, c_ref, h_ref, w1_ref, w2_ref, w3_ref, ws_ref, pf_ref, xh_ref, rawi_ref, raws_ref, xs_ref, bc_ref, y_ref,
     gate_ref, yn_ref, dgate_ref, dy_ref, q_ref, g_ref, mine_ref, sb_ref, whole_ref, hh_ref, ea_ref, bst_ref,
     sel_ref, selt_ref, tri_ref, wot_ref) = take(30)
    send, recv, chain_send, chain_recv, local, moves = take(6)

    tokens, dim = x_ref.shape
    seqs, ext, di = rawi_ref.shape
    span = ext - 16
    per = span // SPAN
    blocks = seqs * per
    sh = bc_ref.shape[1]
    state = sh // 2
    dcol = di // nt
    wa = dcol - 128
    inner = nt * wa
    z = lax.axis_index("tensor")
    store = Moves(moves)
    load_x = store.start(x_hbm, x_ref)
    load_c = store.start(c_hbm, c_ref)

    sends = Sends(send, recv)
    zpeers = [{"tensor": lax.rem(z + dz, nt)} for dz in range(1, nt)]
    if gathers:
        here = place()
        _, d, core, x, y = here
        wot_ref[...] = wo_ref[...].astype(F32).T.astype(BF16)
        greet(zpeers + [{"dp": xor_peer(core, x, y, k)} for k in range(1, 8)])
        shards = (
            (pack_ref.at[:, pl.ds(0, wa)], w1_ref.at[:, pl.ds(0, inner)]),
            (pack_ref.at[:, pl.ds(wa, 256)], w1_ref.at[:, pl.ds(inner, 256 * nt)]),
            (pack_ref.at[:, pl.ds(wa + 256, dcol)], w2_ref),
            (wot_ref, w3_ref),
        )
        secs = [Gather(sends, nt, a, b, here) for a, b in shards]
        secs[0].begin(local.at[0])
        mine = ws_ref.at[dp_rows(d, wsh_ref.shape[0]), :]
        own = [pltpu.make_async_copy(wsh_ref, mine, local.at[4]), pltpu.make_async_copy(par_ref, pf_ref.at[z], local.at[5])]
        for copy in own:
            copy.start()
        got = [sends.start(wsh_ref, mine, {"dp": xor_peer(core, x, y, k)}) for k in range(1, 8)]
        got += [sends.start(par_ref, pf_ref.at[z], to) for to in zpeers]
        edge = sends.make(xl_ref, xh_ref, {"tensor": lax.rem(z + 1, nt)})

        @pl.when(z < nt - 1)
        def _():
            edge.start()

        for k in range(1, len(secs)):
            secs[k].begin(local.at[k])
    else:
        greet(({"tensor": lax.rem(z + nt - 1, nt)}, {"tensor": lax.rem(z + 1, nt)}))
        loads = [store.start(a, b) for a, b in ((w1_hbm, w1_ref), (w2_hbm, w2_ref), (w3_hbm, w3_ref), (ws_hbm, ws_ref))]
        pf_ref[...] = parf_ref[...]
        xh_ref[...] = xhf_ref[...]

    heads_table(sel_ref, di)
    heads_table_t(selt_ref, di)
    ones_below(tri_ref, False)

    def norm(v):
        v = v.astype(F32)
        return (v * lax.rsqrt(jnp.mean(v * v, axis=-1, keepdims=True) + EPSILON) * gain_ref[...]).astype(BF16)

    load_x.wait()

    def norm_step(b, c):
        rows = block_rows(b, SPAN)
        h_ref[rows, :] = norm(x_ref[rows, :])
        return c

    lax.fori_loop(0, blocks, norm_step, 0)
    store.start(h_ref, h_hbm)

    if gathers:
        for copy in own:
            copy.wait()
        secs[0].column()
        secs[1].column()
        for copy in got:
            copy.wait_recv()

        @pl.when(z > 0)
        def _():
            edge.wait_recv()

        @pl.when(z == 0)
        def _():
            xh_ref[...] = jnp.zeros_like(xh_ref)

    hh_ref[...] = norm(xh_ref[...])
    head = pf_ref[0, 8:16, 0:128]
    for t in range(nt):
        chan_ref[:, dcol * t : dcol * (t + 1)] = pf_ref[t, 0:8, :]
        if t > 0:
            head = head + pf_ref[t, 8:16, 0:128]
    ak = -jnp.exp(head[0:1])
    ak = jnp.where(lanes_of(ak.shape) < heads, ak, 0.0)
    dpar_ref[0:1, :] = head[1:2]
    dpar_ref[1:2, :] = ak * LOG2E
    dpar_ref[2:3, :] = ak
    dpar_ref[3:8, :] = jnp.zeros((5, 128), F32)
    sk8 = packed(jnp.broadcast_to(head[2:3], (8, 128)), heads)
    for c0 in range(0, di, WIDE):
        skip_ref[:, c0 : c0 + WIDE] = spread_heads(sk8, sel_ref[:, c0 : c0 + WIDE])

    def conv(raw, par, out, cols):
        def step(r, c):
            s = r // (span // 128)
            r0 = pl.multiple_of((r - s * (span // 128)) * 128, 128)
            v = raw[s, pl.ds(r0, 144), cols]
            acc = par[4:5, cols] + par[0:1, cols] * v[13:141]
            for k in range(1, 4):
                acc = acc + par[k : k + 1, cols] * v[13 + k : 141 + k]
            out[pl.ds(pl.multiple_of(s * span + r0, 128), 128), cols] = (acc * sigmoid(acc)).astype(BF16)
            return c

        lax.fori_loop(0, seqs * span // 128, step, 0)

    for s in range(seqs):
        rows = slice(span * s, span * (s + 1))
        raws_ref[s, 0:16, :] = dot(hh_ref[16 * s : 16 * s + 16, :], ws_ref[...])
        raws_ref[s, 16:ext, :] = dot(h_ref[rows, :], ws_ref[...])
    for c0 in range(0, sh, 256):
        conv(raws_ref, ts_ref, bc_ref, slice(c0, c0 + 256))
    store.start(raws_ref, raws_hbm)
    store.start(bc_ref, bc_hbm)
    store.start(ws_ref, ws_out)

    if gathers:
        secs[0].forward()
        secs[2].column()
        secs[1].forward()
        secs[0].corner()
        secs[0].finish()
    else:
        loads[0].wait()
    for t in range(nt):
        cols = slice(dcol * t, dcol * t + wa)
        for s in range(seqs):
            w = w1_ref[:, wa * t : wa * (t + 1)]
            rawi_ref[s, 0:16, cols] = dot(hh_ref[16 * s : 16 * s + 16, :], w)
            rawi_ref[s, 16:ext, cols] = dot(h_ref[span * s : span * (s + 1), :], w)
        conv(rawi_ref, chan_ref, xs_ref, cols)
    if gathers:
        secs[1].corner()
        secs[2].forward()
        secs[3].column()
        secs[1].finish()
    store.start(w1_ref, w1_out)
    for t in range(nt):
        cols = slice(dcol * t + wa, dcol * (t + 1))
        for s in range(seqs):
            rows = slice(span * s, span * (s + 1))
            w = w1_ref[:, inner + 256 * t : inner + 256 * (t + 1)]
            rawi_ref[s, 0:16, cols] = dot(hh_ref[16 * s : 16 * s + 16, :], w[:, :128])
            both = dot(h_ref[rows, :], w)
            rawi_ref[s, 16:ext, cols] = both[:, :128]
            if t == 0:
                draw_ref[rows, :] = both[:, 128:] + dpar_ref[0:1, :]
            else:
                draw_ref[rows, :] += both[:, 128:]
        conv(rawi_ref, chan_ref, xs_ref, cols)
    store.start(rawi_ref, rawi_hbm)
    store.start(xs_ref, xs_hbm)
    if gathers:
        secs[3].forward()
        secs[2].corner()

    def block_step(b, c):
        rows = block_rows(b, SPAN)
        s = b // per
        j = b - s * per
        x = draw_ref[rows, :]
        dt = jnp.maximum(x, 0.0) + jnp.log1p(jnp.exp(-jnp.abs(x)))
        lg = jnp.where(x < -20.0, x * LOG2E, jnp.log2(jnp.maximum(dt, 1e-30)))
        acs = cumulate(tri_ref[...], dt * dpar_ref[1:2, :], heads)
        bs = acs - lg
        acs_ref[rows, :] = acs
        bs_ref[rows, :] = bs
        end = acs[SPAN - 1 : SPAN, :]
        wk = packed(jnp.exp2(end - bs), heads)
        bt = bc_ref[rows, :state].astype(F32).T.astype(BF16)
        dk = packed(jnp.broadcast_to(jnp.exp2(end), (8, 128)), heads)
        for c0 in range(0, di, WIDE):
            cols = slice(c0, c0 + WIDE)
            w = spread_heads(wk, sel_ref[:, cols])
            wx = (w * xs_ref[rows, cols].astype(F32)).astype(BF16)
            fresh = dot(bt, wx)
            de = spread_heads(dk, sel_ref[:, cols])
            dec_ref[b, :, cols] = de

            @pl.when(j == 0)
            def _(cols=cols, fresh=fresh, de=de):
                fresh_ref[s, :, cols] = fresh.astype(BF16)
                mine_ref[s, :, cols] = fresh
                whole_ref[s, :, cols] = de

            @pl.when(j > 0)
            def _(cols=cols, fresh=fresh, de=de):
                mine_ref[s, :, cols] = de[0:1] * mine_ref[s, :, cols] + fresh
                whole_ref[s, :, cols] = de * whole_ref[s, :, cols]

        return c

    lax.fori_loop(0, blocks, block_step, 0)
    chain = Chain(nt, 1, mine_ref, whole_ref, sin_ref, sb_ref, chain_send, chain_recv)
    chain.begin()
    if gathers:
        secs[3].corner()

    lower = lax.broadcasted_iota(jnp.int32, (HALF, HALF), 0) >= lax.broadcasted_iota(jnp.int32, (HALF, HALF), 1)
    first = lanes_of((HALF, 128)) < P_SIZE
    pairs = di // 128

    def intra_step(b, carry):
        rows = block_rows(b, SPAN)
        bst_ref[...] = bs_ref[rows, :].T
        bb = bc_ref[rows, :state]
        cc = bc_ref[rows, state:]
        g00 = dot_nt(cc[:HALF], bb[:HALF])
        g10 = dot_nt(cc[HALF:], bb[:HALF])
        g11 = dot_nt(cc[HALF:], bb[HALF:])
        for p in range(pairs):
            cols = slice(128 * p, 128 * p + 128)
            xp = xs_ref[rows, cols]
            y0, y1 = [], []
            for h in (2 * p, 2 * p + 1):
                a0 = acs_ref[block_rows(2 * b, HALF), h : h + 1]
                a1 = acs_ref[block_rows(2 * b + 1, HALF), h : h + 1]
                r0 = bst_ref[h : h + 1, :HALF]
                r1 = bst_ref[h : h + 1, HALF:]
                m00 = jnp.where(lower, jnp.exp2(a0 - r0) * g00, 0.0).astype(BF16)
                m10 = (jnp.exp2(a1 - r0) * g10).astype(BF16)
                m11 = jnp.where(lower, jnp.exp2(a1 - r1) * g11, 0.0).astype(BF16)
                y0.append(dot(m00, xp[:HALF]))
                y1.append(dot(jnp.concatenate([m10, m11], axis=1), xp))
            y_ref[block_rows(2 * b, HALF), cols] = jnp.where(first, y0[0], y0[1])
            y_ref[block_rows(2 * b + 1, HALF), cols] = jnp.where(first, y1[0], y1[1])
            if (p + 1) % (pairs // 3) == 0:
                chain.slot(3 * b + (p + 1) // (pairs // 3) - 1)
        return carry

    lax.fori_loop(0, blocks, intra_step, 0)
    if gathers:
        for sec in secs[2:]:
            sec.finish()
    else:
        loads[1].wait()
        loads[2].wait()
    store.start(w2_ref, w2_out)

    def gate_step(b, carry):
        rows = block_rows(b, span)
        for c0 in range(0, di, WIDE):
            cols = slice(c0, c0 + WIDE)
            gate_ref[rows, cols] = dot(h_ref[rows, :], w2_ref[:, cols])
        return carry

    lax.fori_loop(0, seqs, gate_step, 0)
    chain.rest(3 * blocks, 0, chain.pieces)
    load_c.wait()

    gg_ref[...] = jnp.zeros_like(gg_ref)
    sk_ref[...] = jnp.zeros_like(sk_ref)

    def mid_step(b, carry):
        rows = block_rows(b, SPAN)
        s = b // per
        j = b - s * per
        ea_ref[...] = packed(jnp.exp2(acs_ref[rows, :]), heads)
        cc = bc_ref[rows, state:]
        ss = jnp.zeros((SPAN, 1), F32)
        for c0 in range(0, di, WIDE):
            cols = slice(c0, c0 + WIDE)
            prev = sin_ref[s, :, cols].astype(F32)
            later = dec_ref[s * per, 0:1, cols] * prev + fresh_ref[s, :, cols].astype(F32)
            s_in = jnp.where(j == 0, prev, later).astype(BF16)
            ea = spread_heads(ea_ref[...], sel_ref[:, cols])
            ynos = y_ref[rows, cols] + ea * dot(cc, s_in)
            y_ref[rows, cols] = ynos
            y = ynos + skip_ref[0:1, cols] * xs_ref[rows, cols].astype(F32)
            gate = gate_ref[rows, cols]
            g = y * (gate * sigmoid(gate))
            g_ref[:, cols] = g
            ss = ss + jnp.sum(g * g, axis=-1, keepdims=True)
        r2 = lax.rsqrt(ss / di + EPSILON)
        qg = jnp.zeros((SPAN, 1), F32)
        for c0 in range(0, di, WIDE):
            cols = slice(c0, c0 + WIDE)
            g = g_ref[:, cols]
            gain = chan_ref[5:6, cols]
            yn_ref[rows, cols] = (g * r2 * gain).astype(BF16)
            dyn = dot(c_ref[rows, :], w3_ref[:, cols])
            gg_ref[0:1, cols] += jnp.sum(dyn * (g * r2), axis=0, keepdims=True)
            q = dyn * gain
            q_ref[:, cols] = q
            qg = qg + jnp.sum(q * g, axis=-1, keepdims=True)
        x_ref[rows, :] = (x_ref[rows, :].astype(F32) + dot_nt(yn_ref[rows, :], w3_ref[...])).astype(BF16)
        coef = r2 * r2 * r2 * (qg / di)
        rr = jnp.zeros((SPAN, 128), F32)
        dk = jnp.zeros((SPAN, 128), F32)
        ct = cc.astype(F32).T.astype(BF16)
        for c0 in range(0, di, WIDE):
            cols = slice(c0, c0 + WIDE)
            xf = xs_ref[rows, cols].astype(F32)
            ynos = y_ref[rows, cols]
            y = ynos + skip_ref[0:1, cols] * xf
            gate = gate_ref[rows, cols]
            sg = sigmoid(gate)
            dg = r2 * q_ref[:, cols] - coef * g_ref[:, cols]
            dgate_ref[rows, cols] = (dg * y * (sg * (1.0 + gate * (1.0 - sg)))).astype(BF16)
            dyb = (dg * (gate * sg)).astype(BF16)
            dy_ref[rows, cols] = dyb
            dy = dyb.astype(F32)
            rr = rr + gather_heads(dy * ynos, selt_ref[cols, :])
            dk = dk + gather_heads(dy * xf, selt_ref[cols, :])
            ea = spread_heads(ea_ref[...], sel_ref[:, cols])
            vv = dot(ct, (ea * dy).astype(BF16))

            @pl.when(j == 0)
            def _(cols=cols, vv=vv):
                mine_ref[s, :, cols] = vv

            @pl.when(j > 0)
            def _(cols=cols, vv=vv):
                vv_ref[s, :, cols] = vv.astype(BF16)
                mine_ref[s, :, cols] += dec_ref[s * per, 0:1, cols] * vv

        rr_ref[rows, :] = rr
        sk_ref[0:1, :] += jnp.sum(dk, axis=0, keepdims=True)
        return carry

    lax.fori_loop(0, blocks, mid_step, 0)
    for a, b in ((x_ref, out_hbm), (yn_ref, yn_hbm), (dgate_ref, dgate_hbm), (dy_ref, dy_hbm)):
        store.start(a, b)
    mineb_ref[...] = mine_ref[...].astype(BF16)
    chain.finish()
    sends.finish()
    if gathers:

        @pl.when(z < nt - 1)
        def _():
            edge.wait_send()

    store.finish((load_x, load_c) if gathers else (load_x, load_c, *loads))


def back_kernel(
    heads,
    xs_ref, bc_ref, draw_ref, acs_ref, bs_ref, sin_ref, fresh_ref, dec_ref, ds_ref, vv_ref, dy_ref, rr_ref,
    rawi_ref, raws_ref, ti_ref, ts_ref, dpar_ref, skip_ref, sel_ref, selt_ref, tri_ref, triu_ref,
    dpi_ref, dps_ref, dd_ref, small_ref, tgi_ref, tgs_ref,
    acst_ref, ea_ref, w_ref, dg_ref, dx_ref, dbc_ref,
):
    tokens, di = xs_ref.shape
    seqs, ext, _ = rawi_ref.shape
    span = ext - 16
    blocks = tokens // SPAN
    per = blocks // seqs
    state = bc_ref.shape[1] // 2
    sh = 2 * state
    upper = lax.broadcasted_iota(jnp.int32, (HALF, HALF), 0) <= lax.broadcasted_iota(jnp.int32, (HALF, HALF), 1)
    first = lanes_of((HALF, 128)) < P_SIZE
    first_all = lanes_of((SPAN, 128)) < P_SIZE
    small_ref[...] = jnp.zeros_like(small_ref)
    tgi_ref[...] = jnp.zeros_like(tgi_ref)
    tgs_ref[...] = jnp.zeros_like(tgs_ref)

    def block_step(b, carry):
        rows = block_rows(b, SPAN)
        s = b // per
        j = b - s * per
        acst_ref[...] = acs_ref[rows, :].T
        acs = acs_ref[rows, :]
        bs = bs_ref[rows, :]
        end = acs[SPAN - 1 : SPAN, :]
        ea_ref[...] = packed(jnp.exp2(acs), heads)
        w_ref[...] = packed(jnp.exp2(end - bs), heads)
        bb = bc_ref[rows, :state]
        cc = bc_ref[rows, state:]
        g00 = dot_nt(bb[:HALF], cc[:HALF])
        g01 = dot_nt(bb[:HALF], cc[HALF:])
        g11 = dot_nt(bb[HALF:], cc[HALF:])
        dg_ref[...] = jnp.zeros_like(dg_ref)
        for p in range(di // 128):
            cols = slice(128 * p, 128 * p + 128)
            xp = xs_ref[rows, cols]
            dyp = dy_ref[rows, cols]
            d0, d1 = [], []
            for i, h in enumerate((2 * p, 2 * p + 1)):
                keep = first_all if i == 0 else jnp.logical_not(first_all)
                xm = jnp.where(keep, xp, jnp.zeros_like(xp))
                b0 = bs_ref[block_rows(2 * b, HALF), h : h + 1]
                b1 = bs_ref[block_rows(2 * b + 1, HALF), h : h + 1]
                r0 = acst_ref[h : h + 1, :HALF]
                r1 = acst_ref[h : h + 1, HALF:]
                e00 = jnp.where(upper, jnp.exp2(r0 - b0), 0.0)
                e01 = jnp.exp2(r1 - b0)
                e11 = jnp.where(upper, jnp.exp2(r1 - b1), 0.0)
                m0 = jnp.concatenate([(e00 * g00).astype(BF16), (e01 * g01).astype(BF16)], axis=1)
                m1 = (e11 * g11).astype(BF16)
                d0.append(dot(m0, dyp))
                d1.append(dot(m1, dyp[HALF:]))
                dm0 = dot_nt(xm[:HALF], dyp)
                dm1 = dot_nt(xm[HALF:], dyp[HALF:])
                dg_ref[0] += dm0[:, :HALF] * e00
                dg_ref[1] += dm0[:, HALF:] * e01
                dg_ref[2] += dm1 * e11
            dx_ref[0:HALF, cols] = jnp.where(first, d0[0], d0[1])
            dx_ref[HALF:SPAN, cols] = jnp.where(first, d1[0], d1[1])

        dg00 = dg_ref[0]
        dg01 = dg_ref[1]
        dg11 = dg_ref[2]
        db0 = dot(jnp.concatenate([dg00, dg01], axis=1).astype(BF16), cc)
        db1 = dot(dg11.astype(BF16), cc[HALF:])
        dc0 = dot(dg00.T.astype(BF16), bb[:HALF])
        dc1 = dot(jnp.concatenate([dg01.T, dg11.T], axis=1).astype(BF16), bb)
        db = jnp.concatenate([db0, db1], axis=0)
        dc = jnp.concatenate([dc0, dc1], axis=0)
        rr = rr_ref[rows, :]
        pin = jnp.zeros((SPAN, 128), F32)
        pst = jnp.zeros((SPAN, 128), F32)
        endsum = jnp.zeros((8, 128), F32)
        for c0 in range(0, di, WIDE):
            cols = slice(c0, c0 + WIDE)
            prev = sin_ref[s, :, cols].astype(F32)
            later = dec_ref[s * per, 0:1, cols] * prev + fresh_ref[s, :, cols].astype(F32)
            s_in = jnp.where(j == 0, prev, later).astype(BF16)
            dlast = ds_ref[s, :, cols].astype(F32)
            dprev = dec_ref[s * per + per - 1, 0:1, cols] * dlast + vv_ref[s, :, cols].astype(F32)
            ds = jnp.where(j == per - 1, dlast, dprev).astype(BF16)
            w = spread_heads(w_ref[...], sel_ref[:, cols])
            ea = spread_heads(ea_ref[...], sel_ref[:, cols])
            xf = xs_ref[rows, cols].astype(F32)
            dyf = dy_ref[rows, cols].astype(F32)
            dxs = w * dot(bb, ds)
            dxi = dx_ref[:, cols]
            pin = pin + gather_heads(dxi * xf, selt_ref[cols, :])
            pst = pst + gather_heads(dxs * xf, selt_ref[cols, :])
            both = jnp.sum(ds.astype(F32) * s_in.astype(F32), axis=0, keepdims=True) * dec_ref[b, 0:1, cols]
            endsum = endsum + gather_heads(jnp.broadcast_to(both, (8, WIDE)), selt_ref[cols, :])
            dc = dc + dot_nt((ea * dyf).astype(BF16), s_in)
            db = db + dot_nt((w * xf).astype(BF16), ds)
            dx_ref[:, cols] = dxi + dxs + skip_ref[0:1, cols] * dyf
        dbc_ref[:, :state] = db
        dbc_ref[:, state:] = dc
        pp = pin + pst
        da = cumulate(triu_ref[...], rr - pp, heads) + (endsum[0:1, :] + jnp.sum(pst, axis=0, keepdims=True))
        x = draw_ref[rows, :]
        sg = 1.0 / (1.0 + jnp.exp(-x))
        dt = jnp.maximum(x, 0.0) + jnp.log1p(jnp.exp(-jnp.abs(x)))
        ratio = jnp.where(x < -20.0, 1.0, sg / jnp.maximum(dt, 1e-30))
        ak = dpar_ref[2:3, :]
        dd = da * ak * sg + pp * ratio
        dd_ref[rows, :] = dd.astype(BF16)
        small_ref[0:1, :] += jnp.sum(da * dt * ak, axis=0, keepdims=True)
        small_ref[1:2, :] += jnp.sum(dd, axis=0, keepdims=True)

        def conv_back(raw, par, dact, dpre, tg, cols):
            def step(r, c):
                r0 = pl.multiple_of(r * HALF, HALF)
                v = raw[s, pl.ds(pl.multiple_of(j * SPAN + r0, HALF), HALF + 16), cols]
                sh_v = [v[13 + k : 13 + k + HALF] for k in range(4)]
                pre = par[4:5, cols] + par[0:1, cols] * sh_v[0]
                for k in range(1, 4):
                    pre = pre + par[k : k + 1, cols] * sh_v[k]
                sg = sigmoid(pre)
                dp = dact[pl.ds(r0, HALF), cols] * (sg * (1.0 + pre * (1.0 - sg)))
                dpre[pl.ds(pl.multiple_of(b * SPAN + r0, HALF), HALF), cols] = dp
                for k in range(4):
                    tg[k : k + 1, cols] += jnp.sum(dp * sh_v[k], axis=0, keepdims=True)
                tg[4:5, cols] += jnp.sum(dp, axis=0, keepdims=True)
                return c

            lax.fori_loop(0, SPAN // HALF, step, 0)

        for c0 in range(0, di, 256):
            conv_back(rawi_ref, ti_ref, dx_ref, dpi_ref, tgi_ref, slice(c0, c0 + 256))
        for c0 in range(0, sh, 256):
            conv_back(raws_ref, ts_ref, dbc_ref, dps_ref, tgs_ref, slice(c0, c0 + 256))
        return carry

    lax.fori_loop(0, blocks, block_step, 0)


def last_kernel(
    nt,
    x_ref, c_ref, gain_ref, h_ref, dpi_ref, dps_ref, hi_ref, hs_ref, dd_ref, dgate_ref, yn_ref, ti_ref, ts_ref,
    w1_ref, w2_ref, ws_ref,
    ig_ref, g1_ref, g2_ref, g3_ref, ng_ref,
    din_ref,
):
    tokens, di = dgate_ref.shape
    seqs = hi_ref.shape[0]
    span = tokens // seqs
    sh = dps_ref.shape[1]
    inner = w1_ref.shape[1]
    dcol = di // nt
    wa = dcol - 128
    ng_ref[...] = jnp.zeros_like(ng_ref)
    for t in range(nt):
        din_ref[:, wa * nt + 256 * t + 128 : wa * nt + 256 * (t + 1)] = dd_ref[...]

    def conv_t(dpre, halo, par, c0, to):
        cols = slice(c0, c0 + 128)
        for s in range(seqs):
            for r0 in range(0, span, HALF):
                base = s * span + r0
                v = dpre[base : base + HALF, cols]
                if r0 + HALF < span:
                    nxt = dpre[base + HALF : base + HALF + 8, cols]
                else:
                    nxt = halo[s, :, cols]
                v = jnp.concatenate([v, nxt], axis=0)
                acc = par[3:4, cols] * v[0:HALF]
                for k in range(3):
                    acc = acc + par[k : k + 1, cols] * v[3 - k : 3 - k + HALF]
                din_ref[base : base + HALF, to : to + 128] = acc.astype(BF16)

    for c0 in range(0, di, 128):
        t, r = divmod(c0, dcol)
        conv_t(dpi_ref, hi_ref, ti_ref, c0, wa * t + r if r < wa else wa * nt + 256 * t + r - wa)
    for c0 in range(0, sh, 128):
        conv_t(dps_ref, hs_ref, ts_ref, c0, inner + c0)

    for c0 in range(0, inner, WIDE):
        g1_ref[:, c0 : c0 + WIDE] = dot_tn(h_ref[...], din_ref[:, c0 : c0 + WIDE]).astype(BF16)
    g1_ref[:, inner:] = dot_tn(h_ref[...], din_ref[:, inner:]).astype(BF16)
    for c0 in range(0, di, WIDE):
        g2_ref[:, c0 : c0 + WIDE] = dot_tn(h_ref[...], dgate_ref[:, c0 : c0 + WIDE]).astype(BF16)
        g3_ref[:, c0 : c0 + WIDE] = dot_tn(c_ref[...], yn_ref[:, c0 : c0 + WIDE]).astype(BF16)

    def step(b, carry):
        rows = block_rows(b, SPAN)
        dh = dot_nt(dgate_ref[rows, :], w2_ref[...])
        dh = dh + dot_nt(din_ref[rows, :inner], w1_ref[...])
        dh = dh + dot_nt(din_ref[rows, inner:], ws_ref[...])
        u = x_ref[rows, :].astype(F32)
        r1 = lax.rsqrt(jnp.mean(u * u, axis=-1, keepdims=True) + EPSILON)
        ng_ref[0:1, :] += jnp.sum(dh * u * r1, axis=0, keepdims=True)
        e = dh * gain_ref[...]
        m = jnp.mean(e * u, axis=-1, keepdims=True)
        ig_ref[rows, :] = (c_ref[rows, :].astype(F32) + r1 * e - u * (r1 * r1 * r1 * m)).astype(BF16)
        return carry

    lax.fori_loop(0, tokens // SPAN, step, 0)


def call(kernel, outs, scratch, *args, name, collective_id=None):
    params = dict(vmem_limit_bytes=VMEM_LIMIT)
    if collective_id is not None:
        params.update(collective_id=collective_id, has_side_effects=True)
    return pl.pallas_call(
        kernel,
        out_shape=[jax.ShapeDtypeStruct(s, d) for s, d in outs],
        in_specs=[pl.BlockSpec(memory_space=pltpu.VMEM)] * len(args),
        out_specs=[pl.BlockSpec(memory_space=pltpu.VMEM)] * len(outs),
        scratch_shapes=[s if not isinstance(s, tuple) else pltpu.VMEM(*s) for s in scratch],
        compiler_params=pltpu.CompilerParams(**params),
        name=name,
    )(*args)


def semaphores(n):
    return [pltpu.SemaphoreType.DMA((n,)), pltpu.SemaphoreType.DMA((n,))]


def shifted(v, axis, by):
    n = lax.axis_size(axis)
    return lax.ppermute(v, axis, [(i, i + by) for i in range(n) if 0 <= i + by < n])


def gather_all(nt, nd, pack, wo, ws, par, edge):
    both = ("tensor", "dp")
    rows = ws.shape[0]
    dcol = wo.shape[0]
    full = lax.all_gather(jnp.concatenate([pack, wo.T], axis=1), both, axis=0).reshape(nt, nd * rows, -1)
    whole = lambda a, b: full[:, :, a:b].transpose(1, 0, 2).reshape(nd * rows, nt * (b - a))
    w1 = jnp.concatenate([whole(0, dcol - 128), whole(dcol - 128, dcol + 128)], axis=1)
    return (
        w1, whole(dcol + 128, 2 * dcol + 128), whole(2 * dcol + 128, 3 * dcol + 128),
        lax.all_gather(ws, "dp", axis=0, tiled=True), lax.all_gather(par, "tensor", axis=0), shifted(edge, "tensor", 1),
    )


def chain(nt, by, mine, whole):
    seqs, state, di = mine.shape
    return call(
        functools.partial(chain_kernel, nt, by),
        [(mine.shape, BF16)],
        [(mine.shape, BF16)] + semaphores(seqs * di // WIDE),
        mine, whole, name="states" if by > 0 else "states_back", collective_id=1 if by > 0 else 2,
    )[0]


def reduce_all(nt, nd, g1, g2, g3, sm, sh):
    dim = g1.shape[0]
    rows = dim // nd
    dcol = g2.shape[1] // nt
    wa = dcol - 128
    cuts1 = ((0, wa, True), (wa * nt, 256, True), ((wa + 256) * nt, sh, False))
    part = wa + 256
    if nd == 8:
        cuts = ((0, dcol, True),)
        scratch = []
        for g, w in ((g1, part + sh), (g2, dcol), (g3, dcol)):
            scratch += Reduce.scratch(rows, g.shape[1], nt, w)
        scratch += SmallSum.scratch(sm.shape, nt)
        count = 3 * Reduce.MESSAGES + SmallSum.MESSAGES
        return call(
            functools.partial(reduce_kernel, nt, cuts1, cuts),
            [((rows, part), F32), ((rows, sh), F32), ((rows, dcol), F32), ((rows, dcol), F32), (sm.shape, F32)],
            scratch + semaphores(count),
            g1, g2, g3, sm, name="reduce", collective_id=3,
        )
    both = ("tensor", "dp")
    parts = [
        g[:, at : at + nt * w].reshape(dim, nt, w).transpose(1, 0, 2)
        for g, at, w in ((g1, 0, wa), (g1, wa * nt, 256), (g2, 0, dcol), (g3, 0, dcol))
    ]
    big = jnp.concatenate(parts, axis=2).reshape(nt * nd, rows, -1)
    big = lax.psum_scatter(big, both, scatter_dimension=0).astype(F32)
    shared = g1[:, nt * part :].reshape(nd, rows, sh).astype(F32)
    shared = lax.psum(lax.psum_scatter(shared, "dp", scatter_dimension=0), "tensor")
    return big[:, :part], shared, big[:, part : part + dcol], big[:, part + dcol :], lax.psum(sm, both)


def local(
    block_input, norm_gain, input_gate_inner_weight, input_shared_weight, input_delta_weight, conv_inner, shift_inner,
    conv_shared, shift_shared, decay_log, delta_bias, skip_gain, gated_gain, output_projection_weight, cotangent,
):
    nt = lax.axis_size("tensor")
    nd = lax.axis_size("dp")
    me = lax.axis_index("tensor")
    seqs, span, dim = block_input.shape
    tokens = seqs * span
    blocks = tokens // SPAN
    rows, _, dcol = input_gate_inner_weight.shape
    di = dcol * nt
    sh = input_shared_weight.shape[1]
    state = sh // 2
    hloc = input_delta_weight.shape[1]
    heads = hloc * nt
    w1w = (dcol + 128) * nt

    delta_w = lax.dynamic_update_slice(jnp.zeros((rows, 128), BF16), input_delta_weight, (0, me * hloc))
    pack = jnp.concatenate([input_gate_inner_weight[:, 1], delta_w, input_gate_inner_weight[:, 0]], axis=1)
    wo = output_projection_weight
    head = lax.dynamic_update_slice(
        jnp.zeros((8, dcol), F32), jnp.stack([decay_log, delta_bias, skip_gain]), (0, me * hloc)
    )
    par = jnp.concatenate([
        conv_inner.astype(F32), shift_inner.astype(F32)[None], gated_gain[None], jnp.zeros((2, dcol), F32), head], axis=0)
    edge = block_input[:, span - 16 :].reshape(seqs * 16, dim)
    ts = jnp.pad(jnp.concatenate([conv_shared.astype(F32), shift_shared.astype(F32)[None]], axis=0), ((0, 3), (0, 0)))
    gain = norm_gain[None]
    x = block_input.reshape(tokens, dim)
    c = cotangent.reshape(tokens, dim)

    gathers = nd == 8
    args = [x, c, gain, ts]
    kinds = [pl.ANY, pl.ANY, pltpu.VMEM, pltpu.VMEM]
    if gathers:
        args += [pack, wo, input_shared_weight, par, edge]
        kinds += [pltpu.VMEM] * 5
    else:
        args += gather_all(nt, nd, pack, wo, input_shared_weight, par, edge)
        kinds += [pl.ANY] * 4 + [pltpu.VMEM] * 2
    far = [
        ((tokens, dim), BF16), ((tokens, dim), BF16), ((seqs, span + 16, di), F32), ((seqs, span + 16, sh), F32),
        ((tokens, di), BF16), ((tokens, sh), BF16), ((dim, w1w), BF16), ((dim, di), BF16), ((dim, sh), BF16),
        ((tokens, di), BF16), ((tokens, di), BF16), ((tokens, di), BF16),
    ]
    scan_state = ((seqs, state, di), BF16)
    near = [((tokens, 128), F32)] * 4 + [scan_state] * 3 + [
        ((blocks, 8, di), F32), scan_state, ((8, di), F32), ((8, 128), F32), ((8, di), F32), ((8, di), F32),
        ((8, 128), F32)]
    scratch = [
        ((tokens, dim), BF16), ((tokens, dim), BF16), ((tokens, dim), BF16), ((dim, w1w), BF16), ((dim, di), BF16),
        ((dim, di), BF16), ((dim, sh), BF16), ((nt, 16, dcol), F32), ((seqs * 16, dim), BF16),
        ((seqs, span + 16, di), F32), ((seqs, span + 16, sh), F32), ((tokens, di), BF16), ((tokens, sh), BF16),
        ((tokens, di), F32), ((tokens, di), F32), ((tokens, di), BF16), ((tokens, di), BF16), ((tokens, di), BF16),
        ((SPAN, di), F32), ((SPAN, di), F32), ((seqs, state, di), F32), scan_state, ((seqs, 8, di), F32),
        ((seqs * 16, dim), BF16), ((SPAN, 128), BF16), ((128, SPAN), F32), ((128, di), BF16), ((di, 128), BF16),
        ((SPAN, SPAN), BF16), ((rows, dcol), BF16),
    ]
    pieces = seqs * di // WIDE
    out, h, rawi, raws, xs, bc, w1, w2, ws, yn, dgate, dy, *rest = pl.pallas_call(
        functools.partial(forward_kernel, heads, nt, nd, gathers),
        out_shape=[jax.ShapeDtypeStruct(s, d) for s, d in far + near],
        in_specs=[pl.BlockSpec(memory_space=k) for k in kinds],
        out_specs=[pl.BlockSpec(memory_space=pl.ANY)] * len(far) + [pl.BlockSpec(memory_space=pltpu.VMEM)] * len(near),
        scratch_shapes=[pltpu.VMEM(s, d) for s, d in scratch]
        + semaphores(4 * Gather.MESSAGES + 7 + nt) + semaphores(pieces)
        + [pltpu.SemaphoreType.DMA((6,)), pltpu.SemaphoreType.DMA((20,))],
        compiler_params=pltpu.CompilerParams(vmem_limit_bytes=VMEM_LIMIT, collective_id=0, has_side_effects=True),
        name="forward",
    )(*args)
    draw, acs, bs, rr, fresh, vv, mineb, dec, sin, chan, dpar, skip, ggg, skg = rest

    owner = jnp.arange(di) // P_SIZE
    lane = jnp.arange(128)
    sel = ((lane[:, None] % 32 == owner[None]) & (lane[:, None] < 64)).astype(BF16)
    selt = (lane[None] == owner[:, None]).astype(BF16)
    at = jnp.arange(SPAN)
    tri = (at[:, None] >= at[None]).astype(BF16)
    triu = tri.T
    de = dec.reshape(seqs, blocks // seqs, 8, di)
    whole = de[:, 0] * de[:, 1]
    ds = chain(nt, -1, mineb.astype(F32), whole)
    ti = chan

    dpi, dps, dd, small, tgi, tgs = call(
        functools.partial(back_kernel, heads),
        [((tokens, di), F32), ((tokens, sh), F32), ((tokens, 128), BF16), ((8, 128), F32), ((8, di), F32), ((8, sh), F32)],
        [((128, SPAN), F32), ((SPAN, 128), BF16), ((SPAN, 128), BF16), ((3, HALF, HALF), F32), ((SPAN, di), F32),
         ((SPAN, sh), F32)],
        xs, bc, draw, acs, bs, sin, fresh, dec, ds, vv, dy, rr, rawi, raws, ti, ts, dpar, skip, sel, selt, tri, triu,
        name="back",
    )

    hi = shifted(dpi.reshape(seqs, span, di)[:, :8], "tensor", -1)
    hs = shifted(dps.reshape(seqs, span, sh)[:, :8], "tensor", -1)
    ig, g1, g2, g3, ng = call(
        functools.partial(last_kernel, nt),
        [((tokens, dim), BF16), ((dim, w1.shape[1] + sh), BF16), ((dim, di), BF16), ((dim, di), BF16), ((8, dim), F32)],
        [((tokens, w1.shape[1] + sh), BF16)],
        x, c, gain, h, dpi, dps, hi, hs, dd, dgate, yn, ti, ts, w1, w2, ws, name="last",
    )

    sm = jnp.concatenate([
        tgi[:5].reshape(-1), ggg[0], ng[0], tgs[:5].reshape(-1), small[0], small[1], skg[0],
        jnp.zeros(8 * di - 6 * di - dim - 5 * sh - 3 * 128, F32)]).reshape(8, di)
    g1, gs, g2, g3, sm = reduce_all(nt, nd, g1, g2, g3, sm, sh)
    sm = sm.reshape(-1)
    cut = lambda k: lax.dynamic_slice_in_dim(sm, k * di + me * dcol, dcol)
    at = 6 * di
    ng = sm[at : at + dim]
    tgs = sm[at + dim : at + dim + 5 * sh].reshape(5, sh)
    at = at + dim + 5 * sh
    hcut = lambda k: lax.dynamic_slice_in_dim(sm, at + 128 * k + me * hloc, hloc)
    return (
        out.reshape(block_input.shape),
        ig.reshape(block_input.shape),
        ng,
        jnp.stack([g2, g1[:, :dcol]], axis=1),
        gs,
        lax.dynamic_slice_in_dim(g1[:, dcol:], me * hloc, hloc, axis=1),
        jnp.stack([cut(k) for k in range(4)]),
        cut(4),
        tgs[:4],
        tgs[4],
        hcut(0),
        hcut(1),
        hcut(2),
        cut(5),
        g3.T,
    )


def solution(mesh):
    placed = (
        P("dp", "tensor", None), P(), P("dp", None, "tensor"), P("dp", None), P("dp", "tensor"), P(None, "tensor"),
        P("tensor"), P(), P(), P("tensor"), P("tensor"), P("tensor"), P("tensor"), P("tensor", "dp"),
        P("dp", "tensor", None),
    )
    return jax.shard_map(
        local,
        mesh=mesh,
        in_specs=placed,
        out_specs=(
            P("dp", "tensor", None), P("dp", "tensor", None), P(), P("dp", None, "tensor"), P("dp", None),
            P("dp", "tensor"), P(None, "tensor"), P("tensor"), P(), P(), P("tensor"), P("tensor"), P("tensor"),
            P("tensor"), P("tensor", "dp"),
        ),
        check_vma=False,
    )
```

```python
import functools

import jax
import jax.numpy as jnp
from jax import lax
from jax.experimental import pallas as pl
from jax.experimental.pallas import tpu as pltpu
from jax.sharding import PartitionSpec as P

P_SIZE = 64
SPAN = 256
HALF = SPAN // 2
EPSILON = 1e-05
LOG2E = 1.4426950408889634
F32 = jnp.float32
BF16 = jnp.bfloat16
VMEM_LIMIT = 63 * 1024 * 1024
WIDE = 512


def dot(a, b):
    return jnp.dot(a, b, preferred_element_type=F32)


def dot_nt(a, b):
    return lax.dot_general(a, b, (((1,), (1,)), ((), ())), preferred_element_type=F32)


def dot_tn(a, b):
    return lax.dot_general(a, b, (((0,), (0,)), ((), ())), preferred_element_type=F32)


def sigmoid(v):
    return 0.5 * jnp.tanh(0.5 * v) + 0.5


def split2(v):
    hi = v.astype(BF16)
    return hi, (v - hi.astype(F32)).astype(BF16)


def lanes_of(shape):
    return lax.broadcasted_iota(jnp.int32, shape, len(shape) - 1)


def packed(v, heads):
    v = jnp.where(lanes_of(v.shape) < heads, v, 0.0)
    hi = v.astype(BF16).astype(F32)
    low = (v - hi).astype(BF16).astype(F32)
    return (hi + pltpu.roll(low, 32, 1)).astype(BF16)


def spread_heads(pk, sel):
    return dot(pk, sel)


def gather_heads(v, selt):
    hi, low = split2(v)
    return dot(hi, selt) + dot(low, selt)


def cumulate(tri, v, heads):
    v = jnp.where(lanes_of(v.shape) < heads, v, 0.0)
    p0 = v.astype(BF16).astype(F32)
    r = v - p0
    p1 = r.astype(BF16).astype(F32)
    p2 = r - p1
    pk = (p0 + pltpu.roll(p1, 32, 1) + pltpu.roll(p2, 64, 1)).astype(BF16)
    s = dot(tri, pk)
    n = s.shape[1]
    s = s + pltpu.roll(s, n - 32, 1) + pltpu.roll(s, n - 64, 1)
    return jnp.where(lanes_of(v.shape) < heads, s, 0.0)


def block_rows(b, size):
    return pl.ds(pl.multiple_of(b * size, size), size)


MESH = pl.DeviceIdType.MESH


class Sends:
    def __init__(self, send, recv):
        self.send, self.recv, self.used, self.started = send, recv, 0, []

    def make(self, src, dst, to):
        k = self.used
        self.used += 1
        return pltpu.make_async_remote_copy(
            src_ref=src, dst_ref=dst, send_sem=self.send.at[k], recv_sem=self.recv.at[k],
            device_id=to, device_id_type=MESH,
        )

    def start(self, src, dst, to):
        copy = self.make(src, dst, to)
        copy.start()
        self.started.append(copy)
        return copy

    def finish(self):
        for copy in self.started:
            copy.wait_send()


def greet(others):
    barrier = pltpu.get_barrier_semaphore()
    for to in others:
        pl.semaphore_signal(barrier, inc=1, device_id=to, device_id_type=MESH)
    pl.semaphore_wait(barrier, len(others))


def place():
    z = lax.axis_index("tensor")
    d = lax.axis_index("dp")
    core = lax.rem(d, 2)
    x = lax.rem(d // 2, 2)
    y = d // 4
    return z, d, core, x, y


def xor_peer(core, x, y, k):
    c1 = 1 - core if k & 1 else core
    x1 = 1 - x if k & 2 else x
    y1 = 1 - y if k & 4 else y
    return y1 * 4 + x1 * 2 + c1


def dp_rows(d, size, part=None):
    if part is None:
        return pl.ds(pl.multiple_of(d * size, 16), size)
    return pl.ds(pl.multiple_of(d * size + part * (size // 2), 16), size // 2)


def columns(t, size):
    return pl.ds(pl.multiple_of(t * size, 128), size)


def cut_at(base, size, by_t, t):
    return pl.ds(pl.multiple_of(base + t * size, 128), size) if by_t else pl.ds(base, size)


class Gather:
    MESSAGES = 13

    def __init__(self, sends, nt, shard, full, here):
        self.sends, self.nt, self.shard, self.full = sends, nt, shard, full
        self.z, self.d, self.core, self.x, self.y = here
        self.rows, self.width = shard.shape

    def to(self, k):
        return {"dp": xor_peer(self.core, self.x, self.y, k)}

    def ref(self, k, part=None):
        return self.full.at[dp_rows(xor_peer(self.core, self.x, self.y, k), self.rows, part), :]

    def begin(self, sem):
        mine = self.full.at[dp_rows(self.d, self.rows), columns(self.z, self.width)]
        self.local = pltpu.make_async_copy(self.shard, mine, sem)
        self.local.start()
        self.zs = []
        for dz in range(1, self.nt):
            to = {"tensor": lax.rem(self.z + dz, self.nt)}
            self.zs.append(self.sends.start(self.shard, mine, to))

    def column(self):
        self.local.wait()
        for copy in self.zs:
            copy.wait_recv()
        own_a, own_b = self.ref(0, 0), self.ref(0, 1)
        self.x0 = self.sends.start(own_a, own_a, self.to(2))
        self.y0 = self.sends.start(own_b, own_b, self.to(4))
        self.c = [self.sends.start(self.ref(0), self.ref(0), self.to(1))]
        self.y1 = self.sends.start(own_a, own_a, self.to(4))
        self.x1 = self.sends.start(own_b, own_b, self.to(2))

    def forward(self):
        self.x0.wait_recv()
        self.y2 = self.sends.start(self.ref(2, 0), self.ref(2, 0), self.to(4))
        self.y0.wait_recv()
        self.x2 = self.sends.start(self.ref(4, 1), self.ref(4, 1), self.to(2))
        self.x1.wait_recv()
        self.c.append(self.sends.start(self.ref(2), self.ref(2), self.to(1)))
        self.y1.wait_recv()
        self.c.append(self.sends.start(self.ref(4), self.ref(4), self.to(1)))

    def corner(self):
        self.y2.wait_recv()
        self.x2.wait_recv()
        self.c.append(self.sends.start(self.ref(6), self.ref(6), self.to(1)))

    def finish(self):
        for copy in self.c:
            copy.wait_recv()


class Reduce:
    MESSAGES = 18

    @staticmethod
    def scratch(rows, width, nt, wz):
        half = rows // 2
        shapes = [(4, rows, width), (2, half, width), (2, half, width), (half, width), (half, width), (nt, rows, wz)]
        return [pltpu.VMEM(s, BF16) for s in shapes]

    def __init__(self, sends, nt, g, bufs, cuts, here):
        self.sends, self.nt, self.g, self.cuts = sends, nt, g, cuts
        self.rc, self.ra, self.rb, self.ta, self.tb, self.rz = bufs
        self.z, self.d, self.core, self.x, self.y = here
        self.rows = self.rc.shape[1]

    def to(self, k):
        return {"dp": xor_peer(self.core, self.x, self.y, k)}

    def rows_of(self, y, x, core, part=None):
        return dp_rows(4 * y + 2 * x + core, self.rows, part)

    def add(self, rows, other):
        self.g[rows, :] = (self.g[rows, :].astype(F32) + other.astype(F32)).astype(BF16)

    def begin(self):
        self.got = []
        for q in range(4):
            src = self.g.at[self.rows_of(q // 2, q % 2, 1 - self.core), :]
            self.got.append(self.sends.start(src, self.rc.at[q], self.to(1)))

    def first(self):
        for q in range(4):
            self.got[q].wait_recv()
            self.add(self.rows_of(q // 2, q % 2, self.core), self.rc[q])
        self.a = []
        self.b = []
        for i in range(2):
            src = self.g.at[self.rows_of(i, 1 - self.x, self.core, 0), :]
            self.a.append(self.sends.start(src, self.ra.at[i], self.to(2)))
            src = self.g.at[self.rows_of(1 - self.y, i, self.core, 1), :]
            self.b.append(self.sends.start(src, self.rb.at[i], self.to(4)))

    def second(self):
        for i in range(2):
            self.a[i].wait_recv()
            self.add(self.rows_of(i, self.x, self.core, 0), self.ra[i])
            self.b[i].wait_recv()
            self.add(self.rows_of(self.y, i, self.core, 1), self.rb[i])
        src = self.g.at[self.rows_of(1 - self.y, self.x, self.core, 0), :]
        self.a2 = self.sends.start(src, self.ta, self.to(4))
        src = self.g.at[self.rows_of(self.y, 1 - self.x, self.core, 1), :]
        self.b2 = self.sends.start(src, self.tb, self.to(2))

    def third(self):
        self.a2.wait_recv()
        self.add(dp_rows(self.d, self.rows, 0), self.ta[...])
        self.b2.wait_recv()
        self.add(dp_rows(self.d, self.rows, 1), self.tb[...])
        rows = dp_rows(self.d, self.rows)
        self.zs = []
        at = 0
        for base, size, by_t in self.cuts:
            dst = self.rz.at[self.z, :, pl.ds(at, size)]
            for dz in range(1, self.nt):
                t = lax.rem(self.z + dz, self.nt)
                src = self.g.at[rows, cut_at(base, size, by_t, t)]
                self.zs.append(self.sends.start(src, dst, {"tensor": t}))
            self.rz[self.z, :, at : at + size] = self.g[rows, cut_at(base, size, by_t, self.z)]
            at += size

    def last(self, *outs):
        for copy in self.zs:
            copy.wait_recv()
        at = 0
        for out, (_, size, _) in zip(outs, self.cuts):
            total = self.rz[0, :, at : at + size].astype(F32)
            for t in range(1, self.nt):
                total = total + self.rz[t, :, at : at + size].astype(F32)
            out[...] = total
            at += size


class SmallSum:
    MESSAGES = 6

    @staticmethod
    def scratch(shape, nt):
        return [pltpu.VMEM((3,) + shape, F32), pltpu.VMEM((3,) + shape, F32), pltpu.VMEM((nt,) + shape, F32)]

    def __init__(self, sends, nt, v, bufs, here):
        self.sends, self.nt, self.v = sends, nt, v
        self.own, self.got, self.rz = bufs
        self.z, self.d, self.core, self.x, self.y = here

    def begin(self):
        self.own[0] = self.v[...]
        self.copy = self.sends.start(self.own.at[0], self.got.at[0], {"dp": xor_peer(self.core, self.x, self.y, 1)})

    def step(self, k):
        self.copy.wait_recv()
        total = self.own[k - 1] + self.got[k - 1]
        if k < 3:
            self.own[k] = total
            self.copy = self.sends.start(
                self.own.at[k], self.got.at[k], {"dp": xor_peer(self.core, self.x, self.y, 2**k)}
            )
        else:
            self.rz[self.z] = total
            self.zs = [
                self.sends.start(self.rz.at[self.z], self.rz.at[self.z], {"tensor": lax.rem(self.z + dz, self.nt)})
                for dz in range(1, self.nt)
            ]

    def last(self):
        for copy in self.zs:
            copy.wait_recv()
        total = self.rz[0]
        for t in range(1, self.nt):
            total = total + self.rz[t]
        return total


class Chain:
    def __init__(self, nt, by, mine, whole, got, out, send, recv):
        self.mine, self.whole, self.got, self.out, self.send, self.recv = mine, whole, got, out, send, recv
        z = lax.axis_index("tensor")
        self.seqs, _, di = got.shape
        self.per = di // WIDE
        self.pieces = self.seqs * self.per
        self.at = z if by > 0 else nt - 1 - z
        self.has_prev = self.at > 0
        self.has_next = self.at < nt - 1
        self.next = {"tensor": lax.rem(z + by + nt, nt)}
        self.begin_slot = 3 * self.at - 1

    def copy(self, k):
        s = k // self.per
        cols = pl.ds(pl.multiple_of((k - s * self.per) * WIDE, WIDE), WIDE)
        return pltpu.make_async_remote_copy(
            src_ref=self.out.at[s, :, cols], dst_ref=self.got.at[s, :, cols], send_sem=self.send.at[k],
            recv_sem=self.recv.at[k], device_id=self.next, device_id_type=MESH,
        )

    def pass_on(self, k, first):
        s = k // self.per
        cols = pl.ds(pl.multiple_of((k - s * self.per) * WIDE, WIDE), WIDE)
        v = self.mine[s, :, cols].astype(F32)
        if not first:
            v = v + self.whole[s, 0:1, cols] * self.got[s, :, cols].astype(F32)
        self.out[s, :, cols] = v.astype(BF16)
        self.copy(k).start()

    def begin(self):
        @pl.when(jnp.logical_not(self.has_prev))
        def _():
            self.got[...] = jnp.zeros_like(self.got)
            for k in range(self.pieces):
                self.pass_on(k, True)

    def step(self, k):
        self.copy(k).wait_recv()

        @pl.when(self.has_next)
        def _():
            self.pass_on(k, False)

    def slot(self, n):
        since = n - self.begin_slot

        @pl.when(self.has_prev & (since >= 0) & (lax.rem(since + 8, 2) == 0) & (since < 2 * self.pieces))
        def _():
            self.step(since // 2)

    def rest(self, slots, first, last):
        for k in range(first, last):

            @pl.when(self.has_prev & (self.begin_slot + 2 * k >= slots))
            def _(k=k):
                self.step(k)

    def finish(self):
        @pl.when(self.has_next)
        def _():
            for k in range(self.pieces):
                self.copy(k).wait_send()


class Moves:
    def __init__(self, sems):
        self.sems, self.used, self.open = sems, 0, []

    def start(self, src, dst):
        copy = pltpu.make_async_copy(src, dst, self.sems.at[self.used])
        self.used += 1
        copy.start()
        self.open.append(copy)
        return copy

    def finish(self, done=()):
        for copy in self.open:
            if all(copy is not other for other in done):
                copy.wait()


def heads_table(sel_ref, di):
    r = lax.broadcasted_iota(jnp.int32, (128, WIDE), 0)
    c = lax.broadcasted_iota(jnp.int32, (128, WIDE), 1)
    for c0 in range(0, di, WIDE):
        hit = ((r & 31) == ((c + c0) >> 6)) & (r < 64)
        sel_ref[:, c0 : c0 + WIDE] = jnp.where(hit, 1.0, 0.0).astype(BF16)


def heads_table_t(selt_ref, di):
    c = lax.broadcasted_iota(jnp.int32, (WIDE, 128), 0)
    r = lax.broadcasted_iota(jnp.int32, (WIDE, 128), 1)
    for c0 in range(0, di, WIDE):
        selt_ref[c0 : c0 + WIDE, :] = jnp.where(r == ((c + c0) >> 6), 1.0, 0.0).astype(BF16)


def ones_below(tri_ref, up):
    r = lax.broadcasted_iota(jnp.int32, (SPAN, SPAN), 0)
    c = lax.broadcasted_iota(jnp.int32, (SPAN, SPAN), 1)
    tri_ref[...] = jnp.where(r <= c if up else r >= c, 1.0, 0.0).astype(BF16)


def forward_kernel(heads, nt, nd, gathers, *refs):
    refs = list(refs)
    take = lambda n: [refs.pop(0) for _ in range(n)]
    x_hbm, c_hbm, gain_ref, ts_ref = take(4)
    if gathers:
        pack_ref, wo_ref, wsh_ref, par_ref, xl_ref = take(5)
    else:
        w1_hbm, w2_hbm, w3_hbm, ws_hbm, parf_ref, xhf_ref = take(6)
    (out_hbm, h_hbm, rawi_hbm, raws_hbm, xs_hbm, bc_hbm, w1_out, w2_out, ws_out, yn_hbm, dgate_hbm, dy_hbm) = take(12)
    (draw_ref, acs_ref, bs_ref, rr_ref, fresh_ref, vv_ref, mineb_ref, dec_ref, whole_ref, sin_ref, chan_ref, dpar_ref,
     skip_ref, gg_ref, sk_ref) = take(15)
    (x_ref, c_ref, h_ref, w1_ref, w2_ref, w3_ref, ws_ref, pf_ref, xh_ref, rawi_ref, raws_ref, xs_ref, bc_ref, y_ref,
     gate_ref, yn_ref, dgate_ref, dy_ref, q_ref, g_ref, mine_ref, sb_ref, hh_ref, ea_ref, bst_ref,
     sel_ref, selt_ref, tri_ref, wot_ref) = take(29)
    send, recv, chain_send, chain_recv, local, moves = take(6)

    tokens, dim = x_ref.shape
    seqs, ext, di = rawi_ref.shape
    span = ext - 16
    per = span // SPAN
    blocks = seqs * per
    sh = bc_ref.shape[1]
    state = sh // 2
    dcol = di // nt
    wa = dcol - 128
    inner = nt * wa
    z = lax.axis_index("tensor")
    store = Moves(moves)
    load_x = store.start(x_hbm, x_ref)
    load_c = store.start(c_hbm, c_ref)

    sends = Sends(send, recv)
    zpeers = [{"tensor": lax.rem(z + dz, nt)} for dz in range(1, nt)]
    if gathers:
        here = place()
        _, d, core, x, y = here
        wot_ref[...] = wo_ref[...].astype(F32).T.astype(BF16)
        greet(zpeers + [{"dp": xor_peer(core, x, y, k)} for k in range(1, 8)])
        shards = (
            (pack_ref.at[:, pl.ds(0, wa)], w1_ref.at[:, pl.ds(0, inner)]),
            (pack_ref.at[:, pl.ds(wa, 256)], w1_ref.at[:, pl.ds(inner, 256 * nt)]),
            (pack_ref.at[:, pl.ds(wa + 256, dcol)], w2_ref),
            (wot_ref, w3_ref),
        )
        secs = [Gather(sends, nt, a, b, here) for a, b in shards]
        secs[0].begin(local.at[0])
        mine = ws_ref.at[dp_rows(d, wsh_ref.shape[0]), :]
        own = [pltpu.make_async_copy(wsh_ref, mine, local.at[4]), pltpu.make_async_copy(par_ref, pf_ref.at[z], local.at[5])]
        for copy in own:
            copy.start()
        got = [sends.start(wsh_ref, mine, {"dp": xor_peer(core, x, y, k)}) for k in range(1, 8)]
        got += [sends.start(par_ref, pf_ref.at[z], to) for to in zpeers]
        edge = sends.make(xl_ref, xh_ref, {"tensor": lax.rem(z + 1, nt)})

        @pl.when(z < nt - 1)
        def _():
            edge.start()

        for k in range(1, len(secs)):
            secs[k].begin(local.at[k])
    else:
        greet(({"tensor": lax.rem(z + nt - 1, nt)}, {"tensor": lax.rem(z + 1, nt)}))
        loads = [store.start(a, b) for a, b in ((w1_hbm, w1_ref), (w2_hbm, w2_ref), (w3_hbm, w3_ref), (ws_hbm, ws_ref))]
        pf_ref[...] = parf_ref[...]
        xh_ref[...] = xhf_ref[...]

    heads_table(sel_ref, di)
    heads_table_t(selt_ref, di)
    ones_below(tri_ref, False)

    def norm(v):
        v = v.astype(F32)
        return (v * lax.rsqrt(jnp.mean(v * v, axis=-1, keepdims=True) + EPSILON) * gain_ref[...]).astype(BF16)

    load_x.wait()

    def norm_step(b, c):
        rows = block_rows(b, SPAN)
        h_ref[rows, :] = norm(x_ref[rows, :])
        return c

    lax.fori_loop(0, blocks, norm_step, 0)
    store.start(h_ref, h_hbm)

    if gathers:
        for copy in own:
            copy.wait()
        secs[0].column()
        secs[1].column()
        for copy in got:
            copy.wait_recv()

        @pl.when(z > 0)
        def _():
            edge.wait_recv()

        @pl.when(z == 0)
        def _():
            xh_ref[...] = jnp.zeros_like(xh_ref)

    hh_ref[...] = norm(xh_ref[...])
    head = pf_ref[0, 8:16, 0:128]
    for t in range(nt):
        chan_ref[:, dcol * t : dcol * (t + 1)] = pf_ref[t, 0:8, :]
        if t > 0:
            head = head + pf_ref[t, 8:16, 0:128]
    ak = -jnp.exp(head[0:1])
    ak = jnp.where(lanes_of(ak.shape) < heads, ak, 0.0)
    dpar_ref[0:1, :] = head[1:2]
    dpar_ref[1:2, :] = ak * LOG2E
    dpar_ref[2:3, :] = ak
    dpar_ref[3:8, :] = jnp.zeros((5, 128), F32)
    sk8 = packed(jnp.broadcast_to(head[2:3], (8, 128)), heads)
    for c0 in range(0, di, WIDE):
        skip_ref[:, c0 : c0 + WIDE] = spread_heads(sk8, sel_ref[:, c0 : c0 + WIDE])

    def conv(raw, par, out, cols):
        def step(r, c):
            s = r // (span // 128)
            r0 = pl.multiple_of((r - s * (span // 128)) * 128, 128)
            v = raw[s, pl.ds(r0, 144), cols]
            acc = par[4:5, cols] + par[0:1, cols] * v[13:141]
            for k in range(1, 4):
                acc = acc + par[k : k + 1, cols] * v[13 + k : 141 + k]
            out[pl.ds(pl.multiple_of(s * span + r0, 128), 128), cols] = (acc * sigmoid(acc)).astype(BF16)
            return c

        lax.fori_loop(0, seqs * span // 128, step, 0)

    for s in range(seqs):
        rows = slice(span * s, span * (s + 1))
        raws_ref[s, 0:16, :] = dot(hh_ref[16 * s : 16 * s + 16, :], ws_ref[...])
        raws_ref[s, 16:ext, :] = dot(h_ref[rows, :], ws_ref[...])
    for c0 in range(0, sh, 256):
        conv(raws_ref, ts_ref, bc_ref, slice(c0, c0 + 256))
    store.start(raws_ref, raws_hbm)
    store.start(bc_ref, bc_hbm)
    store.start(ws_ref, ws_out)

    if gathers:
        secs[0].forward()
        secs[2].column()
        secs[1].forward()
        secs[0].corner()
        secs[0].finish()
    else:
        loads[0].wait()
    for t in range(nt):
        cols = slice(dcol * t, dcol * t + wa)
        for s in range(seqs):
            w = w1_ref[:, wa * t : wa * (t + 1)]
            rawi_ref[s, 0:16, cols] = dot(hh_ref[16 * s : 16 * s + 16, :], w)
            rawi_ref[s, 16:ext, cols] = dot(h_ref[span * s : span * (s + 1), :], w)
        conv(rawi_ref, chan_ref, xs_ref, cols)
    if gathers:
        secs[1].corner()
        secs[2].forward()
        secs[3].column()
        secs[1].finish()
    store.start(w1_ref, w1_out)
    for t in range(nt):
        cols = slice(dcol * t + wa, dcol * (t + 1))
        for s in range(seqs):
            rows = slice(span * s, span * (s + 1))
            w = w1_ref[:, inner + 256 * t : inner + 256 * (t + 1)]
            rawi_ref[s, 0:16, cols] = dot(hh_ref[16 * s : 16 * s + 16, :], w[:, :128])
            both = dot(h_ref[rows, :], w)
            rawi_ref[s, 16:ext, cols] = both[:, :128]
            if t == 0:
                draw_ref[rows, :] = both[:, 128:] + dpar_ref[0:1, :]
            else:
                draw_ref[rows, :] += both[:, 128:]
        conv(rawi_ref, chan_ref, xs_ref, cols)
    store.start(rawi_ref, rawi_hbm)
    store.start(xs_ref, xs_hbm)
    if gathers:
        secs[3].forward()
        secs[2].corner()

    def block_step(b, c):
        rows = block_rows(b, SPAN)
        s = b // per
        j = b - s * per
        x = draw_ref[rows, :]
        dt = jnp.maximum(x, 0.0) + jnp.log1p(jnp.exp(-jnp.abs(x)))
        lg = jnp.where(x < -20.0, x * LOG2E, jnp.log2(jnp.maximum(dt, 1e-30)))
        acs = cumulate(tri_ref[...], dt * dpar_ref[1:2, :], heads)
        bs = acs - lg
        acs_ref[rows, :] = acs
        bs_ref[rows, :] = bs
        end = acs[SPAN - 1 : SPAN, :]
        wk = packed(jnp.exp2(end - bs), heads)
        bt = bc_ref[rows, :state].astype(F32).T.astype(BF16)
        dk = packed(jnp.broadcast_to(jnp.exp2(end), (8, 128)), heads)
        for c0 in range(0, di, WIDE):
            cols = slice(c0, c0 + WIDE)
            w = spread_heads(wk, sel_ref[:, cols])
            wx = (w * xs_ref[rows, cols].astype(F32)).astype(BF16)
            fresh = dot(bt, wx)
            de = spread_heads(dk, sel_ref[:, cols])
            dec_ref[b, :, cols] = de

            @pl.when(j == 0)
            def _(cols=cols, fresh=fresh, de=de):
                fresh_ref[s, :, cols] = fresh.astype(BF16)
                mine_ref[s, :, cols] = fresh
                whole_ref[s, :, cols] = de

            @pl.when(j > 0)
            def _(cols=cols, fresh=fresh, de=de):
                mine_ref[s, :, cols] = de[0:1] * mine_ref[s, :, cols] + fresh
                whole_ref[s, :, cols] = de * whole_ref[s, :, cols]

        return c

    lax.fori_loop(0, blocks, block_step, 0)
    chain = Chain(nt, 1, mine_ref, whole_ref, sin_ref, sb_ref, chain_send, chain_recv)
    chain.begin()
    if gathers:
        secs[3].corner()

    lower = lax.broadcasted_iota(jnp.int32, (HALF, HALF), 0) >= lax.broadcasted_iota(jnp.int32, (HALF, HALF), 1)
    first = lanes_of((HALF, 128)) < P_SIZE
    pairs = di // 128

    def intra_step(b, carry):
        rows = block_rows(b, SPAN)
        bst_ref[...] = bs_ref[rows, :].T
        bb = bc_ref[rows, :state]
        cc = bc_ref[rows, state:]
        g00 = dot_nt(cc[:HALF], bb[:HALF])
        g10 = dot_nt(cc[HALF:], bb[:HALF])
        g11 = dot_nt(cc[HALF:], bb[HALF:])
        for p in range(pairs):
            cols = slice(128 * p, 128 * p + 128)
            xp = xs_ref[rows, cols]
            y0, y1 = [], []
            for h in (2 * p, 2 * p + 1):
                a0 = acs_ref[block_rows(2 * b, HALF), h : h + 1]
                a1 = acs_ref[block_rows(2 * b + 1, HALF), h : h + 1]
                r0 = bst_ref[h : h + 1, :HALF]
                r1 = bst_ref[h : h + 1, HALF:]
                m00 = jnp.where(lower, jnp.exp2(a0 - r0) * g00, 0.0).astype(BF16)
                m10 = (jnp.exp2(a1 - r0) * g10).astype(BF16)
                m11 = jnp.where(lower, jnp.exp2(a1 - r1) * g11, 0.0).astype(BF16)
                y0.append(dot(m00, xp[:HALF]))
                y1.append(dot(jnp.concatenate([m10, m11], axis=1), xp))
            y_ref[block_rows(2 * b, HALF), cols] = jnp.where(first, y0[0], y0[1])
            y_ref[block_rows(2 * b + 1, HALF), cols] = jnp.where(first, y1[0], y1[1])
            if (p + 1) % (pairs // 3) == 0:
                chain.slot(3 * b + (p + 1) // (pairs // 3) - 1)
        return carry

    lax.fori_loop(0, blocks, intra_step, 0)
    if gathers:
        for sec in secs[2:]:
            sec.finish()
    else:
        loads[1].wait()
        loads[2].wait()
    store.start(w2_ref, w2_out)

    def gate_step(b, carry):
        rows = block_rows(b, span)
        for c0 in range(0, di, WIDE):
            cols = slice(c0, c0 + WIDE)
            gate_ref[rows, cols] = dot(h_ref[rows, :], w2_ref[:, cols])
        return carry

    lax.fori_loop(0, seqs, gate_step, 0)
    chain.rest(3 * blocks, 0, chain.pieces)
    load_c.wait()

    gg_ref[...] = jnp.zeros_like(gg_ref)
    sk_ref[...] = jnp.zeros_like(sk_ref)

    def mid_step(b, carry):
        rows = block_rows(b, SPAN)
        s = b // per
        j = b - s * per
        ea_ref[...] = packed(jnp.exp2(acs_ref[rows, :]), heads)
        cc = bc_ref[rows, state:]
        ss = jnp.zeros((SPAN, 1), F32)
        for c0 in range(0, di, WIDE):
            cols = slice(c0, c0 + WIDE)
            prev = sin_ref[s, :, cols].astype(F32)
            later = dec_ref[s * per, 0:1, cols] * prev + fresh_ref[s, :, cols].astype(F32)
            s_in = jnp.where(j == 0, prev, later).astype(BF16)
            ea = spread_heads(ea_ref[...], sel_ref[:, cols])
            ynos = y_ref[rows, cols] + ea * dot(cc, s_in)
            y_ref[rows, cols] = ynos
            y = ynos + skip_ref[0:1, cols] * xs_ref[rows, cols].astype(F32)
            gate = gate_ref[rows, cols]
            g = y * (gate * sigmoid(gate))
            g_ref[:, cols] = g
            ss = ss + jnp.sum(g * g, axis=-1, keepdims=True)
        r2 = lax.rsqrt(ss / di + EPSILON)
        qg = jnp.zeros((SPAN, 1), F32)
        for c0 in range(0, di, WIDE):
            cols = slice(c0, c0 + WIDE)
            g = g_ref[:, cols]
            gain = chan_ref[5:6, cols]
            yn_ref[rows, cols] = (g * r2 * gain).astype(BF16)
            dyn = dot(c_ref[rows, :], w3_ref[:, cols])
            gg_ref[0:1, cols] += jnp.sum(dyn * (g * r2), axis=0, keepdims=True)
            q = dyn * gain
            q_ref[:, cols] = q
            qg = qg + jnp.sum(q * g, axis=-1, keepdims=True)
        x_ref[rows, :] = (x_ref[rows, :].astype(F32) + dot_nt(yn_ref[rows, :], w3_ref[...])).astype(BF16)
        coef = r2 * r2 * r2 * (qg / di)
        rr = jnp.zeros((SPAN, 128), F32)
        dk = jnp.zeros((SPAN, 128), F32)
        ct = cc.astype(F32).T.astype(BF16)
        for c0 in range(0, di, WIDE):
            cols = slice(c0, c0 + WIDE)
            xf = xs_ref[rows, cols].astype(F32)
            ynos = y_ref[rows, cols]
            y = ynos + skip_ref[0:1, cols] * xf
            gate = gate_ref[rows, cols]
            sg = sigmoid(gate)
            dg = r2 * q_ref[:, cols] - coef * g_ref[:, cols]
            dgate_ref[rows, cols] = (dg * y * (sg * (1.0 + gate * (1.0 - sg)))).astype(BF16)
            dyb = (dg * (gate * sg)).astype(BF16)
            dy_ref[rows, cols] = dyb
            dy = dyb.astype(F32)
            rr = rr + gather_heads(dy * ynos, selt_ref[cols, :])
            dk = dk + gather_heads(dy * xf, selt_ref[cols, :])
            ea = spread_heads(ea_ref[...], sel_ref[:, cols])
            vv = dot(ct, (ea * dy).astype(BF16))

            @pl.when(j == 0)
            def _(cols=cols, vv=vv):
                mine_ref[s, :, cols] = vv

            @pl.when(j > 0)
            def _(cols=cols, vv=vv):
                vv_ref[s, :, cols] = vv.astype(BF16)
                mine_ref[s, :, cols] += dec_ref[s * per, 0:1, cols] * vv

        rr_ref[rows, :] = rr
        sk_ref[0:1, :] += jnp.sum(dk, axis=0, keepdims=True)
        return carry

    lax.fori_loop(0, blocks, mid_step, 0)
    for a, b in ((x_ref, out_hbm), (yn_ref, yn_hbm), (dgate_ref, dgate_hbm), (dy_ref, dy_hbm)):
        store.start(a, b)
    mineb_ref[...] = mine_ref[...].astype(BF16)
    chain.finish()
    sends.finish()
    if gathers:

        @pl.when(z < nt - 1)
        def _():
            edge.wait_send()

    store.finish((load_x, load_c) if gathers else (load_x, load_c, *loads))


def backward_kernel(heads, nt, nd, reduces, *refs):
    refs = list(refs)
    take = lambda n: [refs.pop(0) for _ in range(n)]
    (x_hbm, c_hbm, h_hbm, rawi_hbm, raws_hbm, xs_hbm, bc_hbm, w1_hbm, w2_hbm, ws_hbm, yn_hbm, dgate_hbm, dy_hbm,
     draw_hbm, acs_hbm, bs_hbm, rr_hbm, fresh_hbm, vv_hbm, sin_hbm) = take(20)
    gain_ref, ts_ref, mineb_ref, dec_ref, whole_ref, chan_ref, dpar_ref, skip_ref, gg_ref, sk_ref = take(10)
    (ig_hbm,) = take(1)
    if reduces:
        o1_ref, os_ref, o2_ref, o3_ref, om_ref = take(5)
    else:
        g1_out, g2_out, g3_out, sm_ref = take(4)
    (c_ref, h_ref, rawi_ref, raws_ref, xs_ref, bc_ref, w1_ref, ws_ref, dgate_ref, dy_ref, draw_ref,
     acs_ref, bs_ref, rr_ref, fresh_ref, vv_ref, sin_ref, ds_ref, sb_ref, din_ref, dx_ref, dbc_ref, g_ref, halo_ref,
     edge_ref, keep_ref, acst_ref, dg_ref, sel_ref, selt_ref, triu_ref, tg_ref, small_ref, ng_ref) = take(34)
    if reduces:
        (sm_ref,) = take(1)
        bufs = [take(6) for _ in range(4)]
        small_bufs = take(3)
    chain_send, chain_recv, halo_send, halo_recv, moves = take(5)
    if reduces:
        sems = [take(2) for _ in range(5)]

    tokens, dim = h_ref.shape
    seqs, ext, di = rawi_ref.shape
    span = ext - 16
    per = span // SPAN
    blocks = seqs * per
    sh = bc_ref.shape[1]
    state = sh // 2
    dcol = di // nt
    wa = dcol - 128
    na = nt * wa
    inner = na + 256 * nt
    z = lax.axis_index("tensor")
    move = Moves(moves)
    load = lambda a, b: move.start(a, b)
    yn_ref = din_ref.at[:, pl.ds(0, di)]
    l_c, l_yn, l_h, l_dgate = load(c_hbm, c_ref), load(yn_hbm, yn_ref), load(h_hbm, h_ref), load(dgate_hbm, dgate_ref)
    l_scan = [
        load(a, b)
        for a, b in (
            (xs_hbm, xs_ref), (dy_hbm, dy_ref), (bc_hbm, bc_ref), (acs_hbm, acs_ref), (bs_hbm, bs_ref),
        )
    ]
    l_state = [
        load(a, b)
        for a, b in (
            (draw_hbm, draw_ref), (rr_hbm, rr_ref), (fresh_hbm, fresh_ref), (vv_hbm, vv_ref), (sin_hbm, sin_ref),
            (rawi_hbm, rawi_ref), (raws_hbm, raws_ref),
        )
    ]
    l_last = [load(w1_hbm, w1_ref), load(ws_hbm, ws_ref)]
    w2_ref = dy_ref.at[pl.ds(0, dim), :]
    x_ref = xs_ref.at[:, pl.ds(0, dim)]

    if reduces:
        here = place()
        _, d, core, x, y = here
        others = [{"tensor": lax.rem(z + dz, nt)} for dz in range(1, nt)]
        greet(others + [{"dp": xor_peer(core, x, y, k)} for k in (1, 2, 4)])
        cut = ((0, dcol, True),)
        parts = (
            (g_ref.at[:, pl.ds(0, di)], cut), (g_ref.at[:, pl.ds(di, di)], cut),
            (g_ref.at[:, pl.ds(0, na)], ((0, wa, True),)),
            (g_ref.at[:, pl.ds(na, inner + sh - na)], ((0, 256, True), (256 * nt, sh, False))),
        )
        r3, r2, ra, rb = (Reduce(Sends(*sems[i]), nt, g, bufs[i], cuts, here) for i, (g, cuts) in enumerate(parts))
        small_sum = SmallSum(Sends(*sems[4]), nt, sm_ref, small_bufs, here)
    else:
        greet(({"tensor": lax.rem(z + nt - 1, nt)}, {"tensor": lax.rem(z + 1, nt)}))

    chain = Chain(nt, -1, mineb_ref, whole_ref, ds_ref, sb_ref, chain_send, chain_recv)
    chain.begin()
    heads_table(sel_ref, di)
    heads_table_t(selt_ref, di)
    ones_below(triu_ref, True)
    small_ref[...] = jnp.zeros_like(small_ref)
    ng_ref[...] = jnp.zeros_like(ng_ref)
    tg_ref[...] = jnp.zeros_like(tg_ref)

    l_c.wait()
    l_yn.wait()
    slot = 0
    for c0 in range(0, di, WIDE):
        g_ref[:, c0 : c0 + WIDE] = dot_tn(c_ref[...], din_ref[:, c0 : c0 + WIDE]).astype(BF16)
        chain.slot(slot)
        slot += 1
    if reduces:
        r3.begin()
    else:
        s3 = move.start(g_ref.at[:, pl.ds(0, di)], g3_out)
    l_h.wait()
    l_dgate.wait()
    for c0 in range(0, di, WIDE):
        g_ref[:, di + c0 : di + c0 + WIDE] = dot_tn(h_ref[...], dgate_ref[:, c0 : c0 + WIDE]).astype(BF16)
        chain.slot(slot)
        slot += 1
    if reduces:
        r2.begin()
        r3.first()
    else:
        s2 = move.start(g_ref.at[:, pl.ds(di, di)], g2_out)

    for copy in l_scan:
        copy.wait()
    upper = lax.broadcasted_iota(jnp.int32, (HALF, HALF), 0) <= lax.broadcasted_iota(jnp.int32, (HALF, HALF), 1)
    first = lanes_of((HALF, 128)) < P_SIZE
    first_all = lanes_of((SPAN, 128)) < P_SIZE
    pairs = di // 128
    slot0 = slot

    def intra_step(b, carry):
        rows = block_rows(b, SPAN)
        acst_ref[...] = acs_ref[rows, :].T
        bb = bc_ref[rows, :state]
        cc = bc_ref[rows, state:]
        g00 = dot_nt(bb[:HALF], cc[:HALF])
        g01 = dot_nt(bb[:HALF], cc[HALF:])
        g11 = dot_nt(bb[HALF:], cc[HALF:])
        dg_ref[...] = jnp.zeros_like(dg_ref)
        for p in range(pairs):
            cols = slice(128 * p, 128 * p + 128)
            xp = xs_ref[rows, cols]
            dyp = dy_ref[rows, cols]
            d0, d1 = [], []
            for i, h in enumerate((2 * p, 2 * p + 1)):
                keep = first_all if i == 0 else jnp.logical_not(first_all)
                xm = jnp.where(keep, xp, jnp.zeros_like(xp))
                b0 = bs_ref[block_rows(2 * b, HALF), h : h + 1]
                b1 = bs_ref[block_rows(2 * b + 1, HALF), h : h + 1]
                r0 = acst_ref[h : h + 1, :HALF]
                r1 = acst_ref[h : h + 1, HALF:]
                e00 = jnp.where(upper, jnp.exp2(r0 - b0), 0.0)
                e01 = jnp.exp2(r1 - b0)
                e11 = jnp.where(upper, jnp.exp2(r1 - b1), 0.0)
                m0 = jnp.concatenate([(e00 * g00).astype(BF16), (e01 * g01).astype(BF16)], axis=1)
                m1 = (e11 * g11).astype(BF16)
                d0.append(dot(m0, dyp))
                d1.append(dot(m1, dyp[HALF:]))
                dm0 = dot_nt(xm[:HALF], dyp)
                dm1 = dot_nt(xm[HALF:], dyp[HALF:])
                dg_ref[0] += dm0[:, :HALF] * e00
                dg_ref[1] += dm0[:, HALF:] * e01
                dg_ref[2] += dm1 * e11
            dx_ref[block_rows(2 * b, HALF), cols] = jnp.where(first, d0[0], d0[1])
            dx_ref[block_rows(2 * b + 1, HALF), cols] = jnp.where(first, d1[0], d1[1])
            if (p + 1) % (pairs // 3) == 0:
                chain.slot(slot0 + 3 * b + (p + 1) // (pairs // 3) - 1)
        dg00 = dg_ref[0]
        dg01 = dg_ref[1]
        dg11 = dg_ref[2]
        dbc_ref[block_rows(2 * b, HALF), :state] = dot(jnp.concatenate([dg00, dg01], axis=1).astype(BF16), cc)
        dbc_ref[block_rows(2 * b + 1, HALF), :state] = dot(dg11.astype(BF16), cc[HALF:])
        dbc_ref[block_rows(2 * b, HALF), state:] = dot(dg00.T.astype(BF16), bb[:HALF])
        dbc_ref[block_rows(2 * b + 1, HALF), state:] = dot(
            jnp.concatenate([dg01.T, dg11.T], axis=1).astype(BF16), bb
        )
        return carry

    lax.fori_loop(0, blocks // 2, intra_step, 0)
    if reduces:
        r3.second()
        r2.first()
    lax.fori_loop(blocks // 2, blocks, intra_step, 0)
    if reduces:
        r3.third()
        r2.second()
    chain.rest(slot0 + 3 * blocks, 0, chain.pieces)
    for copy in l_state:
        copy.wait()

    def state_step(s, j):
        b = s * per + j
        rows = block_rows(b, SPAN)
        acs = acs_ref[rows, :]
        end = acs[SPAN - 1 : SPAN, :]
        eak = packed(jnp.exp2(acs), heads)
        wk = packed(jnp.exp2(end - bs_ref[rows, :]), heads)
        bb = bc_ref[rows, :state]
        db = dbc_ref[rows, :state]
        dc = dbc_ref[rows, state:]
        pin = jnp.zeros((SPAN, 128), F32)
        pst = jnp.zeros((SPAN, 128), F32)
        endsum = jnp.zeros((8, 128), F32)
        for c0 in range(0, di, WIDE):
            cols = slice(c0, c0 + WIDE)
            s_in = sin_ref[s, :, cols]
            ds = ds_ref[s, :, cols]
            if j > 0:
                s_in = dec_ref[s * per, 0:1, cols] * s_in.astype(F32) + fresh_ref[s, :, cols].astype(F32)
                s_in = s_in.astype(BF16)
            if j < per - 1:
                ds = dec_ref[s * per + per - 1, 0:1, cols] * ds.astype(F32) + vv_ref[s, :, cols].astype(F32)
                ds = ds.astype(BF16)
            w = spread_heads(wk, sel_ref[:, cols])
            ea = spread_heads(eak, sel_ref[:, cols])
            xf = xs_ref[rows, cols].astype(F32)
            dyf = dy_ref[rows, cols].astype(F32)
            dxs = w * dot(bb, ds)
            dxi = dx_ref[rows, cols]
            pin = pin + gather_heads(dxi * xf, selt_ref[cols, :])
            pst = pst + gather_heads(dxs * xf, selt_ref[cols, :])
            both = jnp.sum(ds.astype(F32) * s_in.astype(F32), axis=0, keepdims=True) * dec_ref[b, 0:1, cols]
            endsum = endsum + gather_heads(jnp.broadcast_to(both, (8, WIDE)), selt_ref[cols, :])
            dc = dc + dot_nt((ea * dyf).astype(BF16), s_in)
            db = db + dot_nt((w * xf).astype(BF16), ds)
            dx_ref[rows, cols] = dxi + dxs + skip_ref[0:1, cols] * dyf
        dbc_ref[rows, :state] = db
        dbc_ref[rows, state:] = dc
        pp = pin + pst
        da = cumulate(triu_ref[...], rr_ref[rows, :] - pp, heads)
        da = da + (endsum[0:1, :] + jnp.sum(pst, axis=0, keepdims=True))
        xx = draw_ref[rows, :]
        sg = 1.0 / (1.0 + jnp.exp(-xx))
        dt = jnp.maximum(xx, 0.0) + jnp.log1p(jnp.exp(-jnp.abs(xx)))
        ratio = jnp.where(xx < -20.0, 1.0, sg / jnp.maximum(dt, 1e-30))
        ak = dpar_ref[2:3, :]
        dd = da * ak * sg + pp * ratio
        for t in range(nt):
            din_ref[rows, na + 256 * t + 128 : na + 256 * (t + 1)] = dd.astype(BF16)
        small_ref[0:1, :] += jnp.sum(da * dt * ak, axis=0, keepdims=True)
        small_ref[1:2, :] += jnp.sum(dd, axis=0, keepdims=True)

        def conv_back(raw, par, dact, off, cols):
            here_cols = slice(off + cols.start, off + cols.stop)

            def step(r, prev):
                r0 = pl.multiple_of(r * HALF, HALF)
                at = pl.ds(pl.multiple_of(16 + j * SPAN + r0, 16), HALF)
                now = raw[s, at, cols]
                v = jnp.concatenate([prev, now], axis=0)
                sh_v = [v[13 + k : 13 + k + HALF] for k in range(4)]
                pre = par[4:5, cols] + par[0:1, cols] * sh_v[0]
                for k in range(1, 4):
                    pre = pre + par[k : k + 1, cols] * sh_v[k]
                sg = sigmoid(pre)
                dp = dact[pl.ds(pl.multiple_of(b * SPAN + r0, HALF), HALF), cols] * (sg * (1.0 + pre * (1.0 - sg)))
                raw[s, at, cols] = dp
                for k in range(4):
                    tg_ref[k : k + 1, here_cols] += jnp.sum(dp * sh_v[k], axis=0, keepdims=True)
                tg_ref[4:5, here_cols] += jnp.sum(dp, axis=0, keepdims=True)
                return now[HALF - 16 :]

            prev = raw[s, 0:16, cols] if j == 0 else keep_ref[s, :, here_cols]
            prev = lax.fori_loop(0, SPAN // HALF, step, prev)
            if j < per - 1:
                keep_ref[s, :, here_cols] = prev

        for c0 in range(0, di, 256):
            conv_back(rawi_ref, chan_ref, dx_ref, 0, slice(c0, c0 + 256))
        for c0 in range(0, sh, 256):
            conv_back(raws_ref, ts_ref, dbc_ref, di, slice(c0, c0 + 256))

    halo_copy = pltpu.make_async_remote_copy(
        src_ref=edge_ref, dst_ref=halo_ref, send_sem=halo_send.at[0], recv_sem=halo_recv.at[0],
        device_id={"tensor": lax.rem(z + nt - 1, nt)}, device_id_type=MESH,
    )
    for j in range(per):

        def seq_step(s, carry, j=j):
            state_step(s, j)
            return carry

        lax.fori_loop(0, seqs, seq_step, 0)
        if j == 0:
            edge_ref[:, :, :di] = rawi_ref[:, 16:24, :]
            edge_ref[:, :, di:] = raws_ref[:, 16:24, :]

            @pl.when(z > 0)
            def _():
                halo_copy.start()

            if reduces:
                r3.last(o3_ref)
                r2.third()
    l_last += [load(w2_hbm, w2_ref), load(x_hbm, x_ref)]
    if reduces:
        r2.last(o2_ref)

    @pl.when(z < nt - 1)
    def _():
        halo_copy.wait_recv()

    @pl.when(z == nt - 1)
    def _():
        halo_ref[...] = jnp.zeros_like(halo_ref)

    def conv_t(dpre, par, off, c0, to):
        cols = slice(c0, c0 + 128)
        for s in range(seqs):
            for r0 in range(0, span, HALF):
                if r0 + HALF < span:
                    v = dpre[s, 16 + r0 : 16 + r0 + HALF + 8, cols]
                else:
                    v = jnp.concatenate([dpre[s, 16 + r0 : ext, cols], halo_ref[s, :, off + c0 : off + c0 + 128]], axis=0)
                acc = par[3:4, cols] * v[0:HALF]
                for k in range(3):
                    acc = acc + par[k : k + 1, cols] * v[3 - k : 3 - k + HALF]
                din_ref[s * span + r0 : s * span + r0 + HALF, to : to + 128] = acc.astype(BF16)

    for c0 in range(0, di, 128):
        t, r = divmod(c0, dcol)
        if r < wa:
            conv_t(rawi_ref, chan_ref, 0, c0, wa * t + r)
    if reduces:
        r3.sends.finish()
        r2.sends.finish()
    else:
        s3.wait()
        s2.wait()
    for c0 in range(0, na, WIDE):
        g_ref[:, c0 : c0 + WIDE] = dot_tn(h_ref[...], din_ref[:, c0 : c0 + WIDE]).astype(BF16)
    if reduces:
        ra.begin()
    for c0 in range(0, di, 128):
        t, r = divmod(c0, dcol)
        if r >= wa:
            conv_t(rawi_ref, chan_ref, 0, c0, na + 256 * t + r - wa)
    for c0 in range(0, sh, 128):
        conv_t(raws_ref, ts_ref, di, c0, inner + c0)
    for c0 in range(na, inner + sh, 256):
        g_ref[:, c0 : c0 + 256] = dot_tn(h_ref[...], din_ref[:, c0 : c0 + 256]).astype(BF16)
    if reduces:
        rb.begin()
        ra.first()
    else:
        move.start(g_ref.at[:, pl.ds(0, inner + sh)], g1_out)
    for copy in l_last:
        copy.wait()

    def last_step(b, carry):
        rows = block_rows(b, SPAN)
        dh = dot_nt(dgate_ref[rows, :], w2_ref[...])
        dh = dh + dot_nt(din_ref[rows, :inner], w1_ref[...])
        dh = dh + dot_nt(din_ref[rows, inner:], ws_ref[...])
        u = x_ref[rows, :].astype(F32)
        r1 = lax.rsqrt(jnp.mean(u * u, axis=-1, keepdims=True) + EPSILON)
        ng_ref[0:1, :] += jnp.sum(dh * u * r1, axis=0, keepdims=True)
        e = dh * gain_ref[...]
        m = jnp.mean(e * u, axis=-1, keepdims=True)
        x_ref[rows, :] = (c_ref[rows, :].astype(F32) + r1 * e - u * (r1 * r1 * r1 * m)).astype(BF16)
        return carry

    lax.fori_loop(0, blocks // 2, last_step, 0)
    if reduces:
        rb.first()
        ra.second()
    lax.fori_loop(blocks // 2, blocks, last_step, 0)
    move.start(x_ref, ig_hbm)
    sm_ref[0:5, :] = tg_ref[0:5, :di]
    sm_ref[5:6, :] = gg_ref[0:1, :]
    sm_ref[6:7, :dim] = ng_ref[0:1, :]
    flat = [(tg_ref, k, di, sh) for k in range(5)] + [(small_ref, 0, 0, 128), (small_ref, 1, 0, 128), (sk_ref, 0, 0, 128)]
    row, at = 6, dim
    for ref, k, c0, width in flat:
        if at + width > di:
            row, at = row + 1, 0
        sm_ref[row : row + 1, at : at + width] = ref[k : k + 1, c0 : c0 + width]
        at += width
    sm_ref[row : row + 1, at:] = jnp.zeros((1, di - at), F32)
    if reduces:
        small_sum.begin()
        rb.second()
        ra.third()
        small_sum.step(1)
        rb.third()
        small_sum.step(2)
        ra.last(o1_ref.at[:, pl.ds(0, wa)])
        small_sum.step(3)
        rb.last(o1_ref.at[:, pl.ds(wa, 256)], os_ref)
        om_ref[...] = small_sum.last()
        for part in (ra, rb, small_sum):
            part.sends.finish()
    chain.finish()

    @pl.when(z > 0)
    def _():
        halo_copy.wait_send()

    move.finish((l_c, l_yn, l_h, l_dgate, *l_scan, *l_state, *l_last) + (() if reduces else (s3, s2)))


def semaphores(n):
    return [pltpu.SemaphoreType.DMA((n,)), pltpu.SemaphoreType.DMA((n,))]


def shifted(v, axis, by):
    n = lax.axis_size(axis)
    return lax.ppermute(v, axis, [(i, i + by) for i in range(n) if 0 <= i + by < n])


def gather_all(nt, nd, pack, wo, ws, par, edge):
    both = ("tensor", "dp")
    rows = ws.shape[0]
    dcol = wo.shape[0]
    full = lax.all_gather(jnp.concatenate([pack, wo.T], axis=1), both, axis=0).reshape(nt, nd * rows, -1)
    whole = lambda a, b: full[:, :, a:b].transpose(1, 0, 2).reshape(nd * rows, nt * (b - a))
    w1 = jnp.concatenate([whole(0, dcol - 128), whole(dcol - 128, dcol + 128)], axis=1)
    return (
        w1, whole(dcol + 128, 2 * dcol + 128), whole(2 * dcol + 128, 3 * dcol + 128),
        lax.all_gather(ws, "dp", axis=0, tiled=True), lax.all_gather(par, "tensor", axis=0), shifted(edge, "tensor", 1),
    )


def reduce_all(nt, nd, g1, g2, g3, sm, sh):
    dim = g1.shape[0]
    rows = dim // nd
    dcol = g2.shape[1] // nt
    wa = dcol - 128
    part = wa + 256
    both = ("tensor", "dp")
    parts = [
        g[:, at : at + nt * w].reshape(dim, nt, w).transpose(1, 0, 2)
        for g, at, w in ((g1, 0, wa), (g1, wa * nt, 256), (g2, 0, dcol), (g3, 0, dcol))
    ]
    big = jnp.concatenate(parts, axis=2).reshape(nt * nd, rows, -1)
    big = lax.psum_scatter(big, both, scatter_dimension=0).astype(F32)
    shared = g1[:, nt * part :].reshape(nd, rows, sh).astype(F32)
    shared = lax.psum(lax.psum_scatter(shared, "dp", scatter_dimension=0), "tensor")
    return big[:, :part], shared, big[:, part : part + dcol], big[:, part + dcol :], lax.psum(sm, both)


def local(
    block_input, norm_gain, input_gate_inner_weight, input_shared_weight, input_delta_weight, conv_inner, shift_inner,
    conv_shared, shift_shared, decay_log, delta_bias, skip_gain, gated_gain, output_projection_weight, cotangent,
):
    nt = lax.axis_size("tensor")
    nd = lax.axis_size("dp")
    me = lax.axis_index("tensor")
    seqs, span, dim = block_input.shape
    tokens = seqs * span
    blocks = tokens // SPAN
    rows, _, dcol = input_gate_inner_weight.shape
    di = dcol * nt
    sh = input_shared_weight.shape[1]
    state = sh // 2
    hloc = input_delta_weight.shape[1]
    heads = hloc * nt
    w1w = (dcol + 128) * nt

    delta_w = lax.dynamic_update_slice(jnp.zeros((rows, 128), BF16), input_delta_weight, (0, me * hloc))
    pack = jnp.concatenate([input_gate_inner_weight[:, 1], delta_w, input_gate_inner_weight[:, 0]], axis=1)
    wo = output_projection_weight
    head = lax.dynamic_update_slice(
        jnp.zeros((8, dcol), F32), jnp.stack([decay_log, delta_bias, skip_gain]), (0, me * hloc)
    )
    par = jnp.concatenate([
        conv_inner.astype(F32), shift_inner.astype(F32)[None], gated_gain[None], jnp.zeros((2, dcol), F32), head], axis=0)
    edge = block_input[:, span - 16 :].reshape(seqs * 16, dim)
    ts = jnp.pad(jnp.concatenate([conv_shared.astype(F32), shift_shared.astype(F32)[None]], axis=0), ((0, 3), (0, 0)))
    gain = norm_gain[None]
    x = block_input.reshape(tokens, dim)
    c = cotangent.reshape(tokens, dim)

    gathers = nd == 8
    args = [x, c, gain, ts]
    kinds = [pl.ANY, pl.ANY, pltpu.VMEM, pltpu.VMEM]
    if gathers:
        args += [pack, wo, input_shared_weight, par, edge]
        kinds += [pltpu.VMEM] * 5
    else:
        args += gather_all(nt, nd, pack, wo, input_shared_weight, par, edge)
        kinds += [pl.ANY] * 4 + [pltpu.VMEM] * 2
    far = [
        ((tokens, dim), BF16), ((tokens, dim), BF16), ((seqs, span + 16, di), F32), ((seqs, span + 16, sh), F32),
        ((tokens, di), BF16), ((tokens, sh), BF16), ((dim, w1w), BF16), ((dim, di), BF16), ((dim, sh), BF16),
        ((tokens, di), BF16), ((tokens, di), BF16), ((tokens, di), BF16),
    ]
    scan_state = ((seqs, state, di), BF16)
    near = [((tokens, 128), F32)] * 4 + [scan_state] * 3 + [
        ((blocks, 8, di), F32), ((seqs, 8, di), F32), scan_state, ((8, di), F32), ((8, 128), F32), ((8, di), F32), ((8, di), F32),
        ((8, 128), F32)]
    scratch = [
        ((tokens, dim), BF16), ((tokens, dim), BF16), ((tokens, dim), BF16), ((dim, w1w), BF16), ((dim, di), BF16),
        ((dim, di), BF16), ((dim, sh), BF16), ((nt, 16, dcol), F32), ((seqs * 16, dim), BF16),
        ((seqs, span + 16, di), F32), ((seqs, span + 16, sh), F32), ((tokens, di), BF16), ((tokens, sh), BF16),
        ((tokens, di), F32), ((tokens, di), F32), ((tokens, di), BF16), ((tokens, di), BF16), ((tokens, di), BF16),
        ((SPAN, di), F32), ((SPAN, di), F32), ((seqs, state, di), F32), scan_state,
        ((seqs * 16, dim), BF16), ((SPAN, 128), BF16), ((128, SPAN), F32), ((128, di), BF16), ((di, 128), BF16),
        ((SPAN, SPAN), BF16), ((rows, dcol), BF16),
    ]
    pieces = seqs * di // WIDE
    out, h, rawi, raws, xs, bc, w1, w2, ws, yn, dgate, dy, *rest = pl.pallas_call(
        functools.partial(forward_kernel, heads, nt, nd, gathers),
        out_shape=[jax.ShapeDtypeStruct(s, d) for s, d in far + near],
        in_specs=[pl.BlockSpec(memory_space=k) for k in kinds],
        out_specs=[pl.BlockSpec(memory_space=pl.ANY)] * len(far) + [pl.BlockSpec(memory_space=pltpu.VMEM)] * len(near),
        scratch_shapes=[pltpu.VMEM(s, d) for s, d in scratch]
        + semaphores(4 * Gather.MESSAGES + 7 + nt) + semaphores(pieces)
        + [pltpu.SemaphoreType.DMA((6,)), pltpu.SemaphoreType.DMA((20,))],
        compiler_params=pltpu.CompilerParams(vmem_limit_bytes=VMEM_LIMIT, collective_id=0, has_side_effects=True),
        name="forward",
    )(*args)
    draw, acs, bs, rr, fresh, vv, mineb, dec, whole, sin, chan, dpar, skip, ggg, skg = rest

    args = [x, c, h, rawi, raws, xs, bc, w1, w2, ws, yn, dgate, dy, draw, acs, bs, rr, fresh, vv, sin]
    kinds = [pl.ANY] * len(args)
    more = [gain, ts, mineb, dec, whole, chan, dpar, skip, ggg, skg]
    args += more
    kinds += [pltpu.VMEM] * len(more)
    wa = dcol - 128
    part = wa + 256
    gw = part * nt + sh
    f128 = ((tokens, 128), F32)
    scratch = [
        ((tokens, dim), BF16), ((tokens, dim), BF16), ((seqs, span + 16, di), F32),
        ((seqs, span + 16, sh), F32), ((tokens, di), BF16), ((tokens, sh), BF16), ((dim, w1w), BF16),
        ((dim, sh), BF16), ((tokens, di), BF16), ((tokens, di), BF16), f128, f128, f128, f128, scan_state, scan_state,
        scan_state, scan_state, scan_state, ((tokens, gw), BF16), ((tokens, di), F32), ((tokens, sh), F32),
        ((dim, max(2 * di, gw)), BF16), ((seqs, 8, di + sh), F32), ((seqs, 8, di + sh), F32), ((seqs, 16, di + sh), F32),
        ((128, SPAN), F32), ((3, HALF, HALF), F32), ((128, di), BF16), ((di, 128), BF16), ((SPAN, SPAN), BF16),
        ((8, di + sh), F32), ((8, 128), F32), ((8, dim), F32),
    ]
    scratch = [pltpu.VMEM(s, d) for s, d in scratch]
    sems = semaphores(pieces) + semaphores(1) + [pltpu.SemaphoreType.DMA((26,))]
    if gathers:
        near = [((rows, part), F32), ((rows, sh), F32), ((rows, dcol), F32), ((rows, dcol), F32), ((8, di), F32)]
        far = []
        scratch += [pltpu.VMEM((8, di), F32)]
        for width, wz in ((di, dcol), (di, dcol), (wa * nt, wa), (256 * nt + sh, 256 + sh)):
            scratch += Reduce.scratch(rows, width, nt, wz)
        scratch += SmallSum.scratch((8, di), nt)
        for _ in range(4):
            sems += semaphores(Reduce.MESSAGES)
        sems += semaphores(SmallSum.MESSAGES)
    else:
        far = [((dim, gw), BF16), ((dim, di), BF16), ((dim, di), BF16)]
        near = [((8, di), F32)]
    outs = [((tokens, dim), BF16)] + far + near
    ig, *rest = pl.pallas_call(
        functools.partial(backward_kernel, heads, nt, nd, gathers),
        out_shape=[jax.ShapeDtypeStruct(s, d) for s, d in outs],
        in_specs=[pl.BlockSpec(memory_space=k) for k in kinds],
        out_specs=[pl.BlockSpec(memory_space=pl.ANY)] * (1 + len(far)) + [pl.BlockSpec(memory_space=pltpu.VMEM)] * len(near),
        scratch_shapes=scratch + sems,
        compiler_params=pltpu.CompilerParams(vmem_limit_bytes=VMEM_LIMIT, collective_id=1, has_side_effects=True),
        name="backward",
    )(*args)
    if gathers:
        g1, gs, g2, g3, sm = rest
    else:
        g1, g2, g3, sm = rest
        g1, gs, g2, g3, sm = reduce_all(nt, nd, g1, g2, g3, sm, sh)
    sm = sm.reshape(-1)
    cut = lambda k: lax.dynamic_slice_in_dim(sm, k * di + me * dcol, dcol)
    at = 6 * di
    ng = sm[at : at + dim]
    tgs = sm[at + dim : at + dim + 5 * sh].reshape(5, sh)
    at = at + dim + 5 * sh
    hcut = lambda k: lax.dynamic_slice_in_dim(sm, at + 128 * k + me * hloc, hloc)
    return (
        out.reshape(block_input.shape),
        ig.reshape(block_input.shape),
        ng,
        jnp.stack([g2, g1[:, :dcol]], axis=1),
        gs,
        lax.dynamic_slice_in_dim(g1[:, dcol:], me * hloc, hloc, axis=1),
        jnp.stack([cut(k) for k in range(4)]),
        cut(4),
        tgs[:4],
        tgs[4],
        hcut(0),
        hcut(1),
        hcut(2),
        cut(5),
        g3.T,
    )


def solution(mesh):
    placed = (
        P("dp", "tensor", None), P(), P("dp", None, "tensor"), P("dp", None), P("dp", "tensor"), P(None, "tensor"),
        P("tensor"), P(), P(), P("tensor"), P("tensor"), P("tensor"), P("tensor"), P("tensor", "dp"),
        P("dp", "tensor", None),
    )
    return jax.shard_map(
        local,
        mesh=mesh,
        in_specs=placed,
        out_specs=(
            P("dp", "tensor", None), P("dp", "tensor", None), P(), P("dp", None, "tensor"), P("dp", None),
            P("dp", "tensor"), P(None, "tensor"), P("tensor"), P(), P(), P("tensor"), P("tensor"), P("tensor"),
            P("tensor"), P("tensor", "dp"),
        ),
        check_vma=False,
    )
```

```python
import functools

import jax
import jax.numpy as jnp
from jax import lax
from jax.experimental import pallas as pl
from jax.experimental.pallas import tpu as pltpu
from jax.sharding import PartitionSpec as P

P_SIZE = 64
SPAN = 256
HALF = SPAN // 2
EPSILON = 1e-05
LOG2E = 1.4426950408889634
F32 = jnp.float32
BF16 = jnp.bfloat16
VMEM_LIMIT = 65024 * 1024
WIDE = 512


def dot(a, b):
    return jnp.dot(a, b, preferred_element_type=F32)


def dot_nt(a, b):
    return lax.dot_general(a, b, (((1,), (1,)), ((), ())), preferred_element_type=F32)


def dot_tn(a, b):
    return lax.dot_general(a, b, (((0,), (0,)), ((), ())), preferred_element_type=F32)


def sigmoid(v):
    return 0.5 * jnp.tanh(0.5 * v) + 0.5


def split2(v):
    hi = v.astype(BF16)
    return hi, (v - hi.astype(F32)).astype(BF16)


def lanes_of(shape):
    return lax.broadcasted_iota(jnp.int32, shape, len(shape) - 1)


def packed(v, heads):
    v = jnp.where(lanes_of(v.shape) < heads, v, 0.0)
    hi = v.astype(BF16).astype(F32)
    low = (v - hi).astype(BF16).astype(F32)
    return (hi + pltpu.roll(low, 32, 1)).astype(BF16)


def spread_heads(pk, sel):
    return dot(pk, sel)


def gather_heads(v, sel):
    hi, low = split2(v)
    return dot_nt(hi, sel) + dot_nt(low, sel)


def cumulate(tri, v, heads):
    v = jnp.where(lanes_of(v.shape) < heads, v, 0.0)
    p0 = v.astype(BF16).astype(F32)
    r = v - p0
    p1 = r.astype(BF16).astype(F32)
    p2 = r - p1
    pk = (p0 + pltpu.roll(p1, 32, 1) + pltpu.roll(p2, 64, 1)).astype(BF16)
    s = dot(tri, pk)
    n = s.shape[1]
    s = s + pltpu.roll(s, n - 32, 1) + pltpu.roll(s, n - 64, 1)
    return jnp.where(lanes_of(v.shape) < heads, s, 0.0)


def lane_tiles(v):
    return sum(v[:, c0 : c0 + 128] for c0 in range(0, v.shape[1], 128))


def row_tiles(v):
    return jnp.sum(v.reshape(v.shape[0] // 8, 8, v.shape[1]), axis=0)


def block_rows(b, size):
    return pl.ds(pl.multiple_of(b * size, size), size)


MESH = pl.DeviceIdType.MESH


class Sends:
    def __init__(self, send, recv):
        self.send, self.recv, self.used, self.started = send, recv, 0, []

    def make(self, src, dst, to):
        k = self.used
        self.used += 1
        return pltpu.make_async_remote_copy(
            src_ref=src, dst_ref=dst, send_sem=self.send.at[k], recv_sem=self.recv.at[k],
            device_id=to, device_id_type=MESH,
        )

    def start(self, src, dst, to):
        copy = self.make(src, dst, to)
        copy.start()
        self.started.append(copy)
        return copy

    def finish(self):
        for copy in self.started:
            copy.wait_send()


def greet(others):
    barrier = pltpu.get_barrier_semaphore()
    for to in others:
        pl.semaphore_signal(barrier, inc=1, device_id=to, device_id_type=MESH)
    pl.semaphore_wait(barrier, len(others))


def place():
    z = lax.axis_index("tensor")
    d = lax.axis_index("dp")
    core = lax.rem(d, 2)
    x = lax.rem(d // 2, 2)
    y = d // 4
    return z, d, core, x, y


def xor_peer(core, x, y, k):
    c1 = 1 - core if k & 1 else core
    x1 = 1 - x if k & 2 else x
    y1 = 1 - y if k & 4 else y
    return y1 * 4 + x1 * 2 + c1


def dp_rows(d, size, part=None):
    if part is None:
        return pl.ds(pl.multiple_of(d * size, 16), size)
    return pl.ds(pl.multiple_of(d * size + part * (size // 2), 16), size // 2)


def columns(t, size):
    return pl.ds(pl.multiple_of(t * size, 128), size)


def cut_at(base, size, by_t, t):
    return pl.ds(pl.multiple_of(base + t * size, 128), size) if by_t else pl.ds(base, size)


class Gather:
    MESSAGES = 13

    def __init__(self, sends, nt, shard, full, here):
        self.sends, self.nt, self.shard, self.full = sends, nt, shard, full
        self.z, self.d, self.core, self.x, self.y = here
        self.rows, self.width = shard.shape

    def to(self, k):
        return {"dp": xor_peer(self.core, self.x, self.y, k)}

    def ref(self, k, part=None):
        return self.full.at[dp_rows(xor_peer(self.core, self.x, self.y, k), self.rows, part), :]

    def begin(self, sem):
        mine = self.full.at[dp_rows(self.d, self.rows), columns(self.z, self.width)]
        self.local = pltpu.make_async_copy(self.shard, mine, sem)
        self.local.start()
        self.zs = []
        for dz in range(1, self.nt):
            to = {"tensor": lax.rem(self.z + dz, self.nt)}
            self.zs.append(self.sends.start(self.shard, mine, to))

    def column(self):
        self.local.wait()
        for copy in self.zs:
            copy.wait_recv()
        own_a, own_b = self.ref(0, 0), self.ref(0, 1)
        self.x0 = self.sends.start(own_a, own_a, self.to(2))
        self.y0 = self.sends.start(own_b, own_b, self.to(4))
        self.c = [self.sends.start(self.ref(0), self.ref(0), self.to(1))]
        self.y1 = self.sends.start(own_a, own_a, self.to(4))
        self.x1 = self.sends.start(own_b, own_b, self.to(2))

    def forward(self):
        self.x0.wait_recv()
        self.y2 = self.sends.start(self.ref(2, 0), self.ref(2, 0), self.to(4))
        self.y0.wait_recv()
        self.x2 = self.sends.start(self.ref(4, 1), self.ref(4, 1), self.to(2))
        self.x1.wait_recv()
        self.c.append(self.sends.start(self.ref(2), self.ref(2), self.to(1)))
        self.y1.wait_recv()
        self.c.append(self.sends.start(self.ref(4), self.ref(4), self.to(1)))

    def corner(self):
        self.y2.wait_recv()
        self.x2.wait_recv()
        self.c.append(self.sends.start(self.ref(6), self.ref(6), self.to(1)))

    def finish(self):
        for copy in self.c:
            copy.wait_recv()


class Reduce:
    MESSAGES = 18

    @staticmethod
    def scratch(rows, width, nt, wz):
        half = rows // 2
        shapes = [(4, rows, width), (2, half, width), (2, half, width), (half, width), (half, width), (nt, rows, wz)]
        return [pltpu.VMEM(s, BF16) for s in shapes]

    def __init__(self, sends, nt, g, bufs, cuts, here):
        self.nt, self.g, self.cuts = nt, g, cuts
        self.rc, self.ra, self.rb, self.ta, self.tb, self.rz = bufs
        self.z, self.d, core, x, y = here
        rows = self.rc.shape[1]
        to = lambda k: {"dp": xor_peer(core, x, y, k)}
        at = lambda y, x, core, part=None: dp_rows(4 * y + 2 * x + core, rows, part)
        send = lambda src, dst, to: sends.make(g.at[src, :], dst, to)
        self.core = [send(at(q // 2, q % 2, 1 - core), self.rc.at[q], to(1)) for q in range(4)]
        self.core_rows = [at(q // 2, q % 2, core) for q in range(4)]
        self.a = [send(at(i, 1 - x, core, 0), self.ra.at[i], to(2)) for i in range(2)]
        self.b = [send(at(1 - y, i, core, 1), self.rb.at[i], to(4)) for i in range(2)]
        self.a_rows = [at(i, x, core, 0) for i in range(2)]
        self.b_rows = [at(y, i, core, 1) for i in range(2)]
        self.a2 = send(at(1 - y, x, core, 0), self.ta, to(4))
        self.b2 = send(at(y, 1 - x, core, 1), self.tb, to(2))
        self.halves = [dp_rows(self.d, rows, i) for i in range(2)]
        self.own = dp_rows(self.d, rows)
        self.zs = []
        self.places = []
        first = 0
        for base, size, by_t in cuts:
            dst = self.rz.at[self.z, :, pl.ds(first, size)]
            for dz in range(1, nt):
                t = lax.rem(self.z + dz, nt)
                src = g.at[self.own, cut_at(base, size, by_t, t)]
                self.zs.append(sends.make(src, dst, {"tensor": t}))
            self.places.append((first, size, cut_at(base, size, by_t, self.z)))
            first += size

    def add(self, rows, other):
        self.g[rows, :] = (self.g[rows, :].astype(F32) + other.astype(F32)).astype(BF16)

    def begin(self):
        for copy in self.core:
            copy.start()

    def first(self):
        for q in range(4):
            self.core[q].wait_recv()
            self.add(self.core_rows[q], self.rc[q])
        for copy in self.a + self.b:
            copy.start()

    def second(self):
        for i in range(2):
            self.a[i].wait_recv()
            self.add(self.a_rows[i], self.ra[i])
            self.b[i].wait_recv()
            self.add(self.b_rows[i], self.rb[i])
        self.a2.start()
        self.b2.start()

    def third(self):
        self.a2.wait_recv()
        self.add(self.halves[0], self.ta[...])
        self.b2.wait_recv()
        self.add(self.halves[1], self.tb[...])
        for copy in self.zs:
            copy.start()
        for first, size, cols in self.places:
            self.rz[self.z, :, first : first + size] = self.g[self.own, cols]

    def last(self, *outs):
        for copy in self.zs:
            copy.wait_recv()
        for out, (first, size, _) in zip(outs, self.places):
            total = self.rz[0, :, first : first + size].astype(F32)
            for t in range(1, self.nt):
                total = total + self.rz[t, :, first : first + size].astype(F32)
            out[...] = total

    def finish(self):
        for copy in self.core + self.a + self.b + [self.a2, self.b2] + self.zs:
            copy.wait_send()


class SmallSum:
    MESSAGES = 6

    @staticmethod
    def scratch(shape, nt):
        return [pltpu.VMEM((2,) + shape, F32), pltpu.VMEM((3,) + shape, F32), pltpu.VMEM((nt,) + shape, F32)]

    def __init__(self, sends, nt, v, bufs, here):
        self.nt, self.v = nt, v
        self.own, self.got, self.rz = bufs
        self.z, d, core, x, y = here
        self.copies = [
            sends.make(self.own.at[k - 1] if k else v, self.got.at[k], {"dp": xor_peer(core, x, y, 2**k)}) for k in range(3)
        ]
        part = self.rz.at[self.z]
        self.zs = [sends.make(part, part, {"tensor": lax.rem(self.z + dz, nt)}) for dz in range(1, nt)]

    def begin(self):
        self.copies[0].start()

    def step(self, k):
        self.copies[k - 1].wait_recv()
        total = (self.own[k - 2] if k > 1 else self.v[...]) + self.got[k - 1]
        if k < 3:
            self.own[k - 1] = total
            self.copies[k].start()
        else:
            self.rz[self.z] = total
            for copy in self.zs:
                copy.start()

    def finish(self):
        for copy in self.copies + self.zs:
            copy.wait_send()

    def last(self):
        for copy in self.zs:
            copy.wait_recv()
        total = self.rz[0]
        for t in range(1, self.nt):
            total = total + self.rz[t]
        return total


class Chain:
    def __init__(self, nt, by, mine, whole, got, out, send, recv):
        self.mine, self.whole, self.got, self.out, self.send, self.recv = mine, whole, got, out, send, recv
        z = lax.axis_index("tensor")
        self.seqs, _, di = got.shape
        self.per = di // WIDE
        self.pieces = self.seqs * self.per
        self.at = z if by > 0 else nt - 1 - z
        self.has_prev = self.at > 0
        self.has_next = self.at < nt - 1
        self.next = {"tensor": lax.rem(z + by + nt, nt)}
        self.begin_slot = 3 * self.at - 1

    def copy(self, k):
        s = k // self.per
        cols = pl.ds(pl.multiple_of((k - s * self.per) * WIDE, WIDE), WIDE)
        return pltpu.make_async_remote_copy(
            src_ref=self.out.at[s, :, cols], dst_ref=self.got.at[s, :, cols], send_sem=self.send.at[k],
            recv_sem=self.recv.at[k], device_id=self.next, device_id_type=MESH,
        )

    def pass_on(self, k, first):
        s = k // self.per
        cols = pl.ds(pl.multiple_of((k - s * self.per) * WIDE, WIDE), WIDE)
        v = self.mine[s, :, cols].astype(F32)
        if not first:
            v = v + self.whole[s, 0:1, cols] * self.got[s, :, cols].astype(F32)
        self.out[s, :, cols] = v.astype(BF16)
        self.copy(k).start()

    def begin(self, s):
        @pl.when(jnp.logical_not(self.has_prev))
        def _():
            self.got[s] = jnp.zeros(self.got.shape[1:], BF16)
            for k in range(self.per * s, self.per * (s + 1)):
                self.pass_on(k, True)

    def step(self, k):
        self.copy(k).wait_recv()

        @pl.when(self.has_next)
        def _():
            self.pass_on(k, False)

    def slot(self, n):
        since = n - self.begin_slot

        @pl.when(self.has_prev & self.has_next & (since >= 0) & (lax.rem(since + 8, 2) == 0) & (since < 2 * self.pieces))
        def _():
            self.step(since // 2)

    def rest(self, slots):
        for k in range(self.pieces):

            @pl.when(self.has_prev & self.has_next & (self.begin_slot + 2 * k >= slots))
            def _(k=k):
                self.step(k)

    def arrive(self, s):
        for i in range(self.per):

            @pl.when(jnp.logical_not(self.has_next))
            def _(i=i):
                self.copy(self.per * s + i).wait_recv()

    def finish(self):
        @pl.when(self.has_next)
        def _():
            for k in range(self.pieces):
                self.copy(k).wait_send()


class Moves:
    def __init__(self, sems):
        self.sems, self.used, self.open = sems, 0, []

    def start(self, src, dst):
        copy = pltpu.make_async_copy(src, dst, self.sems.at[self.used])
        self.used += 1
        copy.start()
        self.open.append(copy)
        return copy

    def finish(self, done=()):
        for copy in self.open:
            if all(copy is not other for other in done):
                copy.wait()


def heads_table(sel_ref, di):
    r = lax.broadcasted_iota(jnp.int32, (128, WIDE), 0)
    c = lax.broadcasted_iota(jnp.int32, (128, WIDE), 1)
    for c0 in range(0, di, WIDE):
        hit = ((r & 31) == ((c + c0) >> 6)) & (r < 64)
        sel_ref[:, c0 : c0 + WIDE] = jnp.where(hit, 1.0, 0.0).astype(BF16)


def ones_below(tri_ref, up):
    r = lax.broadcasted_iota(jnp.int32, (SPAN, SPAN), 0)
    c = lax.broadcasted_iota(jnp.int32, (SPAN, SPAN), 1)
    tri_ref[...] = jnp.where(r <= c if up else r >= c, 1.0, 0.0).astype(BF16)


def forward_kernel(heads, nt, nd, gathers, *refs):
    refs = list(refs)
    take = lambda n: [refs.pop(0) for _ in range(n)]
    x_hbm, c_hbm, norm_gain_ref, conv_shared_ref, shift_shared_ref = take(5)
    if gathers:
        (wgi_ref, wdelta_ref, wo_ref, wsh_ref, conv_inner_ref, shift_inner_ref, gated_gain_ref, decay_ref, bias_ref,
         skip_gain_ref) = take(10)
    else:
        w1_hbm, w2_hbm, w3_hbm, ws_hbm, parf_ref, xhf_ref = take(6)
    (out_hbm, h_hbm, rawi_hbm, raws_hbm, xs_hbm, bc_hbm, w1_out, w2_out, ws_out, yn_hbm, dgate_hbm, dy_hbm) = take(12)
    (draw_ref, acs_ref, bs_ref, rr_ref, fresh_ref, vv_ref, mineb_ref, dec_ref, whole_ref, sin_ref, chan_ref, dpar_ref,
     skip_ref, gg_ref, sk_ref, ts_ref) = take(16)
    (x_ref, c_ref, h_ref, w1_ref, w2_ref, w3_ref, ws_ref, pf_ref, xh_ref, rawi_ref, raws_ref, xs_ref, bc_ref, y_ref,
     skc_ref, yn_ref, dgate_ref, dy_ref, g_ref, mine_ref, sb_ref, hh_ref, ea_ref, bst_ref,
     sel_ref, tri_ref, wot_ref, pack_ref, par_ref) = take(29)
    send, recv, chain_send, chain_recv, local, moves, result_sems = take(7)

    tokens, dim = x_ref.shape
    seqs, ext, di = rawi_ref.shape
    span = ext - 16
    per = span // SPAN
    blocks = seqs * per
    sh = bc_ref.shape[1]
    state = sh // 2
    dcol = di // nt
    wa = dcol - 128
    inner = nt * wa
    z = lax.axis_index("tensor")
    store = Moves(moves)
    load_x = store.start(x_hbm, x_ref)
    load_c = store.start(c_hbm, c_ref)

    sends = Sends(send, recv)
    zpeers = [{"tensor": lax.rem(z + dz, nt)} for dz in range(1, nt)]
    if gathers:
        here = place()
        _, d, core, x, y = here
        pack_ref[:, :dcol] = wgi_ref[:, 1, :]
        pack_ref[:, dcol : dcol + 128] = jnp.zeros((pack_ref.shape[0], 128), BF16)
        pack_ref[:, dcol : dcol + wdelta_ref.shape[1]] = wdelta_ref[...]
        pack_ref[:, dcol + 128 :] = wgi_ref[:, 0, :]
        wot_ref[...] = wo_ref[...].astype(F32).T.astype(BF16)
        par_ref[...] = jnp.zeros_like(par_ref)
        par_ref[0:4, :] = conv_inner_ref[...].astype(F32)
        par_ref[4:5, :] = shift_inner_ref[...].astype(F32).reshape(1, dcol)
        par_ref[5:6, :] = gated_gain_ref[...].reshape(1, dcol)
        for k, ref in enumerate((decay_ref, bias_ref, skip_gain_ref)):
            par_ref[8 + k : 9 + k, 0 : heads // nt] = ref[...].reshape(1, heads // nt)
        greet(zpeers + [{"dp": xor_peer(core, x, y, k)} for k in range(1, 8)])
        shards = (
            (pack_ref.at[:, pl.ds(0, wa)], w1_ref.at[:, pl.ds(0, inner)]),
            (pack_ref.at[:, pl.ds(wa, 256)], w1_ref.at[:, pl.ds(inner, 256 * nt)]),
            (pack_ref.at[:, pl.ds(wa + 256, dcol)], w2_ref),
            (wot_ref, w3_ref),
        )
        secs = [Gather(sends, nt, a, b, here) for a, b in shards]
        secs[0].begin(local.at[0])
        mine = ws_ref.at[dp_rows(d, wsh_ref.shape[0]), :]
        own = [pltpu.make_async_copy(wsh_ref, mine, local.at[4]), pltpu.make_async_copy(par_ref, pf_ref.at[z], local.at[5])]
        for copy in own:
            copy.start()
        got = [sends.start(wsh_ref, mine, {"dp": xor_peer(core, x, y, k)}) for k in range(1, 8)]
        got += [sends.start(par_ref, pf_ref.at[z], to) for to in zpeers]
        edges = [
            sends.make(
                x_hbm.at[pl.ds((s + 1) * span - 16, 16), :], xh_ref.at[pl.ds(16 * s, 16), :],
                {"tensor": lax.rem(z + 1, nt)},
            )
            for s in range(seqs)
        ]

        @pl.when(z < nt - 1)
        def _():
            for copy in edges:
                copy.start()

        secs[1].begin(local.at[1])
    else:
        greet(({"tensor": lax.rem(z + nt - 1, nt)}, {"tensor": lax.rem(z + 1, nt)}))
        loads = [store.start(a, b) for a, b in ((w1_hbm, w1_ref), (w2_hbm, w2_ref), (w3_hbm, w3_ref), (ws_hbm, ws_ref))]
        pf_ref[...] = parf_ref[...]
        xh_ref[...] = xhf_ref[...]

    heads_table(sel_ref, di)
    ones_below(tri_ref, False)

    gain = norm_gain_ref[...].reshape(1, dim)
    ts_ref[...] = jnp.zeros_like(ts_ref)
    ts_ref[0:4, :] = conv_shared_ref[...].astype(F32)
    ts_ref[4:5, :] = shift_shared_ref[...].astype(F32).reshape(1, sh)

    def norm(v):
        v = v.astype(F32)
        return (v * lax.rsqrt(jnp.mean(v * v, axis=-1, keepdims=True) + EPSILON) * gain).astype(BF16)

    load_x.wait()

    def norm_step(b, c):
        rows = block_rows(b, SPAN)
        h_ref[rows, :] = norm(x_ref[rows, :])
        return c

    lax.fori_loop(0, blocks, norm_step, 0)
    store.start(h_ref, h_hbm)

    if gathers:
        for copy in own:
            copy.wait()
        secs[0].column()
        secs[2].begin(local.at[2])
        secs[1].column()
        secs[3].begin(local.at[3])
        for copy in got:
            copy.wait_recv()

        @pl.when(z > 0)
        def _():
            for copy in edges:
                copy.wait_recv()

        @pl.when(z == 0)
        def _():
            xh_ref[...] = jnp.zeros_like(xh_ref)

    hh_ref[...] = norm(xh_ref[...])
    head = pf_ref[0, 8:16, 0:128]
    for t in range(nt):
        chan_ref[:, dcol * t : dcol * (t + 1)] = pf_ref[t, 0:8, :]
        if t > 0:
            head = head + pltpu.roll(pf_ref[t, 8:16, 0:128], heads // nt * t, 1)
    ak = -jnp.exp(head[0:1])
    ak = jnp.where(lanes_of(ak.shape) < heads, ak, 0.0)
    dpar_ref[0:1, :] = head[1:2]
    dpar_ref[1:2, :] = ak * LOG2E
    dpar_ref[2:3, :] = ak
    dpar_ref[3:8, :] = jnp.zeros((5, 128), F32)
    sk8 = packed(jnp.broadcast_to(head[2:3], (8, 128)), heads)
    for c0 in range(0, di, WIDE):
        skip_ref[:, c0 : c0 + WIDE] = spread_heads(sk8, sel_ref[:, c0 : c0 + WIDE])

    def conv(raw, par, out, s, cols):
        def step(r, c):
            r0 = pl.multiple_of(r * 128, 128)
            v = raw[s, pl.ds(r0 + 8, 136), cols]
            acc = par[4:5, cols] + par[3:4, cols] * v[8:]
            for k in range(3):
                acc = acc + par[k : k + 1, cols] * v[5 + k : 133 + k]
            out[pl.ds(pl.multiple_of(s * span + r0, 128), 128), cols] = (acc * sigmoid(acc)).astype(BF16)
            return c

        lax.fori_loop(0, span // 128, step, 0)

    if not gathers:
        loads[3].wait()
    for s in range(seqs):
        rows = slice(span * s, span * (s + 1))
        raws_ref[s, 0:16, :] = dot(hh_ref[16 * s : 16 * s + 16, :], ws_ref[...])
        raws_ref[s, 16:ext, :] = dot(h_ref[rows, :], ws_ref[...])
        for c0 in range(0, sh, 256):
            conv(raws_ref, ts_ref, bc_ref, s, slice(c0, c0 + 256))
    store.start(raws_ref, raws_hbm)
    store.start(bc_ref, bc_hbm)
    store.start(ws_ref, ws_out)

    def first_part(s):
        for t in range(nt):
            cols = slice(dcol * t, dcol * t + wa)
            w = w1_ref[:, wa * t : wa * (t + 1)]
            rawi_ref[s, 0:16, cols] = dot(hh_ref[16 * s : 16 * s + 16, :], w)
            rawi_ref[s, 16:ext, cols] = dot(h_ref[span * s : span * (s + 1), :], w)
            conv(rawi_ref, chan_ref, xs_ref, s, cols)

    def second_part(s):
        rows = slice(span * s, span * (s + 1))
        for t in range(nt):
            cols = slice(dcol * t + wa, dcol * (t + 1))
            w = w1_ref[:, inner + 256 * t : inner + 256 * (t + 1)]
            rawi_ref[s, 0:16, cols] = dot(hh_ref[16 * s : 16 * s + 16, :], w[:, :128])
            both = dot(h_ref[rows, :], w)
            rawi_ref[s, 16:ext, cols] = both[:, :128]
            if t == 0:
                draw_ref[rows, :] = both[:, 128:] + dpar_ref[0:1, :]
            else:
                draw_ref[rows, :] += pltpu.roll(both[:, 128:], heads // nt * t, 1)
            conv(rawi_ref, chan_ref, xs_ref, s, cols)
        store.start(rawi_ref.at[s], rawi_hbm.at[s])
        store.start(xs_ref.at[rows, :], xs_hbm.at[rows, :])

    def block_step(s, j, c):
        b = s * per + j
        rows = block_rows(b, SPAN)
        x = draw_ref[rows, :]
        dt = jnp.maximum(x, 0.0) + jnp.log1p(jnp.exp(-jnp.abs(x)))
        lg = jnp.where(x < -20.0, x * LOG2E, jnp.log2(jnp.maximum(dt, 1e-30)))
        acs = cumulate(tri_ref[...], dt * dpar_ref[1:2, :], heads)
        bs = acs - lg
        acs_ref[rows, :] = acs
        bs_ref[rows, :] = bs
        end = acs[SPAN - 1 : SPAN, :]
        wk = packed(jnp.exp2(end - bs), heads)
        bt = bc_ref[rows, :state].astype(F32).T.astype(BF16)
        dk = packed(jnp.broadcast_to(jnp.exp2(end), (8, 128)), heads)
        for c0 in range(0, di, WIDE):
            cols = slice(c0, c0 + WIDE)
            w = spread_heads(wk, sel_ref[:, cols])
            wx = (w * xs_ref[rows, cols].astype(F32)).astype(BF16)
            fresh = dot(bt, wx)
            de = spread_heads(dk, sel_ref[:, cols])
            dec_ref[b, :, cols] = de

            @pl.when(j == 0)
            def _(cols=cols, fresh=fresh, de=de):
                fresh_ref[s, :, cols] = fresh.astype(BF16)
                mine_ref[s, :, cols] = fresh
                whole_ref[s, :, cols] = de

            @pl.when(j > 0)
            def _(cols=cols, fresh=fresh, de=de):
                mine_ref[s, :, cols] = de[0:1] * mine_ref[s, :, cols] + fresh
                whole_ref[s, :, cols] = de * whole_ref[s, :, cols]

        return c

    chain = Chain(nt, 1, mine_ref, whole_ref, sin_ref, sb_ref, chain_send, chain_recv)
    if gathers:
        secs[0].forward()
        secs[1].forward()
        secs[0].corner()
        secs[0].finish()
    else:
        loads[0].wait()
    first_part(0)
    if gathers:
        secs[2].column()
        secs[1].corner()
    for s in range(1, seqs):
        first_part(s)
    if gathers:
        secs[1].finish()
        secs[2].forward()
        secs[3].column()
    store.start(w1_ref, w1_out)
    for s in range(seqs):
        second_part(s)
        lax.fori_loop(0, per, functools.partial(block_step, s), 0)
        chain.begin(s)
        if gathers and s == 0:
            secs[2].corner()
            secs[3].forward()
    if gathers:
        secs[3].corner()

    lower = lax.broadcasted_iota(jnp.int32, (HALF, HALF), 0) >= lax.broadcasted_iota(jnp.int32, (HALF, HALF), 1)
    first = lanes_of((HALF, 128)) < P_SIZE
    pairs = di // 128

    def intra_step(b, carry):
        rows = block_rows(b, SPAN)
        bst_ref[...] = bs_ref[rows, :].T
        bb = bc_ref[rows, :state]
        cc = bc_ref[rows, state:]
        g00 = dot_nt(cc[:HALF], bb[:HALF])
        g10 = dot_nt(cc[HALF:], bb[:HALF])
        g11 = dot_nt(cc[HALF:], bb[HALF:])
        for p in range(pairs):
            cols = slice(128 * p, 128 * p + 128)
            xp = xs_ref[rows, cols]
            y0, y1 = [], []
            for h in (2 * p, 2 * p + 1):
                a0 = acs_ref[block_rows(2 * b, HALF), h : h + 1]
                a1 = acs_ref[block_rows(2 * b + 1, HALF), h : h + 1]
                r0 = bst_ref[h : h + 1, :HALF]
                r1 = bst_ref[h : h + 1, HALF:]
                m00 = jnp.where(lower, jnp.exp2(a0 - r0) * g00, 0.0).astype(BF16)
                m10 = (jnp.exp2(a1 - r0) * g10).astype(BF16)
                m11 = jnp.where(lower, jnp.exp2(a1 - r1) * g11, 0.0).astype(BF16)
                y0.append(dot(m00, xp[:HALF]))
                y1.append(dot(jnp.concatenate([m10, m11], axis=1), xp))
            y_ref[block_rows(2 * b, HALF), cols] = jnp.where(first, y0[0], y0[1])
            y_ref[block_rows(2 * b + 1, HALF), cols] = jnp.where(first, y1[0], y1[1])
            if (p + 1) % (pairs // 3) == 0:
                chain.slot(3 * b + (p + 1) // (pairs // 3) - 1)
        return carry

    lax.fori_loop(0, blocks, intra_step, 0)
    if gathers:
        for sec in secs[2:]:
            sec.finish()
    else:
        loads[1].wait()
        loads[2].wait()
    store.start(w2_ref, w2_out)

    load_c.wait()

    def products_step(b, carry):
        rows = block_rows(b, span)
        for c0 in range(0, di, WIDE):
            cols = slice(c0, c0 + WIDE)
            dy_ref[rows, cols] = dot(h_ref[rows, :], w2_ref[:, cols]).astype(BF16)
            dgate_ref[rows, cols] = (dot(c_ref[rows, :], w3_ref[:, cols]) * chan_ref[5:6, cols]).astype(BF16)
        return carry

    lax.fori_loop(0, seqs, products_step, 0)
    chain.rest(3 * blocks)

    gg_ref[...] = jnp.zeros_like(gg_ref)
    skc_ref[...] = jnp.zeros_like(skc_ref)
    results = ((x_ref, out_hbm), (yn_ref, yn_hbm), (dgate_ref, dgate_hbm), (dy_ref, dy_hbm))

    def result_copy(k, b):
        rows = block_rows(b, SPAN)
        return pltpu.make_async_copy(results[k][0].at[rows, :], results[k][1].at[rows, :], result_sems.at[k, b])

    def mid_step(s, j, carry):
        b = s * per + j
        rows = block_rows(b, SPAN)
        ea_ref[...] = packed(jnp.exp2(acs_ref[rows, :]), heads)
        cc = bc_ref[rows, state:]
        ss = jnp.zeros((SPAN, 128), F32)
        for c0 in range(0, di, WIDE):
            cols = slice(c0, c0 + WIDE)
            prev = sin_ref[s, :, cols].astype(F32)
            later = dec_ref[s * per, 0:1, cols] * prev + fresh_ref[s, :, cols].astype(F32)
            s_in = jnp.where(j == 0, prev, later).astype(BF16)
            ea = spread_heads(ea_ref[...], sel_ref[:, cols])
            ynos = y_ref[rows, cols] + ea * dot(cc, s_in)
            y_ref[rows, cols] = ynos
            y = ynos + skip_ref[0:1, cols] * xs_ref[rows, cols].astype(F32)
            gate = dy_ref[rows, cols].astype(F32)
            g = y * (gate * sigmoid(gate))
            g_ref[:, cols] = g
            ss = ss + lane_tiles(g * g)
        r2 = lax.rsqrt(jnp.sum(ss, axis=-1, keepdims=True) / di + EPSILON)
        qg = jnp.zeros((SPAN, 128), F32)
        for c0 in range(0, di, WIDE):
            cols = slice(c0, c0 + WIDE)
            g = g_ref[:, cols]
            gain = chan_ref[5:6, cols]
            yn_ref[rows, cols] = (g * r2 * gain).astype(BF16)
            qg_here = dgate_ref[rows, cols].astype(F32) * g
            gg_ref[:, cols] += row_tiles(qg_here * r2)
            qg = qg + lane_tiles(qg_here)
        x_ref[rows, :] = (x_ref[rows, :].astype(F32) + dot_nt(yn_ref[rows, :], w3_ref[...])).astype(BF16)
        coef = r2 * r2 * r2 * (jnp.sum(qg, axis=-1, keepdims=True) / di)
        rr = jnp.zeros((SPAN, 128), F32)
        ct = cc.astype(F32).T.astype(BF16)
        for c0 in range(0, di, WIDE):
            cols = slice(c0, c0 + WIDE)
            xf = xs_ref[rows, cols].astype(F32)
            ynos = y_ref[rows, cols]
            y = ynos + skip_ref[0:1, cols] * xf
            gate = dy_ref[rows, cols].astype(F32)
            sg = sigmoid(gate)
            dg = r2 * dgate_ref[rows, cols].astype(F32) - coef * g_ref[:, cols]
            dgate_ref[rows, cols] = (dg * y * (sg * (1.0 + gate * (1.0 - sg)))).astype(BF16)
            dyb = (dg * (gate * sg)).astype(BF16)
            dy_ref[rows, cols] = dyb
            dy = dyb.astype(F32)
            rr = rr + gather_heads(dy * ynos, sel_ref[:, cols])
            skc_ref[:, cols] += row_tiles(dy * xf)
            ea = spread_heads(ea_ref[...], sel_ref[:, cols])
            vv = dot(ct, (ea * dy).astype(BF16))

            @pl.when(j == 0)
            def _(cols=cols, vv=vv):
                mine_ref[s, :, cols] = vv

            @pl.when(j > 0)
            def _(cols=cols, vv=vv):
                vv_ref[s, :, cols] = vv.astype(BF16)
                mine_ref[s, :, cols] += dec_ref[s * per, 0:1, cols] * vv

        rr_ref[rows, :] = rr
        for k in range(len(results)):
            result_copy(k, b).start()
        return carry

    def mid_sequence(s, carry):
        chain.arrive(s)
        lax.fori_loop(0, per, functools.partial(mid_step, s), 0)
        return carry

    lax.fori_loop(0, seqs, mid_sequence, 0)
    gg_ref[...] = gg_ref[...] / chan_ref[5:6, :]
    sk_ref[...] = jnp.zeros_like(sk_ref)
    for c0 in range(0, di, WIDE):
        sk_ref[...] += gather_heads(skc_ref[:, c0 : c0 + WIDE], sel_ref[:, c0 : c0 + WIDE])
    mineb_ref[...] = mine_ref[...].astype(BF16)
    chain.finish()
    sends.finish()
    if gathers:

        @pl.when(z < nt - 1)
        def _():
            for copy in edges:
                copy.wait_send()

    for b in range(blocks):
        for k in range(len(results)):
            result_copy(k, b).wait()
    store.finish((load_x, load_c) if gathers else (load_x, load_c, *loads))


def backward_kernel(heads, nt, nd, reduces, *refs):
    refs = list(refs)
    take = lambda n: [refs.pop(0) for _ in range(n)]
    (x_hbm, c_hbm, h_hbm, rawi_hbm, raws_hbm, xs_hbm, bc_hbm, w1_hbm, w2_hbm, ws_hbm, yn_hbm, dgate_hbm, dy_hbm,
     draw_hbm, acs_hbm, bs_hbm, rr_hbm, fresh_hbm, vv_hbm, sin_hbm, mineb_hbm) = take(21)
    norm_gain_ref, ts_ref, dec_ref, whole_ref, chan_ref, dpar_ref, skip_ref, gg_ref, sk_ref = take(9)
    (ig_hbm,) = take(1)
    if reduces:
        o1_ref, osd_ref, o2_ref, o3_ref, om_ref = take(5)
    else:
        g1_out, g2_out, g3_out, sm_ref = take(4)
    (c_ref, h_ref, rawi_ref, raws_ref, xs_ref, bc_ref, w1_ref, ws_ref, dgate_ref, dy_ref, draw_ref,
     acs_ref, bs_ref, rr_ref, fresh_ref, vv_ref, sin_ref, ds_ref, sb_ref, din_ref, dx_ref, dbc_ref, g_ref, halo_ref,
     edge_ref, keep_ref, acst_ref, dg_ref, sel_ref, triu_ref, tg_ref, small_ref, ng_ref, w2_ref) = take(34)
    if reduces:
        (sm_ref,) = take(1)
        bufs = [take(6) for _ in range(4)]
        small_bufs = take(3)
    chain_send, chain_recv, halo_send, halo_recv, moves = take(5)
    if reduces:
        sems = [take(2) for _ in range(5)]

    tokens, dim = h_ref.shape
    seqs, ext, di = rawi_ref.shape
    span = ext - 16
    per = span // SPAN
    blocks = seqs * per
    sh = bc_ref.shape[1]
    state = sh // 2
    dcol = di // nt
    wa = dcol - 128
    na = nt * wa
    inner = na + 256 * nt
    z = lax.axis_index("tensor")
    move = Moves(moves)
    load = lambda a, b: move.start(a, b)
    yn_ref = din_ref.at[:, pl.ds(0, di)]
    l_mine, l_c, l_yn = load(mineb_hbm, sb_ref), load(c_hbm, c_ref), load(yn_hbm, yn_ref)
    x_ref = xs_ref.at[:, pl.ds(0, dim)]

    if reduces:
        here = place()
        _, d, core, x, y = here
        others = [{"tensor": lax.rem(z + dz, nt)} for dz in range(1, nt)]
        greet(others + [{"dp": xor_peer(core, x, y, k)} for k in (1, 2, 4)])
        cut = ((0, dcol, True),)
        parts = (
            (g_ref.at[:, pl.ds(di, di)], cut), (g_ref.at[:, pl.ds(0, di)], cut),
            (g_ref.at[:, pl.ds(di, na)], ((0, wa, True),)),
            (g_ref.at[:, pl.ds(di + na, 128 * nt + sh + 128)], ((0, 128, True), (128 * nt, sh + 128, False))),
        )
        r3, r2, ra, rb = (Reduce(Sends(*sems[i]), nt, g, bufs[i], cuts, here) for i, (g, cuts) in enumerate(parts))
        small_sum = SmallSum(Sends(*sems[4]), nt, sm_ref, small_bufs, here)
    else:
        greet(({"tensor": lax.rem(z + nt - 1, nt)}, {"tensor": lax.rem(z + 1, nt)}))

    chain = Chain(nt, -1, sb_ref, whole_ref, ds_ref, sb_ref, chain_send, chain_recv)
    l_mine.wait()
    for s in range(seqs):
        chain.begin(s)
    heads_table(sel_ref, di)
    ones_below(triu_ref, True)
    small_ref[...] = jnp.zeros_like(small_ref)
    ng_ref[...] = jnp.zeros_like(ng_ref)
    tg_ref[...] = jnp.zeros_like(tg_ref)

    def weight_gradient(dv, w, at):
        g = dot_tn(h_ref[...], dv)
        g_ref[:, at : at + g.shape[1]] = g.astype(BF16)
        ng_ref[...] += lane_tiles(g * w.astype(F32))

    l_c.wait()
    l_yn.wait()
    l_h, l_dgate, l_w2 = load(h_hbm, h_ref), load(dgate_hbm, dgate_ref), load(w2_hbm, w2_ref)
    slot = 0
    for c0 in range(0, di, WIDE):
        g_ref[:, di + c0 : di + c0 + WIDE] = dot_tn(c_ref[...], din_ref[:, c0 : c0 + WIDE]).astype(BF16)
        chain.slot(slot)
        slot += 1
    if reduces:
        r3.begin()
    else:
        s3 = move.start(g_ref.at[:, pl.ds(di, di)], g3_out)
    l_h.wait()
    l_dgate.wait()
    l_w2.wait()
    l_scan = [
        load(a, b)
        for a, b in (
            (xs_hbm, xs_ref), (dy_hbm, dy_ref), (bc_hbm, bc_ref), (acs_hbm, acs_ref), (bs_hbm, bs_ref),
        )
    ]
    for c0 in range(0, di, WIDE):
        weight_gradient(dgate_ref[:, c0 : c0 + WIDE], w2_ref[:, c0 : c0 + WIDE], c0)
        chain.slot(slot)
        slot += 1
    if reduces:
        r2.begin()
    else:
        s2 = move.start(g_ref.at[:, pl.ds(0, di)], g2_out)

    for copy in l_scan:
        copy.wait()
    l_state = [
        load(a, b)
        for a, b in (
            (draw_hbm, draw_ref), (rr_hbm, rr_ref), (fresh_hbm, fresh_ref), (vv_hbm, vv_ref), (sin_hbm, sin_ref),
            (rawi_hbm, rawi_ref), (raws_hbm, raws_ref),
        )
    ]
    l_last = [load(w1_hbm, w1_ref), load(ws_hbm, ws_ref)]
    upper = lax.broadcasted_iota(jnp.int32, (HALF, HALF), 0) <= lax.broadcasted_iota(jnp.int32, (HALF, HALF), 1)
    first = lanes_of((HALF, 128)) < P_SIZE
    first_all = lanes_of((SPAN, 128)) < P_SIZE
    pairs = di // 128
    slot0 = slot

    def intra_step(b, carry):
        rows = block_rows(b, SPAN)
        acst_ref[...] = acs_ref[rows, :].T
        bb = bc_ref[rows, :state]
        cc = bc_ref[rows, state:]
        g00 = dot_nt(bb[:HALF], cc[:HALF])
        g01 = dot_nt(bb[:HALF], cc[HALF:])
        g11 = dot_nt(bb[HALF:], cc[HALF:])
        dg_ref[...] = jnp.zeros_like(dg_ref)
        for p in range(pairs):
            cols = slice(128 * p, 128 * p + 128)
            xp = xs_ref[rows, cols]
            dyp = dy_ref[rows, cols]
            d0, d1 = [], []
            for i, h in enumerate((2 * p, 2 * p + 1)):
                keep = first_all if i == 0 else jnp.logical_not(first_all)
                xm = jnp.where(keep, xp, jnp.zeros_like(xp))
                b0 = bs_ref[block_rows(2 * b, HALF), h : h + 1]
                b1 = bs_ref[block_rows(2 * b + 1, HALF), h : h + 1]
                r0 = acst_ref[h : h + 1, :HALF]
                r1 = acst_ref[h : h + 1, HALF:]
                e00 = jnp.where(upper, jnp.exp2(r0 - b0), 0.0)
                e01 = jnp.exp2(r1 - b0)
                e11 = jnp.where(upper, jnp.exp2(r1 - b1), 0.0)
                m0 = jnp.concatenate([(e00 * g00).astype(BF16), (e01 * g01).astype(BF16)], axis=1)
                m1 = (e11 * g11).astype(BF16)
                d0.append(dot(m0, dyp))
                d1.append(dot(m1, dyp[HALF:]))
                dm0 = dot_nt(xm[:HALF], dyp)
                dm1 = dot_nt(xm[HALF:], dyp[HALF:])
                dg_ref[0] += dm0[:, :HALF] * e00
                dg_ref[1] += dm0[:, HALF:] * e01
                dg_ref[2] += dm1 * e11
            dx_ref[block_rows(2 * b, HALF), cols] = jnp.where(first, d0[0], d0[1])
            dx_ref[block_rows(2 * b + 1, HALF), cols] = jnp.where(first, d1[0], d1[1])
            if reduces and p == pairs // 2:
                pl.when(b == blocks // 4)(r3.first)
            if (p + 1) % (pairs // 3) == 0:
                chain.slot(slot0 + 3 * b + (p + 1) // (pairs // 3) - 1)
        dg00 = dg_ref[0]
        dg01 = dg_ref[1]
        dg11 = dg_ref[2]
        dbc_ref[block_rows(2 * b, HALF), :state] = dot(jnp.concatenate([dg00, dg01], axis=1).astype(BF16), cc)
        dbc_ref[block_rows(2 * b + 1, HALF), :state] = dot(dg11.astype(BF16), cc[HALF:])
        dbc_ref[block_rows(2 * b, HALF), state:] = dot(dg00.T.astype(BF16), bb[:HALF])
        dbc_ref[block_rows(2 * b + 1, HALF), state:] = dot(
            jnp.concatenate([dg01.T, dg11.T], axis=1).astype(BF16), bb
        )
        return carry

    lax.fori_loop(0, blocks, intra_step, 0)
    if reduces:
        r3.second()
        r2.first()
    chain.rest(slot0 + 3 * blocks)
    for copy in l_state:
        copy.wait()

    def state_step(s, j):
        b = s * per + j
        rows = block_rows(b, SPAN)
        acs = acs_ref[rows, :]
        end = acs[SPAN - 1 : SPAN, :]
        eak = packed(jnp.exp2(acs), heads)
        wk = packed(jnp.exp2(end - bs_ref[rows, :]), heads)
        bb = bc_ref[rows, :state]
        db = dbc_ref[rows, :state]
        dc = dbc_ref[rows, state:]
        pp = jnp.zeros((SPAN, 128), F32)
        endsum = jnp.zeros((8, 128), F32)
        for c0 in range(0, di, WIDE):
            cols = slice(c0, c0 + WIDE)
            s_in = sin_ref[s, :, cols]
            ds = ds_ref[s, :, cols]
            if j > 0:
                s_in = dec_ref[s * per, 0:1, cols] * s_in.astype(F32) + fresh_ref[s, :, cols].astype(F32)
                s_in = s_in.astype(BF16)
            if j < per - 1:
                ds = dec_ref[s * per + per - 1, 0:1, cols] * ds.astype(F32) + vv_ref[s, :, cols].astype(F32)
                ds = ds.astype(BF16)
            w = spread_heads(wk, sel_ref[:, cols])
            ea = spread_heads(eak, sel_ref[:, cols])
            xf = xs_ref[rows, cols].astype(F32)
            dyf = dy_ref[rows, cols].astype(F32)
            dxs = w * dot(bb, ds)
            dxn = dx_ref[rows, cols] + dxs
            pp = pp + gather_heads(dxn * xf, sel_ref[:, cols])
            at_end = jnp.sum(ds.astype(F32) * s_in.astype(F32), axis=0, keepdims=True) * dec_ref[b, 0:1, cols]
            first_row = lax.broadcasted_iota(jnp.int32, (8, WIDE), 0) == 0
            at_end = row_tiles(dxs * xf) + jnp.where(first_row, jnp.broadcast_to(at_end, (8, WIDE)), 0.0)
            endsum = endsum + gather_heads(at_end, sel_ref[:, cols])
            dc = dc + dot_nt((ea * dyf).astype(BF16), s_in)
            db = db + dot_nt((w * xf).astype(BF16), ds)
            dx_ref[rows, cols] = dxn + skip_ref[0:1, cols] * dyf
        dbc_ref[rows, :state] = db
        dbc_ref[rows, state:] = dc
        da = cumulate(triu_ref[...], rr_ref[rows, :] - pp, heads)
        da = da + jnp.sum(endsum, axis=0, keepdims=True)
        xx = draw_ref[rows, :]
        sg = 1.0 / (1.0 + jnp.exp(-xx))
        dt = jnp.maximum(xx, 0.0) + jnp.log1p(jnp.exp(-jnp.abs(xx)))
        ratio = jnp.where(xx < -20.0, 1.0, sg / jnp.maximum(dt, 1e-30))
        ak = dpar_ref[2:3, :]
        dd = da * ak * sg + pp * ratio
        for t in range(nt):
            ddt = pltpu.roll(dd, 128 - heads // nt * t, 1) if t > 0 else dd
            din_ref[rows, na + 256 * t + 128 : na + 256 * (t + 1)] = ddt.astype(BF16)
        small_ref[0:1, :] += jnp.sum(da * dt * ak, axis=0, keepdims=True)
        small_ref[1:2, :] += jnp.sum(dd, axis=0, keepdims=True)

        def conv_back(raw, par, dact, off, cols):
            here_cols = slice(off + cols.start, off + cols.stop)

            def step(r, prev):
                r0 = pl.multiple_of(r * HALF, HALF)
                at = pl.ds(pl.multiple_of(16 + j * SPAN + r0, 16), HALF)
                now = raw[s, at, cols]
                v = jnp.concatenate([prev, now], axis=0)
                sh_v = [v[5 + k : 5 + k + HALF] for k in range(3)] + [now]
                pre = par[4:5, cols] + par[0:1, cols] * sh_v[0]
                for k in range(1, 4):
                    pre = pre + par[k : k + 1, cols] * sh_v[k]
                sg = sigmoid(pre)
                dp = dact[pl.ds(pl.multiple_of(b * SPAN + r0, HALF), HALF), cols] * (sg * (1.0 + pre * (1.0 - sg)))
                raw[s, at, cols] = dp
                for k in range(4):
                    tg_ref[k, :, here_cols] += row_tiles(dp * sh_v[k])
                tg_ref[4, :, here_cols] += row_tiles(dp)
                return now[HALF - 8 :]

            prev = raw[s, 8:16, cols] if j == 0 else keep_ref[s, :, here_cols]
            prev = lax.fori_loop(0, SPAN // HALF, step, prev)
            if j < per - 1:
                keep_ref[s, :, here_cols] = prev

        for c0 in range(0, di, 256):
            conv_back(rawi_ref, chan_ref, dx_ref, 0, slice(c0, c0 + 256))
        for c0 in range(0, sh, 256):
            conv_back(raws_ref, ts_ref, dbc_ref, di, slice(c0, c0 + 256))

    halo_copy = pltpu.make_async_remote_copy(
        src_ref=edge_ref, dst_ref=halo_ref, send_sem=halo_send.at[0], recv_sem=halo_recv.at[0],
        device_id={"tensor": lax.rem(z + nt - 1, nt)}, device_id_type=MESH,
    )
    for j in range(per):

        def seq_step(s, carry, j=j):
            if j == 0:
                chain.arrive(s)
            state_step(s, j)
            return carry

        lax.fori_loop(0, seqs, seq_step, 0)
        if j == 0:
            edge_ref[:, :, :di] = rawi_ref[:, 16:24, :]
            edge_ref[:, :, di:] = raws_ref[:, 16:24, :]

            @pl.when(z > 0)
            def _():
                halo_copy.start()

            if reduces:
                r3.third()
    l_last += [load(x_hbm, x_ref)]
    if reduces:
        r3.last(o3_ref)
        r2.second()

    @pl.when(z < nt - 1)
    def _():
        halo_copy.wait_recv()

    @pl.when(z == nt - 1)
    def _():
        halo_ref[...] = jnp.zeros_like(halo_ref)

    def conv_t(dpre, par, off, c0, to):
        cols = slice(c0, c0 + 128)
        for s in range(seqs):
            for r0 in range(0, span, HALF):
                if r0 + HALF < span:
                    v = dpre[s, 16 + r0 : 16 + r0 + HALF + 8, cols]
                else:
                    v = jnp.concatenate([dpre[s, 16 + r0 : ext, cols], halo_ref[s, :, off + c0 : off + c0 + 128]], axis=0)
                acc = par[3:4, cols] * v[0:HALF]
                for k in range(3):
                    acc = acc + par[k : k + 1, cols] * v[3 - k : 3 - k + HALF]
                din_ref[s * span + r0 : s * span + r0 + HALF, to : to + 128] = acc.astype(BF16)

    for c0 in range(0, di, 128):
        t, r = divmod(c0, dcol)
        if r < wa:
            conv_t(rawi_ref, chan_ref, 0, c0, wa * t + r)
    if reduces:
        r3.finish()
        r2.third()
    else:
        s3.wait()
    for copy in l_last:
        copy.wait()
    for c0 in range(0, na, WIDE):
        weight_gradient(din_ref[:, c0 : c0 + WIDE], w1_ref[:, c0 : c0 + WIDE], di + c0)
    if reduces:
        ra.begin()
    for c0 in range(0, di, 128):
        t, r = divmod(c0, dcol)
        if r >= wa:
            conv_t(rawi_ref, chan_ref, 0, c0, na + 256 * t + r - wa)
    for c0 in range(0, sh, 128):
        conv_t(raws_ref, ts_ref, di, c0, inner + c0)
    low = di + na + 128 * nt
    for t in range(nt):
        cols = slice(na + 256 * t, na + 256 * (t + 1))
        g = dot_tn(h_ref[...], din_ref[:, cols])
        g_ref[:, di + na + 128 * t : di + na + 128 * (t + 1)] = g[:, :128].astype(BF16)
        ng_ref[...] += lane_tiles(g * w1_ref[:, cols].astype(F32))
        if t == 0:
            g_ref[:, low + sh : low + sh + 128] = g[:, 128:].astype(BF16)
    weight_gradient(din_ref[:, inner:], ws_ref[...], low)
    column = lambda v: jnp.sum(v, axis=0, keepdims=True)
    for k in range(5):
        sm_ref[k : k + 1, :] = column(tg_ref[k, :, :di])
    sm_ref[5:6, :] = column(gg_ref[...])
    gain = norm_gain_ref[...].reshape(1, dim)
    sm_ref[6:7, :dim] = column(ng_ref[...].T) / gain
    flat = [column(tg_ref[k, :, di:]) for k in range(5)] + [small_ref[0:1, :], small_ref[1:2, :], column(sk_ref[...])]
    row, at = 6, dim
    for v in flat:
        width = v.shape[1]
        if at + width > di:
            row, at = row + 1, 0
        sm_ref[row : row + 1, at : at + width] = v
        at += width
    sm_ref[row : row + 1, at:] = jnp.zeros((1, di - at), F32)
    if reduces:
        rb.begin()
        small_sum.begin()
    else:
        move.start(g_ref.at[:, pl.ds(di, g_ref.shape[1] - di)], g1_out)
    def last_step(b, carry):
        if reduces:
            pl.when(b == 0)(ra.first)

            @pl.when(b == blocks // 4)
            def _():
                small_sum.step(1)
                rb.first()

            @pl.when(b == 2 * blocks // 4)
            def _():
                small_sum.step(2)

            @pl.when(b == 3 * blocks // 4)
            def _():
                ra.second()
                small_sum.step(3)

        rows = block_rows(b, SPAN)
        dh = dot_nt(dgate_ref[rows, :], w2_ref[...])
        dh = dh + dot_nt(din_ref[rows, :inner], w1_ref[...])
        dh = dh + dot_nt(din_ref[rows, inner:], ws_ref[...])
        u = x_ref[rows, :].astype(F32)
        r1 = lax.rsqrt(jnp.mean(u * u, axis=-1, keepdims=True) + EPSILON)
        e = dh * gain
        m = jnp.mean(e * u, axis=-1, keepdims=True)
        x_ref[rows, :] = (c_ref[rows, :].astype(F32) + r1 * e - u * (r1 * r1 * r1 * m)).astype(BF16)
        return carry

    lax.fori_loop(0, blocks, last_step, 0)
    move.start(x_ref, ig_hbm)
    if reduces:
        rb.second()
        ra.third()
        r2.last(o2_ref)
        rb.third()
        om_ref[...] = small_sum.last()
        ra.last(o1_ref.at[:, pl.ds(0, wa)])
        rb.last(o1_ref.at[:, pl.ds(wa, 128)], osd_ref)
        for part in (r2, ra, rb, small_sum):
            part.finish()
    chain.finish()

    @pl.when(z > 0)
    def _():
        halo_copy.wait_send()

    move.finish((l_mine, l_c, l_yn, l_h, l_dgate, l_w2, *l_scan, *l_state, *l_last) + (() if reduces else (s3,)))


def finish_kernel(nt, hloc, out_hbm, ig_hbm, o1_ref, osd_ref, o2_ref, o3_ref, om_ref, *refs):
    (out_to, ig_to, ng_ref, gi_ref, gs_ref, delta_ref, ci_ref, si_ref, cs_ref, ss_ref, decay_ref, bias_ref, bypass_ref,
     gg_ref, ow_ref, out_ref, ig_ref, sems) = refs
    ways = ((out_hbm, out_ref, out_to), (ig_hbm, ig_ref, ig_to))
    into = [pltpu.make_async_copy(a, b, sems.at[k]) for k, (a, b, _) in enumerate(ways)]
    onto = [pltpu.make_async_copy(b, c, sems.at[2 + k]) for k, (_, b, c) in enumerate(ways)]
    for copy in into:
        copy.start()
    z = lax.axis_index("tensor")
    dcol = o1_ref.shape[1]
    sh = gs_ref.shape[1]
    dim = ng_ref.shape[0]
    cols = pl.ds(pl.multiple_of(z * dcol, 128), dcol)
    back = lax.rem(128 - z * hloc, 128)
    ng_ref[...] = om_ref[6, :dim]
    gi_ref[:, 0, :] = o2_ref[...]
    gi_ref[:, 1, :] = o1_ref[...]
    gs_ref[...] = osd_ref[:, :sh]
    delta_ref[...] = pltpu.roll(osd_ref[:, sh:], back, 1)[:, :hloc]
    ci_ref[...] = om_ref[0:4, cols]
    si_ref[...] = om_ref[4, cols]
    gg_ref[...] = om_ref[5, cols]
    row, at = 6, dim
    taps = []
    for _ in range(5):
        if at + sh > om_ref.shape[1]:
            row, at = row + 1, 0
        taps.append(om_ref[row : row + 1, at : at + sh])
        at += sh
    for k in range(4):
        cs_ref[k : k + 1, :] = taps[k]
    ss_ref[...] = taps[4][0]
    for ref in (decay_ref, bias_ref, bypass_ref):
        if at + 128 > om_ref.shape[1]:
            row, at = row + 1, 0
        v = jnp.broadcast_to(om_ref[row : row + 1, at : at + 128], (8, 128))
        ref[...] = pltpu.roll(v, back, 1)[0, :hloc]
        at += 128
    for copy, after in zip(into, onto):
        copy.wait()
        after.start()
    ow_ref[...] = o3_ref[...].T
    for copy in onto:
        copy.wait()


def semaphores(n):
    return [pltpu.SemaphoreType.DMA((n,)), pltpu.SemaphoreType.DMA((n,))]


def shifted(v, axis, by):
    n = lax.axis_size(axis)
    return lax.ppermute(v, axis, [(i, i + by) for i in range(n) if 0 <= i + by < n])


def gather_all(nt, nd, wgi, wdelta, wo, ws, par, edge):
    both = ("tensor", "dp")
    rows = ws.shape[0]
    dcol = wo.shape[0]
    delta = jnp.pad(wdelta, ((0, 0), (0, 128 - wdelta.shape[1])))
    pack = jnp.concatenate([wgi[:, 1], delta, wgi[:, 0], wo.T], axis=1)
    full = lax.all_gather(pack, both, axis=0).reshape(nt, nd * rows, -1)
    whole = lambda a, b: full[:, :, a:b].transpose(1, 0, 2).reshape(nd * rows, nt * (b - a))
    w1 = jnp.concatenate([whole(0, dcol - 128), whole(dcol - 128, dcol + 128)], axis=1)
    return (
        w1, whole(dcol + 128, 2 * dcol + 128), whole(2 * dcol + 128, 3 * dcol + 128),
        lax.all_gather(ws, "dp", axis=0, tiled=True), lax.all_gather(par, "tensor", axis=0), shifted(edge, "tensor", 1),
    )


def reduce_all(nt, nd, g1, g2, g3, sm, sh):
    dim = g1.shape[0]
    rows = dim // nd
    dcol = g2.shape[1] // nt
    wa = dcol - 128
    both = ("tensor", "dp")
    parts = [
        g[:, at : at + nt * w].reshape(dim, nt, w).transpose(1, 0, 2)
        for g, at, w in ((g1, 0, wa), (g1, wa * nt, 128), (g2, 0, dcol), (g3, 0, dcol))
    ]
    big = jnp.concatenate(parts, axis=2).reshape(nt * nd, rows, -1)
    big = lax.psum_scatter(big, both, scatter_dimension=0).astype(F32)
    shared = g1[:, nt * dcol :].reshape(nd, rows, sh + 128).astype(F32)
    shared = lax.psum(lax.psum_scatter(shared, "dp", scatter_dimension=0), "tensor")
    return big[:, :dcol], shared, big[:, dcol : 2 * dcol], big[:, 2 * dcol :], lax.psum(sm, both)


def local(
    block_input, norm_gain, input_gate_inner_weight, input_shared_weight, input_delta_weight, conv_inner, shift_inner,
    conv_shared, shift_shared, decay_log, delta_bias, skip_gain, gated_gain, output_projection_weight, cotangent,
):
    nt = lax.axis_size("tensor")
    nd = lax.axis_size("dp")
    me = lax.axis_index("tensor")
    seqs, span, dim = block_input.shape
    tokens = seqs * span
    blocks = tokens // SPAN
    rows, _, dcol = input_gate_inner_weight.shape
    di = dcol * nt
    sh = input_shared_weight.shape[1]
    state = sh // 2
    hloc = input_delta_weight.shape[1]
    heads = hloc * nt
    w1w = (dcol + 128) * nt

    x = block_input.reshape(tokens, dim)
    c = cotangent.reshape(tokens, dim)
    gathers = nd == 8
    args = [x, c, norm_gain, conv_shared, shift_shared]
    kinds = [pl.ANY, pl.ANY] + [pltpu.VMEM] * 3
    if gathers:
        args += [
            input_gate_inner_weight, input_delta_weight, output_projection_weight, input_shared_weight, conv_inner,
            shift_inner, gated_gain, decay_log, delta_bias, skip_gain,
        ]
        kinds += [pltpu.VMEM] * 10
    else:
        head = jnp.pad(jnp.stack([decay_log, delta_bias, skip_gain]), ((0, 5), (0, dcol - hloc)))
        par = [conv_inner.astype(F32), shift_inner.astype(F32)[None], gated_gain[None], jnp.zeros((2, dcol), F32), head]
        args += gather_all(
            nt, nd, input_gate_inner_weight, input_delta_weight, output_projection_weight, input_shared_weight,
            jnp.concatenate(par, axis=0), block_input[:, span - 16 :].reshape(seqs * 16, dim),
        )
        kinds += [pl.ANY] * 4 + [pltpu.VMEM] * 2
    far = [
        ((tokens, dim), BF16), ((tokens, dim), BF16), ((seqs, span + 16, di), F32), ((seqs, span + 16, sh), F32),
        ((tokens, di), BF16), ((tokens, sh), BF16), ((dim, w1w), BF16), ((dim, di), BF16), ((dim, sh), BF16),
        ((tokens, di), BF16), ((tokens, di), BF16), ((tokens, di), BF16),
    ]
    scan_state = ((seqs, state, di), BF16)
    near = [((tokens, 128), F32)] * 4 + [scan_state] * 3 + [
        ((blocks, 8, di), F32), ((seqs, 8, di), F32), scan_state, ((8, di), F32), ((8, 128), F32), ((8, di), F32), ((8, di), F32),
        ((8, 128), F32), ((8, sh), F32)]
    scratch = [
        ((tokens, dim), BF16), ((tokens, dim), BF16), ((tokens, dim), BF16), ((dim, w1w), BF16), ((dim, di), BF16),
        ((dim, di), BF16), ((dim, sh), BF16), ((nt, 16, dcol), F32), ((seqs * 16, dim), BF16),
        ((seqs, span + 16, di), F32), ((seqs, span + 16, sh), F32), ((tokens, di), BF16), ((tokens, sh), BF16),
        ((tokens, di), F32), ((8, di), F32), ((tokens, di), BF16), ((tokens, di), BF16), ((tokens, di), BF16),
        ((SPAN, di), F32), ((seqs, state, di), F32), scan_state,
        ((seqs * 16, dim), BF16), ((SPAN, 128), BF16), ((128, SPAN), F32), ((128, di), BF16),
        ((SPAN, SPAN), BF16), ((rows, dcol), BF16), ((rows, 2 * dcol + 128), BF16), ((16, dcol), F32),
    ]
    pieces = seqs * di // WIDE
    out, h, rawi, raws, xs, bc, w1, w2, ws, yn, dgate, dy, *rest = pl.pallas_call(
        functools.partial(forward_kernel, heads, nt, nd, gathers),
        out_shape=[jax.ShapeDtypeStruct(s, d) for s, d in far + near],
        in_specs=[pl.BlockSpec(memory_space=k) for k in kinds],
        out_specs=[pl.BlockSpec(memory_space=pl.ANY)] * len(far) + [pl.BlockSpec(memory_space=pltpu.VMEM)] * len(near),
        scratch_shapes=[pltpu.VMEM(s, d) for s, d in scratch]
        + semaphores(4 * Gather.MESSAGES + 6 + nt + seqs) + semaphores(pieces)
        + [pltpu.SemaphoreType.DMA((6,)), pltpu.SemaphoreType.DMA((24,)), pltpu.SemaphoreType.DMA((4, blocks))],
        compiler_params=pltpu.CompilerParams(vmem_limit_bytes=VMEM_LIMIT, collective_id=0, has_side_effects=True),
        name="forward",
    )(*args)
    draw, acs, bs, rr, fresh, vv, mineb, dec, whole, sin, chan, dpar, skip, ggg, skg, ts = rest

    args = [x, c, h, rawi, raws, xs, bc, w1, w2, ws, yn, dgate, dy, draw, acs, bs, rr, fresh, vv, sin, mineb]
    kinds = [pl.ANY] * len(args)
    more = [norm_gain, ts, dec, whole, chan, dpar, skip, ggg, skg]
    args += more
    kinds += [pltpu.VMEM] * len(more)
    wa = dcol - 128
    gw = (wa + 256) * nt + sh
    f128 = ((tokens, 128), F32)
    scratch = [
        ((tokens, dim), BF16), ((tokens, dim), BF16), ((seqs, span + 16, di), F32),
        ((seqs, span + 16, sh), F32), ((tokens, di), BF16), ((tokens, sh), BF16), ((dim, w1w), BF16),
        ((dim, sh), BF16), ((tokens, di), BF16), ((tokens, di), BF16), f128, f128, f128, f128, scan_state, scan_state,
        scan_state, scan_state, scan_state, ((tokens, gw), BF16), ((tokens, di), F32), ((tokens, sh), F32),
        ((dim, 2 * di + sh + 128), BF16), ((seqs, 8, di + sh), F32), ((seqs, 8, di + sh), F32), ((seqs, 8, di + sh), F32),
        ((128, SPAN), F32), ((3, HALF, HALF), F32), ((128, di), BF16), ((SPAN, SPAN), BF16),
        ((5, 8, di + sh), F32), ((8, 128), F32), ((dim, 128), F32), ((dim, di), BF16),
    ]
    scratch = [pltpu.VMEM(s, d) for s, d in scratch]
    sems = semaphores(pieces) + semaphores(1) + [pltpu.SemaphoreType.DMA((26,))]
    if gathers:
        near = [
            ((rows, dcol), F32), ((rows, sh + 128), F32), ((rows, dcol), F32), ((rows, dcol), F32), ((8, di), F32)
        ]
        far = []
        scratch += [pltpu.VMEM((8, di), F32)]
        for width, wz in ((di, dcol), (di, dcol), (wa * nt, wa), (128 * nt + sh + 128, sh + 256)):
            scratch += Reduce.scratch(rows, width, nt, wz)
        scratch += SmallSum.scratch((8, di), nt)
        for _ in range(4):
            sems += semaphores(Reduce.MESSAGES)
        sems += semaphores(SmallSum.MESSAGES)
    else:
        far = [((dim, di + sh + 128), BF16), ((dim, di), BF16), ((dim, di), BF16)]
        near = [((8, di), F32)]
    outs = [((tokens, dim), BF16)] + far + near
    ig, *rest = pl.pallas_call(
        functools.partial(backward_kernel, heads, nt, nd, gathers),
        out_shape=[jax.ShapeDtypeStruct(s, d) for s, d in outs],
        in_specs=[pl.BlockSpec(memory_space=k) for k in kinds],
        out_specs=[pl.BlockSpec(memory_space=pl.ANY)] * (1 + len(far)) + [pl.BlockSpec(memory_space=pltpu.VMEM)] * len(near),
        scratch_shapes=scratch + sems,
        compiler_params=pltpu.CompilerParams(vmem_limit_bytes=VMEM_LIMIT, collective_id=1, has_side_effects=True),
        name="backward",
    )(*args)
    if gathers:
        sums = rest
    else:
        sums = reduce_all(nt, nd, *rest, sh)
    finals = [
        ((tokens, dim), BF16), ((tokens, dim), BF16), ((dim,), F32), ((rows, 2, dcol), F32), ((rows, sh), F32),
        ((rows, hloc), F32), ((4, dcol), F32), ((dcol,), F32), ((4, sh), F32), ((sh,), F32), ((hloc,), F32), ((hloc,), F32),
        ((hloc,), F32), ((dcol,), F32), ((dcol, rows), F32),
    ]
    out, ig, *rest = pl.pallas_call(
        functools.partial(finish_kernel, nt, hloc),
        out_shape=[jax.ShapeDtypeStruct(s, d) for s, d in finals],
        in_specs=[pl.BlockSpec(memory_space=pl.ANY)] * 2 + [pl.BlockSpec(memory_space=pltpu.VMEM)] * 5,
        out_specs=[pl.BlockSpec(memory_space=pl.ANY)] * 2 + [pl.BlockSpec(memory_space=pltpu.VMEM)] * 13,
        scratch_shapes=[pltpu.VMEM((tokens, dim), BF16)] * 2 + [pltpu.SemaphoreType.DMA((4,))],
        name="finish",
    )(out, ig, *sums)
    return (out.reshape(block_input.shape), ig.reshape(block_input.shape), *rest)


def solution(mesh):
    placed = (
        P("dp", "tensor", None), P(), P("dp", None, "tensor"), P("dp", None), P("dp", "tensor"), P(None, "tensor"),
        P("tensor"), P(), P(), P("tensor"), P("tensor"), P("tensor"), P("tensor"), P("tensor", "dp"),
        P("dp", "tensor", None),
    )
    return jax.shard_map(
        local,
        mesh=mesh,
        in_specs=placed,
        out_specs=(
            P("dp", "tensor", None), P("dp", "tensor", None), P(), P("dp", None, "tensor"), P("dp", None),
            P("dp", "tensor"), P(None, "tensor"), P("tensor"), P(), P(), P("tensor"), P("tensor"), P("tensor"),
            P("tensor"), P("tensor", "dp"),
        ),
        check_vma=False,
    )
```

```python
import functools

import jax
import jax.numpy as jnp
from jax import lax
from jax.experimental import pallas as pl
from jax.experimental.pallas import tpu as pltpu
from jax.sharding import PartitionSpec as P

P_SIZE = 64
SPAN = 256
HALF = SPAN // 2
EPSILON = 1e-05
LOG2E = 1.4426950408889634
F32 = jnp.float32
BF16 = jnp.bfloat16
VMEM_LIMIT = 65024 * 1024
WIDE = 512


def dot(a, b):
    return jnp.dot(a, b, preferred_element_type=F32)


def dot_nt(a, b):
    return lax.dot_general(a, b, (((1,), (1,)), ((), ())), preferred_element_type=F32)


def dot_tn(a, b):
    return lax.dot_general(a, b, (((0,), (0,)), ((), ())), preferred_element_type=F32)


def sigmoid(v):
    return 0.5 * jnp.tanh(0.5 * v) + 0.5


def split2(v):
    hi = v.astype(BF16)
    return hi, (v - hi.astype(F32)).astype(BF16)


def lanes_of(shape):
    return lax.broadcasted_iota(jnp.int32, shape, len(shape) - 1)


def packed(v, heads):
    v = jnp.where(lanes_of(v.shape) < heads, v, 0.0)
    hi = v.astype(BF16).astype(F32)
    low = (v - hi).astype(BF16).astype(F32)
    return (hi + pltpu.roll(low, 32, 1)).astype(BF16)


def spread_heads(pk, sel):
    return dot(pk, sel)


def gather_heads(v, sel):
    hi, low = split2(v)
    return dot_nt(hi, sel) + dot_nt(low, sel)


def cumulate(tri, v, heads):
    v = jnp.where(lanes_of(v.shape) < heads, v, 0.0)
    p0 = v.astype(BF16).astype(F32)
    r = v - p0
    p1 = r.astype(BF16).astype(F32)
    p2 = r - p1
    pk = (p0 + pltpu.roll(p1, 32, 1) + pltpu.roll(p2, 64, 1)).astype(BF16)
    s = dot(tri, pk)
    n = s.shape[1]
    s = s + pltpu.roll(s, n - 32, 1) + pltpu.roll(s, n - 64, 1)
    return jnp.where(lanes_of(v.shape) < heads, s, 0.0)


def lane_tiles(v):
    return sum(v[:, c0 : c0 + 128] for c0 in range(0, v.shape[1], 128))


def row_tiles(v):
    return jnp.sum(v.reshape(v.shape[0] // 8, 8, v.shape[1]), axis=0)


def block_rows(b, size):
    return pl.ds(pl.multiple_of(b * size, size), size)


MESH = pl.DeviceIdType.MESH


class Sends:
    def __init__(self, send, recv):
        self.send, self.recv, self.used, self.started = send, recv, 0, []

    def make(self, src, dst, to):
        k = self.used
        self.used += 1
        return pltpu.make_async_remote_copy(
            src_ref=src, dst_ref=dst, send_sem=self.send.at[k], recv_sem=self.recv.at[k],
            device_id=to, device_id_type=MESH,
        )

    def start(self, src, dst, to):
        copy = self.make(src, dst, to)
        copy.start()
        self.started.append(copy)
        return copy

    def finish(self):
        for copy in self.started:
            copy.wait_send()


def greet(others):
    barrier = pltpu.get_barrier_semaphore()
    for to in others:
        pl.semaphore_signal(barrier, inc=1, device_id=to, device_id_type=MESH)
    pl.semaphore_wait(barrier, len(others))


def place():
    z = lax.axis_index("tensor")
    d = lax.axis_index("dp")
    core = lax.rem(d, 2)
    x = lax.rem(d // 2, 2)
    y = d // 4
    return z, d, core, x, y


def xor_peer(core, x, y, k):
    c1 = 1 - core if k & 1 else core
    x1 = 1 - x if k & 2 else x
    y1 = 1 - y if k & 4 else y
    return y1 * 4 + x1 * 2 + c1


def dp_rows(d, size, part=None):
    if part is None:
        return pl.ds(pl.multiple_of(d * size, 16), size)
    return pl.ds(pl.multiple_of(d * size + part * (size // 2), 16), size // 2)


def columns(t, size):
    return pl.ds(pl.multiple_of(t * size, 128), size)


def cut_at(base, size, by_t, t):
    return pl.ds(pl.multiple_of(base + t * size, 128), size) if by_t else pl.ds(base, size)


class Gather:
    MESSAGES = 13

    def __init__(self, sends, nt, shard, full, here):
        self.sends, self.nt, self.shard, self.full = sends, nt, shard, full
        self.z, self.d, self.core, self.x, self.y = here
        self.rows, self.width = shard.shape

    def to(self, k):
        return {"dp": xor_peer(self.core, self.x, self.y, k)}

    def ref(self, k, part=None):
        return self.full.at[dp_rows(xor_peer(self.core, self.x, self.y, k), self.rows, part), :]

    def begin(self, sem):
        mine = self.full.at[dp_rows(self.d, self.rows), columns(self.z, self.width)]
        self.local = pltpu.make_async_copy(self.shard, mine, sem)
        self.local.start()
        self.zs = []
        for dz in range(1, self.nt):
            to = {"tensor": lax.rem(self.z + dz, self.nt)}
            self.zs.append(self.sends.start(self.shard, mine, to))

    def column(self):
        self.local.wait()
        for copy in self.zs:
            copy.wait_recv()
        own_a, own_b = self.ref(0, 0), self.ref(0, 1)
        self.x0 = self.sends.start(own_a, own_a, self.to(2))
        self.y0 = self.sends.start(own_b, own_b, self.to(4))
        self.c = [self.sends.start(self.ref(0), self.ref(0), self.to(1))]
        self.y1 = self.sends.start(own_a, own_a, self.to(4))
        self.x1 = self.sends.start(own_b, own_b, self.to(2))

    def forward(self):
        self.x0.wait_recv()
        self.y2 = self.sends.start(self.ref(2, 0), self.ref(2, 0), self.to(4))
        self.y0.wait_recv()
        self.x2 = self.sends.start(self.ref(4, 1), self.ref(4, 1), self.to(2))
        self.x1.wait_recv()
        self.c.append(self.sends.start(self.ref(2), self.ref(2), self.to(1)))
        self.y1.wait_recv()
        self.c.append(self.sends.start(self.ref(4), self.ref(4), self.to(1)))

    def corner(self):
        self.y2.wait_recv()
        self.x2.wait_recv()
        self.c.append(self.sends.start(self.ref(6), self.ref(6), self.to(1)))

    def finish(self):
        for copy in self.c:
            copy.wait_recv()


class Reduce:
    MESSAGES = 18

    @staticmethod
    def scratch(rows, width, nt, wz):
        half = rows // 2
        shapes = [(4, rows, width), (2, half, width), (2, half, width), (half, width), (half, width), (nt, rows, wz)]
        return [pltpu.VMEM(s, BF16) for s in shapes]

    def __init__(self, sends, nt, g, bufs, cuts, here):
        self.nt, self.g, self.cuts = nt, g, cuts
        self.rc, self.ra, self.rb, self.ta, self.tb, self.rz = bufs
        self.z, self.d, core, x, y = here
        rows = self.rc.shape[1]
        to = lambda k: {"dp": xor_peer(core, x, y, k)}
        at = lambda y, x, core, part=None: dp_rows(4 * y + 2 * x + core, rows, part)
        send = lambda src, dst, to: sends.make(g.at[src, :], dst, to)
        self.core = [send(at(q // 2, q % 2, 1 - core), self.rc.at[q], to(1)) for q in range(4)]
        self.core_rows = [at(q // 2, q % 2, core) for q in range(4)]
        self.a = [send(at(i, 1 - x, core, 0), self.ra.at[i], to(2)) for i in range(2)]
        self.b = [send(at(1 - y, i, core, 1), self.rb.at[i], to(4)) for i in range(2)]
        self.a_rows = [at(i, x, core, 0) for i in range(2)]
        self.b_rows = [at(y, i, core, 1) for i in range(2)]
        self.a2 = send(at(1 - y, x, core, 0), self.ta, to(4))
        self.b2 = send(at(y, 1 - x, core, 1), self.tb, to(2))
        self.halves = [dp_rows(self.d, rows, i) for i in range(2)]
        self.own = dp_rows(self.d, rows)
        self.zs = []
        self.places = []
        first = 0
        for base, size, by_t in cuts:
            dst = self.rz.at[self.z, :, pl.ds(first, size)]
            for dz in range(1, nt):
                t = lax.rem(self.z + dz, nt)
                src = g.at[self.own, cut_at(base, size, by_t, t)]
                self.zs.append(sends.make(src, dst, {"tensor": t}))
            self.places.append((first, size, cut_at(base, size, by_t, self.z)))
            first += size

    def add(self, rows, other):
        self.g[rows, :] = (self.g[rows, :].astype(F32) + other.astype(F32)).astype(BF16)

    def begin(self):
        for copy in self.core:
            copy.start()

    def first(self):
        for q in range(4):
            self.core[q].wait_recv()
            self.add(self.core_rows[q], self.rc[q])
        for copy in self.a + self.b:
            copy.start()

    def second(self):
        for i in range(2):
            self.a[i].wait_recv()
            self.add(self.a_rows[i], self.ra[i])
            self.b[i].wait_recv()
            self.add(self.b_rows[i], self.rb[i])
        self.a2.start()
        self.b2.start()

    def third(self):
        self.a2.wait_recv()
        self.add(self.halves[0], self.ta[...])
        self.b2.wait_recv()
        self.add(self.halves[1], self.tb[...])
        for copy in self.zs:
            copy.start()
        for first, size, cols in self.places:
            self.rz[self.z, :, first : first + size] = self.g[self.own, cols]

    def last(self, *outs):
        for copy in self.zs:
            copy.wait_recv()
        for out, (first, size, _) in zip(outs, self.places):
            total = self.rz[0, :, first : first + size].astype(F32)
            for t in range(1, self.nt):
                total = total + self.rz[t, :, first : first + size].astype(F32)
            out[...] = total

    def finish(self):
        for copy in self.core + self.a + self.b + [self.a2, self.b2] + self.zs:
            copy.wait_send()


class SmallSum:
    MESSAGES = 6

    @staticmethod
    def scratch(shape, nt):
        return [pltpu.VMEM((2,) + shape, F32), pltpu.VMEM((3,) + shape, F32), pltpu.VMEM((nt,) + shape, F32)]

    def __init__(self, sends, nt, v, bufs, here):
        self.nt, self.v = nt, v
        self.own, self.got, self.rz = bufs
        self.z, d, core, x, y = here
        self.copies = [
            sends.make(self.own.at[k - 1] if k else v, self.got.at[k], {"dp": xor_peer(core, x, y, 2**k)}) for k in range(3)
        ]
        part = self.rz.at[self.z]
        self.zs = [sends.make(part, part, {"tensor": lax.rem(self.z + dz, nt)}) for dz in range(1, nt)]

    def begin(self):
        self.copies[0].start()

    def step(self, k):
        self.copies[k - 1].wait_recv()
        total = (self.own[k - 2] if k > 1 else self.v[...]) + self.got[k - 1]
        if k < 3:
            self.own[k - 1] = total
            self.copies[k].start()
        else:
            self.rz[self.z] = total
            for copy in self.zs:
                copy.start()

    def finish(self):
        for copy in self.copies + self.zs:
            copy.wait_send()

    def last(self):
        for copy in self.zs:
            copy.wait_recv()
        total = self.rz[0]
        for t in range(1, self.nt):
            total = total + self.rz[t]
        return total


class Chain:
    def __init__(self, nt, by, mine, whole, got, out, send, recv):
        self.mine, self.whole, self.got, self.out, self.send, self.recv = mine, whole, got, out, send, recv
        z = lax.axis_index("tensor")
        self.seqs, _, di = got.shape
        self.per = di // WIDE
        self.pieces = self.seqs * self.per
        self.at = z if by > 0 else nt - 1 - z
        self.has_prev = self.at > 0
        self.has_next = self.at < nt - 1
        self.next = {"tensor": lax.rem(z + by + nt, nt)}
        self.begin_slot = 3 * self.at - 1

    def copy(self, k):
        s = k // self.per
        cols = pl.ds(pl.multiple_of((k - s * self.per) * WIDE, WIDE), WIDE)
        return pltpu.make_async_remote_copy(
            src_ref=self.out.at[s, :, cols], dst_ref=self.got.at[s, :, cols], send_sem=self.send.at[k],
            recv_sem=self.recv.at[k], device_id=self.next, device_id_type=MESH,
        )

    def pass_on(self, k, first):
        s = k // self.per
        cols = pl.ds(pl.multiple_of((k - s * self.per) * WIDE, WIDE), WIDE)
        v = self.mine[s, :, cols].astype(F32)
        if not first:
            v = v + self.whole[s, 0:1, cols] * self.got[s, :, cols].astype(F32)
        self.out[s, :, cols] = v.astype(BF16)
        self.copy(k).start()

    def begin(self, s):
        @pl.when(jnp.logical_not(self.has_prev))
        def _():
            self.got[s] = jnp.zeros(self.got.shape[1:], BF16)
            for k in range(self.per * s, self.per * (s + 1)):
                self.pass_on(k, True)

    def step(self, k):
        self.copy(k).wait_recv()

        @pl.when(self.has_next)
        def _():
            self.pass_on(k, False)

    def slot(self, n):
        since = n - self.begin_slot

        @pl.when(self.has_prev & self.has_next & (since >= 0) & (lax.rem(since + 8, 2) == 0) & (since < 2 * self.pieces))
        def _():
            self.step(since // 2)

    def rest(self, slots):
        for k in range(self.pieces):

            @pl.when(self.has_prev & self.has_next & (self.begin_slot + 2 * k >= slots))
            def _(k=k):
                self.step(k)

    def arrive(self, s):
        for i in range(self.per):

            @pl.when(jnp.logical_not(self.has_next))
            def _(i=i):
                self.copy(self.per * s + i).wait_recv()

    def finish(self):
        @pl.when(self.has_next)
        def _():
            for k in range(self.pieces):
                self.copy(k).wait_send()


class Moves:
    def __init__(self, sems):
        self.sems, self.used, self.open = sems, 0, []

    def start(self, src, dst):
        copy = pltpu.make_async_copy(src, dst, self.sems.at[self.used])
        self.used += 1
        copy.start()
        self.open.append(copy)
        return copy

    def finish(self, done=()):
        for copy in self.open:
            if all(copy is not other for other in done):
                copy.wait()


def heads_table(sel_ref, di):
    r = lax.broadcasted_iota(jnp.int32, (128, WIDE), 0)
    c = lax.broadcasted_iota(jnp.int32, (128, WIDE), 1)
    for c0 in range(0, di, WIDE):
        hit = ((r & 31) == ((c + c0) >> 6)) & (r < 64)
        sel_ref[:, c0 : c0 + WIDE] = jnp.where(hit, 1.0, 0.0).astype(BF16)


def ones_below(tri_ref, up):
    r = lax.broadcasted_iota(jnp.int32, (SPAN, SPAN), 0)
    c = lax.broadcasted_iota(jnp.int32, (SPAN, SPAN), 1)
    tri_ref[...] = jnp.where(r <= c if up else r >= c, 1.0, 0.0).astype(BF16)


def forward_kernel(heads, nt, nd, gathers, *refs):
    refs = list(refs)
    take = lambda n: [refs.pop(0) for _ in range(n)]
    x_hbm, c_hbm, norm_gain_ref, conv_shared_ref, shift_shared_ref = take(5)
    if gathers:
        (wgi_ref, wdelta_ref, wo_ref, wsh_ref, conv_inner_ref, shift_inner_ref, gated_gain_ref, decay_ref, bias_ref,
         skip_gain_ref) = take(10)
    else:
        w1_hbm, w2_hbm, w3_hbm, ws_hbm, parf_ref, xhf_ref = take(6)
    (h_hbm, rawi_hbm, raws_hbm, xs_hbm, bc_hbm, w1_out, w2_out, w3_out, ws_out, yn_hbm, dgate_hbm, dy_hbm, draw_hbm,
     acs_hbm, bs_hbm, rr_hbm, fresh_hbm) = take(17)
    (vv_ref, mineb_ref, dec_ref, whole_ref, sin_ref, chan_ref, dpar_ref, skip_ref, gg_ref, sk_ref, ts_ref) = take(11)
    (x_ref, c_ref, h_ref, w1_ref, w2_ref, w3_ref, ws_ref, pf_ref, xh_ref, rawi_ref, raws_ref, xs_ref, bc_ref, y_ref,
     skc_ref, yn_ref, dgate_ref, dy_ref, g_ref, mine_ref, sb_ref, hh_ref, ea_ref, bst_ref,
     sel_ref, tri_ref, pack_ref, par_ref, zd_ref, wss_ref, turn_ref,
     draw_ref, acs_ref, bs_ref, rr_ref, fresh_ref, eaf_ref) = take(37)
    send, recv, chain_send, chain_recv, local, moves, result_sems = take(7)

    tokens, dim = x_ref.shape
    seqs, ext, di = rawi_ref.shape
    span = ext - 16
    per = span // SPAN
    blocks = seqs * per
    sh = bc_ref.shape[1]
    state = sh // 2
    dcol = di // nt
    wa = dcol - 128
    inner = nt * wa
    z = lax.axis_index("tensor")
    store = Moves(moves)
    load_x = store.start(x_hbm, x_ref)
    load_c = store.start(c_hbm, c_ref)

    sends = Sends(send, recv)
    zpeers = [{"tensor": lax.rem(z + dz, nt)} for dz in range(1, nt)]
    if gathers:
        here = place()
        _, d, core, x, y = here
        rows = wgi_ref.shape[0]
        hloc = heads // nt
        pack_ref[:, :dcol] = wgi_ref[:, 1, :]
        pack_ref[:, dcol:] = wgi_ref[:, 0, :]
        turn_ref[...] = jnp.zeros_like(turn_ref)
        turn_ref[0:hloc, 0:rows] = wdelta_ref[...].astype(F32)
        zd_ref[z] = turn_ref[...].T[0:rows].astype(BF16)
        wss_ref[:, :sh] = wsh_ref[...]
        par_ref[...] = jnp.zeros_like(par_ref)
        par_ref[0:4, :] = conv_inner_ref[...].astype(F32)
        par_ref[4:5, :] = shift_inner_ref[...].astype(F32).reshape(1, dcol)
        par_ref[5:6, :] = gated_gain_ref[...].reshape(1, dcol)
        for k, ref in enumerate((decay_ref, bias_ref, skip_gain_ref)):
            par_ref[8 + k : 9 + k, 0:hloc] = ref[...].reshape(1, hloc)
        greet(zpeers + [{"dp": xor_peer(core, x, y, k)} for k in range(1, 8)])
        shards = (
            (pack_ref.at[:, pl.ds(0, wa)], w1_ref.at[:, pl.ds(0, inner)]),
            (pack_ref.at[:, pl.ds(wa, 128)], w1_ref.at[:, pl.ds(inner, 128 * nt)]),
            (pack_ref.at[:, pl.ds(dcol, dcol)], w2_ref),
            (wo_ref, w3_ref),
        )
        secs = [Gather(sends, nt, a, b, here) for a, b in shards]
        deltas = [sends.start(zd_ref.at[z], zd_ref.at[z], to) for to in zpeers]
        secs[0].begin(local.at[0])
        mine = ws_ref.at[dp_rows(d, rows), :]
        own = [pltpu.make_async_copy(wss_ref, mine, local.at[4]), pltpu.make_async_copy(par_ref, pf_ref.at[z], local.at[5])]
        own[1].start()
        got = [sends.start(par_ref, pf_ref.at[z], to) for to in zpeers]
        edges = [
            sends.make(
                x_hbm.at[pl.ds((s + 1) * span - 16, 16), :], xh_ref.at[pl.ds(16 * s, 16), :],
                {"tensor": lax.rem(z + 1, nt)},
            )
            for s in range(seqs)
        ]

        @pl.when(z < nt - 1)
        def _():
            for copy in edges:
                copy.start()

        secs[1].begin(local.at[1])
    else:
        greet(({"tensor": lax.rem(z + nt - 1, nt)}, {"tensor": lax.rem(z + 1, nt)}))
        loads = [store.start(a, b) for a, b in ((w1_hbm, w1_ref), (w2_hbm, w2_ref), (w3_hbm, w3_ref), (ws_hbm, ws_ref))]
        pf_ref[...] = parf_ref[...]
        xh_ref[...] = xhf_ref[...]

    heads_table(sel_ref, di)
    ones_below(tri_ref, False)

    gain = norm_gain_ref[...].reshape(1, dim)
    ts_ref[...] = jnp.zeros_like(ts_ref)
    ts_ref[0:4, :] = conv_shared_ref[...].astype(F32)
    ts_ref[4:5, :] = shift_shared_ref[...].astype(F32).reshape(1, sh)

    def norm(v):
        v = v.astype(F32)
        return (v * lax.rsqrt(jnp.mean(v * v, axis=-1, keepdims=True) + EPSILON) * gain).astype(BF16)

    load_x.wait()

    def norm_step(b, c):
        rows = block_rows(b, SPAN)
        h_ref[rows, :] = norm(x_ref[rows, :])
        return c

    lax.fori_loop(0, blocks, norm_step, 0)
    store.start(h_ref, h_hbm)

    if gathers:
        for copy in deltas:
            copy.wait_recv()
        delta = zd_ref[0].astype(F32)
        for t in range(1, nt):
            delta = delta + pltpu.roll(zd_ref[t].astype(F32), hloc * t, 1)
        wss_ref[:, sh:] = delta.astype(BF16)
        own[0].start()
        got += [sends.start(wss_ref, mine, {"dp": xor_peer(core, x, y, k)}) for k in range(1, 8)]
        for copy in own:
            copy.wait()
        secs[0].column()
        secs[2].begin(local.at[2])
        secs[1].column()
        secs[3].begin(local.at[3])
        for copy in got:
            copy.wait_recv()

        @pl.when(z > 0)
        def _():
            for copy in edges:
                copy.wait_recv()

        @pl.when(z == 0)
        def _():
            xh_ref[...] = jnp.zeros_like(xh_ref)

    hh_ref[...] = norm(xh_ref[...])
    head = pf_ref[0, 8:16, 0:128]
    for t in range(nt):
        chan_ref[:, dcol * t : dcol * (t + 1)] = pf_ref[t, 0:8, :]
        if t > 0:
            head = head + pltpu.roll(pf_ref[t, 8:16, 0:128], heads // nt * t, 1)
    ak = -jnp.exp(head[0:1])
    ak = jnp.where(lanes_of(ak.shape) < heads, ak, 0.0)
    dpar_ref[0:1, :] = head[1:2]
    dpar_ref[1:2, :] = ak * LOG2E
    dpar_ref[2:3, :] = ak
    dpar_ref[3:8, :] = jnp.zeros((5, 128), F32)
    sk8 = packed(jnp.broadcast_to(head[2:3], (8, 128)), heads)
    for c0 in range(0, di, WIDE):
        skip_ref[:, c0 : c0 + WIDE] = spread_heads(sk8, sel_ref[:, c0 : c0 + WIDE])

    def conv(raw, par, out, s, cols):
        def step(r, c):
            r0 = pl.multiple_of(r * 128, 128)
            v = raw[s, pl.ds(r0 + 8, 136), cols]
            acc = par[4:5, cols] + par[3:4, cols] * v[8:]
            for k in range(3):
                acc = acc + par[k : k + 1, cols] * v[5 + k : 133 + k]
            out[pl.ds(pl.multiple_of(s * span + r0, 128), 128), cols] = (acc * sigmoid(acc)).astype(BF16)
            return c

        lax.fori_loop(0, span // 128, step, 0)

    if not gathers:
        loads[3].wait()
    for s in range(seqs):
        rows = slice(span * s, span * (s + 1))
        raws_ref[s, 0:16, :] = dot(hh_ref[16 * s : 16 * s + 16, :], ws_ref[:, :sh])
        both = dot(h_ref[rows, :], ws_ref[...])
        raws_ref[s, 16:ext, :] = both[:, :sh]
        draw_ref[rows, :] = both[:, sh:] + dpar_ref[0:1, :]
        for c0 in range(0, sh, 256):
            conv(raws_ref, ts_ref, bc_ref, s, slice(c0, c0 + 256))
    store.start(raws_ref, raws_hbm)
    store.start(bc_ref, bc_hbm)
    store.start(ws_ref, ws_out)

    def first_part(s):
        for t in range(nt):
            cols = slice(dcol * t, dcol * t + wa)
            w = w1_ref[:, wa * t : wa * (t + 1)]
            rawi_ref[s, 0:16, cols] = dot(hh_ref[16 * s : 16 * s + 16, :], w)
            rawi_ref[s, 16:ext, cols] = dot(h_ref[span * s : span * (s + 1), :], w)
            conv(rawi_ref, chan_ref, xs_ref, s, cols)

    def second_part(s):
        rows = slice(span * s, span * (s + 1))
        for t in range(nt):
            cols = slice(dcol * t + wa, dcol * (t + 1))
            w = w1_ref[:, inner + 128 * t : inner + 128 * (t + 1)]
            rawi_ref[s, 0:16, cols] = dot(hh_ref[16 * s : 16 * s + 16, :], w)
            rawi_ref[s, 16:ext, cols] = dot(h_ref[rows, :], w)
            conv(rawi_ref, chan_ref, xs_ref, s, cols)
        store.start(rawi_ref.at[s], rawi_hbm.at[s])
        store.start(xs_ref.at[rows, :], xs_hbm.at[rows, :])

    def block_step(s, j, c):
        b = s * per + j
        rows = block_rows(b, SPAN)
        x = draw_ref[rows, :]
        dt = jnp.maximum(x, 0.0) + jnp.log1p(jnp.exp(-jnp.abs(x)))
        lg = jnp.where(x < -20.0, x * LOG2E, jnp.log2(jnp.maximum(dt, 1e-30)))
        acs = cumulate(tri_ref[...], dt * dpar_ref[1:2, :], heads)
        bs = acs - lg
        acs_ref[rows, :] = acs
        bs_ref[rows, :] = bs
        end = acs[SPAN - 1 : SPAN, :]
        wk = packed(jnp.exp2(end - bs), heads)
        bt = bc_ref[rows, :state].astype(F32).T.astype(BF16)
        dk = packed(jnp.broadcast_to(jnp.exp2(end), (8, 128)), heads)
        for c0 in range(0, di, WIDE):
            cols = slice(c0, c0 + WIDE)
            w = spread_heads(wk, sel_ref[:, cols])
            wx = (w * xs_ref[rows, cols].astype(F32)).astype(BF16)
            fresh = dot(bt, wx)
            de = spread_heads(dk, sel_ref[:, cols])
            dec_ref[b, :, cols] = de

            @pl.when(j == 0)
            def _(cols=cols, fresh=fresh, de=de):
                fresh_ref[s, :, cols] = fresh.astype(BF16)
                mine_ref[s, :, cols] = fresh
                whole_ref[s, :, cols] = de

            @pl.when(j > 0)
            def _(cols=cols, fresh=fresh, de=de):
                mine_ref[s, :, cols] = de[0:1] * mine_ref[s, :, cols] + fresh
                whole_ref[s, :, cols] = de * whole_ref[s, :, cols]

        return c

    chain = Chain(nt, 1, mine_ref, whole_ref, sin_ref, sb_ref, chain_send, chain_recv)
    if gathers:
        secs[0].forward()
        secs[1].forward()
        secs[0].corner()
        secs[0].finish()
    else:
        loads[0].wait()
    first_part(0)
    if gathers:
        secs[2].column()
        secs[1].corner()
    for s in range(1, seqs):
        first_part(s)
    if gathers:
        secs[1].finish()
        secs[2].forward()
        secs[3].column()
    store.start(w1_ref, w1_out)
    for s in range(seqs):
        second_part(s)
        lax.fori_loop(0, per, functools.partial(block_step, s), 0)
        chain.begin(s)
        if s == seqs - 1:
            for a, b in ((draw_ref, draw_hbm), (acs_ref, acs_hbm), (bs_ref, bs_hbm), (fresh_ref, fresh_hbm)):
                store.start(a, b)
        if gathers and s == 0:
            secs[2].corner()
            secs[3].forward()
    if gathers:
        secs[3].corner()

    lower = lax.broadcasted_iota(jnp.int32, (HALF, HALF), 0) >= lax.broadcasted_iota(jnp.int32, (HALF, HALF), 1)
    first = lanes_of((HALF, 128)) < P_SIZE
    pairs = di // 128

    def intra_step(b, carry):
        rows = block_rows(b, SPAN)
        bst_ref[...] = bs_ref[rows, :].T
        bb = bc_ref[rows, :state]
        cc = bc_ref[rows, state:]
        g00 = dot_nt(cc[:HALF], bb[:HALF])
        g10 = dot_nt(cc[HALF:], bb[:HALF])
        g11 = dot_nt(cc[HALF:], bb[HALF:])
        for p in range(pairs):
            cols = slice(128 * p, 128 * p + 128)
            xp = xs_ref[rows, cols]
            y0, y1 = [], []
            for h in (2 * p, 2 * p + 1):
                a0 = acs_ref[block_rows(2 * b, HALF), h : h + 1]
                a1 = acs_ref[block_rows(2 * b + 1, HALF), h : h + 1]
                r0 = bst_ref[h : h + 1, :HALF]
                r1 = bst_ref[h : h + 1, HALF:]
                m00 = jnp.where(lower, jnp.exp2(a0 - r0) * g00, 0.0).astype(BF16)
                m10 = (jnp.exp2(a1 - r0) * g10).astype(BF16)
                m11 = jnp.where(lower, jnp.exp2(a1 - r1) * g11, 0.0).astype(BF16)
                y0.append(dot(m00, xp[:HALF]))
                y1.append(dot(jnp.concatenate([m10, m11], axis=1), xp))
            y_ref[block_rows(2 * b, HALF), cols] = jnp.where(first, y0[0], y0[1])
            y_ref[block_rows(2 * b + 1, HALF), cols] = jnp.where(first, y1[0], y1[1])
            if (p + 1) % (pairs // 3) == 0:
                chain.slot(3 * b + (p + 1) // (pairs // 3) - 1)
        return carry

    lax.fori_loop(0, blocks, intra_step, 0)
    if gathers:
        for sec in secs[2:]:
            sec.finish()
    else:
        loads[1].wait()
        loads[2].wait()
    store.start(w2_ref, w2_out)
    store.start(w3_ref, w3_out)

    load_c.wait()

    def products_step(b, carry):
        rows = block_rows(b, span)
        for c0 in range(0, di, WIDE):
            cols = slice(c0, c0 + WIDE)
            dy_ref[rows, cols] = dot(h_ref[rows, :], w2_ref[:, cols]).astype(BF16)
            dgate_ref[rows, cols] = (dot(c_ref[rows, :], w3_ref[:, cols]) * chan_ref[5:6, cols]).astype(BF16)
        return carry

    lax.fori_loop(0, seqs, products_step, 0)
    chain.rest(3 * blocks)

    gg_ref[...] = jnp.zeros_like(gg_ref)
    skc_ref[...] = jnp.zeros_like(skc_ref)
    results = ((yn_ref, yn_hbm), (dgate_ref, dgate_hbm), (dy_ref, dy_hbm), (rr_ref, rr_hbm))

    def result_copy(k, b):
        rows = block_rows(b, SPAN)
        return pltpu.make_async_copy(results[k][0].at[rows, :], results[k][1].at[rows, :], result_sems.at[k, b])

    def mid_step(s, j, carry):
        b = s * per + j
        rows = block_rows(b, SPAN)
        ea_ref[...] = packed(jnp.exp2(acs_ref[rows, :]), heads)
        cc = bc_ref[rows, state:]
        ss = jnp.zeros((SPAN, 128), F32)
        for c0 in range(0, di, WIDE):
            cols = slice(c0, c0 + WIDE)
            prev = sin_ref[s, :, cols].astype(F32)
            later = dec_ref[s * per, 0:1, cols] * prev + fresh_ref[s, :, cols].astype(F32)
            s_in = jnp.where(j == 0, prev, later).astype(BF16)
            ea = spread_heads(ea_ref[...], sel_ref[:, cols])
            eaf_ref[:, cols] = ea
            ynos = y_ref[rows, cols] + ea * dot(cc, s_in)
            y_ref[rows, cols] = ynos
            y = ynos + skip_ref[0:1, cols] * xs_ref[rows, cols].astype(F32)
            gate = dy_ref[rows, cols].astype(F32)
            g = y * (gate * sigmoid(gate))
            g_ref[:, cols] = g
            ss = ss + lane_tiles(g * g)
        r2 = lax.rsqrt(jnp.sum(ss, axis=-1, keepdims=True) / di + EPSILON)
        qg = jnp.zeros((SPAN, 128), F32)
        for c0 in range(0, di, WIDE):
            cols = slice(c0, c0 + WIDE)
            g = g_ref[:, cols]
            gain = chan_ref[5:6, cols]
            yn_ref[rows, cols] = (g * r2 * gain).astype(BF16)
            qg_here = dgate_ref[rows, cols].astype(F32) * g
            gg_ref[:, cols] += row_tiles(qg_here * r2)
            qg = qg + lane_tiles(qg_here)
        coef = r2 * r2 * r2 * (jnp.sum(qg, axis=-1, keepdims=True) / di)
        rr = jnp.zeros((SPAN, 128), F32)
        ct = cc.astype(F32).T.astype(BF16)
        for c0 in range(0, di, WIDE):
            cols = slice(c0, c0 + WIDE)
            xf = xs_ref[rows, cols].astype(F32)
            ynos = y_ref[rows, cols]
            y = ynos + skip_ref[0:1, cols] * xf
            gate = dy_ref[rows, cols].astype(F32)
            sg = sigmoid(gate)
            dg = r2 * dgate_ref[rows, cols].astype(F32) - coef * g_ref[:, cols]
            dgate_ref[rows, cols] = (dg * y * (sg * (1.0 + gate * (1.0 - sg)))).astype(BF16)
            dyb = (dg * (gate * sg)).astype(BF16)
            dy_ref[rows, cols] = dyb
            dy = dyb.astype(F32)
            rr = rr + gather_heads(dy * ynos, sel_ref[:, cols])
            skc_ref[:, cols] += row_tiles(dy * xf)
            vv = dot(ct, (eaf_ref[:, cols] * dy).astype(BF16))

            @pl.when(j == 0)
            def _(cols=cols, vv=vv):
                mine_ref[s, :, cols] = vv

            @pl.when(j > 0)
            def _(cols=cols, vv=vv):
                vv_ref[s, :, cols] = vv.astype(BF16)
                mine_ref[s, :, cols] += dec_ref[s * per, 0:1, cols] * vv

        rr_ref[rows, :] = rr
        for k in range(len(results)):
            result_copy(k, b).start()
        return carry

    def mid_sequence(s, carry):
        chain.arrive(s)
        lax.fori_loop(0, per, functools.partial(mid_step, s), 0)
        return carry

    lax.fori_loop(0, seqs, mid_sequence, 0)
    gg_ref[...] = gg_ref[...] / chan_ref[5:6, :]
    sk_ref[...] = jnp.zeros_like(sk_ref)
    for c0 in range(0, di, WIDE):
        sk_ref[...] += gather_heads(skc_ref[:, c0 : c0 + WIDE], sel_ref[:, c0 : c0 + WIDE])
    mineb_ref[...] = mine_ref[...].astype(BF16)
    chain.finish()
    sends.finish()
    if gathers:

        @pl.when(z < nt - 1)
        def _():
            for copy in edges:
                copy.wait_send()

    for b in range(blocks):
        for k in range(len(results)):
            result_copy(k, b).wait()
    store.finish((load_x, load_c) if gathers else (load_x, load_c, *loads))


def backward_kernel(heads, nt, nd, reduces, *refs):
    refs = list(refs)
    take = lambda n: [refs.pop(0) for _ in range(n)]
    (x_hbm, c_hbm, h_hbm, rawi_hbm, raws_hbm, xs_hbm, bc_hbm, w1_hbm, w2_hbm, w3_hbm, ws_hbm, yn_hbm, dgate_hbm, dy_hbm,
     draw_hbm, acs_hbm, bs_hbm, rr_hbm, fresh_hbm, vv_hbm, sin_hbm, mineb_hbm) = take(22)
    norm_gain_ref, ts_ref, dec_ref, whole_ref, chan_ref, dpar_ref, skip_ref, gg_ref, sk_ref = take(9)
    out_hbm, ig_hbm = take(2)
    if reduces:
        o1_ref, osd_ref, o2_ref, o3_ref, om_ref = take(5)
    else:
        g1_out, g2_out, g3_out, sm_ref = take(4)
    (c_ref, h_ref, rawi_ref, raws_ref, xs_ref, bc_ref, w1_ref, ws_ref, dgate_ref, dy_ref, draw_ref,
     acs_ref, bs_ref, rr_ref, fresh_ref, vv_ref, sin_ref, ds_ref, sb_ref, din_ref, dx_ref, dbc_ref, g_ref, halo_ref,
     edge_ref, keep_ref, acst_ref, dg_ref, sel_ref, triu_ref, tg_ref, small_ref, ng_ref, w2_ref) = take(34)
    if reduces:
        (sm_ref,) = take(1)
        bufs = [take(6) for _ in range(4)]
        small_bufs = take(3)
    chain_send, chain_recv, halo_send, halo_recv, moves = take(5)
    if reduces:
        sems = [take(2) for _ in range(5)]

    tokens, dim = h_ref.shape
    seqs, ext, di = rawi_ref.shape
    span = ext - 16
    per = span // SPAN
    blocks = seqs * per
    sh = bc_ref.shape[1]
    state = sh // 2
    dcol = di // nt
    wa = dcol - 128
    na = nt * wa
    z = lax.axis_index("tensor")
    move = Moves(moves)
    load = lambda a, b: move.start(a, b)
    yn_ref = din_ref.at[:, pl.ds(0, di)]
    l_mine, l_c, l_yn0 = load(mineb_hbm, sb_ref), load(c_hbm, c_ref), load(yn_hbm, yn_ref)
    x_ref = xs_ref.at[:, pl.ds(0, dim)]
    w3_ref = din_ref.at[pl.ds(0, dim), pl.ds(0, di)]

    if reduces:
        here = place()
        _, d, core, x, y = here
        others = [{"tensor": lax.rem(z + dz, nt)} for dz in range(1, nt)]
        greet(others + [{"dp": xor_peer(core, x, y, k)} for k in (1, 2, 4)])
        cut = ((0, dcol, True),)
        parts = (
            (g_ref.at[:, pl.ds(di, di)], cut), (g_ref.at[:, pl.ds(0, di)], cut),
            (g_ref.at[:, pl.ds(di, na)], ((0, wa, True),)),
            (g_ref.at[:, pl.ds(di + na, 128 * nt + sh + 128)], ((0, 128, True), (128 * nt, sh + 128, False))),
        )
        r3, r2, ra, rb = (Reduce(Sends(*sems[i]), nt, g, bufs[i], cuts, here) for i, (g, cuts) in enumerate(parts))
        small_sum = SmallSum(Sends(*sems[4]), nt, sm_ref, small_bufs, here)
    else:
        greet(({"tensor": lax.rem(z + nt - 1, nt)}, {"tensor": lax.rem(z + 1, nt)}))

    chain = Chain(nt, -1, sb_ref, whole_ref, ds_ref, sb_ref, chain_send, chain_recv)
    l_mine.wait()
    for s in range(seqs):
        chain.begin(s)
    heads_table(sel_ref, di)
    ones_below(triu_ref, True)
    small_ref[...] = jnp.zeros_like(small_ref)
    ng_ref[...] = jnp.zeros_like(ng_ref)
    tg_ref[...] = jnp.zeros_like(tg_ref)

    def weight_gradient(dv, w, at):
        g = dot_tn(h_ref[...], dv)
        g_ref[:, at : at + g.shape[1]] = g.astype(BF16)
        ng_ref[...] += lane_tiles(g * w.astype(F32))

    l_c.wait()
    l_yn0.wait()
    l_h, l_dgate, l_w2 = load(h_hbm, h_ref), load(dgate_hbm, dgate_ref), load(w2_hbm, w2_ref)
    slot = 0
    for c0 in range(0, di, WIDE):
        g_ref[:, di + c0 : di + c0 + WIDE] = dot_tn(c_ref[...], din_ref[:, c0 : c0 + WIDE]).astype(BF16)
        chain.slot(slot)
        slot += 1
    if reduces:
        r3.begin()
    else:
        s3 = move.start(g_ref.at[:, pl.ds(di, di)], g3_out)
    l_h.wait()
    l_dgate.wait()
    l_w2.wait()
    l_scan = [
        load(a, b)
        for a, b in (
            (xs_hbm, xs_ref), (dy_hbm, dy_ref), (bc_hbm, bc_ref), (acs_hbm, acs_ref), (bs_hbm, bs_ref),
        )
    ]
    for c0 in range(0, di, WIDE):
        weight_gradient(dgate_ref[:, c0 : c0 + WIDE], w2_ref[:, c0 : c0 + WIDE], c0)
        chain.slot(slot)
        slot += 1
    if reduces:
        r2.begin()
    else:
        s2 = move.start(g_ref.at[:, pl.ds(0, di)], g2_out)

    for copy in l_scan:
        copy.wait()
    l_state = [
        load(a, b)
        for a, b in (
            (draw_hbm, draw_ref), (rr_hbm, rr_ref), (fresh_hbm, fresh_ref), (vv_hbm, vv_ref), (sin_hbm, sin_ref),
            (rawi_hbm, rawi_ref), (raws_hbm, raws_ref),
        )
    ]
    l_last = [load(w1_hbm, w1_ref), load(ws_hbm, ws_ref)]
    upper = lax.broadcasted_iota(jnp.int32, (HALF, HALF), 0) <= lax.broadcasted_iota(jnp.int32, (HALF, HALF), 1)
    first = lanes_of((HALF, 128)) < P_SIZE
    first_all = lanes_of((SPAN, 128)) < P_SIZE
    pairs = di // 128
    slot0 = slot

    def intra_step(b, carry):
        rows = block_rows(b, SPAN)
        acst_ref[...] = acs_ref[rows, :].T
        bb = bc_ref[rows, :state]
        cc = bc_ref[rows, state:]
        g00 = dot_nt(bb[:HALF], cc[:HALF])
        g01 = dot_nt(bb[:HALF], cc[HALF:])
        g11 = dot_nt(bb[HALF:], cc[HALF:])
        dg_ref[...] = jnp.zeros_like(dg_ref)
        for p in range(pairs):
            cols = slice(128 * p, 128 * p + 128)
            xp = xs_ref[rows, cols]
            dyp = dy_ref[rows, cols]
            d0, d1 = [], []
            for i, h in enumerate((2 * p, 2 * p + 1)):
                keep = first_all if i == 0 else jnp.logical_not(first_all)
                xm = jnp.where(keep, xp, jnp.zeros_like(xp))
                b0 = bs_ref[block_rows(2 * b, HALF), h : h + 1]
                b1 = bs_ref[block_rows(2 * b + 1, HALF), h : h + 1]
                r0 = acst_ref[h : h + 1, :HALF]
                r1 = acst_ref[h : h + 1, HALF:]
                e00 = jnp.where(upper, jnp.exp2(r0 - b0), 0.0)
                e01 = jnp.exp2(r1 - b0)
                e11 = jnp.where(upper, jnp.exp2(r1 - b1), 0.0)
                m0 = jnp.concatenate([(e00 * g00).astype(BF16), (e01 * g01).astype(BF16)], axis=1)
                m1 = (e11 * g11).astype(BF16)
                d0.append(dot(m0, dyp))
                d1.append(dot(m1, dyp[HALF:]))
                dm0 = dot_nt(xm[:HALF], dyp)
                dm1 = dot_nt(xm[HALF:], dyp[HALF:])
                dg_ref[0] += dm0[:, :HALF] * e00
                dg_ref[1] += dm0[:, HALF:] * e01
                dg_ref[2] += dm1 * e11
            dx_ref[block_rows(2 * b, HALF), cols] = jnp.where(first, d0[0], d0[1])
            dx_ref[block_rows(2 * b + 1, HALF), cols] = jnp.where(first, d1[0], d1[1])
            if reduces and p == pairs // 2:
                pl.when(b == blocks // 4)(r3.first)
            if (p + 1) % (pairs // 3) == 0:
                chain.slot(slot0 + 3 * b + (p + 1) // (pairs // 3) - 1)
        dg00 = dg_ref[0]
        dg01 = dg_ref[1]
        dg11 = dg_ref[2]
        dbc_ref[block_rows(2 * b, HALF), :state] = dot(jnp.concatenate([dg00, dg01], axis=1).astype(BF16), cc)
        dbc_ref[block_rows(2 * b + 1, HALF), :state] = dot(dg11.astype(BF16), cc[HALF:])
        dbc_ref[block_rows(2 * b, HALF), state:] = dot(dg00.T.astype(BF16), bb[:HALF])
        dbc_ref[block_rows(2 * b + 1, HALF), state:] = dot(
            jnp.concatenate([dg01.T, dg11.T], axis=1).astype(BF16), bb
        )
        return carry

    lax.fori_loop(0, blocks, intra_step, 0)
    if reduces:
        r3.second()
        r2.first()
    chain.rest(slot0 + 3 * blocks)
    for copy in l_state:
        copy.wait()

    def state_step(s, j):
        b = s * per + j
        rows = block_rows(b, SPAN)
        acs = acs_ref[rows, :]
        end = acs[SPAN - 1 : SPAN, :]
        eak = packed(jnp.exp2(acs), heads)
        wk = packed(jnp.exp2(end - bs_ref[rows, :]), heads)
        bb = bc_ref[rows, :state]
        db = dbc_ref[rows, :state]
        dc = dbc_ref[rows, state:]
        pp = jnp.zeros((SPAN, 128), F32)
        endsum = jnp.zeros((8, 128), F32)
        for c0 in range(0, di, WIDE):
            cols = slice(c0, c0 + WIDE)
            s_in = sin_ref[s, :, cols]
            ds = ds_ref[s, :, cols]
            if j > 0:
                s_in = dec_ref[s * per, 0:1, cols] * s_in.astype(F32) + fresh_ref[s, :, cols].astype(F32)
                s_in = s_in.astype(BF16)
            if j < per - 1:
                ds = dec_ref[s * per + per - 1, 0:1, cols] * ds.astype(F32) + vv_ref[s, :, cols].astype(F32)
                ds = ds.astype(BF16)
            w = spread_heads(wk, sel_ref[:, cols])
            ea = spread_heads(eak, sel_ref[:, cols])
            xf = xs_ref[rows, cols].astype(F32)
            dyf = dy_ref[rows, cols].astype(F32)
            dxs = w * dot(bb, ds)
            dxn = dx_ref[rows, cols] + dxs
            pp = pp + gather_heads(dxn * xf, sel_ref[:, cols])
            at_end = jnp.sum(ds.astype(F32) * s_in.astype(F32), axis=0, keepdims=True) * dec_ref[b, 0:1, cols]
            first_row = lax.broadcasted_iota(jnp.int32, (8, WIDE), 0) == 0
            at_end = row_tiles(dxs * xf) + jnp.where(first_row, jnp.broadcast_to(at_end, (8, WIDE)), 0.0)
            endsum = endsum + gather_heads(at_end, sel_ref[:, cols])
            dc = dc + dot_nt((ea * dyf).astype(BF16), s_in)
            db = db + dot_nt((w * xf).astype(BF16), ds)
            dx_ref[rows, cols] = dxn + skip_ref[0:1, cols] * dyf
        dbc_ref[rows, :state] = db
        dbc_ref[rows, state:] = dc
        da = cumulate(triu_ref[...], rr_ref[rows, :] - pp, heads)
        da = da + jnp.sum(endsum, axis=0, keepdims=True)
        xx = draw_ref[rows, :]
        sg = 1.0 / (1.0 + jnp.exp(-xx))
        dt = jnp.maximum(xx, 0.0) + jnp.log1p(jnp.exp(-jnp.abs(xx)))
        ratio = jnp.where(xx < -20.0, 1.0, sg / jnp.maximum(dt, 1e-30))
        ak = dpar_ref[2:3, :]
        dd = da * ak * sg + pp * ratio
        din_ref[rows, di + sh :] = dd.astype(BF16)
        small_ref[0:1, :] += jnp.sum(da * dt * ak, axis=0, keepdims=True)
        small_ref[1:2, :] += jnp.sum(dd, axis=0, keepdims=True)

        def conv_back(raw, par, dact, off, cols):
            here_cols = slice(off + cols.start, off + cols.stop)

            def step(r, prev):
                r0 = pl.multiple_of(r * HALF, HALF)
                at = pl.ds(pl.multiple_of(16 + j * SPAN + r0, 16), HALF)
                now = raw[s, at, cols]
                v = jnp.concatenate([prev, now], axis=0)
                sh_v = [v[5 + k : 5 + k + HALF] for k in range(3)] + [now]
                pre = par[4:5, cols] + par[0:1, cols] * sh_v[0]
                for k in range(1, 4):
                    pre = pre + par[k : k + 1, cols] * sh_v[k]
                sg = sigmoid(pre)
                dp = dact[pl.ds(pl.multiple_of(b * SPAN + r0, HALF), HALF), cols] * (sg * (1.0 + pre * (1.0 - sg)))
                raw[s, at, cols] = dp
                for k in range(4):
                    tg_ref[k, :, here_cols] += row_tiles(dp * sh_v[k])
                tg_ref[4, :, here_cols] += row_tiles(dp)
                return now[HALF - 8 :]

            prev = raw[s, 8:16, cols] if j == 0 else keep_ref[s, :, here_cols]
            prev = lax.fori_loop(0, SPAN // HALF, step, prev)
            if j < per - 1:
                keep_ref[s, :, here_cols] = prev

        for c0 in range(0, di, 256):
            conv_back(rawi_ref, chan_ref, dx_ref, 0, slice(c0, c0 + 256))
        for c0 in range(0, sh, 256):
            conv_back(raws_ref, ts_ref, dbc_ref, di, slice(c0, c0 + 256))

    halo_copy = pltpu.make_async_remote_copy(
        src_ref=edge_ref, dst_ref=halo_ref, send_sem=halo_send.at[0], recv_sem=halo_recv.at[0],
        device_id={"tensor": lax.rem(z + nt - 1, nt)}, device_id_type=MESH,
    )
    for j in range(per):

        def seq_step(s, carry, j=j):
            if j == 0:
                chain.arrive(s)
            state_step(s, j)
            return carry

        lax.fori_loop(0, seqs, seq_step, 0)
        if j == 0:
            edge_ref[:, :, :di] = rawi_ref[:, 16:24, :]
            edge_ref[:, :, di:] = raws_ref[:, 16:24, :]

            @pl.when(z > 0)
            def _():
                halo_copy.start()

            if reduces:
                r3.third()
    l_last += [load(x_hbm, x_ref)]
    l_yn = load(yn_hbm, dy_ref)
    if reduces:
        r3.last(o3_ref)
        r2.second()

    @pl.when(z < nt - 1)
    def _():
        halo_copy.wait_recv()

    @pl.when(z == nt - 1)
    def _():
        halo_ref[...] = jnp.zeros_like(halo_ref)

    def conv_t(dpre, par, off, c0, to):
        cols = slice(c0, c0 + 128)
        for s in range(seqs):
            for r0 in range(0, span, HALF):
                if r0 + HALF < span:
                    v = dpre[s, 16 + r0 : 16 + r0 + HALF + 8, cols]
                else:
                    v = jnp.concatenate([dpre[s, 16 + r0 : ext, cols], halo_ref[s, :, off + c0 : off + c0 + 128]], axis=0)
                acc = par[3:4, cols] * v[0:HALF]
                for k in range(3):
                    acc = acc + par[k : k + 1, cols] * v[3 - k : 3 - k + HALF]
                din_ref[s * span + r0 : s * span + r0 + HALF, to : to + 128] = acc.astype(BF16)

    for c0 in range(0, di, 128):
        t, r = divmod(c0, dcol)
        if r < wa:
            conv_t(rawi_ref, chan_ref, 0, c0, wa * t + r)
    if reduces:
        r3.finish()
        r2.third()
    else:
        s3.wait()
    for copy in l_last:
        copy.wait()
    for c0 in range(0, na, WIDE):
        weight_gradient(din_ref[:, c0 : c0 + WIDE], w1_ref[:, c0 : c0 + WIDE], di + c0)
    if reduces:
        ra.begin()
    for c0 in range(0, di, 128):
        t, r = divmod(c0, dcol)
        if r >= wa:
            conv_t(rawi_ref, chan_ref, 0, c0, na + 128 * t + r - wa)
    for c0 in range(0, sh, 128):
        conv_t(raws_ref, ts_ref, di, c0, di + c0)
    for c0 in range(na, di, WIDE):
        weight_gradient(din_ref[:, c0 : c0 + WIDE], w1_ref[:, c0 : c0 + WIDE], di + c0)
    weight_gradient(din_ref[:, di:], ws_ref[...], 2 * di)
    column = lambda v: jnp.sum(v, axis=0, keepdims=True)
    for k in range(5):
        sm_ref[k : k + 1, :] = column(tg_ref[k, :, :di])
    sm_ref[5:6, :] = column(gg_ref[...])
    gain = norm_gain_ref[...].reshape(1, dim)
    sm_ref[6:7, :dim] = column(ng_ref[...].T) / gain
    flat = [column(tg_ref[k, :, di:]) for k in range(5)] + [small_ref[0:1, :], small_ref[1:2, :], column(sk_ref[...])]
    row, at = 6, dim
    for v in flat:
        width = v.shape[1]
        if at + width > di:
            row, at = row + 1, 0
        sm_ref[row : row + 1, at : at + width] = v
        at += width
    sm_ref[row : row + 1, at:] = jnp.zeros((1, di - at), F32)
    if reduces:
        rb.begin()
        small_sum.begin()
    else:
        move.start(g_ref.at[:, pl.ds(di, g_ref.shape[1] - di)], g1_out)
    def last_step(b, carry):
        if reduces:
            pl.when(b == 0)(ra.first)

            @pl.when(b == blocks // 4)
            def _():
                small_sum.step(1)
                rb.first()

            @pl.when(b == 2 * blocks // 4)
            def _():
                small_sum.step(2)

            @pl.when(b == 3 * blocks // 4)
            def _():
                ra.second()
                small_sum.step(3)

        rows = block_rows(b, SPAN)
        dh = dot_nt(dgate_ref[rows, :], w2_ref[...])
        dh = dh + dot_nt(din_ref[rows, :di], w1_ref[...])
        dh = dh + dot_nt(din_ref[rows, di:], ws_ref[...])
        u = x_ref[rows, :].astype(F32)
        r1 = lax.rsqrt(jnp.mean(u * u, axis=-1, keepdims=True) + EPSILON)
        e = dh * gain
        m = jnp.mean(e * u, axis=-1, keepdims=True)
        c_ref[rows, :] = (c_ref[rows, :].astype(F32) + r1 * e - u * (r1 * r1 * r1 * m)).astype(BF16)
        return carry

    lax.fori_loop(0, blocks, last_step, 0)
    move.start(c_ref, ig_hbm)
    l_w3 = load(w3_hbm, w3_ref)

    def output_step(b, carry):
        rows = block_rows(b, SPAN)
        x_ref[rows, :] = (x_ref[rows, :].astype(F32) + dot_nt(dy_ref[rows, :], w3_ref[...])).astype(BF16)
        return carry

    if reduces:
        rb.second()
        ra.third()
    l_w3.wait()
    l_yn.wait()
    lax.fori_loop(0, blocks // 2, output_step, 0)
    if reduces:
        rb.third()
    lax.fori_loop(blocks // 2, blocks, output_step, 0)
    move.start(x_ref, out_hbm)
    if reduces:
        r2.last(o2_ref)
        om_ref[...] = small_sum.last()
        ra.last(o1_ref.at[:, pl.ds(0, wa)])
        rb.last(o1_ref.at[:, pl.ds(wa, 128)], osd_ref)
        for part in (r2, ra, rb, small_sum):
            part.finish()
    chain.finish()

    @pl.when(z > 0)
    def _():
        halo_copy.wait_send()

    move.finish((l_mine, l_c, l_yn0, l_yn, l_w3, l_h, l_dgate, l_w2, *l_scan, *l_state, *l_last) + (() if reduces else (s3,)))


def finish_kernel(nt, hloc, out_hbm, ig_hbm, o1_ref, osd_ref, o2_ref, o3_ref, om_ref, *refs):
    (out_to, ig_to, ng_ref, gi_ref, gs_ref, delta_ref, ci_ref, si_ref, cs_ref, ss_ref, decay_ref, bias_ref, bypass_ref,
     gg_ref, ow_ref, out_ref, ig_ref, sems) = refs
    ways = ((out_hbm, out_ref, out_to), (ig_hbm, ig_ref, ig_to))
    into = [pltpu.make_async_copy(a, b, sems.at[k]) for k, (a, b, _) in enumerate(ways)]
    onto = [pltpu.make_async_copy(b, c, sems.at[2 + k]) for k, (_, b, c) in enumerate(ways)]
    for copy in into:
        copy.start()
    z = lax.axis_index("tensor")
    dcol = o1_ref.shape[1]
    sh = gs_ref.shape[1]
    dim = ng_ref.shape[0]
    cols = pl.ds(pl.multiple_of(z * dcol, 128), dcol)
    back = lax.rem(128 - z * hloc, 128)
    ng_ref[...] = om_ref[6, :dim]
    gi_ref[:, 0, :] = o2_ref[...]
    gi_ref[:, 1, :] = o1_ref[...]
    gs_ref[...] = osd_ref[:, :sh]
    delta_ref[...] = pltpu.roll(osd_ref[:, sh:], back, 1).T[:hloc]
    ci_ref[...] = om_ref[0:4, cols]
    si_ref[...] = om_ref[4, cols]
    gg_ref[...] = om_ref[5, cols]
    row, at = 6, dim
    taps = []
    for _ in range(5):
        if at + sh > om_ref.shape[1]:
            row, at = row + 1, 0
        taps.append(om_ref[row : row + 1, at : at + sh])
        at += sh
    for k in range(4):
        cs_ref[k : k + 1, :] = taps[k]
    ss_ref[...] = taps[4][0]
    for ref in (decay_ref, bias_ref, bypass_ref):
        if at + 128 > om_ref.shape[1]:
            row, at = row + 1, 0
        v = jnp.broadcast_to(om_ref[row : row + 1, at : at + 128], (8, 128))
        ref[...] = pltpu.roll(v, back, 1)[0, :hloc]
        at += 128
    for copy, after in zip(into, onto):
        copy.wait()
        after.start()
    ow_ref[...] = o3_ref[...]
    for copy in onto:
        copy.wait()


def semaphores(n):
    return [pltpu.SemaphoreType.DMA((n,)), pltpu.SemaphoreType.DMA((n,))]


def shifted(v, axis, by):
    n = lax.axis_size(axis)
    return lax.ppermute(v, axis, [(i, i + by) for i in range(n) if 0 <= i + by < n])


def gather_all(nt, nd, wgi, wdelta, wo, ws, par, edge):
    both = ("tensor", "dp")
    rows = ws.shape[0]
    dcol = wo.shape[0]
    pack = jnp.concatenate([wgi[:, 1], wgi[:, 0], wo.T], axis=1)
    full = lax.all_gather(pack, both, axis=0).reshape(nt, nd * rows, -1)
    whole = lambda a, b: full[:, :, a:b].transpose(1, 0, 2).reshape(nd * rows, nt * (b - a))
    w1 = jnp.concatenate([whole(0, dcol - 128), whole(dcol - 128, dcol)], axis=1)
    delta = lax.all_gather(wdelta, "tensor", axis=1, tiled=True)
    delta = jnp.pad(delta, ((0, 0), (0, 128 - delta.shape[1])))
    return (
        w1, whole(dcol, 2 * dcol), whole(2 * dcol, 3 * dcol),
        lax.all_gather(jnp.concatenate([ws, delta], axis=1), "dp", axis=0, tiled=True),
        lax.all_gather(par, "tensor", axis=0), shifted(edge, "tensor", 1),
    )


def reduce_all(nt, nd, g1, g2, g3, sm, sh):
    dim = g1.shape[0]
    rows = dim // nd
    dcol = g2.shape[1] // nt
    wa = dcol - 128
    both = ("tensor", "dp")
    parts = [
        g[:, at : at + nt * w].reshape(dim, nt, w).transpose(1, 0, 2)
        for g, at, w in ((g1, 0, wa), (g1, wa * nt, 128), (g2, 0, dcol), (g3, 0, dcol))
    ]
    big = jnp.concatenate(parts, axis=2).reshape(nt * nd, rows, -1)
    big = lax.psum_scatter(big, both, scatter_dimension=0).astype(F32)
    shared = g1[:, nt * dcol :].reshape(nd, rows, sh + 128).astype(F32)
    shared = lax.psum(lax.psum_scatter(shared, "dp", scatter_dimension=0), "tensor")
    return big[:, :dcol], shared, big[:, dcol : 2 * dcol], big[:, 2 * dcol :], lax.psum(sm, both)


def local(
    block_input, norm_gain, input_gate_inner_weight, input_shared_weight, input_delta_weight, conv_inner, shift_inner,
    conv_shared, shift_shared, decay_log, delta_bias, skip_gain, gated_gain, output_projection_weight, cotangent,
):
    nt = lax.axis_size("tensor")
    nd = lax.axis_size("dp")
    me = lax.axis_index("tensor")
    seqs, span, dim = block_input.shape
    tokens = seqs * span
    blocks = tokens // SPAN
    rows, _, dcol = input_gate_inner_weight.shape
    di = dcol * nt
    sh = input_shared_weight.shape[1]
    state = sh // 2
    hloc = input_delta_weight.shape[1]
    heads = hloc * nt

    x = block_input.reshape(tokens, dim)
    c = cotangent.reshape(tokens, dim)
    gathers = nd == 8
    args = [x, c, norm_gain, conv_shared, shift_shared]
    kinds = [pl.ANY, pl.ANY] + [pltpu.VMEM] * 3
    if gathers:
        args += [
            input_gate_inner_weight, input_delta_weight.T, output_projection_weight.T, input_shared_weight, conv_inner,
            shift_inner, gated_gain, decay_log, delta_bias, skip_gain,
        ]
        kinds += [pltpu.VMEM] * 10
    else:
        head = jnp.pad(jnp.stack([decay_log, delta_bias, skip_gain]), ((0, 5), (0, dcol - hloc)))
        par = [conv_inner.astype(F32), shift_inner.astype(F32)[None], gated_gain[None], jnp.zeros((2, dcol), F32), head]
        args += gather_all(
            nt, nd, input_gate_inner_weight, input_delta_weight, output_projection_weight, input_shared_weight,
            jnp.concatenate(par, axis=0), block_input[:, span - 16 :].reshape(seqs * 16, dim),
        )
        kinds += [pl.ANY] * 4 + [pltpu.VMEM] * 2
    scan_state = ((seqs, state, di), BF16)
    f128 = ((tokens, 128), F32)
    far = [
        ((tokens, dim), BF16), ((seqs, span + 16, di), F32), ((seqs, span + 16, sh), F32), ((tokens, di), BF16),
        ((tokens, sh), BF16), ((dim, di), BF16), ((dim, di), BF16), ((dim, di), BF16), ((dim, sh + 128), BF16),
        ((tokens, di), BF16), ((tokens, di), BF16), ((tokens, di), BF16), f128, f128, f128, f128, scan_state,
    ]
    near = [scan_state] * 2 + [
        ((blocks, 8, di), F32), ((seqs, 8, di), F32), scan_state, ((8, di), F32), ((8, 128), F32), ((8, di), F32), ((8, di), F32),
        ((8, 128), F32), ((8, sh), F32)]
    scratch = [
        ((tokens, dim), BF16), ((tokens, dim), BF16), ((tokens, dim), BF16), ((dim, di), BF16), ((dim, di), BF16),
        ((dim, di), BF16), ((dim, sh + 128), BF16), ((nt, 16, dcol), F32), ((seqs * 16, dim), BF16),
        ((seqs, span + 16, di), F32), ((seqs, span + 16, sh), F32), ((tokens, di), BF16), ((tokens, sh), BF16),
        ((tokens, di), F32), ((8, di), F32), ((tokens, di), BF16), ((tokens, di), BF16), ((tokens, di), BF16),
        ((SPAN, di), F32), ((seqs, state, di), F32), scan_state,
        ((seqs * 16, dim), BF16), ((SPAN, 128), BF16), ((128, SPAN), F32), ((128, di), BF16),
        ((SPAN, SPAN), BF16), ((rows, 2 * dcol), BF16), ((16, dcol), F32), ((nt, rows, 128), BF16), ((rows, sh + 128), BF16),
        ((128, 128), F32), f128, f128, f128, f128, scan_state, ((SPAN, di), F32),
    ]
    pieces = seqs * di // WIDE
    h, rawi, raws, xs, bc, w1, w2, w3, ws, yn, dgate, dy, draw, acs, bs, rr, fresh, *rest = pl.pallas_call(
        functools.partial(forward_kernel, heads, nt, nd, gathers),
        out_shape=[jax.ShapeDtypeStruct(s, d) for s, d in far + near],
        in_specs=[pl.BlockSpec(memory_space=k) for k in kinds],
        out_specs=[pl.BlockSpec(memory_space=pl.ANY)] * len(far) + [pl.BlockSpec(memory_space=pltpu.VMEM)] * len(near),
        scratch_shapes=[pltpu.VMEM(s, d) for s, d in scratch]
        + semaphores(4 * Gather.MESSAGES + 5 + 2 * nt + seqs) + semaphores(pieces)
        + [pltpu.SemaphoreType.DMA((6,)), pltpu.SemaphoreType.DMA((24,)), pltpu.SemaphoreType.DMA((4, blocks))],
        compiler_params=pltpu.CompilerParams(vmem_limit_bytes=VMEM_LIMIT, collective_id=0, has_side_effects=True),
        name="forward",
    )(*args)
    vv, mineb, dec, whole, sin, chan, dpar, skip, ggg, skg, ts = rest

    args = [x, c, h, rawi, raws, xs, bc, w1, w2, w3, ws, yn, dgate, dy, draw, acs, bs, rr, fresh, vv, sin, mineb]
    kinds = [pl.ANY] * len(args)
    more = [norm_gain, ts, dec, whole, chan, dpar, skip, ggg, skg]
    args += more
    kinds += [pltpu.VMEM] * len(more)
    wa = dcol - 128
    scratch = [
        ((tokens, dim), BF16), ((tokens, dim), BF16), ((seqs, span + 16, di), F32),
        ((seqs, span + 16, sh), F32), ((tokens, di), BF16), ((tokens, sh), BF16), ((dim, di), BF16),
        ((dim, sh + 128), BF16), ((tokens, di), BF16), ((tokens, di), BF16), f128, f128, f128, f128, scan_state, scan_state,
        scan_state, scan_state, scan_state, ((tokens, di + sh + 128), BF16), ((tokens, di), F32), ((tokens, sh), F32),
        ((dim, 2 * di + sh + 128), BF16), ((seqs, 8, di + sh), F32), ((seqs, 8, di + sh), F32), ((seqs, 8, di + sh), F32),
        ((128, SPAN), F32), ((3, HALF, HALF), F32), ((128, di), BF16), ((SPAN, SPAN), BF16),
        ((5, 8, di + sh), F32), ((8, 128), F32), ((dim, 128), F32), ((dim, di), BF16),
    ]
    scratch = [pltpu.VMEM(s, d) for s, d in scratch]
    sems = semaphores(pieces) + semaphores(1) + [pltpu.SemaphoreType.DMA((32,))]
    if gathers:
        near = [
            ((rows, dcol), F32), ((rows, sh + 128), F32), ((rows, dcol), F32), ((rows, dcol), F32), ((8, di), F32)
        ]
        far = []
        scratch += [pltpu.VMEM((8, di), F32)]
        for width, wz in ((di, dcol), (di, dcol), (wa * nt, wa), (128 * nt + sh + 128, sh + 256)):
            scratch += Reduce.scratch(rows, width, nt, wz)
        scratch += SmallSum.scratch((8, di), nt)
        for _ in range(4):
            sems += semaphores(Reduce.MESSAGES)
        sems += semaphores(SmallSum.MESSAGES)
    else:
        far = [((dim, di + sh + 128), BF16), ((dim, di), BF16), ((dim, di), BF16)]
        near = [((8, di), F32)]
    outs = [((tokens, dim), BF16)] * 2 + far + near
    out, ig, *rest = pl.pallas_call(
        functools.partial(backward_kernel, heads, nt, nd, gathers),
        out_shape=[jax.ShapeDtypeStruct(s, d) for s, d in outs],
        in_specs=[pl.BlockSpec(memory_space=k) for k in kinds],
        out_specs=[pl.BlockSpec(memory_space=pl.ANY)] * (2 + len(far)) + [pl.BlockSpec(memory_space=pltpu.VMEM)] * len(near),
        scratch_shapes=scratch + sems,
        compiler_params=pltpu.CompilerParams(vmem_limit_bytes=VMEM_LIMIT, collective_id=1, has_side_effects=True),
        name="backward",
    )(*args)
    if gathers:
        sums = rest
    else:
        sums = reduce_all(nt, nd, *rest, sh)
    finals = [
        ((tokens, dim), BF16), ((tokens, dim), BF16), ((dim,), F32), ((rows, 2, dcol), F32), ((rows, sh), F32),
        ((hloc, rows), F32), ((4, dcol), F32), ((dcol,), F32), ((4, sh), F32), ((sh,), F32), ((hloc,), F32), ((hloc,), F32),
        ((hloc,), F32), ((dcol,), F32), ((rows, dcol), F32),
    ]
    out, ig, *rest = pl.pallas_call(
        functools.partial(finish_kernel, nt, hloc),
        out_shape=[jax.ShapeDtypeStruct(s, d) for s, d in finals],
        in_specs=[pl.BlockSpec(memory_space=pl.ANY)] * 2 + [pl.BlockSpec(memory_space=pltpu.VMEM)] * 5,
        out_specs=[pl.BlockSpec(memory_space=pl.ANY)] * 2 + [pl.BlockSpec(memory_space=pltpu.VMEM)] * 13,
        scratch_shapes=[pltpu.VMEM((tokens, dim), BF16)] * 2 + [pltpu.SemaphoreType.DMA((4,))],
        name="finish",
    )(out, ig, *sums)
    rest[3] = rest[3].T
    rest[-1] = rest[-1].T
    return (out.reshape(block_input.shape), ig.reshape(block_input.shape), *rest)


def solution(mesh):
    placed = (
        P("dp", "tensor", None), P(), P("dp", None, "tensor"), P("dp", None), P("dp", "tensor"), P(None, "tensor"),
        P("tensor"), P(), P(), P("tensor"), P("tensor"), P("tensor"), P("tensor"), P("tensor", "dp"),
        P("dp", "tensor", None),
    )
    return jax.shard_map(
        local,
        mesh=mesh,
        in_specs=placed,
        out_specs=(
            P("dp", "tensor", None), P("dp", "tensor", None), P(), P("dp", None, "tensor"), P("dp", None),
            P("dp", "tensor"), P(None, "tensor"), P("tensor"), P(), P(), P("tensor"), P("tensor"), P("tensor"),
            P("tensor"), P("tensor", "dp"),
        ),
        check_vma=False,
    )
```

```python
import functools

import jax
import jax.numpy as jnp
from jax import lax
from jax.experimental import pallas as pl
from jax.experimental.pallas import tpu as pltpu
from jax.sharding import PartitionSpec as P

P_SIZE = 64
SPAN = 256
HALF = SPAN // 2
EPSILON = 1e-05
LOG2E = 1.4426950408889634
F32 = jnp.float32
BF16 = jnp.bfloat16
VMEM_LIMIT = 65024 * 1024
WIDE = 512


def dot(a, b):
    return jnp.dot(a, b, preferred_element_type=F32)


def dot_nt(a, b):
    return lax.dot_general(a, b, (((1,), (1,)), ((), ())), preferred_element_type=F32)


def dot_tn(a, b):
    return lax.dot_general(a, b, (((0,), (0,)), ((), ())), preferred_element_type=F32)


def sigmoid(v):
    return 0.5 * jnp.tanh(0.5 * v) + 0.5


def split2(v):
    hi = v.astype(BF16)
    return hi, (v - hi.astype(F32)).astype(BF16)


def lanes_of(shape):
    return lax.broadcasted_iota(jnp.int32, shape, len(shape) - 1)


def packed(v, heads):
    v = jnp.where(lanes_of(v.shape) < heads, v, 0.0)
    hi = v.astype(BF16).astype(F32)
    low = (v - hi).astype(BF16).astype(F32)
    return (hi + pltpu.roll(low, 32, 1)).astype(BF16)


def spread_heads(pk, sel):
    return dot(pk, sel)


def gather_heads(v, sel):
    hi, low = split2(v)
    return dot_nt(hi, sel) + dot_nt(low, sel)


def cumulate(tri, v, heads):
    v = jnp.where(lanes_of(v.shape) < heads, v, 0.0)
    p0 = v.astype(BF16).astype(F32)
    r = v - p0
    p1 = r.astype(BF16).astype(F32)
    p2 = r - p1
    pk = (p0 + pltpu.roll(p1, 32, 1) + pltpu.roll(p2, 64, 1)).astype(BF16)
    s = dot(tri, pk)
    n = s.shape[1]
    s = s + pltpu.roll(s, n - 32, 1) + pltpu.roll(s, n - 64, 1)
    return jnp.where(lanes_of(v.shape) < heads, s, 0.0)


def lane_tiles(v):
    return sum(v[:, c0 : c0 + 128] for c0 in range(0, v.shape[1], 128))


def row_tiles(v):
    return jnp.sum(v.reshape(v.shape[0] // 8, 8, v.shape[1]), axis=0)


def block_rows(b, size):
    return pl.ds(pl.multiple_of(b * size, size), size)


MESH = pl.DeviceIdType.MESH


class Sends:
    def __init__(self, send, recv):
        self.send, self.recv, self.used, self.started = send, recv, 0, []

    def make(self, src, dst, to):
        k = self.used
        self.used += 1
        return pltpu.make_async_remote_copy(
            src_ref=src, dst_ref=dst, send_sem=self.send.at[k], recv_sem=self.recv.at[k],
            device_id=to, device_id_type=MESH,
        )

    def start(self, src, dst, to):
        copy = self.make(src, dst, to)
        copy.start()
        self.started.append(copy)
        return copy

    def finish(self):
        for copy in self.started:
            copy.wait_send()


def hello(others):
    barrier = pltpu.get_barrier_semaphore()
    for to in others:
        pl.semaphore_signal(barrier, inc=1, device_id=to, device_id_type=MESH)


def greet(others):
    hello(others)
    pl.semaphore_wait(pltpu.get_barrier_semaphore(), len(others))


def place():
    z = lax.axis_index("tensor")
    d = lax.axis_index("dp")
    core = lax.rem(d, 2)
    x = lax.rem(d // 2, 2)
    y = d // 4
    return z, d, core, x, y


def xor_peer(core, x, y, k):
    c1 = 1 - core if k & 1 else core
    x1 = 1 - x if k & 2 else x
    y1 = 1 - y if k & 4 else y
    return y1 * 4 + x1 * 2 + c1


def dp_rows(d, size, part=None):
    if part is None:
        return pl.ds(pl.multiple_of(d * size, 16), size)
    return pl.ds(pl.multiple_of(d * size + part * (size // 2), 16), size // 2)


def columns(t, size):
    return pl.ds(pl.multiple_of(t * size, 128), size)


def cut_at(base, size, by_t, t):
    return pl.ds(pl.multiple_of(base + t * size, 128), size) if by_t else pl.ds(base, size)


class Gather:
    MESSAGES = 13

    def __init__(self, sends, nt, shard, full, here):
        self.sends, self.nt, self.shard, self.full = sends, nt, shard, full
        self.z, self.d, self.core, self.x, self.y = here
        self.rows, self.width = shard.shape

    def to(self, k):
        return {"dp": xor_peer(self.core, self.x, self.y, k)}

    def ref(self, k, part=None):
        return self.full.at[dp_rows(xor_peer(self.core, self.x, self.y, k), self.rows, part), :]

    def begin(self, sem):
        mine = self.full.at[dp_rows(self.d, self.rows), columns(self.z, self.width)]
        self.local = pltpu.make_async_copy(self.shard, mine, sem)
        self.local.start()
        self.zs = []
        for dz in range(1, self.nt):
            to = {"tensor": lax.rem(self.z + dz, self.nt)}
            self.zs.append(self.sends.start(self.shard, mine, to))

    def column(self):
        self.local.wait()
        for copy in self.zs:
            copy.wait_recv()
        own_a, own_b = self.ref(0, 0), self.ref(0, 1)
        self.x0 = self.sends.start(own_a, own_a, self.to(2))
        self.y0 = self.sends.start(own_b, own_b, self.to(4))
        self.c = [self.sends.start(self.ref(0), self.ref(0), self.to(1))]
        self.y1 = self.sends.start(own_a, own_a, self.to(4))
        self.x1 = self.sends.start(own_b, own_b, self.to(2))

    def forward(self):
        self.forward_first()
        self.forward_second()

    def forward_first(self):
        self.x0.wait_recv()
        self.y2 = self.sends.start(self.ref(2, 0), self.ref(2, 0), self.to(4))
        self.y0.wait_recv()
        self.x2 = self.sends.start(self.ref(4, 1), self.ref(4, 1), self.to(2))

    def forward_second(self):
        self.x1.wait_recv()
        self.c.append(self.sends.start(self.ref(2), self.ref(2), self.to(1)))
        self.y1.wait_recv()
        self.c.append(self.sends.start(self.ref(4), self.ref(4), self.to(1)))

    def corner(self):
        self.y2.wait_recv()
        self.x2.wait_recv()
        self.c.append(self.sends.start(self.ref(6), self.ref(6), self.to(1)))

    def finish(self):
        for copy in self.c:
            copy.wait_recv()


class Reduce:
    MESSAGES = 18

    @staticmethod
    def scratch(rows, width, nt, wz):
        half = rows // 2
        shapes = [(4, rows, width), (2, half, width), (2, half, width), (half, width), (half, width), (nt, rows, wz)]
        return [pltpu.VMEM(s, BF16) for s in shapes]

    def __init__(self, sends, nt, g, bufs, cuts, here):
        self.nt, self.g, self.cuts = nt, g, cuts
        self.rc, self.ra, self.rb, self.ta, self.tb, self.rz = bufs
        self.z, self.d, core, x, y = here
        rows = self.rc.shape[1]
        to = lambda k: {"dp": xor_peer(core, x, y, k)}
        at = lambda y, x, core, part=None: dp_rows(4 * y + 2 * x + core, rows, part)
        send = lambda src, dst, to: sends.make(g.at[src, :], dst, to)
        self.core = [send(at(q // 2, q % 2, 1 - core), self.rc.at[q], to(1)) for q in range(4)]
        self.core_rows = [at(q // 2, q % 2, core) for q in range(4)]
        self.a = [send(at(i, 1 - x, core, 0), self.ra.at[i], to(2)) for i in range(2)]
        self.b = [send(at(1 - y, i, core, 1), self.rb.at[i], to(4)) for i in range(2)]
        self.a_rows = [at(i, x, core, 0) for i in range(2)]
        self.b_rows = [at(y, i, core, 1) for i in range(2)]
        self.a2 = send(at(1 - y, x, core, 0), self.ta, to(4))
        self.b2 = send(at(y, 1 - x, core, 1), self.tb, to(2))
        self.halves = [dp_rows(self.d, rows, i) for i in range(2)]
        self.own = dp_rows(self.d, rows)
        self.zs = []
        self.places = []
        first = 0
        for base, size, by_t in cuts:
            dst = self.rz.at[self.z, :, pl.ds(first, size)]
            for dz in range(1, nt):
                t = lax.rem(self.z + dz, nt)
                src = g.at[self.own, cut_at(base, size, by_t, t)]
                self.zs.append(sends.make(src, dst, {"tensor": t}))
            self.places.append((first, size, cut_at(base, size, by_t, self.z)))
            first += size

    def add(self, rows, other):
        self.g[rows, :] = (self.g[rows, :].astype(F32) + other.astype(F32)).astype(BF16)

    def begin(self):
        for copy in self.core:
            copy.start()

    def first(self):
        for q in range(4):
            self.core[q].wait_recv()
            self.add(self.core_rows[q], self.rc[q])
        for copy in self.a + self.b:
            copy.start()

    def second(self):
        for i in range(2):
            self.a[i].wait_recv()
            self.add(self.a_rows[i], self.ra[i])
            self.b[i].wait_recv()
            self.add(self.b_rows[i], self.rb[i])
        self.a2.start()
        self.b2.start()

    def third(self):
        self.a2.wait_recv()
        self.add(self.halves[0], self.ta[...])
        self.b2.wait_recv()
        self.add(self.halves[1], self.tb[...])
        for copy in self.zs:
            copy.start()
        for first, size, cols in self.places:
            self.rz[self.z, :, first : first + size] = self.g[self.own, cols]

    def last(self, *outs):
        for copy in self.zs:
            copy.wait_recv()
        for out, (first, size, _) in zip(outs, self.places):
            total = self.rz[0, :, first : first + size].astype(F32)
            for t in range(1, self.nt):
                total = total + self.rz[t, :, first : first + size].astype(F32)
            out[...] = total

    def finish(self):
        for copy in self.core + self.a + self.b + [self.a2, self.b2] + self.zs:
            copy.wait_send()


class SmallSum:
    MESSAGES = 6

    @staticmethod
    def scratch(shape, nt):
        return [pltpu.VMEM((2,) + shape, F32), pltpu.VMEM((3,) + shape, F32), pltpu.VMEM((nt,) + shape, F32)]

    def __init__(self, sends, nt, v, bufs, here):
        self.nt, self.v = nt, v
        self.own, self.got, self.rz = bufs
        self.z, d, core, x, y = here
        self.copies = [
            sends.make(self.own.at[k - 1] if k else v, self.got.at[k], {"dp": xor_peer(core, x, y, 2**k)}) for k in range(3)
        ]
        part = self.rz.at[self.z]
        self.zs = [sends.make(part, part, {"tensor": lax.rem(self.z + dz, nt)}) for dz in range(1, nt)]

    def begin(self):
        self.copies[0].start()

    def step(self, k):
        self.copies[k - 1].wait_recv()
        total = (self.own[k - 2] if k > 1 else self.v[...]) + self.got[k - 1]
        if k < 3:
            self.own[k - 1] = total
            self.copies[k].start()
        else:
            self.rz[self.z] = total
            for copy in self.zs:
                copy.start()

    def finish(self):
        for copy in self.copies + self.zs:
            copy.wait_send()

    def last(self):
        for copy in self.zs:
            copy.wait_recv()
        total = self.rz[0]
        for t in range(1, self.nt):
            total = total + self.rz[t]
        return total


class Chain:
    def __init__(self, nt, by, mine, whole, got, out, send, recv):
        self.mine, self.whole, self.got, self.out, self.send, self.recv = mine, whole, got, out, send, recv
        z = lax.axis_index("tensor")
        self.seqs, _, di = got.shape
        self.per = di // WIDE
        self.pieces = self.seqs * self.per
        self.at = z if by > 0 else nt - 1 - z
        self.has_prev = self.at > 0
        self.has_next = self.at < nt - 1
        self.next = {"tensor": lax.rem(z + by + nt, nt)}
        self.begin_slot = 3 * self.at - 1

    def copy(self, k):
        s = k // self.per
        cols = pl.ds(pl.multiple_of((k - s * self.per) * WIDE, WIDE), WIDE)
        return pltpu.make_async_remote_copy(
            src_ref=self.out.at[s, :, cols], dst_ref=self.got.at[s, :, cols], send_sem=self.send.at[k],
            recv_sem=self.recv.at[k], device_id=self.next, device_id_type=MESH,
        )

    def pass_on(self, k, first):
        s = k // self.per
        cols = pl.ds(pl.multiple_of((k - s * self.per) * WIDE, WIDE), WIDE)
        v = self.mine[s, :, cols].astype(F32)
        if not first:
            v = v + self.whole[s, 0:1, cols] * self.got[s, :, cols].astype(F32)
        self.out[s, :, cols] = v.astype(BF16)
        self.copy(k).start()

    def begin(self, s):
        @pl.when(jnp.logical_not(self.has_prev))
        def _():
            self.got[s] = jnp.zeros(self.got.shape[1:], BF16)
            for k in range(self.per * s, self.per * (s + 1)):
                self.pass_on(k, True)

    def step(self, k):
        self.copy(k).wait_recv()

        @pl.when(self.has_next)
        def _():
            self.pass_on(k, False)

    def slot(self, n):
        since = n - self.begin_slot

        @pl.when(self.has_prev & self.has_next & (since >= 0) & (lax.rem(since + 8, 2) == 0) & (since < 2 * self.pieces))
        def _():
            self.step(since // 2)

    def rest(self, slots):
        for k in range(self.pieces):

            @pl.when(self.has_prev & self.has_next & (self.begin_slot + 2 * k >= slots))
            def _(k=k):
                self.step(k)

    def arrive(self, s):
        for i in range(self.per):

            @pl.when(jnp.logical_not(self.has_next))
            def _(i=i):
                self.copy(self.per * s + i).wait_recv()

    def finish(self):
        @pl.when(self.has_next)
        def _():
            for k in range(self.pieces):
                self.copy(k).wait_send()


class Moves:
    def __init__(self, sems):
        self.sems, self.used, self.open = sems, 0, []

    def start(self, src, dst):
        copy = pltpu.make_async_copy(src, dst, self.sems.at[self.used])
        self.used += 1
        copy.start()
        self.open.append(copy)
        return copy

    def finish(self, done=()):
        for copy in self.open:
            if all(copy is not other for other in done):
                copy.wait()


def heads_table(sel_ref, di):
    r = lax.broadcasted_iota(jnp.int32, (128, WIDE), 0)
    c = lax.broadcasted_iota(jnp.int32, (128, WIDE), 1)
    for c0 in range(0, di, WIDE):
        hit = ((r & 31) == ((c + c0) >> 6)) & (r < 64)
        sel_ref[:, c0 : c0 + WIDE] = jnp.where(hit, 1.0, 0.0).astype(BF16)


def ones_below(tri_ref, up):
    r = lax.broadcasted_iota(jnp.int32, (SPAN, SPAN), 0)
    c = lax.broadcasted_iota(jnp.int32, (SPAN, SPAN), 1)
    tri_ref[...] = jnp.where(r <= c if up else r >= c, 1.0, 0.0).astype(BF16)


def forward_kernel(heads, nt, nd, gathers, *refs):
    refs = list(refs)
    take = lambda n: [refs.pop(0) for _ in range(n)]
    x_hbm, c_hbm, norm_gain_ref, conv_shared_ref, shift_shared_ref = take(5)
    if gathers:
        (wgi_ref, wdelta_ref, wo_ref, wsh_ref, conv_inner_ref, shift_inner_ref, gated_gain_ref, decay_ref, bias_ref,
         skip_gain_ref) = take(10)
    else:
        w1_hbm, w2_hbm, w3_hbm, ws_hbm, parf_ref, xhf_ref = take(6)
    (h_hbm, rawi_hbm, raws_hbm, xs_hbm, bc_hbm, w1_out, w2_out, w3_out, ws_out, yn_hbm, dgate_hbm, dy_hbm, draw_hbm,
     acs_hbm, bs_hbm, rr_hbm, fresh_hbm, vv_hbm, mineb_hbm, sin_hbm) = take(20)
    (dec_ref, whole_ref, chan_ref, dpar_ref, skip_ref, gg_ref, sk_ref, ts_ref) = take(8)
    (x_ref, c_ref, h_ref, w1_ref, w2_ref, w3_ref, ws_ref, pf_ref, xh_ref, rawi_ref, raws_ref, xs_ref, bc_ref, y_ref,
     skc_ref, yn_ref, dgate_ref, dy_ref, g_ref, mine_ref, sb_ref, hh_ref, ea_ref, bst_ref,
     sel_ref, tri_ref, pack_ref, par_ref, zd_ref, wss_ref, turn_ref,
     draw_ref, acs_ref, bs_ref, rr_ref, fresh_ref, eaf_ref, vv_ref, mineb_ref, sin_ref, wk_ref) = take(41)
    send, recv, chain_send, chain_recv, local, moves, result_sems = take(7)

    tokens, dim = x_ref.shape
    seqs, ext, di = rawi_ref.shape
    span = ext - 16
    per = span // SPAN
    blocks = seqs * per
    sh = bc_ref.shape[1]
    state = sh // 2
    dcol = di // nt
    wa = dcol - 128
    inner = nt * wa
    z = lax.axis_index("tensor")
    store = Moves(moves)
    load_x = store.start(x_hbm, x_ref)
    load_c = store.start(c_hbm, c_ref)

    sends = Sends(send, recv)
    zpeers = [{"tensor": lax.rem(z + dz, nt)} for dz in range(1, nt)]
    if gathers:
        here = place()
        _, d, core, x, y = here
        others = zpeers + [{"dp": xor_peer(core, x, y, k)} for k in range(1, 8)]
        hello(others)
        rows = wgi_ref.shape[0]
        hloc = heads // nt
        pack_ref[:, :dcol] = wgi_ref[:, 1, :]
        pl.semaphore_wait(pltpu.get_barrier_semaphore(), len(others))
        shards = (
            (pack_ref.at[:, pl.ds(0, wa)], w1_ref.at[:, pl.ds(0, inner)]),
            (pack_ref.at[:, pl.ds(wa, 128)], w1_ref.at[:, pl.ds(inner, 128 * nt)]),
            (pack_ref.at[:, pl.ds(dcol, dcol)], w2_ref),
            (wo_ref, w3_ref),
        )
        secs = [Gather(sends, nt, a, b, here) for a, b in shards]
        secs[0].begin(local.at[0])
        secs[1].begin(local.at[1])
        pack_ref[:, dcol:] = wgi_ref[:, 0, :]
        turn_ref[...] = jnp.zeros_like(turn_ref)
        turn_ref[0:hloc, 0:rows] = wdelta_ref[...].astype(F32)
        zd_ref[z] = turn_ref[...].T[0:rows].astype(BF16)
        wss_ref[:, :sh] = wsh_ref[...]
        par_ref[...] = jnp.zeros_like(par_ref)
        par_ref[0:4, :] = conv_inner_ref[...].astype(F32)
        par_ref[4:5, :] = shift_inner_ref[...].astype(F32).reshape(1, dcol)
        par_ref[5:6, :] = gated_gain_ref[...].reshape(1, dcol)
        for k, ref in enumerate((decay_ref, bias_ref, skip_gain_ref)):
            par_ref[8 + k : 9 + k, 0:hloc] = ref[...].reshape(1, hloc)
        deltas = [sends.start(zd_ref.at[z], zd_ref.at[z], to) for to in zpeers]
        mine = ws_ref.at[dp_rows(d, rows), :]
        own = [pltpu.make_async_copy(wss_ref, mine, local.at[4]), pltpu.make_async_copy(par_ref, pf_ref.at[z], local.at[5])]
        own[1].start()
        got = [sends.start(par_ref, pf_ref.at[z], to) for to in zpeers]
        edges = [
            sends.make(
                x_hbm.at[pl.ds((s + 1) * span - 16, 16), :], xh_ref.at[pl.ds(16 * s, 16), :],
                {"tensor": lax.rem(z + 1, nt)},
            )
            for s in range(seqs)
        ]

        @pl.when(z < nt - 1)
        def _():
            for copy in edges:
                copy.start()

    else:
        greet(({"tensor": lax.rem(z + nt - 1, nt)}, {"tensor": lax.rem(z + 1, nt)}))
        loads = [store.start(a, b) for a, b in ((w1_hbm, w1_ref), (w2_hbm, w2_ref), (w3_hbm, w3_ref), (ws_hbm, ws_ref))]
        pf_ref[...] = parf_ref[...]
        xh_ref[...] = xhf_ref[...]

    heads_table(sel_ref, di)
    ones_below(tri_ref, False)

    gain = norm_gain_ref[...].reshape(1, dim)
    ts_ref[...] = jnp.zeros_like(ts_ref)
    ts_ref[0:4, :] = conv_shared_ref[...].astype(F32)
    ts_ref[4:5, :] = shift_shared_ref[...].astype(F32).reshape(1, sh)

    def norm(v):
        v = v.astype(F32)
        return (v * lax.rsqrt(jnp.mean(v * v, axis=-1, keepdims=True) + EPSILON) * gain).astype(BF16)

    load_x.wait()

    def norm_step(b, c):
        rows = block_rows(b, SPAN)
        h_ref[rows, :] = norm(x_ref[rows, :])
        return c

    lax.fori_loop(0, blocks, norm_step, 0)
    store.start(h_ref, h_hbm)

    if gathers:
        secs[0].column()
        for copy in deltas:
            copy.wait_recv()
        delta = zd_ref[0].astype(F32)
        for t in range(1, nt):
            delta = delta + pltpu.roll(zd_ref[t].astype(F32), hloc * t, 1)
        wss_ref[:, sh:] = delta.astype(BF16)
        own[0].start()
        got += [sends.start(wss_ref, mine, {"dp": xor_peer(core, x, y, k)}) for k in range(1, 8)]
        secs[1].column()
        secs[0].forward()
        secs[2].begin(local.at[2])
        secs[1].forward_first()

        @pl.when(z > 0)
        def _():
            for copy in edges:
                copy.wait_recv()

        @pl.when(z == 0)
        def _():
            xh_ref[...] = jnp.zeros_like(xh_ref)

        for copy in own:
            copy.wait()
        for copy in got:
            copy.wait_recv()

    hh_ref[...] = norm(xh_ref[...])
    head = pf_ref[0, 8:16, 0:128]
    for t in range(nt):
        chan_ref[:, dcol * t : dcol * (t + 1)] = pf_ref[t, 0:8, :]
        if t > 0:
            head = head + pltpu.roll(pf_ref[t, 8:16, 0:128], heads // nt * t, 1)
    ak = -jnp.exp(head[0:1])
    ak = jnp.where(lanes_of(ak.shape) < heads, ak, 0.0)
    dpar_ref[0:1, :] = head[1:2]
    dpar_ref[1:2, :] = ak * LOG2E
    dpar_ref[2:3, :] = ak
    dpar_ref[3:8, :] = jnp.zeros((5, 128), F32)
    sk8 = packed(jnp.broadcast_to(head[2:3], (8, 128)), heads)
    for c0 in range(0, di, WIDE):
        skip_ref[:, c0 : c0 + WIDE] = spread_heads(sk8, sel_ref[:, c0 : c0 + WIDE])

    def conv(raw, par, out, s, cols):
        def step(r, c):
            r0 = pl.multiple_of(r * 128, 128)
            v = raw[s, pl.ds(r0 + 8, 136), cols]
            acc = par[4:5, cols] + par[3:4, cols] * v[8:]
            for k in range(3):
                acc = acc + par[k : k + 1, cols] * v[5 + k : 133 + k]
            out[pl.ds(pl.multiple_of(s * span + r0, 128), 128), cols] = (acc * sigmoid(acc)).astype(BF16)
            return c

        lax.fori_loop(0, span // 128, step, 0)

    if not gathers:
        loads[3].wait()
    for s in range(seqs):
        rows = slice(span * s, span * (s + 1))
        raws_ref[s, 0:16, :] = dot(hh_ref[16 * s : 16 * s + 16, :], ws_ref[:, :sh])
        both = dot(h_ref[rows, :], ws_ref[...])
        raws_ref[s, 16:ext, :] = both[:, :sh]
        draw_ref[rows, :] = both[:, sh:] + dpar_ref[0:1, :]
        for c0 in range(0, sh, 256):
            conv(raws_ref, ts_ref, bc_ref, s, slice(c0, c0 + 256))
    store.start(raws_ref, raws_hbm)
    store.start(bc_ref, bc_hbm)
    store.start(ws_ref, ws_out)

    def first_part(s):
        def step(t, carry):
            cols = pl.ds(pl.multiple_of(dcol * t, 128), wa)
            w = w1_ref[:, pl.ds(pl.multiple_of(wa * t, 128), wa)]
            rawi_ref[s, 0:16, cols] = dot(hh_ref[16 * s : 16 * s + 16, :], w)
            rawi_ref[s, 16:ext, cols] = dot(h_ref[span * s : span * (s + 1), :], w)
            conv(rawi_ref, chan_ref, xs_ref, s, cols)
            return carry

        lax.fori_loop(0, nt, step, 0)

    def second_part(s):
        rows = slice(span * s, span * (s + 1))

        def step(t, carry):
            cols = pl.ds(pl.multiple_of(dcol * t + wa, 128), 128)
            w = w1_ref[:, pl.ds(pl.multiple_of(inner + 128 * t, 128), 128)]
            rawi_ref[s, 0:16, cols] = dot(hh_ref[16 * s : 16 * s + 16, :], w)
            rawi_ref[s, 16:ext, cols] = dot(h_ref[rows, :], w)
            conv(rawi_ref, chan_ref, xs_ref, s, cols)
            return carry

        lax.fori_loop(0, nt, step, 0)
        store.start(rawi_ref.at[s], rawi_hbm.at[s])
        store.start(xs_ref.at[rows, :], xs_hbm.at[rows, :])

    def block_step(s, j, c):
        b = s * per + j
        rows = block_rows(b, SPAN)
        bt = bc_ref[rows, :state].astype(F32).T.astype(BF16)
        w = spread_heads(wk_ref[rows, :], sel_ref[...])
        fresh = dot(bt, (w * xs_ref[rows, :].astype(F32)).astype(BF16))

        @pl.when(j == 0)
        def _():
            fresh_ref[s] = fresh.astype(BF16)
            mine_ref[s] = fresh

        @pl.when(j > 0)
        def _():
            mine_ref[s] = dec_ref[b, 0:1, :] * mine_ref[s] + fresh

        return c

    def decay_step(b, c):
        rows = block_rows(b, SPAN)
        s = b // per
        j = b - s * per
        x = draw_ref[rows, :]
        dt = jnp.maximum(x, 0.0) + jnp.log1p(jnp.exp(-jnp.abs(x)))
        lg = jnp.where(x < -20.0, x * LOG2E, jnp.log2(jnp.maximum(dt, 1e-30)))
        acs = cumulate(tri_ref[...], dt * dpar_ref[1:2, :], heads)
        bs = acs - lg
        acs_ref[rows, :] = acs
        bs_ref[rows, :] = bs
        bst_ref[b] = bs.T
        end = acs[SPAN - 1 : SPAN, :]
        wk_ref[rows, :] = packed(jnp.exp2(end - bs), heads)
        ea_ref[rows, :] = packed(jnp.exp2(acs), heads)
        de = spread_heads(packed(jnp.broadcast_to(jnp.exp2(end), (8, 128)), heads), sel_ref[...])
        dec_ref[b] = de

        @pl.when(j == 0)
        def _():
            whole_ref[s] = de

        @pl.when(j > 0)
        def _():
            whole_ref[s] = de * whole_ref[s]

        return c

    chain = Chain(nt, 1, mine_ref, whole_ref, sin_ref, sb_ref, chain_send, chain_recv)
    if gathers:
        secs[1].forward_second()
        secs[0].corner()
        secs[2].column()
        secs[3].begin(local.at[3])
        secs[1].corner()
    lax.fori_loop(0, blocks, decay_step, 0)
    for a, b in ((draw_ref, draw_hbm), (acs_ref, acs_hbm), (bs_ref, bs_hbm)):
        store.start(a, b)
    if gathers:
        secs[0].finish()
    else:
        loads[0].wait()
    for s in range(seqs):
        first_part(s)
        if gathers and s == 0:
            secs[2].forward_first()
    if gathers:
        secs[1].finish()
        secs[2].forward_second()
        secs[3].column()
    store.start(w1_ref, w1_out)
    for s in range(seqs):
        second_part(s)
        lax.fori_loop(0, per, functools.partial(block_step, s), 0)
        chain.begin(s)
        if s == seqs - 1:
            store.start(fresh_ref, fresh_hbm)
        if gathers and s == 0:
            secs[2].corner()
            secs[3].forward()
    if gathers:
        secs[3].corner()

    lower = lax.broadcasted_iota(jnp.int32, (HALF, HALF), 0) >= lax.broadcasted_iota(jnp.int32, (HALF, HALF), 1)
    first = lanes_of((HALF, 128)) < P_SIZE
    pairs = di // 128

    def intra_step(b, carry):
        rows = block_rows(b, SPAN)
        bb = bc_ref[rows, :state]
        cc = bc_ref[rows, state:]
        g00 = dot_nt(cc[:HALF], bb[:HALF])
        g10 = dot_nt(cc[HALF:], bb[:HALF])
        g11 = dot_nt(cc[HALF:], bb[HALF:])
        for p in range(pairs):
            cols = slice(128 * p, 128 * p + 128)
            xp = xs_ref[rows, cols]
            y0, y1 = [], []
            for h in (2 * p, 2 * p + 1):
                a0 = acs_ref[block_rows(2 * b, HALF), h : h + 1]
                a1 = acs_ref[block_rows(2 * b + 1, HALF), h : h + 1]
                r0 = bst_ref[b, h : h + 1, :HALF]
                r1 = bst_ref[b, h : h + 1, HALF:]
                m00 = jnp.where(lower, jnp.exp2(a0 - r0) * g00, 0.0).astype(BF16)
                m10 = (jnp.exp2(a1 - r0) * g10).astype(BF16)
                m11 = jnp.where(lower, jnp.exp2(a1 - r1) * g11, 0.0).astype(BF16)
                y0.append(dot(m00, xp[:HALF]))
                y1.append(dot(jnp.concatenate([m10, m11], axis=1), xp))
            y_ref[block_rows(2 * b, HALF), cols] = jnp.where(first, y0[0], y0[1])
            y_ref[block_rows(2 * b + 1, HALF), cols] = jnp.where(first, y1[0], y1[1])
            if (p + 1) % (pairs // 3) == 0:
                chain.slot(3 * b + (p + 1) // (pairs // 3) - 1)
        return carry

    lax.fori_loop(0, blocks, intra_step, 0)
    load_c.wait()
    if gathers:
        secs[2].finish()
    else:
        loads[1].wait()
        loads[2].wait()
    store.start(w2_ref, w2_out)

    def gate_step(b, carry):
        rows = block_rows(b, span)
        for c0 in range(0, di, WIDE):
            cols = slice(c0, c0 + WIDE)
            dy_ref[rows, cols] = dot(h_ref[rows, :], w2_ref[:, cols]).astype(BF16)
        return carry

    def products_step(b, carry):
        rows = block_rows(b, span)
        for c0 in range(0, di, WIDE):
            cols = slice(c0, c0 + WIDE)
            dgate_ref[rows, cols] = (dot(c_ref[rows, :], w3_ref[:, cols]) * chan_ref[5:6, cols]).astype(BF16)
        return carry

    lax.fori_loop(0, seqs, gate_step, 0)
    if gathers:
        secs[3].finish()
    store.start(w3_ref, w3_out)
    lax.fori_loop(0, seqs, products_step, 0)
    chain.rest(3 * blocks)

    gg_ref[...] = jnp.zeros_like(gg_ref)
    skc_ref[...] = jnp.zeros_like(skc_ref)
    results = ((yn_ref, yn_hbm), (dgate_ref, dgate_hbm), (dy_ref, dy_hbm), (rr_ref, rr_hbm))

    def result_copy(k, b):
        rows = block_rows(b, SPAN)
        return pltpu.make_async_copy(results[k][0].at[rows, :], results[k][1].at[rows, :], result_sems.at[k, b])

    def sin_copy(s):
        return pltpu.make_async_copy(sin_ref.at[s], sin_hbm.at[s], result_sems.at[len(results), s])

    def mid_step(s, j, carry):
        b = s * per + j
        rows = block_rows(b, SPAN)
        cc = bc_ref[rows, state:]
        ss = jnp.zeros((SPAN, 128), F32)
        for c0 in range(0, di, WIDE):
            cols = slice(c0, c0 + WIDE)
            prev = sin_ref[s, :, cols].astype(F32)
            later = dec_ref[s * per, 0:1, cols] * prev + fresh_ref[s, :, cols].astype(F32)
            s_in = jnp.where(j == 0, prev, later).astype(BF16)
            ea = spread_heads(ea_ref[rows, :], sel_ref[:, cols])
            eaf_ref[:, cols] = ea
            ynos = y_ref[rows, cols] + ea * dot(cc, s_in)
            y_ref[rows, cols] = ynos
            y = ynos + skip_ref[0:1, cols] * xs_ref[rows, cols].astype(F32)
            gate = dy_ref[rows, cols].astype(F32)
            g = y * (gate * sigmoid(gate))
            g_ref[:, cols] = g
            ss = ss + lane_tiles(g * g)
        r2 = lax.rsqrt(jnp.sum(ss, axis=-1, keepdims=True) / di + EPSILON)
        qg = jnp.zeros((SPAN, 128), F32)
        for c0 in range(0, di, WIDE):
            cols = slice(c0, c0 + WIDE)
            g = g_ref[:, cols]
            gain = chan_ref[5:6, cols]
            yn_ref[rows, cols] = (g * r2 * gain).astype(BF16)
            qg_here = dgate_ref[rows, cols].astype(F32) * g
            gg_ref[:, cols] += row_tiles(qg_here * r2)
            qg = qg + lane_tiles(qg_here)
        coef = r2 * r2 * r2 * (jnp.sum(qg, axis=-1, keepdims=True) / di)
        rr = jnp.zeros((SPAN, 128), F32)
        ct = cc.astype(F32).T.astype(BF16)
        for c0 in range(0, di, WIDE):
            cols = slice(c0, c0 + WIDE)
            xf = xs_ref[rows, cols].astype(F32)
            ynos = y_ref[rows, cols]
            y = ynos + skip_ref[0:1, cols] * xf
            gate = dy_ref[rows, cols].astype(F32)
            sg = sigmoid(gate)
            dg = r2 * dgate_ref[rows, cols].astype(F32) - coef * g_ref[:, cols]
            dgate_ref[rows, cols] = (dg * y * (sg * (1.0 + gate * (1.0 - sg)))).astype(BF16)
            dyb = (dg * (gate * sg)).astype(BF16)
            dy_ref[rows, cols] = dyb
            dy = dyb.astype(F32)
            rr = rr + gather_heads(dy * ynos, sel_ref[:, cols])
            skc_ref[:, cols] += row_tiles(dy * xf)
            vv = dot(ct, (eaf_ref[:, cols] * dy).astype(BF16))

            @pl.when(j == 0)
            def _(cols=cols, vv=vv):
                mine_ref[s, :, cols] = vv

            @pl.when(j > 0)
            def _(cols=cols, vv=vv):
                vv_ref[s, :, cols] = vv.astype(BF16)
                mine_ref[s, :, cols] += dec_ref[s * per, 0:1, cols] * vv

        rr_ref[rows, :] = rr
        for k in range(len(results)):
            result_copy(k, b).start()
        return carry

    def mid_sequence(s, carry):
        chain.arrive(s)
        sin_copy(s).start()
        lax.fori_loop(0, per, functools.partial(mid_step, s), 0)
        return carry

    lax.fori_loop(0, seqs, mid_sequence, 0)
    gg_ref[...] = gg_ref[...] / chan_ref[5:6, :]
    sk_ref[...] = jnp.zeros_like(sk_ref)
    for c0 in range(0, di, WIDE):
        sk_ref[...] += gather_heads(skc_ref[:, c0 : c0 + WIDE], sel_ref[:, c0 : c0 + WIDE])
    mineb_ref[...] = mine_ref[...].astype(BF16)
    chain.finish()
    sends.finish()
    if gathers:

        @pl.when(z < nt - 1)
        def _():
            for copy in edges:
                copy.wait_send()

    for s in range(seqs):
        sin_copy(s).wait()
    store.start(mineb_ref, mineb_hbm)
    store.start(vv_ref, vv_hbm)
    for b in range(blocks):
        for k in range(len(results)):
            result_copy(k, b).wait()
    store.finish((load_x, load_c) if gathers else (load_x, load_c, *loads))


def backward_kernel(heads, nt, nd, reduces, *refs):
    refs = list(refs)
    take = lambda n: [refs.pop(0) for _ in range(n)]
    (x_hbm, c_hbm, h_hbm, rawi_hbm, raws_hbm, xs_hbm, bc_hbm, w1_hbm, w2_hbm, w3_hbm, ws_hbm, yn_hbm, dgate_hbm, dy_hbm,
     draw_hbm, acs_hbm, bs_hbm, rr_hbm, fresh_hbm, vv_hbm, sin_hbm, mineb_hbm) = take(22)
    norm_gain_ref, ts_ref, dec_ref, whole_ref, chan_ref, dpar_ref, skip_ref, gg_ref, sk_ref = take(9)
    out_hbm, ig_hbm = take(2)
    if reduces:
        o1_ref, osd_ref, o2_ref, o3_ref, om_ref = take(5)
    else:
        g1_out, g2_out, g3_out, sm_ref = take(4)
    (c_ref, h_ref, rawi_ref, raws_ref, xs_ref, bc_ref, w1_ref, ws_ref, dgate_ref, dy_ref, draw_ref,
     acs_ref, bs_ref, rr_ref, fresh_ref, vv_ref, sin_ref, ds_ref, sb_ref, din_ref, dx_ref, dbc_ref, g_ref, halo_ref,
     edge_ref, keep_ref, acst_ref, dg_ref, sel_ref, triu_ref, tg_ref, small_ref, ng_ref, w2_ref) = take(34)
    if reduces:
        (sm_ref,) = take(1)
        bufs = [take(6) for _ in range(4)]
        small_bufs = take(3)
    chain_send, chain_recv, halo_send, halo_recv, moves = take(5)
    if reduces:
        sems = [take(2) for _ in range(5)]

    tokens, dim = h_ref.shape
    seqs, ext, di = rawi_ref.shape
    span = ext - 16
    per = span // SPAN
    blocks = seqs * per
    sh = bc_ref.shape[1]
    state = sh // 2
    dcol = di // nt
    wa = dcol - 128
    na = nt * wa
    z = lax.axis_index("tensor")
    move = Moves(moves)
    load = lambda a, b: move.start(a, b)
    yn_ref = din_ref.at[:, pl.ds(0, di)]
    l_mine, l_c, l_yn0 = load(mineb_hbm, sb_ref), load(c_hbm, c_ref), load(yn_hbm, yn_ref)
    x_ref = xs_ref.at[:, pl.ds(0, dim)]
    w3_ref = din_ref.at[pl.ds(0, dim), pl.ds(0, di)]

    if reduces:
        here = place()
        _, d, core, x, y = here
        others = [{"tensor": lax.rem(z + dz, nt)} for dz in range(1, nt)]
        others += [{"dp": xor_peer(core, x, y, k)} for k in (1, 2, 4)]
        hello(others)
        cut = ((0, dcol, True),)
        parts = (
            (g_ref.at[:, pl.ds(di, di)], cut), (g_ref.at[:, pl.ds(0, di)], cut),
            (g_ref.at[:, pl.ds(di, na)], ((0, wa, True),)),
            (g_ref.at[:, pl.ds(di + na, 128 * nt + sh + 128)], ((0, 128, True), (128 * nt, sh + 128, False))),
        )
        r3, r2, ra, rb = (Reduce(Sends(*sems[i]), nt, g, bufs[i], cuts, here) for i, (g, cuts) in enumerate(parts))
        small_sum = SmallSum(Sends(*sems[4]), nt, sm_ref, small_bufs, here)
    else:
        others = [{"tensor": lax.rem(z + nt - 1, nt)}, {"tensor": lax.rem(z + 1, nt)}]
        hello(others)
    heads_table(sel_ref, di)
    ones_below(triu_ref, True)
    small_ref[...] = jnp.zeros_like(small_ref)
    ng_ref[...] = jnp.zeros_like(ng_ref)
    tg_ref[...] = jnp.zeros_like(tg_ref)
    pl.semaphore_wait(pltpu.get_barrier_semaphore(), len(others))

    chain = Chain(nt, -1, sb_ref, whole_ref, ds_ref, sb_ref, chain_send, chain_recv)
    l_mine.wait()
    for s in range(seqs):
        chain.begin(s)

    def weight_gradient(dv, w, at):
        g = dot_tn(h_ref[...], dv)
        g_ref[:, at : at + g.shape[1]] = g.astype(BF16)
        ng_ref[...] += lane_tiles(g * w.astype(F32))

    l_c.wait()
    l_yn0.wait()
    l_h, l_dgate, l_w2 = load(h_hbm, h_ref), load(dgate_hbm, dgate_ref), load(w2_hbm, w2_ref)
    slot = 0
    for c0 in range(0, di, WIDE):
        g_ref[:, di + c0 : di + c0 + WIDE] = dot_tn(c_ref[...], din_ref[:, c0 : c0 + WIDE]).astype(BF16)
        chain.slot(slot)
        slot += 1
    if reduces:
        r3.begin()
    else:
        s3 = move.start(g_ref.at[:, pl.ds(di, di)], g3_out)
    l_h.wait()
    l_dgate.wait()
    l_w2.wait()
    l_scan = [
        load(a, b)
        for a, b in (
            (xs_hbm, xs_ref), (dy_hbm, dy_ref), (bc_hbm, bc_ref), (acs_hbm, acs_ref), (bs_hbm, bs_ref),
        )
    ]
    for c0 in range(0, di, WIDE):
        weight_gradient(dgate_ref[:, c0 : c0 + WIDE], w2_ref[:, c0 : c0 + WIDE], c0)
        chain.slot(slot)
        slot += 1
    if reduces:
        r2.begin()
    else:
        s2 = move.start(g_ref.at[:, pl.ds(0, di)], g2_out)

    for copy in l_scan:
        copy.wait()
    l_state = [
        load(a, b)
        for a, b in (
            (draw_hbm, draw_ref), (rr_hbm, rr_ref), (fresh_hbm, fresh_ref), (vv_hbm, vv_ref), (sin_hbm, sin_ref),
            (rawi_hbm, rawi_ref), (raws_hbm, raws_ref),
        )
    ]
    l_last = [load(w1_hbm, w1_ref), load(ws_hbm, ws_ref)]
    upper = lax.broadcasted_iota(jnp.int32, (HALF, HALF), 0) <= lax.broadcasted_iota(jnp.int32, (HALF, HALF), 1)
    first = lanes_of((HALF, 128)) < P_SIZE
    first_all = lanes_of((SPAN, 128)) < P_SIZE
    pairs = di // 128
    slot0 = slot

    def intra_step(b, carry):
        rows = block_rows(b, SPAN)
        acst_ref[...] = acs_ref[rows, :].T
        bb = bc_ref[rows, :state]
        cc = bc_ref[rows, state:]
        g00 = dot_nt(bb[:HALF], cc[:HALF])
        g01 = dot_nt(bb[:HALF], cc[HALF:])
        g11 = dot_nt(bb[HALF:], cc[HALF:])
        dg_ref[...] = jnp.zeros_like(dg_ref)
        for p in range(pairs):
            cols = slice(128 * p, 128 * p + 128)
            xp = xs_ref[rows, cols]
            dyp = dy_ref[rows, cols]
            d0, d1 = [], []
            for i, h in enumerate((2 * p, 2 * p + 1)):
                keep = first_all if i == 0 else jnp.logical_not(first_all)
                xm = jnp.where(keep, xp, jnp.zeros_like(xp))
                b0 = bs_ref[block_rows(2 * b, HALF), h : h + 1]
                b1 = bs_ref[block_rows(2 * b + 1, HALF), h : h + 1]
                r0 = acst_ref[h : h + 1, :HALF]
                r1 = acst_ref[h : h + 1, HALF:]
                e00 = jnp.where(upper, jnp.exp2(r0 - b0), 0.0)
                e01 = jnp.exp2(r1 - b0)
                e11 = jnp.where(upper, jnp.exp2(r1 - b1), 0.0)
                m0 = jnp.concatenate([(e00 * g00).astype(BF16), (e01 * g01).astype(BF16)], axis=1)
                m1 = (e11 * g11).astype(BF16)
                d0.append(dot(m0, dyp))
                d1.append(dot(m1, dyp[HALF:]))
                dm0 = dot_nt(xm[:HALF], dyp)
                dm1 = dot_nt(xm[HALF:], dyp[HALF:])
                dg_ref[0] += dm0[:, :HALF] * e00
                dg_ref[1] += dm0[:, HALF:] * e01
                dg_ref[2] += dm1 * e11
            dx_ref[block_rows(2 * b, HALF), cols] = jnp.where(first, d0[0], d0[1])
            dx_ref[block_rows(2 * b + 1, HALF), cols] = jnp.where(first, d1[0], d1[1])
            if reduces and p == pairs // 2:
                pl.when(b == blocks // 4)(r3.first)
            if (p + 1) % (pairs // 3) == 0:
                chain.slot(slot0 + 3 * b + (p + 1) // (pairs // 3) - 1)
        dg00 = dg_ref[0]
        dg01 = dg_ref[1]
        dg11 = dg_ref[2]
        dbc_ref[block_rows(2 * b, HALF), :state] = dot(jnp.concatenate([dg00, dg01], axis=1).astype(BF16), cc)
        dbc_ref[block_rows(2 * b + 1, HALF), :state] = dot(dg11.astype(BF16), cc[HALF:])
        dbc_ref[block_rows(2 * b, HALF), state:] = dot(dg00.T.astype(BF16), bb[:HALF])
        dbc_ref[block_rows(2 * b + 1, HALF), state:] = dot(
            jnp.concatenate([dg01.T, dg11.T], axis=1).astype(BF16), bb
        )
        return carry

    lax.fori_loop(0, blocks, intra_step, 0)
    if reduces:
        r3.second()
        r2.first()
    chain.rest(slot0 + 3 * blocks)
    for copy in l_state:
        copy.wait()

    def state_step(s, j):
        b = s * per + j
        rows = block_rows(b, SPAN)
        acs = acs_ref[rows, :]
        end = acs[SPAN - 1 : SPAN, :]
        eak = packed(jnp.exp2(acs), heads)
        wk = packed(jnp.exp2(end - bs_ref[rows, :]), heads)
        bb = bc_ref[rows, :state]
        db = dbc_ref[rows, :state]
        dc = dbc_ref[rows, state:]
        pp = jnp.zeros((SPAN, 128), F32)
        endsum = jnp.zeros((8, 128), F32)
        for c0 in range(0, di, WIDE):
            cols = slice(c0, c0 + WIDE)
            s_in = sin_ref[s, :, cols]
            ds = ds_ref[s, :, cols]
            if j > 0:
                s_in = dec_ref[s * per, 0:1, cols] * s_in.astype(F32) + fresh_ref[s, :, cols].astype(F32)
                s_in = s_in.astype(BF16)
            if j < per - 1:
                ds = dec_ref[s * per + per - 1, 0:1, cols] * ds.astype(F32) + vv_ref[s, :, cols].astype(F32)
                ds = ds.astype(BF16)
            w = spread_heads(wk, sel_ref[:, cols])
            ea = spread_heads(eak, sel_ref[:, cols])
            xf = xs_ref[rows, cols].astype(F32)
            dyf = dy_ref[rows, cols].astype(F32)
            dxs = w * dot(bb, ds)
            dxn = dx_ref[rows, cols] + dxs
            pp = pp + gather_heads(dxn * xf, sel_ref[:, cols])
            at_end = jnp.sum(ds.astype(F32) * s_in.astype(F32), axis=0, keepdims=True) * dec_ref[b, 0:1, cols]
            first_row = lax.broadcasted_iota(jnp.int32, (8, WIDE), 0) == 0
            at_end = row_tiles(dxs * xf) + jnp.where(first_row, jnp.broadcast_to(at_end, (8, WIDE)), 0.0)
            endsum = endsum + gather_heads(at_end, sel_ref[:, cols])
            dc = dc + dot_nt((ea * dyf).astype(BF16), s_in)
            db = db + dot_nt((w * xf).astype(BF16), ds)
            dx_ref[rows, cols] = dxn + skip_ref[0:1, cols] * dyf
        dbc_ref[rows, :state] = db
        dbc_ref[rows, state:] = dc
        da = cumulate(triu_ref[...], rr_ref[rows, :] - pp, heads)
        da = da + jnp.sum(endsum, axis=0, keepdims=True)
        xx = draw_ref[rows, :]
        sg = 1.0 / (1.0 + jnp.exp(-xx))
        dt = jnp.maximum(xx, 0.0) + jnp.log1p(jnp.exp(-jnp.abs(xx)))
        ratio = jnp.where(xx < -20.0, 1.0, sg / jnp.maximum(dt, 1e-30))
        ak = dpar_ref[2:3, :]
        dd = da * ak * sg + pp * ratio
        din_ref[rows, di + sh :] = dd.astype(BF16)
        small_ref[0:1, :] += jnp.sum(da * dt * ak, axis=0, keepdims=True)
        small_ref[1:2, :] += jnp.sum(dd, axis=0, keepdims=True)

        def conv_back(raw, par, dact, off, cols):
            here_cols = pl.ds(pl.multiple_of(off + cols.start, 128), cols.size)

            def step(r, prev):
                r0 = pl.multiple_of(r * HALF, HALF)
                at = pl.ds(pl.multiple_of(16 + j * SPAN + r0, 16), HALF)
                now = raw[s, at, cols]
                v = jnp.concatenate([prev, now], axis=0)
                sh_v = [v[5 + k : 5 + k + HALF] for k in range(3)] + [now]
                pre = par[4:5, cols] + par[0:1, cols] * sh_v[0]
                for k in range(1, 4):
                    pre = pre + par[k : k + 1, cols] * sh_v[k]
                sg = sigmoid(pre)
                dp = dact[pl.ds(pl.multiple_of(b * SPAN + r0, HALF), HALF), cols] * (sg * (1.0 + pre * (1.0 - sg)))
                raw[s, at, cols] = dp
                for k in range(4):
                    tg_ref[k, :, here_cols] += row_tiles(dp * sh_v[k])
                tg_ref[4, :, here_cols] += row_tiles(dp)
                return now[HALF - 8 :]

            prev = raw[s, 8:16, cols] if j == 0 else keep_ref[s, :, here_cols]
            prev = lax.fori_loop(0, SPAN // HALF, step, prev)
            if j < per - 1:
                keep_ref[s, :, here_cols] = prev

        def inner_step(i, carry):
            conv_back(rawi_ref, chan_ref, dx_ref, 0, pl.ds(pl.multiple_of(256 * i, 256), 256))
            return carry

        lax.fori_loop(0, di // 256, inner_step, 0)
        for c0 in range(0, sh, 256):
            conv_back(raws_ref, ts_ref, dbc_ref, di, pl.ds(c0, 256))

    halo_copy = pltpu.make_async_remote_copy(
        src_ref=edge_ref, dst_ref=halo_ref, send_sem=halo_send.at[0], recv_sem=halo_recv.at[0],
        device_id={"tensor": lax.rem(z + nt - 1, nt)}, device_id_type=MESH,
    )
    for j in range(per):

        def seq_step(s, carry, j=j):
            if j == 0:
                chain.arrive(s)
            state_step(s, j)
            return carry

        lax.fori_loop(0, seqs, seq_step, 0)
        if j == 0:
            edge_ref[:, :, :di] = rawi_ref[:, 16:24, :]
            edge_ref[:, :, di:] = raws_ref[:, 16:24, :]

            @pl.when(z > 0)
            def _():
                halo_copy.start()

            if reduces:
                r3.third()
    l_last += [load(x_hbm, x_ref)]
    l_yn = load(yn_hbm, dy_ref)
    if reduces:
        r3.last(o3_ref)
        r2.second()

    @pl.when(z < nt - 1)
    def _():
        halo_copy.wait_recv()

    @pl.when(z == nt - 1)
    def _():
        halo_ref[...] = jnp.zeros_like(halo_ref)

    def conv_t(dpre, par, off, c0, to):
        cols = pl.ds(pl.multiple_of(c0, 128), 128)
        halo_cols = pl.ds(pl.multiple_of(off + c0, 128), 128)
        to_cols = pl.ds(pl.multiple_of(to, 128), 128)

        def step(s, carry):
            def rows_step(r, nxt):
                r0 = pl.multiple_of(span - HALF * (r + 1), HALF)
                now = dpre[s, pl.ds(pl.multiple_of(16 + r0, 16), HALF), cols]
                v = jnp.concatenate([now, nxt], axis=0)
                acc = par[3:4, cols] * now
                for k in range(3):
                    acc = acc + par[k : k + 1, cols] * v[3 - k : 3 - k + HALF]
                din_ref[pl.ds(pl.multiple_of(s * span + r0, HALF), HALF), to_cols] = acc.astype(BF16)
                return now[0:8]

            lax.fori_loop(0, span // HALF, rows_step, halo_ref[s, :, halo_cols])
            return carry

        lax.fori_loop(0, seqs, step, 0)

    def inner_first(i, carry):
        t = i // (wa // 128)
        r = 128 * (i - t * (wa // 128))
        conv_t(rawi_ref, chan_ref, 0, dcol * t + r, wa * t + r)
        return carry

    def inner_second(t, carry):
        conv_t(rawi_ref, chan_ref, 0, dcol * t + wa, na + 128 * t)
        return carry

    def shared_part(i, carry):
        conv_t(raws_ref, ts_ref, di, 128 * i, di + 128 * i)
        return carry

    lax.fori_loop(0, na // 128, inner_first, 0)
    if reduces:
        r3.finish()
        r2.third()
    else:
        s3.wait()
    for copy in l_last:
        copy.wait()
    for c0 in range(0, na, WIDE):
        weight_gradient(din_ref[:, c0 : c0 + WIDE], w1_ref[:, c0 : c0 + WIDE], di + c0)
    if reduces:
        ra.begin()
    lax.fori_loop(0, nt, inner_second, 0)
    lax.fori_loop(0, sh // 128, shared_part, 0)
    for c0 in range(na, di, WIDE):
        weight_gradient(din_ref[:, c0 : c0 + WIDE], w1_ref[:, c0 : c0 + WIDE], di + c0)
    weight_gradient(din_ref[:, di:], ws_ref[...], 2 * di)
    column = lambda v: jnp.sum(v, axis=0, keepdims=True)
    for k in range(5):
        sm_ref[k : k + 1, :] = column(tg_ref[k, :, :di])
    sm_ref[5:6, :] = column(gg_ref[...])
    gain = norm_gain_ref[...].reshape(1, dim)
    sm_ref[6:7, :dim] = column(ng_ref[...].T) / gain
    flat = [column(tg_ref[k, :, di:]) for k in range(5)] + [small_ref[0:1, :], small_ref[1:2, :], column(sk_ref[...])]
    row, at = 6, dim
    for v in flat:
        width = v.shape[1]
        if at + width > di:
            row, at = row + 1, 0
        sm_ref[row : row + 1, at : at + width] = v
        at += width
    sm_ref[row : row + 1, at:] = jnp.zeros((1, di - at), F32)
    if reduces:
        rb.begin()
        small_sum.begin()
    else:
        move.start(g_ref.at[:, pl.ds(di, g_ref.shape[1] - di)], g1_out)
    def last_step(b, carry):
        if reduces:
            pl.when(b == 0)(ra.first)

            @pl.when(b == blocks // 4)
            def _():
                small_sum.step(1)
                rb.first()

            @pl.when(b == 2 * blocks // 4)
            def _():
                small_sum.step(2)

            @pl.when(b == 3 * blocks // 4)
            def _():
                ra.second()
                small_sum.step(3)

        rows = block_rows(b, SPAN)
        dh = dot_nt(dgate_ref[rows, :], w2_ref[...])
        dh = dh + dot_nt(din_ref[rows, :di], w1_ref[...])
        dh = dh + dot_nt(din_ref[rows, di:], ws_ref[...])
        u = x_ref[rows, :].astype(F32)
        r1 = lax.rsqrt(jnp.mean(u * u, axis=-1, keepdims=True) + EPSILON)
        e = dh * gain
        m = jnp.mean(e * u, axis=-1, keepdims=True)
        c_ref[rows, :] = (c_ref[rows, :].astype(F32) + r1 * e - u * (r1 * r1 * r1 * m)).astype(BF16)
        return carry

    lax.fori_loop(0, blocks, last_step, 0)
    move.start(c_ref, ig_hbm)
    l_w3 = load(w3_hbm, w3_ref)

    def output_step(b, carry):
        rows = block_rows(b, SPAN)
        x_ref[rows, :] = (x_ref[rows, :].astype(F32) + dot_nt(dy_ref[rows, :], w3_ref[...])).astype(BF16)
        return carry

    if reduces:
        rb.second()
        ra.third()
    l_w3.wait()
    l_yn.wait()
    lax.fori_loop(0, blocks // 2, output_step, 0)
    if reduces:
        rb.third()
    lax.fori_loop(blocks // 2, blocks, output_step, 0)
    move.start(x_ref, out_hbm)
    if reduces:
        r2.last(o2_ref)
        om_ref[...] = small_sum.last()
        ra.last(o1_ref.at[:, pl.ds(0, wa)])
        rb.last(o1_ref.at[:, pl.ds(wa, 128)], osd_ref)
        for part in (r2, ra, rb, small_sum):
            part.finish()
    chain.finish()

    @pl.when(z > 0)
    def _():
        halo_copy.wait_send()

    move.finish((l_mine, l_c, l_yn0, l_yn, l_w3, l_h, l_dgate, l_w2, *l_scan, *l_state, *l_last) + (() if reduces else (s3,)))


def finish_kernel(nt, hloc, out_hbm, ig_hbm, o1_ref, osd_ref, o2_ref, o3_ref, om_ref, *refs):
    (out_to, ig_to, ng_ref, gi_ref, gs_ref, delta_ref, ci_ref, si_ref, cs_ref, ss_ref, decay_ref, bias_ref, bypass_ref,
     gg_ref, ow_ref, out_ref, ig_ref, sems) = refs
    ways = ((out_hbm, out_ref, out_to), (ig_hbm, ig_ref, ig_to))
    into = [pltpu.make_async_copy(a, b, sems.at[k]) for k, (a, b, _) in enumerate(ways)]
    onto = [pltpu.make_async_copy(b, c, sems.at[2 + k]) for k, (_, b, c) in enumerate(ways)]
    for copy in into:
        copy.start()
    z = lax.axis_index("tensor")
    dcol = o1_ref.shape[1]
    sh = gs_ref.shape[1]
    dim = ng_ref.shape[0]
    cols = pl.ds(pl.multiple_of(z * dcol, 128), dcol)
    back = lax.rem(128 - z * hloc, 128)
    ng_ref[...] = om_ref[6, :dim]
    gi_ref[:, 0, :] = o2_ref[...]
    gi_ref[:, 1, :] = o1_ref[...]
    gs_ref[...] = osd_ref[:, :sh]
    delta_ref[...] = pltpu.roll(osd_ref[:, sh:], back, 1).T[:hloc]
    ci_ref[...] = om_ref[0:4, cols]
    si_ref[...] = om_ref[4, cols]
    gg_ref[...] = om_ref[5, cols]
    row, at = 6, dim
    taps = []
    for _ in range(5):
        if at + sh > om_ref.shape[1]:
            row, at = row + 1, 0
        taps.append(om_ref[row : row + 1, at : at + sh])
        at += sh
    for k in range(4):
        cs_ref[k : k + 1, :] = taps[k]
    ss_ref[...] = taps[4][0]
    for ref in (decay_ref, bias_ref, bypass_ref):
        if at + 128 > om_ref.shape[1]:
            row, at = row + 1, 0
        v = jnp.broadcast_to(om_ref[row : row + 1, at : at + 128], (8, 128))
        ref[...] = pltpu.roll(v, back, 1)[0, :hloc]
        at += 128
    for copy, after in zip(into, onto):
        copy.wait()
        after.start()
    ow_ref[...] = o3_ref[...]
    for copy in onto:
        copy.wait()


def semaphores(n):
    return [pltpu.SemaphoreType.DMA((n,)), pltpu.SemaphoreType.DMA((n,))]


def shifted(v, axis, by):
    n = lax.axis_size(axis)
    return lax.ppermute(v, axis, [(i, i + by) for i in range(n) if 0 <= i + by < n])


def gather_all(nt, nd, wgi, wdelta, wo, ws, par, edge):
    both = ("tensor", "dp")
    rows = ws.shape[0]
    dcol = wo.shape[0]
    pack = jnp.concatenate([wgi[:, 1], wgi[:, 0], wo.T], axis=1)
    full = lax.all_gather(pack, both, axis=0).reshape(nt, nd * rows, -1)
    whole = lambda a, b: full[:, :, a:b].transpose(1, 0, 2).reshape(nd * rows, nt * (b - a))
    w1 = jnp.concatenate([whole(0, dcol - 128), whole(dcol - 128, dcol)], axis=1)
    delta = lax.all_gather(wdelta, "tensor", axis=1, tiled=True)
    delta = jnp.pad(delta, ((0, 0), (0, 128 - delta.shape[1])))
    return (
        w1, whole(dcol, 2 * dcol), whole(2 * dcol, 3 * dcol),
        lax.all_gather(jnp.concatenate([ws, delta], axis=1), "dp", axis=0, tiled=True),
        lax.all_gather(par, "tensor", axis=0), shifted(edge, "tensor", 1),
    )


def reduce_all(nt, nd, g1, g2, g3, sm, sh):
    dim = g1.shape[0]
    rows = dim // nd
    dcol = g2.shape[1] // nt
    wa = dcol - 128
    both = ("tensor", "dp")
    parts = [
        g[:, at : at + nt * w].reshape(dim, nt, w).transpose(1, 0, 2)
        for g, at, w in ((g1, 0, wa), (g1, wa * nt, 128), (g2, 0, dcol), (g3, 0, dcol))
    ]
    big = jnp.concatenate(parts, axis=2).reshape(nt * nd, rows, -1)
    big = lax.psum_scatter(big, both, scatter_dimension=0).astype(F32)
    shared = g1[:, nt * dcol :].reshape(nd, rows, sh + 128).astype(F32)
    shared = lax.psum(lax.psum_scatter(shared, "dp", scatter_dimension=0), "tensor")
    return big[:, :dcol], shared, big[:, dcol : 2 * dcol], big[:, 2 * dcol :], lax.psum(sm, both)


def local(
    block_input, norm_gain, input_gate_inner_weight, input_shared_weight, input_delta_weight, conv_inner, shift_inner,
    conv_shared, shift_shared, decay_log, delta_bias, skip_gain, gated_gain, output_projection_weight, cotangent,
):
    nt = lax.axis_size("tensor")
    nd = lax.axis_size("dp")
    me = lax.axis_index("tensor")
    seqs, span, dim = block_input.shape
    tokens = seqs * span
    blocks = tokens // SPAN
    rows, _, dcol = input_gate_inner_weight.shape
    di = dcol * nt
    sh = input_shared_weight.shape[1]
    state = sh // 2
    hloc = input_delta_weight.shape[1]
    heads = hloc * nt

    x = block_input.reshape(tokens, dim)
    c = cotangent.reshape(tokens, dim)
    gathers = nd == 8
    args = [x, c, norm_gain, conv_shared, shift_shared]
    kinds = [pl.ANY, pl.ANY] + [pltpu.VMEM] * 3
    if gathers:
        args += [
            input_gate_inner_weight, input_delta_weight.T, output_projection_weight.T, input_shared_weight, conv_inner,
            shift_inner, gated_gain, decay_log, delta_bias, skip_gain,
        ]
        kinds += [pltpu.VMEM] * 10
    else:
        head = jnp.pad(jnp.stack([decay_log, delta_bias, skip_gain]), ((0, 5), (0, dcol - hloc)))
        par = [conv_inner.astype(F32), shift_inner.astype(F32)[None], gated_gain[None], jnp.zeros((2, dcol), F32), head]
        args += gather_all(
            nt, nd, input_gate_inner_weight, input_delta_weight, output_projection_weight, input_shared_weight,
            jnp.concatenate(par, axis=0), block_input[:, span - 16 :].reshape(seqs * 16, dim),
        )
        kinds += [pl.ANY] * 4 + [pltpu.VMEM] * 2
    scan_state = ((seqs, state, di), BF16)
    f128 = ((tokens, 128), F32)
    far = [
        ((tokens, dim), BF16), ((seqs, span + 16, di), F32), ((seqs, span + 16, sh), F32), ((tokens, di), BF16),
        ((tokens, sh), BF16), ((dim, di), BF16), ((dim, di), BF16), ((dim, di), BF16), ((dim, sh + 128), BF16),
        ((tokens, di), BF16), ((tokens, di), BF16), ((tokens, di), BF16), f128, f128, f128, f128, scan_state,
        scan_state, scan_state, scan_state,
    ]
    near = [
        ((blocks, 8, di), F32), ((seqs, 8, di), F32), ((8, di), F32), ((8, 128), F32), ((8, di), F32), ((8, di), F32),
        ((8, 128), F32), ((8, sh), F32)]
    scratch = [
        ((tokens, dim), BF16), ((tokens, dim), BF16), ((tokens, dim), BF16), ((dim, di), BF16), ((dim, di), BF16),
        ((dim, di), BF16), ((dim, sh + 128), BF16), ((nt, 16, dcol), F32), ((seqs * 16, dim), BF16),
        ((seqs, span + 16, di), F32), ((seqs, span + 16, sh), F32), ((tokens, di), BF16), ((tokens, sh), BF16),
        ((tokens, di), F32), ((8, di), F32), ((tokens, di), BF16), ((tokens, di), BF16), ((tokens, di), BF16),
        ((SPAN, di), F32), ((seqs, state, di), F32), scan_state,
        ((seqs * 16, dim), BF16), ((tokens, 128), BF16), ((blocks, 128, SPAN), F32), ((128, di), BF16),
        ((SPAN, SPAN), BF16), ((rows, 2 * dcol), BF16), ((16, dcol), F32), ((nt, rows, 128), BF16), ((rows, sh + 128), BF16),
        ((128, 128), F32), f128, f128, f128, f128, scan_state, ((SPAN, di), F32), scan_state, scan_state, scan_state,
        ((tokens, 128), BF16),
    ]
    pieces = seqs * di // WIDE
    h, rawi, raws, xs, bc, w1, w2, w3, ws, yn, dgate, dy, draw, acs, bs, rr, fresh, vv, mineb, sin, *rest = pl.pallas_call(
        functools.partial(forward_kernel, heads, nt, nd, gathers),
        out_shape=[jax.ShapeDtypeStruct(s, d) for s, d in far + near],
        in_specs=[pl.BlockSpec(memory_space=k) for k in kinds],
        out_specs=[pl.BlockSpec(memory_space=pl.ANY)] * len(far) + [pl.BlockSpec(memory_space=pltpu.VMEM)] * len(near),
        scratch_shapes=[pltpu.VMEM(s, d) for s, d in scratch]
        + semaphores(4 * Gather.MESSAGES + 5 + 2 * nt + seqs) + semaphores(pieces)
        + [pltpu.SemaphoreType.DMA((6,)), pltpu.SemaphoreType.DMA((24,)), pltpu.SemaphoreType.DMA((5, blocks))],
        compiler_params=pltpu.CompilerParams(vmem_limit_bytes=VMEM_LIMIT, collective_id=0, has_side_effects=True),
        name="forward",
    )(*args)
    dec, whole, chan, dpar, skip, ggg, skg, ts = rest

    args = [x, c, h, rawi, raws, xs, bc, w1, w2, w3, ws, yn, dgate, dy, draw, acs, bs, rr, fresh, vv, sin, mineb]
    kinds = [pl.ANY] * len(args)
    more = [norm_gain, ts, dec, whole, chan, dpar, skip, ggg, skg]
    args += more
    kinds += [pltpu.VMEM] * len(more)
    wa = dcol - 128
    scratch = [
        ((tokens, dim), BF16), ((tokens, dim), BF16), ((seqs, span + 16, di), F32),
        ((seqs, span + 16, sh), F32), ((tokens, di), BF16), ((tokens, sh), BF16), ((dim, di), BF16),
        ((dim, sh + 128), BF16), ((tokens, di), BF16), ((tokens, di), BF16), f128, f128, f128, f128, scan_state, scan_state,
        scan_state, scan_state, scan_state, ((tokens, di + sh + 128), BF16), ((tokens, di), F32), ((tokens, sh), F32),
        ((dim, 2 * di + sh + 128), BF16), ((seqs, 8, di + sh), F32), ((seqs, 8, di + sh), F32), ((seqs, 8, di + sh), F32),
        ((128, SPAN), F32), ((3, HALF, HALF), F32), ((128, di), BF16), ((SPAN, SPAN), BF16),
        ((5, 8, di + sh), F32), ((8, 128), F32), ((dim, 128), F32), ((dim, di), BF16),
    ]
    scratch = [pltpu.VMEM(s, d) for s, d in scratch]
    sems = semaphores(pieces) + semaphores(1) + [pltpu.SemaphoreType.DMA((32,))]
    if gathers:
        near = [
            ((rows, dcol), F32), ((rows, sh + 128), F32), ((rows, dcol), F32), ((rows, dcol), F32), ((8, di), F32)
        ]
        far = []
        scratch += [pltpu.VMEM((8, di), F32)]
        for width, wz in ((di, dcol), (di, dcol), (wa * nt, wa), (128 * nt + sh + 128, sh + 256)):
            scratch += Reduce.scratch(rows, width, nt, wz)
        scratch += SmallSum.scratch((8, di), nt)
        for _ in range(4):
            sems += semaphores(Reduce.MESSAGES)
        sems += semaphores(SmallSum.MESSAGES)
    else:
        far = [((dim, di + sh + 128), BF16), ((dim, di), BF16), ((dim, di), BF16)]
        near = [((8, di), F32)]
    outs = [((tokens, dim), BF16)] * 2 + far + near
    out, ig, *rest = pl.pallas_call(
        functools.partial(backward_kernel, heads, nt, nd, gathers),
        out_shape=[jax.ShapeDtypeStruct(s, d) for s, d in outs],
        in_specs=[pl.BlockSpec(memory_space=k) for k in kinds],
        out_specs=[pl.BlockSpec(memory_space=pl.ANY)] * (2 + len(far)) + [pl.BlockSpec(memory_space=pltpu.VMEM)] * len(near),
        scratch_shapes=scratch + sems,
        compiler_params=pltpu.CompilerParams(vmem_limit_bytes=VMEM_LIMIT, collective_id=1, has_side_effects=True),
        name="backward",
    )(*args)
    if gathers:
        sums = rest
    else:
        sums = reduce_all(nt, nd, *rest, sh)
    finals = [
        ((tokens, dim), BF16), ((tokens, dim), BF16), ((dim,), F32), ((rows, 2, dcol), F32), ((rows, sh), F32),
        ((hloc, rows), F32), ((4, dcol), F32), ((dcol,), F32), ((4, sh), F32), ((sh,), F32), ((hloc,), F32), ((hloc,), F32),
        ((hloc,), F32), ((dcol,), F32), ((rows, dcol), F32),
    ]
    out, ig, *rest = pl.pallas_call(
        functools.partial(finish_kernel, nt, hloc),
        out_shape=[jax.ShapeDtypeStruct(s, d) for s, d in finals],
        in_specs=[pl.BlockSpec(memory_space=pl.ANY)] * 2 + [pl.BlockSpec(memory_space=pltpu.VMEM)] * 5,
        out_specs=[pl.BlockSpec(memory_space=pl.ANY)] * 2 + [pl.BlockSpec(memory_space=pltpu.VMEM)] * 13,
        scratch_shapes=[pltpu.VMEM((tokens, dim), BF16)] * 2 + [pltpu.SemaphoreType.DMA((4,))],
        name="finish",
    )(out, ig, *sums)
    rest[3] = rest[3].T
    rest[-1] = rest[-1].T
    return (out.reshape(block_input.shape), ig.reshape(block_input.shape), *rest)


def solution(mesh):
    placed = (
        P("dp", "tensor", None), P(), P("dp", None, "tensor"), P("dp", None), P("dp", "tensor"), P(None, "tensor"),
        P("tensor"), P(), P(), P("tensor"), P("tensor"), P("tensor"), P("tensor"), P("tensor", "dp"),
        P("dp", "tensor", None),
    )
    return jax.shard_map(
        local,
        mesh=mesh,
        in_specs=placed,
        out_specs=(
            P("dp", "tensor", None), P("dp", "tensor", None), P(), P("dp", None, "tensor"), P("dp", None),
            P("dp", "tensor"), P(None, "tensor"), P("tensor"), P(), P(), P("tensor"), P("tensor"), P("tensor"),
            P("tensor"), P("tensor", "dp"),
        ),
        check_vma=False,
    )
```

```python
import functools

import jax
import jax.numpy as jnp
from jax import lax
from jax.experimental import pallas as pl
from jax.experimental.pallas import tpu as pltpu
from jax.sharding import PartitionSpec as P

P_SIZE = 64
SPAN = 256
HALF = SPAN // 2
EPSILON = 1e-05
LOG2E = 1.4426950408889634
F32 = jnp.float32
BF16 = jnp.bfloat16
VMEM_LIMIT = 65024 * 1024
WIDE = 512
PIECES = 512, 256


def dot(a, b):
    return jnp.dot(a, b, preferred_element_type=F32)


def dot_nt(a, b):
    return lax.dot_general(a, b, (((1,), (1,)), ((), ())), preferred_element_type=F32)


def dot_tn(a, b):
    return lax.dot_general(a, b, (((0,), (0,)), ((), ())), preferred_element_type=F32)


def sigmoid(v):
    return 0.5 * jnp.tanh(0.5 * v) + 0.5


def split2(v):
    hi = v.astype(BF16)
    return hi, (v - hi.astype(F32)).astype(BF16)


def lanes_of(shape):
    return lax.broadcasted_iota(jnp.int32, shape, len(shape) - 1)


def packed(v, heads):
    v = jnp.where(lanes_of(v.shape) < heads, v, 0.0)
    hi = v.astype(BF16).astype(F32)
    low = (v - hi).astype(BF16).astype(F32)
    return (hi + pltpu.roll(low, 32, 1)).astype(BF16)


def spread_heads(pk, sel):
    return dot(pk, sel)


def gather_heads(v, sel):
    hi, low = split2(v)
    return dot_nt(hi, sel) + dot_nt(low, sel)


def cumulate(tri, v, heads):
    v = jnp.where(lanes_of(v.shape) < heads, v, 0.0)
    p0 = v.astype(BF16).astype(F32)
    r = v - p0
    p1 = r.astype(BF16).astype(F32)
    p2 = r - p1
    pk = (p0 + pltpu.roll(p1, 32, 1) + pltpu.roll(p2, 64, 1)).astype(BF16)
    s = dot(tri, pk)
    n = s.shape[1]
    s = s + pltpu.roll(s, n - 32, 1) + pltpu.roll(s, n - 64, 1)
    return jnp.where(lanes_of(v.shape) < heads, s, 0.0)


def lane_tiles(v):
    return sum(v[:, c0 : c0 + 128] for c0 in range(0, v.shape[1], 128))


def row_tiles(v):
    return jnp.sum(v.reshape(v.shape[0] // 8, 8, v.shape[1]), axis=0)


def block_rows(b, size):
    return pl.ds(pl.multiple_of(b * size, size), size)


MESH = pl.DeviceIdType.MESH


class Sends:
    def __init__(self, send, recv):
        self.send, self.recv, self.used, self.started = send, recv, 0, []

    def make(self, src, dst, to):
        k = self.used
        self.used += 1
        return pltpu.make_async_remote_copy(
            src_ref=src, dst_ref=dst, send_sem=self.send.at[k], recv_sem=self.recv.at[k],
            device_id=to, device_id_type=MESH,
        )

    def start(self, src, dst, to):
        copy = self.make(src, dst, to)
        copy.start()
        self.started.append(copy)
        return copy

    def finish(self):
        for copy in self.started:
            copy.wait_send()


def hello(others):
    barrier = pltpu.get_barrier_semaphore()
    for to in others:
        pl.semaphore_signal(barrier, inc=1, device_id=to, device_id_type=MESH)


def greet(others):
    hello(others)
    pl.semaphore_wait(pltpu.get_barrier_semaphore(), len(others))


def place():
    z = lax.axis_index("tensor")
    d = lax.axis_index("dp")
    core = lax.rem(d, 2)
    x = lax.rem(d // 2, 2)
    y = d // 4
    return z, d, core, x, y


def xor_peer(core, x, y, k):
    c1 = 1 - core if k & 1 else core
    x1 = 1 - x if k & 2 else x
    y1 = 1 - y if k & 4 else y
    return y1 * 4 + x1 * 2 + c1


def dp_rows(d, size, part=None):
    if part is None:
        return pl.ds(pl.multiple_of(d * size, 16), size)
    return pl.ds(pl.multiple_of(d * size + part * (size // 2), 16), size // 2)


def columns(t, size):
    return pl.ds(pl.multiple_of(t * size, 128), size)


def cut_at(base, size, by_t, t):
    return pl.ds(pl.multiple_of(base + t * size, 128), size) if by_t else pl.ds(base, size)


class Gather:
    MESSAGES = 13

    def __init__(self, sends, nt, shard, full, here):
        self.sends, self.nt, self.shard, self.full = sends, nt, shard, full
        self.z, self.d, self.core, self.x, self.y = here
        self.rows, self.width = shard.shape

    def to(self, k):
        return {"dp": xor_peer(self.core, self.x, self.y, k)}

    def ref(self, k, part=None):
        return self.full.at[dp_rows(xor_peer(self.core, self.x, self.y, k), self.rows, part), :]

    def begin(self, sem):
        mine = self.full.at[dp_rows(self.d, self.rows), columns(self.z, self.width)]
        self.local = pltpu.make_async_copy(self.shard, mine, sem)
        self.local.start()
        self.zs = []
        for dz in range(1, self.nt):
            to = {"tensor": lax.rem(self.z + dz, self.nt)}
            self.zs.append(self.sends.start(self.shard, mine, to))

    def column(self):
        self.local.wait()
        for copy in self.zs:
            copy.wait_recv()
        own_a, own_b = self.ref(0, 0), self.ref(0, 1)
        self.x0 = self.sends.start(own_a, own_a, self.to(2))
        self.y0 = self.sends.start(own_b, own_b, self.to(4))
        self.c = [self.sends.start(self.ref(0), self.ref(0), self.to(1))]
        self.y1 = self.sends.start(own_a, own_a, self.to(4))
        self.x1 = self.sends.start(own_b, own_b, self.to(2))

    def forward(self):
        self.forward_first()
        self.forward_second()

    def forward_first(self):
        self.x0.wait_recv()
        self.y2 = self.sends.start(self.ref(2, 0), self.ref(2, 0), self.to(4))
        self.y0.wait_recv()
        self.x2 = self.sends.start(self.ref(4, 1), self.ref(4, 1), self.to(2))

    def forward_second(self):
        self.x1.wait_recv()
        self.c.append(self.sends.start(self.ref(2), self.ref(2), self.to(1)))
        self.y1.wait_recv()
        self.c.append(self.sends.start(self.ref(4), self.ref(4), self.to(1)))

    def corner(self):
        self.y2.wait_recv()
        self.x2.wait_recv()
        self.c.append(self.sends.start(self.ref(6), self.ref(6), self.to(1)))

    def finish(self):
        for copy in self.c:
            copy.wait_recv()


class Reduce:
    MESSAGES = 18

    @staticmethod
    def scratch(rows, width, nt, wz):
        half = rows // 2
        shapes = [(4, rows, width), (2, half, width), (2, half, width), (half, width), (half, width), (nt, rows, wz)]
        return [pltpu.VMEM(s, BF16) for s in shapes]

    def __init__(self, sends, nt, g, bufs, cuts, here):
        self.nt, self.g, self.cuts = nt, g, cuts
        self.rc, self.ra, self.rb, self.ta, self.tb, self.rz = bufs
        self.z, self.d, core, x, y = here
        rows = self.rc.shape[1]
        to = lambda k: {"dp": xor_peer(core, x, y, k)}
        at = lambda y, x, core, part=None: dp_rows(4 * y + 2 * x + core, rows, part)
        send = lambda src, dst, to: sends.make(g.at[src, :], dst, to)
        self.core = [send(at(q // 2, q % 2, 1 - core), self.rc.at[q], to(1)) for q in range(4)]
        self.core_rows = [at(q // 2, q % 2, core) for q in range(4)]
        self.a = [send(at(i, 1 - x, core, 0), self.ra.at[i], to(2)) for i in range(2)]
        self.b = [send(at(1 - y, i, core, 1), self.rb.at[i], to(4)) for i in range(2)]
        self.a_rows = [at(i, x, core, 0) for i in range(2)]
        self.b_rows = [at(y, i, core, 1) for i in range(2)]
        self.a2 = send(at(1 - y, x, core, 0), self.ta, to(4))
        self.b2 = send(at(y, 1 - x, core, 1), self.tb, to(2))
        self.halves = [dp_rows(self.d, rows, i) for i in range(2)]
        self.own = dp_rows(self.d, rows)
        self.zs = []
        self.places = []
        first = 0
        for base, size, by_t in cuts:
            dst = self.rz.at[self.z, :, pl.ds(first, size)]
            for dz in range(1, nt):
                t = lax.rem(self.z + dz, nt)
                src = g.at[self.own, cut_at(base, size, by_t, t)]
                self.zs.append(sends.make(src, dst, {"tensor": t}))
            self.places.append((first, size, cut_at(base, size, by_t, self.z)))
            first += size

    def add(self, rows, other):
        self.g[rows, :] = (self.g[rows, :].astype(F32) + other.astype(F32)).astype(BF16)

    def begin(self):
        for copy in self.core:
            copy.start()

    def first(self):
        for q in range(4):
            self.core[q].wait_recv()
            self.add(self.core_rows[q], self.rc[q])
        for copy in self.a + self.b:
            copy.start()

    def second(self):
        for i in range(2):
            self.a[i].wait_recv()
            self.add(self.a_rows[i], self.ra[i])
            self.b[i].wait_recv()
            self.add(self.b_rows[i], self.rb[i])
        self.a2.start()
        self.b2.start()

    def third(self):
        self.a2.wait_recv()
        self.add(self.halves[0], self.ta[...])
        self.b2.wait_recv()
        self.add(self.halves[1], self.tb[...])
        for copy in self.zs:
            copy.start()
        for first, size, cols in self.places:
            self.rz[self.z, :, first : first + size] = self.g[self.own, cols]

    def last(self, *outs):
        for copy in self.zs:
            copy.wait_recv()
        for out, (first, size, _) in zip(outs, self.places):
            total = self.rz[0, :, first : first + size].astype(F32)
            for t in range(1, self.nt):
                total = total + self.rz[t, :, first : first + size].astype(F32)
            out[...] = total

    def finish(self):
        for copy in self.core + self.a + self.b + [self.a2, self.b2] + self.zs:
            copy.wait_send()


class SmallSum:
    MESSAGES = 6

    @staticmethod
    def scratch(shape, nt):
        return [pltpu.VMEM((2,) + shape, F32), pltpu.VMEM((3,) + shape, F32), pltpu.VMEM((nt,) + shape, F32)]

    def __init__(self, sends, nt, v, bufs, here):
        self.nt, self.v = nt, v
        self.own, self.got, self.rz = bufs
        self.z, d, core, x, y = here
        self.copies = [
            sends.make(self.own.at[k - 1] if k else v, self.got.at[k], {"dp": xor_peer(core, x, y, 2**k)}) for k in range(3)
        ]
        part = self.rz.at[self.z]
        self.zs = [sends.make(part, part, {"tensor": lax.rem(self.z + dz, nt)}) for dz in range(1, nt)]

    def begin(self):
        self.copies[0].start()

    def step(self, k):
        self.copies[k - 1].wait_recv()
        total = (self.own[k - 2] if k > 1 else self.v[...]) + self.got[k - 1]
        if k < 3:
            self.own[k - 1] = total
            self.copies[k].start()
        else:
            self.rz[self.z] = total
            for copy in self.zs:
                copy.start()

    def finish(self):
        for copy in self.copies + self.zs:
            copy.wait_send()

    def last(self):
        for copy in self.zs:
            copy.wait_recv()
        total = self.rz[0]
        for t in range(1, self.nt):
            total = total + self.rz[t]
        return total


class Chain:
    def __init__(self, nt, by, mine, whole, got, out, send, recv, piece, slots, near, far):
        self.mine, self.whole, self.got, self.out, self.send, self.recv = mine, whole, got, out, send, recv
        z = lax.axis_index("tensor")
        self.seqs, _, di = got.shape
        self.piece = piece
        self.per = di // piece
        self.pieces = self.seqs * self.per
        self.at = z if by > 0 else nt - 1 - z
        self.has_prev = self.at > 0
        self.has_next = self.at < nt - 1
        self.next = {"tensor": lax.rem(z + by + nt, nt)}
        self.slots = slots
        self.when = [jnp.where(self.at == 1, a, b) for a, b in zip(near, far)]

    def copy(self, k):
        s = k // self.per
        cols = pl.ds(pl.multiple_of((k - s * self.per) * self.piece, self.piece), self.piece)
        return pltpu.make_async_remote_copy(
            src_ref=self.out.at[s, :, cols], dst_ref=self.got.at[s, :, cols], send_sem=self.send.at[k],
            recv_sem=self.recv.at[k], device_id=self.next, device_id_type=MESH,
        )

    def pass_on(self, k, first):
        s = k // self.per
        cols = pl.ds(pl.multiple_of((k - s * self.per) * self.piece, self.piece), self.piece)
        v = self.mine[s, :, cols].astype(F32)
        if not first:
            v = v + self.whole[s, 0:1, cols] * self.got[s, :, cols].astype(F32)
        self.out[s, :, cols] = v.astype(BF16)
        self.copy(k).start()

    def begin(self, s):
        @pl.when(jnp.logical_not(self.has_prev))
        def _():
            self.got[s] = jnp.zeros(self.got.shape[1:], BF16)
            for k in range(self.per * s, self.per * (s + 1)):
                self.pass_on(k, True)

    def step(self, k):
        self.copy(k).wait_recv()

        @pl.when(self.has_next)
        def _():
            self.pass_on(k, False)

    def slot(self, n):
        k, hit = 0, 0
        for at in self.when:
            k = k + jnp.where(at < n, 1, 0)
            hit = hit + jnp.where(at == n, 1, 0)

        @pl.when(self.has_prev & self.has_next & (hit == 1))
        def _():
            self.step(k)

    def rest(self, first, last, now=True):
        for k in range(first, last):

            @pl.when(self.has_prev & self.has_next & (self.when[k] >= self.slots) & now)
            def _(k=k):
                self.step(k)

    def arrive(self, s):
        for i in range(self.per):

            @pl.when(jnp.logical_not(self.has_next))
            def _(i=i):
                self.copy(self.per * s + i).wait_recv()

    def finish(self):
        @pl.when(self.has_next)
        def _():
            for k in range(self.pieces):
                self.copy(k).wait_send()


class Moves:
    def __init__(self, sems):
        self.sems, self.used, self.open = sems, 0, []

    def start(self, src, dst):
        copy = pltpu.make_async_copy(src, dst, self.sems.at[self.used])
        self.used += 1
        copy.start()
        self.open.append(copy)
        return copy

    def finish(self, done=()):
        for copy in self.open:
            if all(copy is not other for other in done):
                copy.wait()


def heads_table(sel_ref, di):
    r = lax.broadcasted_iota(jnp.int32, (128, WIDE), 0)
    c = lax.broadcasted_iota(jnp.int32, (128, WIDE), 1)
    for c0 in range(0, di, WIDE):
        hit = ((r & 31) == ((c + c0) >> 6)) & (r < 64)
        sel_ref[:, c0 : c0 + WIDE] = jnp.where(hit, 1.0, 0.0).astype(BF16)


def ones_below(tri_ref, up):
    r = lax.broadcasted_iota(jnp.int32, (SPAN, SPAN), 0)
    c = lax.broadcasted_iota(jnp.int32, (SPAN, SPAN), 1)
    tri_ref[...] = jnp.where(r <= c if up else r >= c, 1.0, 0.0).astype(BF16)


def forward_kernel(heads, nt, nd, gathers, *refs):
    refs = list(refs)
    take = lambda n: [refs.pop(0) for _ in range(n)]
    x_hbm, c_hbm, norm_gain_ref, conv_shared_ref, shift_shared_ref = take(5)
    if gathers:
        (wgi_ref, wdelta_ref, wo_ref, wsh_ref, conv_inner_ref, shift_inner_ref, gated_gain_ref, decay_ref, bias_ref,
         skip_gain_ref) = take(10)
    else:
        w1_hbm, w2_hbm, w3_hbm, ws_hbm, parf_ref, xhf_ref = take(6)
    (h_hbm, rawi_hbm, raws_hbm, xs_hbm, bc_hbm, w1_out, w2_out, w3_out, ws_out, yn_hbm, dgate_hbm, dy_hbm, draw_hbm,
     acs_hbm, bs_hbm, rr_hbm, fresh_hbm, vv_hbm, mineb_hbm, sin_hbm) = take(20)
    (dec_ref, whole_ref, chan_ref, dpar_ref, skip_ref, gg_ref, sk_ref, ts_ref) = take(8)
    (x_ref, c_ref, h_ref, w1_ref, w2_ref, w3_ref, ws_ref, pf_ref, xh_ref, rawi_ref, raws_ref, xs_ref, bc_ref, y_ref,
     skc_ref, yn_ref, dgate_ref, dy_ref, g_ref, mine_ref, sb_ref, hh_ref, ea_ref, bst_ref,
     sel_ref, tri_ref, pack_ref, par_ref, zd_ref, wss_ref, turn_ref,
     draw_ref, acs_ref, bs_ref, rr_ref, fresh_ref, eaf_ref, vv_ref, mineb_ref, sin_ref, wk_ref) = take(41)
    send, recv, chain_send, chain_recv, local, moves, result_sems = take(7)

    tokens, dim = x_ref.shape
    seqs, ext, di = rawi_ref.shape
    span = ext - 16
    per = span // SPAN
    blocks = seqs * per
    sh = bc_ref.shape[1]
    state = sh // 2
    dcol = di // nt
    wa = dcol - 128
    inner = nt * wa
    z = lax.axis_index("tensor")
    store = Moves(moves)
    load_x = store.start(x_hbm, x_ref)
    load_c = store.start(c_hbm, c_ref)

    sends = Sends(send, recv)
    zpeers = [{"tensor": lax.rem(z + dz, nt)} for dz in range(1, nt)]
    if gathers:
        here = place()
        _, d, core, x, y = here
        others = zpeers + [{"dp": xor_peer(core, x, y, k)} for k in range(1, 8)]
        hello(others)
        rows = wgi_ref.shape[0]
        hloc = heads // nt
        pack_ref[:, :dcol] = wgi_ref[:, 1, :]
        pl.semaphore_wait(pltpu.get_barrier_semaphore(), len(others))
        shards = (
            (pack_ref.at[:, pl.ds(0, wa)], w1_ref.at[:, pl.ds(0, inner)]),
            (pack_ref.at[:, pl.ds(wa, 128)], w1_ref.at[:, pl.ds(inner, 128 * nt)]),
            (pack_ref.at[:, pl.ds(dcol, dcol)], w2_ref),
            (wo_ref, w3_ref),
        )
        secs = [Gather(sends, nt, a, b, here) for a, b in shards]
        secs[1].begin(local.at[1])
        secs[0].begin(local.at[0])
        pack_ref[:, dcol:] = wgi_ref[:, 0, :]
        turn_ref[...] = jnp.zeros_like(turn_ref)
        turn_ref[0:hloc, 0:rows] = wdelta_ref[...].astype(F32)
        zd_ref[z] = turn_ref[...].T[0:rows].astype(BF16)
        wss_ref[:, :sh] = wsh_ref[...]
        par_ref[...] = jnp.zeros_like(par_ref)
        par_ref[0:4, :] = conv_inner_ref[...].astype(F32)
        par_ref[4:5, :] = shift_inner_ref[...].astype(F32).reshape(1, dcol)
        par_ref[5:6, :] = gated_gain_ref[...].reshape(1, dcol)
        for k, ref in enumerate((decay_ref, bias_ref, skip_gain_ref)):
            par_ref[8 + k : 9 + k, 0:hloc] = ref[...].reshape(1, hloc)
        deltas = [sends.start(zd_ref.at[z], zd_ref.at[z], to) for to in zpeers]
        mine = ws_ref.at[dp_rows(d, rows), :]
        own = [pltpu.make_async_copy(wss_ref, mine, local.at[4]), pltpu.make_async_copy(par_ref, pf_ref.at[z], local.at[5])]
        own[1].start()
        got = [sends.start(par_ref, pf_ref.at[z], to) for to in zpeers]
        edges = [
            sends.make(
                x_hbm.at[pl.ds((s + 1) * span - 16, 16), :], xh_ref.at[pl.ds(16 * s, 16), :],
                {"tensor": lax.rem(z + 1, nt)},
            )
            for s in range(seqs)
        ]

        @pl.when(z < nt - 1)
        def _():
            for copy in edges:
                copy.start()

    else:
        greet(({"tensor": lax.rem(z + nt - 1, nt)}, {"tensor": lax.rem(z + 1, nt)}))
        loads = [store.start(a, b) for a, b in ((w1_hbm, w1_ref), (w2_hbm, w2_ref), (w3_hbm, w3_ref), (ws_hbm, ws_ref))]
        pf_ref[...] = parf_ref[...]
        xh_ref[...] = xhf_ref[...]

    heads_table(sel_ref, di)
    ones_below(tri_ref, False)

    gain = norm_gain_ref[...].reshape(1, dim)
    ts_ref[...] = jnp.zeros_like(ts_ref)
    ts_ref[0:4, :] = conv_shared_ref[...].astype(F32)
    ts_ref[4:5, :] = shift_shared_ref[...].astype(F32).reshape(1, sh)

    def norm(v):
        v = v.astype(F32)
        return (v * lax.rsqrt(jnp.mean(v * v, axis=-1, keepdims=True) + EPSILON) * gain).astype(BF16)

    load_x.wait()

    def norm_step(b, c):
        rows = block_rows(b, SPAN)
        h_ref[rows, :] = norm(x_ref[rows, :])
        return c

    lax.fori_loop(0, blocks, norm_step, 0)
    store.start(h_ref, h_hbm)

    if gathers:
        secs[1].column()
        for copy in deltas:
            copy.wait_recv()
        delta = zd_ref[0].astype(F32)
        for t in range(1, nt):
            delta = delta + pltpu.roll(zd_ref[t].astype(F32), hloc * t, 1)
        wss_ref[:, sh:] = delta.astype(BF16)
        own[0].start()
        got += [sends.start(wss_ref, mine, {"dp": xor_peer(core, x, y, k)}) for k in range(1, 8)]
        secs[0].column()
        secs[1].forward()
        secs[2].begin(local.at[2])
        secs[0].forward_first()

        @pl.when(z > 0)
        def _():
            for copy in edges:
                copy.wait_recv()

        @pl.when(z == 0)
        def _():
            xh_ref[...] = jnp.zeros_like(xh_ref)

        for copy in own:
            copy.wait()
        for copy in got:
            copy.wait_recv()

    hh_ref[...] = norm(xh_ref[...])
    head = pf_ref[0, 8:16, 0:128]
    for t in range(nt):
        chan_ref[:, dcol * t : dcol * (t + 1)] = pf_ref[t, 0:8, :]
        if t > 0:
            head = head + pltpu.roll(pf_ref[t, 8:16, 0:128], heads // nt * t, 1)
    ak = -jnp.exp(head[0:1])
    ak = jnp.where(lanes_of(ak.shape) < heads, ak, 0.0)
    dpar_ref[0:1, :] = head[1:2]
    dpar_ref[1:2, :] = ak * LOG2E
    dpar_ref[2:3, :] = ak
    dpar_ref[3:8, :] = jnp.zeros((5, 128), F32)
    sk8 = packed(jnp.broadcast_to(head[2:3], (8, 128)), heads)
    for c0 in range(0, di, WIDE):
        skip_ref[:, c0 : c0 + WIDE] = spread_heads(sk8, sel_ref[:, c0 : c0 + WIDE])

    def conv(raw, par, out, s, cols):
        def step(r, c):
            r0 = pl.multiple_of(r * 128, 128)
            v = raw[s, pl.ds(r0 + 8, 136), cols]
            acc = par[4:5, cols] + par[3:4, cols] * v[8:]
            for k in range(3):
                acc = acc + par[k : k + 1, cols] * v[5 + k : 133 + k]
            out[pl.ds(pl.multiple_of(s * span + r0, 128), 128), cols] = (acc * sigmoid(acc)).astype(BF16)
            return c

        lax.fori_loop(0, span // 128, step, 0)

    if not gathers:
        loads[3].wait()
    for s in range(seqs):
        rows = slice(span * s, span * (s + 1))
        raws_ref[s, 0:16, :] = dot(hh_ref[16 * s : 16 * s + 16, :], ws_ref[:, :sh])
        both = dot(h_ref[rows, :], ws_ref[...])
        raws_ref[s, 16:ext, :] = both[:, :sh]
        draw_ref[rows, :] = both[:, sh:] + dpar_ref[0:1, :]
        for c0 in range(0, sh, 256):
            conv(raws_ref, ts_ref, bc_ref, s, slice(c0, c0 + 256))
    store.start(raws_ref, raws_hbm)
    store.start(bc_ref, bc_hbm)
    store.start(ws_ref, ws_out)

    def first_part(s):
        def step(t, carry):
            cols = pl.ds(pl.multiple_of(dcol * t, 128), wa)
            w = w1_ref[:, pl.ds(pl.multiple_of(wa * t, 128), wa)]
            rawi_ref[s, 0:16, cols] = dot(hh_ref[16 * s : 16 * s + 16, :], w)
            rawi_ref[s, 16:ext, cols] = dot(h_ref[span * s : span * (s + 1), :], w)
            conv(rawi_ref, chan_ref, xs_ref, s, cols)
            return carry

        lax.fori_loop(0, nt, step, 0)

    def second_part(s):
        rows = slice(span * s, span * (s + 1))

        def step(t, carry):
            cols = pl.ds(pl.multiple_of(dcol * t + wa, 128), 128)
            w = w1_ref[:, pl.ds(pl.multiple_of(inner + 128 * t, 128), 128)]
            rawi_ref[s, 0:16, cols] = dot(hh_ref[16 * s : 16 * s + 16, :], w)
            rawi_ref[s, 16:ext, cols] = dot(h_ref[rows, :], w)
            conv(rawi_ref, chan_ref, xs_ref, s, cols)
            return carry

        lax.fori_loop(0, nt, step, 0)

    def block_step(s, j, c):
        b = s * per + j
        rows = block_rows(b, SPAN)
        bt = bc_ref[rows, :state].astype(F32).T.astype(BF16)
        w = spread_heads(wk_ref[rows, :], sel_ref[...])
        fresh = dot(bt, (w * xs_ref[rows, :].astype(F32)).astype(BF16))

        @pl.when(j == 0)
        def _():
            fresh_ref[s] = fresh.astype(BF16)
            mine_ref[s] = fresh

        @pl.when(j > 0)
        def _():
            mine_ref[s] = dec_ref[b, 0:1, :] * mine_ref[s] + fresh

        return c

    def decay_step(b, c):
        rows = block_rows(b, SPAN)
        s = b // per
        j = b - s * per
        x = draw_ref[rows, :]
        dt = jnp.maximum(x, 0.0) + jnp.log1p(jnp.exp(-jnp.abs(x)))
        lg = jnp.where(x < -20.0, x * LOG2E, jnp.log2(jnp.maximum(dt, 1e-30)))
        acs = cumulate(tri_ref[...], dt * dpar_ref[1:2, :], heads)
        bs = acs - lg
        acs_ref[rows, :] = acs
        bs_ref[rows, :] = bs
        bst_ref[b] = bs.T
        end = acs[SPAN - 1 : SPAN, :]
        wk_ref[rows, :] = packed(jnp.exp2(end - bs), heads)
        ea_ref[rows, :] = packed(jnp.exp2(acs), heads)
        de = spread_heads(packed(jnp.broadcast_to(jnp.exp2(end), (8, 128)), heads), sel_ref[...])
        dec_ref[b] = de

        @pl.when(j == 0)
        def _():
            whole_ref[s] = de

        @pl.when(j > 0)
        def _():
            whole_ref[s] = de * whole_ref[s]

        return c

    chain = Chain(
        nt, 1, mine_ref, whole_ref, sin_ref, sb_ref, chain_send, chain_recv, PIECES[0],
        3 * blocks + 2 * seqs, (2, 7, 12, 13, 14, 15), (10, 12, 14, 16, 17, 18),
    )
    if gathers:
        secs[1].corner()
        secs[0].forward_second()
    lax.fori_loop(0, blocks, decay_step, 0)
    for a, b in ((draw_ref, draw_hbm), (acs_ref, acs_hbm), (bs_ref, bs_hbm)):
        store.start(a, b)
    if gathers:
        secs[1].finish()
        secs[0].corner()
        secs[2].column()
        secs[3].begin(local.at[3])
    else:
        loads[0].wait()
    for s in range(seqs):
        second_part(s)
    if gathers:
        secs[0].finish()
        secs[2].forward_first()
    store.start(w1_ref, w1_out)
    for s in range(seqs):
        first_part(s)
        store.start(rawi_ref.at[s], rawi_hbm.at[s])
        store.start(xs_ref.at[pl.ds(span * s, span), :], xs_hbm.at[pl.ds(span * s, span), :])
        lax.fori_loop(0, per, functools.partial(block_step, s), 0)
        chain.begin(s)
        if s == seqs - 1:
            store.start(fresh_ref, fresh_hbm)
        if gathers and s == 0:
            secs[2].forward_second()
            secs[3].column()
            secs[2].corner()
    if gathers:
        secs[3].forward()

    lower = lax.broadcasted_iota(jnp.int32, (HALF, HALF), 0) >= lax.broadcasted_iota(jnp.int32, (HALF, HALF), 1)
    first = lanes_of((HALF, 128)) < P_SIZE
    pairs = di // 128

    def intra_step(b, carry):
        rows = block_rows(b, SPAN)
        bb = bc_ref[rows, :state]
        cc = bc_ref[rows, state:]
        g00 = dot_nt(cc[:HALF], bb[:HALF])
        g10 = dot_nt(cc[HALF:], bb[:HALF])
        g11 = dot_nt(cc[HALF:], bb[HALF:])
        for p in range(pairs):
            cols = slice(128 * p, 128 * p + 128)
            xp = xs_ref[rows, cols]
            y0, y1 = [], []
            for h in (2 * p, 2 * p + 1):
                a0 = acs_ref[block_rows(2 * b, HALF), h : h + 1]
                a1 = acs_ref[block_rows(2 * b + 1, HALF), h : h + 1]
                r0 = bst_ref[b, h : h + 1, :HALF]
                r1 = bst_ref[b, h : h + 1, HALF:]
                m00 = jnp.where(lower, jnp.exp2(a0 - r0) * g00, 0.0).astype(BF16)
                m10 = (jnp.exp2(a1 - r0) * g10).astype(BF16)
                m11 = jnp.where(lower, jnp.exp2(a1 - r1) * g11, 0.0).astype(BF16)
                y0.append(m00)
                y1.append(jnp.concatenate([m10, m11], axis=1))
            y0 = dot(jnp.concatenate(y0, axis=0), xp[:HALF])
            y1 = dot(jnp.concatenate(y1, axis=0), xp)
            y_ref[block_rows(2 * b, HALF), cols] = jnp.where(first, y0[:HALF], y0[HALF:])
            y_ref[block_rows(2 * b + 1, HALF), cols] = jnp.where(first, y1[:HALF], y1[HALF:])
            if (p + 1) % (pairs // 3) == 0:
                chain.slot(3 * b + (p + 1) // (pairs // 3) - 1)
        return carry

    lax.fori_loop(0, blocks, intra_step, 0)
    load_c.wait()
    if gathers:
        secs[3].corner()
        secs[2].finish()
    else:
        loads[1].wait()
        loads[2].wait()
    store.start(w2_ref, w2_out)

    def gate_step(b, carry):
        rows = block_rows(b, span)

        def column_step(i, c):
            cols = columns(i, WIDE)
            dy_ref[rows, cols] = dot(h_ref[rows, :], w2_ref[:, cols]).astype(BF16)
            return c

        lax.fori_loop(0, di // WIDE, column_step, 0)
        chain.slot(3 * blocks + b)
        return carry

    def products_step(b, carry):
        rows = block_rows(b, span)

        def column_step(i, c):
            cols = columns(i, WIDE)
            dgate_ref[rows, cols] = (dot(c_ref[rows, :], w3_ref[:, cols]) * chan_ref[5:6, cols]).astype(BF16)
            return c

        lax.fori_loop(0, di // WIDE, column_step, 0)
        chain.slot(3 * blocks + seqs + b)
        return carry

    lax.fori_loop(0, seqs, gate_step, 0)
    if gathers:
        secs[3].finish()
    store.start(w3_ref, w3_out)
    lax.fori_loop(0, seqs, products_step, 0)
    chain.rest(0, chain.per)

    gg_ref[...] = jnp.zeros_like(gg_ref)
    skc_ref[...] = jnp.zeros_like(skc_ref)
    results = ((yn_ref, yn_hbm), (dgate_ref, dgate_hbm), (dy_ref, dy_hbm), (rr_ref, rr_hbm))

    def result_copy(k, b):
        rows = block_rows(b, SPAN)
        return pltpu.make_async_copy(results[k][0].at[rows, :], results[k][1].at[rows, :], result_sems.at[k, b])

    def sin_copy(s):
        return pltpu.make_async_copy(sin_ref.at[s], sin_hbm.at[s], result_sems.at[len(results), s])

    def mid_step(s, j, carry):
        b = s * per + j
        rows = block_rows(b, SPAN)
        cc = bc_ref[rows, state:]
        ss = jnp.zeros((SPAN, 128), F32)
        for c0 in range(0, di, WIDE):
            cols = slice(c0, c0 + WIDE)
            prev = sin_ref[s, :, cols].astype(F32)
            later = dec_ref[s * per, 0:1, cols] * prev + fresh_ref[s, :, cols].astype(F32)
            s_in = jnp.where(j == 0, prev, later).astype(BF16)
            ea = spread_heads(ea_ref[rows, :], sel_ref[:, cols])
            eaf_ref[:, cols] = ea
            ynos = y_ref[rows, cols] + ea * dot(cc, s_in)
            y_ref[rows, cols] = ynos
            y = ynos + skip_ref[0:1, cols] * xs_ref[rows, cols].astype(F32)
            gate = dy_ref[rows, cols].astype(F32)
            g = y * (gate * sigmoid(gate))
            g_ref[:, cols] = g
            ss = ss + lane_tiles(g * g)
        r2 = lax.rsqrt(jnp.sum(ss, axis=-1, keepdims=True) / di + EPSILON)
        qg = jnp.zeros((SPAN, 128), F32)
        for c0 in range(0, di, WIDE):
            cols = slice(c0, c0 + WIDE)
            g = g_ref[:, cols]
            gain = chan_ref[5:6, cols]
            yn_ref[rows, cols] = (g * r2 * gain).astype(BF16)
            qg_here = dgate_ref[rows, cols].astype(F32) * g
            gg_ref[:, cols] += row_tiles(qg_here * r2)
            qg = qg + lane_tiles(qg_here)
        coef = r2 * r2 * r2 * (jnp.sum(qg, axis=-1, keepdims=True) / di)
        rr = jnp.zeros((SPAN, 128), F32)
        ct = cc.astype(F32).T.astype(BF16)
        for c0 in range(0, di, WIDE):
            cols = slice(c0, c0 + WIDE)
            xf = xs_ref[rows, cols].astype(F32)
            ynos = y_ref[rows, cols]
            y = ynos + skip_ref[0:1, cols] * xf
            gate = dy_ref[rows, cols].astype(F32)
            sg = sigmoid(gate)
            dg = r2 * dgate_ref[rows, cols].astype(F32) - coef * g_ref[:, cols]
            dgate_ref[rows, cols] = (dg * y * (sg * (1.0 + gate * (1.0 - sg)))).astype(BF16)
            dyb = (dg * (gate * sg)).astype(BF16)
            dy_ref[rows, cols] = dyb
            dy = dyb.astype(F32)
            rr = rr + gather_heads(dy * ynos, sel_ref[:, cols])
            skc_ref[:, cols] += row_tiles(dy * xf)
            vv = dot(ct, (eaf_ref[:, cols] * dy).astype(BF16))

            @pl.when(j == 0)
            def _(cols=cols, vv=vv):
                mine_ref[s, :, cols] = vv

            @pl.when(j > 0)
            def _(cols=cols, vv=vv):
                vv_ref[s, :, cols] = vv.astype(BF16)
                mine_ref[s, :, cols] += dec_ref[s * per, 0:1, cols] * vv

        rr_ref[rows, :] = rr
        for k in range(len(results)):
            result_copy(k, b).start()
        chain.rest(chain.per, chain.pieces - 1, (s == 0) & (j == 0))
        chain.rest(chain.pieces - 1, chain.pieces, (s == 0) & (j == per - 1))
        return carry

    def mid_sequence(s, carry):
        chain.arrive(s)
        sin_copy(s).start()
        lax.fori_loop(0, per, functools.partial(mid_step, s), 0)
        return carry

    lax.fori_loop(0, seqs, mid_sequence, 0)
    gg_ref[...] = gg_ref[...] / chan_ref[5:6, :]
    sk_ref[...] = jnp.zeros_like(sk_ref)
    for c0 in range(0, di, WIDE):
        sk_ref[...] += gather_heads(skc_ref[:, c0 : c0 + WIDE], sel_ref[:, c0 : c0 + WIDE])
    mineb_ref[...] = mine_ref[...].astype(BF16)
    chain.finish()
    sends.finish()
    if gathers:

        @pl.when(z < nt - 1)
        def _():
            for copy in edges:
                copy.wait_send()

    for s in range(seqs):
        sin_copy(s).wait()
    store.start(mineb_ref, mineb_hbm)
    store.start(vv_ref, vv_hbm)
    for b in range(blocks):
        for k in range(len(results)):
            result_copy(k, b).wait()
    store.finish((load_x, load_c) if gathers else (load_x, load_c, *loads))


def backward_kernel(heads, nt, nd, reduces, *refs):
    refs = list(refs)
    take = lambda n: [refs.pop(0) for _ in range(n)]
    (x_hbm, c_hbm, h_hbm, rawi_hbm, raws_hbm, xs_hbm, bc_hbm, w1_hbm, w2_hbm, w3_hbm, ws_hbm, yn_hbm, dgate_hbm, dy_hbm,
     draw_hbm, acs_hbm, bs_hbm, rr_hbm, fresh_hbm, vv_hbm, sin_hbm, mineb_hbm) = take(22)
    norm_gain_ref, ts_ref, dec_ref, whole_ref, chan_ref, dpar_ref, skip_ref, gg_ref, sk_ref = take(9)
    out_hbm, ig_hbm = take(2)
    if reduces:
        o1_ref, osd_ref, o2_ref, o3_ref, om_ref = take(5)
    else:
        g1_out, g2_out, g3_out, sm_ref = take(4)
    (c_ref, h_ref, rawi_ref, raws_ref, xs_ref, bc_ref, w1_ref, ws_ref, dgate_ref, dy_ref, draw_ref,
     acs_ref, bs_ref, rr_ref, fresh_ref, vv_ref, sin_ref, ds_ref, sb_ref, din_ref, dx_ref, dbc_ref, g_ref, halo_ref,
     edge_ref, keep_ref, acst_ref, dg_ref, sel_ref, triu_ref, tg_ref, small_ref, ng_ref, w2_ref) = take(34)
    if reduces:
        (sm_ref,) = take(1)
        bufs = [take(6) for _ in range(4)]
        small_bufs = take(3)
    chain_send, chain_recv, halo_send, halo_recv, moves = take(5)
    if reduces:
        sems = [take(2) for _ in range(5)]

    tokens, dim = h_ref.shape
    seqs, ext, di = rawi_ref.shape
    span = ext - 16
    per = span // SPAN
    blocks = seqs * per
    sh = bc_ref.shape[1]
    state = sh // 2
    dcol = di // nt
    wa = dcol - 128
    na = nt * wa
    z = lax.axis_index("tensor")
    move = Moves(moves)
    load = lambda a, b: move.start(a, b)
    yn_ref = din_ref.at[:, pl.ds(0, di)]
    l_mine, l_c, l_yn0 = load(mineb_hbm, sb_ref), load(c_hbm, c_ref), load(yn_hbm, yn_ref)
    x_ref = xs_ref.at[:, pl.ds(0, dim)]
    w3_ref = din_ref.at[pl.ds(0, dim), pl.ds(0, di)]

    if reduces:
        here = place()
        _, d, core, x, y = here
        others = [{"tensor": lax.rem(z + dz, nt)} for dz in range(1, nt)]
        others += [{"dp": xor_peer(core, x, y, k)} for k in (1, 2, 4)]
        hello(others)
        cut = ((0, dcol, True),)
        parts = (
            (g_ref.at[:, pl.ds(di, di)], cut), (g_ref.at[:, pl.ds(0, di)], cut),
            (g_ref.at[:, pl.ds(di, na)], ((0, wa, True),)),
            (g_ref.at[:, pl.ds(di + na, 128 * nt + sh + 128)], ((0, 128, True), (128 * nt, sh + 128, False))),
        )
        r3, r2, ra, rb = (Reduce(Sends(*sems[i]), nt, g, bufs[i], cuts, here) for i, (g, cuts) in enumerate(parts))
        small_sum = SmallSum(Sends(*sems[4]), nt, sm_ref, small_bufs, here)
    else:
        others = [{"tensor": lax.rem(z + nt - 1, nt)}, {"tensor": lax.rem(z + 1, nt)}]
        hello(others)
    heads_table(sel_ref, di)
    ones_below(triu_ref, True)
    small_ref[...] = jnp.zeros_like(small_ref)
    ng_ref[...] = jnp.zeros_like(ng_ref)
    tg_ref[...] = jnp.zeros_like(tg_ref)
    pl.semaphore_wait(pltpu.get_barrier_semaphore(), len(others))

    chain = Chain(
        nt, -1, sb_ref, whole_ref, ds_ref, sb_ref, chain_send, chain_recv, PIECES[1], 2 * (di // WIDE) + 3 * blocks,
        (1, 2, 3, 4, 5, 6, 7, 8, 9, 10, 11, 12), (4, 5, 6, 7, 8, 9, 10, 11, 12, 13, 14, 15),
    )
    l_mine.wait()
    for s in range(seqs):
        chain.begin(s)

    def weight_gradient(dv, w, at):
        g = dot_tn(h_ref[...], dv)
        g_ref[:, pl.ds(pl.multiple_of(at, 128), g.shape[1])] = g.astype(BF16)
        ng_ref[...] += lane_tiles(g * w.astype(F32))

    l_c.wait()
    l_yn0.wait()
    l_h, l_dgate, l_w2 = load(h_hbm, h_ref), load(dgate_hbm, dgate_ref), load(w2_hbm, w2_ref)
    parts = di // WIDE

    def output_gradient(i, carry):
        g_ref[:, columns(parts + i, WIDE)] = dot_tn(c_ref[...], din_ref[:, columns(i, WIDE)]).astype(BF16)
        chain.slot(i)
        return carry

    lax.fori_loop(0, parts, output_gradient, 0)
    if reduces:
        r3.begin()
    else:
        s3 = move.start(g_ref.at[:, pl.ds(di, di)], g3_out)
    l_h.wait()
    l_dgate.wait()
    l_w2.wait()
    l_scan = [
        load(a, b)
        for a, b in (
            (xs_hbm, xs_ref), (dy_hbm, dy_ref), (bc_hbm, bc_ref), (acs_hbm, acs_ref), (bs_hbm, bs_ref),
        )
    ]

    def gate_gradient(i, carry):
        cols = columns(i, WIDE)
        weight_gradient(dgate_ref[:, cols], w2_ref[:, cols], i * WIDE)
        chain.slot(parts + i)
        return carry

    lax.fori_loop(0, parts, gate_gradient, 0)
    slot0 = 2 * parts
    if reduces:
        r2.begin()
    else:
        s2 = move.start(g_ref.at[:, pl.ds(0, di)], g2_out)

    for copy in l_scan:
        copy.wait()
    l_state = [
        load(a, b)
        for a, b in (
            (draw_hbm, draw_ref), (rr_hbm, rr_ref), (fresh_hbm, fresh_ref), (vv_hbm, vv_ref), (sin_hbm, sin_ref),
            (rawi_hbm, rawi_ref), (raws_hbm, raws_ref),
        )
    ]
    l_last = [load(w1_hbm, w1_ref), load(ws_hbm, ws_ref)]
    upper = lax.broadcasted_iota(jnp.int32, (HALF, HALF), 0) <= lax.broadcasted_iota(jnp.int32, (HALF, HALF), 1)
    first = lanes_of((HALF, 128)) < P_SIZE
    first_all = lanes_of((SPAN, 128)) < P_SIZE
    pairs = di // 128

    def intra_step(b, carry):
        rows = block_rows(b, SPAN)
        acst_ref[...] = acs_ref[rows, :].T
        bb = bc_ref[rows, :state]
        cc = bc_ref[rows, state:]
        g00 = dot_nt(bb[:HALF], cc[:HALF])
        g01 = dot_nt(bb[:HALF], cc[HALF:])
        g11 = dot_nt(bb[HALF:], cc[HALF:])
        dg_ref[...] = jnp.zeros_like(dg_ref)
        for p in range(pairs):
            cols = slice(128 * p, 128 * p + 128)
            xp = xs_ref[rows, cols]
            dyp = dy_ref[rows, cols]
            zero = jnp.zeros_like(xp)
            xa, xb = jnp.where(first_all, xp, zero), jnp.where(first_all, zero, xp)
            dm0 = dot_nt(jnp.concatenate([xa[:HALF], xb[:HALF]], axis=0), dyp)
            dm1 = dot_nt(jnp.concatenate([xa[HALF:], xb[HALF:]], axis=0), dyp[HALF:])
            d0, d1, de = [], [], []
            for h in (2 * p, 2 * p + 1):
                b0 = bs_ref[block_rows(2 * b, HALF), h : h + 1]
                b1 = bs_ref[block_rows(2 * b + 1, HALF), h : h + 1]
                r0 = acst_ref[h : h + 1, :HALF]
                r1 = acst_ref[h : h + 1, HALF:]
                e00 = jnp.where(upper, jnp.exp2(r0 - b0), 0.0)
                e01 = jnp.exp2(r1 - b0)
                e11 = jnp.where(upper, jnp.exp2(r1 - b1), 0.0)
                m0 = jnp.concatenate([(e00 * g00).astype(BF16), (e01 * g01).astype(BF16)], axis=1)
                m1 = (e11 * g11).astype(BF16)
                d0.append(m0)
                d1.append(m1)
                de.append((e00, e01, e11))
            d0 = dot(jnp.concatenate(d0, axis=0), dyp)
            d1 = dot(jnp.concatenate(d1, axis=0), dyp[HALF:])
            dg_ref[0] += dm0[:HALF, :HALF] * de[0][0] + dm0[HALF:, :HALF] * de[1][0]
            dg_ref[1] += dm0[:HALF, HALF:] * de[0][1] + dm0[HALF:, HALF:] * de[1][1]
            dg_ref[2] += dm1[:HALF] * de[0][2] + dm1[HALF:] * de[1][2]
            dx_ref[block_rows(2 * b, HALF), cols] = jnp.where(first, d0[:HALF], d0[HALF:])
            dx_ref[block_rows(2 * b + 1, HALF), cols] = jnp.where(first, d1[:HALF], d1[HALF:])
            if reduces and p == pairs // 2:
                pl.when(b == blocks // 4)(r3.first)
            if (p + 1) % (pairs // 3) == 0:
                chain.slot(slot0 + 3 * b + (p + 1) // (pairs // 3) - 1)
        dg00 = dg_ref[0]
        dg01 = dg_ref[1]
        dg11 = dg_ref[2]
        dbc_ref[block_rows(2 * b, HALF), :state] = dot(jnp.concatenate([dg00, dg01], axis=1).astype(BF16), cc)
        dbc_ref[block_rows(2 * b + 1, HALF), :state] = dot(dg11.astype(BF16), cc[HALF:])
        dbc_ref[block_rows(2 * b, HALF), state:] = dot(dg00.T.astype(BF16), bb[:HALF])
        dbc_ref[block_rows(2 * b + 1, HALF), state:] = dot(
            jnp.concatenate([dg01.T, dg11.T], axis=1).astype(BF16), bb
        )
        return carry

    lax.fori_loop(0, blocks, intra_step, 0)
    if reduces:
        r3.second()
        r2.first()
    chain.rest(0, chain.per + 1)
    for copy in l_state:
        copy.wait()

    def state_step(s, j):
        b = s * per + j
        rows = block_rows(b, SPAN)
        acs = acs_ref[rows, :]
        end = acs[SPAN - 1 : SPAN, :]
        eak = packed(jnp.exp2(acs), heads)
        wk = packed(jnp.exp2(end - bs_ref[rows, :]), heads)
        bb = bc_ref[rows, :state]
        db = dbc_ref[rows, :state]
        dc = dbc_ref[rows, state:]
        pp = jnp.zeros((SPAN, 128), F32)
        endsum = jnp.zeros((8, 128), F32)
        for c0 in range(0, di, WIDE):
            cols = slice(c0, c0 + WIDE)
            s_in = sin_ref[s, :, cols]
            ds = ds_ref[s, :, cols]
            if j > 0:
                s_in = dec_ref[s * per, 0:1, cols] * s_in.astype(F32) + fresh_ref[s, :, cols].astype(F32)
                s_in = s_in.astype(BF16)
            if j < per - 1:
                ds = dec_ref[s * per + per - 1, 0:1, cols] * ds.astype(F32) + vv_ref[s, :, cols].astype(F32)
                ds = ds.astype(BF16)
            w = spread_heads(wk, sel_ref[:, cols])
            ea = spread_heads(eak, sel_ref[:, cols])
            xf = xs_ref[rows, cols].astype(F32)
            dyf = dy_ref[rows, cols].astype(F32)
            dxs = w * dot(bb, ds)
            dxn = dx_ref[rows, cols] + dxs
            pp = pp + gather_heads(dxn * xf, sel_ref[:, cols])
            at_end = jnp.sum(ds.astype(F32) * s_in.astype(F32), axis=0, keepdims=True) * dec_ref[b, 0:1, cols]
            first_row = lax.broadcasted_iota(jnp.int32, (8, WIDE), 0) == 0
            at_end = row_tiles(dxs * xf) + jnp.where(first_row, jnp.broadcast_to(at_end, (8, WIDE)), 0.0)
            endsum = endsum + gather_heads(at_end, sel_ref[:, cols])
            dc = dc + dot_nt((ea * dyf).astype(BF16), s_in)
            db = db + dot_nt((w * xf).astype(BF16), ds)
            dx_ref[rows, cols] = dxn + skip_ref[0:1, cols] * dyf
        dbc_ref[rows, :state] = db
        dbc_ref[rows, state:] = dc
        da = cumulate(triu_ref[...], rr_ref[rows, :] - pp, heads)
        da = da + jnp.sum(endsum, axis=0, keepdims=True)
        xx = draw_ref[rows, :]
        sg = 1.0 / (1.0 + jnp.exp(-xx))
        dt = jnp.maximum(xx, 0.0) + jnp.log1p(jnp.exp(-jnp.abs(xx)))
        ratio = jnp.where(xx < -20.0, 1.0, sg / jnp.maximum(dt, 1e-30))
        ak = dpar_ref[2:3, :]
        dd = da * ak * sg + pp * ratio
        din_ref[rows, di + sh :] = dd.astype(BF16)
        small_ref[0:1, :] += jnp.sum(da * dt * ak, axis=0, keepdims=True)
        small_ref[1:2, :] += jnp.sum(dd, axis=0, keepdims=True)

        def conv_back(raw, par, dact, off, cols):
            here_cols = pl.ds(pl.multiple_of(off + cols.start, 128), cols.size)

            def step(r, prev):
                r0 = pl.multiple_of(r * HALF, HALF)
                at = pl.ds(pl.multiple_of(16 + j * SPAN + r0, 16), HALF)
                now = raw[s, at, cols]
                v = jnp.concatenate([prev, now], axis=0)
                sh_v = [v[5 + k : 5 + k + HALF] for k in range(3)] + [now]
                pre = par[4:5, cols] + par[0:1, cols] * sh_v[0]
                for k in range(1, 4):
                    pre = pre + par[k : k + 1, cols] * sh_v[k]
                sg = sigmoid(pre)
                dp = dact[pl.ds(pl.multiple_of(b * SPAN + r0, HALF), HALF), cols] * (sg * (1.0 + pre * (1.0 - sg)))
                raw[s, at, cols] = dp
                for k in range(4):
                    tg_ref[k, :, here_cols] += row_tiles(dp * sh_v[k])
                tg_ref[4, :, here_cols] += row_tiles(dp)
                return now[HALF - 8 :]

            prev = raw[s, 8:16, cols] if j == 0 else keep_ref[s, :, here_cols]
            prev = lax.fori_loop(0, SPAN // HALF, step, prev)
            if j < per - 1:
                keep_ref[s, :, here_cols] = prev

        def inner_step(i, carry):
            conv_back(rawi_ref, chan_ref, dx_ref, 0, pl.ds(pl.multiple_of(256 * i, 256), 256))
            return carry

        lax.fori_loop(0, di // 256, inner_step, 0)
        for c0 in range(0, sh, 256):
            conv_back(raws_ref, ts_ref, dbc_ref, di, pl.ds(c0, 256))

    halo_copy = pltpu.make_async_remote_copy(
        src_ref=edge_ref, dst_ref=halo_ref, send_sem=halo_send.at[0], recv_sem=halo_recv.at[0],
        device_id={"tensor": lax.rem(z + nt - 1, nt)}, device_id_type=MESH,
    )
    for j in range(per):

        def seq_step(s, carry, j=j):
            if j == 0:
                chain.rest(chain.per + 1, chain.pieces, s == 1)
                chain.arrive(s)
            state_step(s, j)
            return carry

        lax.fori_loop(0, seqs, seq_step, 0)
        if j == 0:
            edge_ref[:, :, :di] = rawi_ref[:, 16:24, :]
            edge_ref[:, :, di:] = raws_ref[:, 16:24, :]

            @pl.when(z > 0)
            def _():
                halo_copy.start()

            if reduces:
                r3.third()
    l_last += [load(x_hbm, x_ref)]
    l_yn = load(yn_hbm, dy_ref)
    if reduces:
        r3.last(o3_ref)
        r2.second()

    @pl.when(z < nt - 1)
    def _():
        halo_copy.wait_recv()

    @pl.when(z == nt - 1)
    def _():
        halo_ref[...] = jnp.zeros_like(halo_ref)

    def conv_t(dpre, par, off, c0, to):
        cols = pl.ds(pl.multiple_of(c0, 128), 128)
        halo_cols = pl.ds(pl.multiple_of(off + c0, 128), 128)
        to_cols = pl.ds(pl.multiple_of(to, 128), 128)

        def step(s, carry):
            def rows_step(r, nxt):
                r0 = pl.multiple_of(span - HALF * (r + 1), HALF)
                now = dpre[s, pl.ds(pl.multiple_of(16 + r0, 16), HALF), cols]
                v = jnp.concatenate([now, nxt], axis=0)
                acc = par[3:4, cols] * now
                for k in range(3):
                    acc = acc + par[k : k + 1, cols] * v[3 - k : 3 - k + HALF]
                din_ref[pl.ds(pl.multiple_of(s * span + r0, HALF), HALF), to_cols] = acc.astype(BF16)
                return now[0:8]

            lax.fori_loop(0, span // HALF, rows_step, halo_ref[s, :, halo_cols])
            return carry

        lax.fori_loop(0, seqs, step, 0)

    def inner_first(i, carry):
        t = i // (wa // 128)
        r = 128 * (i - t * (wa // 128))
        conv_t(rawi_ref, chan_ref, 0, dcol * t + r, wa * t + r)
        return carry

    def inner_second(t, carry):
        conv_t(rawi_ref, chan_ref, 0, dcol * t + wa, na + 128 * t)
        return carry

    def shared_part(i, carry):
        conv_t(raws_ref, ts_ref, di, 128 * i, di + 128 * i)
        return carry

    lax.fori_loop(0, na // 128, inner_first, 0)
    if reduces:
        r3.finish()
        r2.third()
    else:
        s3.wait()
    for copy in l_last:
        copy.wait()

    def inner_gradient(i, carry):
        cols = columns(i, WIDE)
        weight_gradient(din_ref[:, cols], w1_ref[:, cols], di + i * WIDE)
        return carry

    lax.fori_loop(0, na // WIDE, inner_gradient, 0)
    if reduces:
        ra.begin()
    lax.fori_loop(0, nt, inner_second, 0)
    lax.fori_loop(0, sh // 128, shared_part, 0)
    lax.fori_loop(na // WIDE, di // WIDE, inner_gradient, 0)
    weight_gradient(din_ref[:, di:], ws_ref[...], 2 * di)
    column = lambda v: jnp.sum(v, axis=0, keepdims=True)
    for k in range(5):
        sm_ref[k : k + 1, :] = column(tg_ref[k, :, :di])
    sm_ref[5:6, :] = column(gg_ref[...])
    gain = norm_gain_ref[...].reshape(1, dim)
    sm_ref[6:7, :dim] = column(ng_ref[...].T) / gain
    flat = [column(tg_ref[k, :, di:]) for k in range(5)] + [small_ref[0:1, :], small_ref[1:2, :], column(sk_ref[...])]
    row, at = 6, dim
    for v in flat:
        width = v.shape[1]
        if at + width > di:
            row, at = row + 1, 0
        sm_ref[row : row + 1, at : at + width] = v
        at += width
    sm_ref[row : row + 1, at:] = jnp.zeros((1, di - at), F32)
    if reduces:
        rb.begin()
        small_sum.begin()
    else:
        move.start(g_ref.at[:, pl.ds(di, g_ref.shape[1] - di)], g1_out)
    def last_step(b, carry):
        if reduces:
            pl.when(b == 0)(ra.first)

            @pl.when(b == blocks // 4)
            def _():
                small_sum.step(1)
                rb.first()

            @pl.when(b == 2 * blocks // 4)
            def _():
                small_sum.step(2)

            @pl.when(b == 3 * blocks // 4)
            def _():
                ra.second()
                small_sum.step(3)

        rows = block_rows(b, SPAN)
        dh = dot_nt(dgate_ref[rows, :], w2_ref[...])
        dh = dh + dot_nt(din_ref[rows, :di], w1_ref[...])
        dh = dh + dot_nt(din_ref[rows, di:], ws_ref[...])
        u = x_ref[rows, :].astype(F32)
        r1 = lax.rsqrt(jnp.mean(u * u, axis=-1, keepdims=True) + EPSILON)
        e = dh * gain
        m = jnp.mean(e * u, axis=-1, keepdims=True)
        c_ref[rows, :] = (c_ref[rows, :].astype(F32) + r1 * e - u * (r1 * r1 * r1 * m)).astype(BF16)
        return carry

    lax.fori_loop(0, blocks, last_step, 0)
    move.start(c_ref, ig_hbm)
    l_w3 = load(w3_hbm, w3_ref)

    def output_step(b, carry):
        rows = block_rows(b, SPAN)
        x_ref[rows, :] = (x_ref[rows, :].astype(F32) + dot_nt(dy_ref[rows, :], w3_ref[...])).astype(BF16)
        return carry

    if reduces:
        rb.second()
        ra.third()
    l_w3.wait()
    l_yn.wait()
    lax.fori_loop(0, blocks // 2, output_step, 0)
    if reduces:
        rb.third()
    lax.fori_loop(blocks // 2, blocks, output_step, 0)
    move.start(x_ref, out_hbm)
    if reduces:
        r2.last(o2_ref)
        om_ref[...] = small_sum.last()
        ra.last(o1_ref.at[:, pl.ds(0, wa)])
        rb.last(o1_ref.at[:, pl.ds(wa, 128)], osd_ref)
        for part in (r2, ra, rb, small_sum):
            part.finish()
    chain.finish()

    @pl.when(z > 0)
    def _():
        halo_copy.wait_send()

    move.finish((l_mine, l_c, l_yn0, l_yn, l_w3, l_h, l_dgate, l_w2, *l_scan, *l_state, *l_last) + (() if reduces else (s3,)))


def finish_kernel(nt, hloc, out_hbm, ig_hbm, o1_ref, osd_ref, o2_ref, o3_ref, om_ref, *refs):
    (out_to, ig_to, ng_ref, gi_ref, gs_ref, delta_ref, ci_ref, si_ref, cs_ref, ss_ref, decay_ref, bias_ref, bypass_ref,
     gg_ref, ow_ref, out_ref, ig_ref, sems) = refs
    ways = ((out_hbm, out_ref, out_to), (ig_hbm, ig_ref, ig_to))
    into = [pltpu.make_async_copy(a, b, sems.at[k]) for k, (a, b, _) in enumerate(ways)]
    onto = [pltpu.make_async_copy(b, c, sems.at[2 + k]) for k, (_, b, c) in enumerate(ways)]
    for copy in into:
        copy.start()
    z = lax.axis_index("tensor")
    dcol = o1_ref.shape[1]
    sh = gs_ref.shape[1]
    dim = ng_ref.shape[0]
    cols = pl.ds(pl.multiple_of(z * dcol, 128), dcol)
    back = lax.rem(128 - z * hloc, 128)
    ng_ref[...] = om_ref[6, :dim]
    gi_ref[:, 0, :] = o2_ref[...]
    gi_ref[:, 1, :] = o1_ref[...]
    gs_ref[...] = osd_ref[:, :sh]
    delta_ref[...] = pltpu.roll(osd_ref[:, sh:], back, 1).T[:hloc]
    ci_ref[...] = om_ref[0:4, cols]
    si_ref[...] = om_ref[4, cols]
    gg_ref[...] = om_ref[5, cols]
    row, at = 6, dim
    taps = []
    for _ in range(5):
        if at + sh > om_ref.shape[1]:
            row, at = row + 1, 0
        taps.append(om_ref[row : row + 1, at : at + sh])
        at += sh
    for k in range(4):
        cs_ref[k : k + 1, :] = taps[k]
    ss_ref[...] = taps[4][0]
    for ref in (decay_ref, bias_ref, bypass_ref):
        if at + 128 > om_ref.shape[1]:
            row, at = row + 1, 0
        v = jnp.broadcast_to(om_ref[row : row + 1, at : at + 128], (8, 128))
        ref[...] = pltpu.roll(v, back, 1)[0, :hloc]
        at += 128
    for copy, after in zip(into, onto):
        copy.wait()
        after.start()
    ow_ref[...] = o3_ref[...]
    for copy in onto:
        copy.wait()


def semaphores(n):
    return [pltpu.SemaphoreType.DMA((n,)), pltpu.SemaphoreType.DMA((n,))]


def shifted(v, axis, by):
    n = lax.axis_size(axis)
    return lax.ppermute(v, axis, [(i, i + by) for i in range(n) if 0 <= i + by < n])


def gather_all(nt, nd, wgi, wdelta, wo, ws, par, edge):
    both = ("tensor", "dp")
    rows = ws.shape[0]
    dcol = wo.shape[0]
    pack = jnp.concatenate([wgi[:, 1], wgi[:, 0], wo.T], axis=1)
    full = lax.all_gather(pack, both, axis=0).reshape(nt, nd * rows, -1)
    whole = lambda a, b: full[:, :, a:b].transpose(1, 0, 2).reshape(nd * rows, nt * (b - a))
    w1 = jnp.concatenate([whole(0, dcol - 128), whole(dcol - 128, dcol)], axis=1)
    delta = lax.all_gather(wdelta, "tensor", axis=1, tiled=True)
    delta = jnp.pad(delta, ((0, 0), (0, 128 - delta.shape[1])))
    return (
        w1, whole(dcol, 2 * dcol), whole(2 * dcol, 3 * dcol),
        lax.all_gather(jnp.concatenate([ws, delta], axis=1), "dp", axis=0, tiled=True),
        lax.all_gather(par, "tensor", axis=0), shifted(edge, "tensor", 1),
    )


def reduce_all(nt, nd, g1, g2, g3, sm, sh):
    dim = g1.shape[0]
    rows = dim // nd
    dcol = g2.shape[1] // nt
    wa = dcol - 128
    both = ("tensor", "dp")
    parts = [
        g[:, at : at + nt * w].reshape(dim, nt, w).transpose(1, 0, 2)
        for g, at, w in ((g1, 0, wa), (g1, wa * nt, 128), (g2, 0, dcol), (g3, 0, dcol))
    ]
    big = jnp.concatenate(parts, axis=2).reshape(nt * nd, rows, -1)
    big = lax.psum_scatter(big, both, scatter_dimension=0).astype(F32)
    shared = g1[:, nt * dcol :].reshape(nd, rows, sh + 128).astype(F32)
    shared = lax.psum(lax.psum_scatter(shared, "dp", scatter_dimension=0), "tensor")
    return big[:, :dcol], shared, big[:, dcol : 2 * dcol], big[:, 2 * dcol :], lax.psum(sm, both)


def local(
    block_input, norm_gain, input_gate_inner_weight, input_shared_weight, input_delta_weight, conv_inner, shift_inner,
    conv_shared, shift_shared, decay_log, delta_bias, skip_gain, gated_gain, output_projection_weight, cotangent,
):
    nt = lax.axis_size("tensor")
    nd = lax.axis_size("dp")
    me = lax.axis_index("tensor")
    seqs, span, dim = block_input.shape
    tokens = seqs * span
    blocks = tokens // SPAN
    rows, _, dcol = input_gate_inner_weight.shape
    di = dcol * nt
    sh = input_shared_weight.shape[1]
    state = sh // 2
    hloc = input_delta_weight.shape[1]
    heads = hloc * nt

    x = block_input.reshape(tokens, dim)
    c = cotangent.reshape(tokens, dim)
    gathers = nd == 8
    args = [x, c, norm_gain, conv_shared, shift_shared]
    kinds = [pl.ANY, pl.ANY] + [pltpu.VMEM] * 3
    if gathers:
        args += [
            input_gate_inner_weight, input_delta_weight.T, output_projection_weight.T, input_shared_weight, conv_inner,
            shift_inner, gated_gain, decay_log, delta_bias, skip_gain,
        ]
        kinds += [pltpu.VMEM] * 10
    else:
        head = jnp.pad(jnp.stack([decay_log, delta_bias, skip_gain]), ((0, 5), (0, dcol - hloc)))
        par = [conv_inner.astype(F32), shift_inner.astype(F32)[None], gated_gain[None], jnp.zeros((2, dcol), F32), head]
        args += gather_all(
            nt, nd, input_gate_inner_weight, input_delta_weight, output_projection_weight, input_shared_weight,
            jnp.concatenate(par, axis=0), block_input[:, span - 16 :].reshape(seqs * 16, dim),
        )
        kinds += [pl.ANY] * 4 + [pltpu.VMEM] * 2
    scan_state = ((seqs, state, di), BF16)
    f128 = ((tokens, 128), F32)
    far = [
        ((tokens, dim), BF16), ((seqs, span + 16, di), F32), ((seqs, span + 16, sh), F32), ((tokens, di), BF16),
        ((tokens, sh), BF16), ((dim, di), BF16), ((dim, di), BF16), ((dim, di), BF16), ((dim, sh + 128), BF16),
        ((tokens, di), BF16), ((tokens, di), BF16), ((tokens, di), BF16), f128, f128, f128, f128, scan_state,
        scan_state, scan_state, scan_state,
    ]
    near = [
        ((blocks, 8, di), F32), ((seqs, 8, di), F32), ((8, di), F32), ((8, 128), F32), ((8, di), F32), ((8, di), F32),
        ((8, 128), F32), ((8, sh), F32)]
    scratch = [
        ((tokens, dim), BF16), ((tokens, dim), BF16), ((tokens, dim), BF16), ((dim, di), BF16), ((dim, di), BF16),
        ((dim, di), BF16), ((dim, sh + 128), BF16), ((nt, 16, dcol), F32), ((seqs * 16, dim), BF16),
        ((seqs, span + 16, di), F32), ((seqs, span + 16, sh), F32), ((tokens, di), BF16), ((tokens, sh), BF16),
        ((tokens, di), F32), ((8, di), F32), ((tokens, di), BF16), ((tokens, di), BF16), ((tokens, di), BF16),
        ((SPAN, di), F32), ((seqs, state, di), F32), scan_state,
        ((seqs * 16, dim), BF16), ((tokens, 128), BF16), ((blocks, 128, SPAN), F32), ((128, di), BF16),
        ((SPAN, SPAN), BF16), ((rows, 2 * dcol), BF16), ((16, dcol), F32), ((nt, rows, 128), BF16), ((rows, sh + 128), BF16),
        ((128, 128), F32), f128, f128, f128, f128, scan_state, ((SPAN, di), F32), scan_state, scan_state, scan_state,
        ((tokens, 128), BF16),
    ]
    pieces = seqs * di // min(PIECES)
    h, rawi, raws, xs, bc, w1, w2, w3, ws, yn, dgate, dy, draw, acs, bs, rr, fresh, vv, mineb, sin, *rest = pl.pallas_call(
        functools.partial(forward_kernel, heads, nt, nd, gathers),
        out_shape=[jax.ShapeDtypeStruct(s, d) for s, d in far + near],
        in_specs=[pl.BlockSpec(memory_space=k) for k in kinds],
        out_specs=[pl.BlockSpec(memory_space=pl.ANY)] * len(far) + [pl.BlockSpec(memory_space=pltpu.VMEM)] * len(near),
        scratch_shapes=[pltpu.VMEM(s, d) for s, d in scratch]
        + semaphores(4 * Gather.MESSAGES + 5 + 2 * nt + seqs) + semaphores(pieces)
        + [pltpu.SemaphoreType.DMA((6,)), pltpu.SemaphoreType.DMA((24,)), pltpu.SemaphoreType.DMA((5, blocks))],
        compiler_params=pltpu.CompilerParams(vmem_limit_bytes=VMEM_LIMIT, collective_id=0, has_side_effects=True),
        name="forward",
    )(*args)
    dec, whole, chan, dpar, skip, ggg, skg, ts = rest

    args = [x, c, h, rawi, raws, xs, bc, w1, w2, w3, ws, yn, dgate, dy, draw, acs, bs, rr, fresh, vv, sin, mineb]
    kinds = [pl.ANY] * len(args)
    more = [norm_gain, ts, dec, whole, chan, dpar, skip, ggg, skg]
    args += more
    kinds += [pltpu.VMEM] * len(more)
    wa = dcol - 128
    scratch = [
        ((tokens, dim), BF16), ((tokens, dim), BF16), ((seqs, span + 16, di), F32),
        ((seqs, span + 16, sh), F32), ((tokens, di), BF16), ((tokens, sh), BF16), ((dim, di), BF16),
        ((dim, sh + 128), BF16), ((tokens, di), BF16), ((tokens, di), BF16), f128, f128, f128, f128, scan_state, scan_state,
        scan_state, scan_state, scan_state, ((tokens, di + sh + 128), BF16), ((tokens, di), F32), ((tokens, sh), F32),
        ((dim, 2 * di + sh + 128), BF16), ((seqs, 8, di + sh), F32), ((seqs, 8, di + sh), F32), ((seqs, 8, di + sh), F32),
        ((128, SPAN), F32), ((3, HALF, HALF), F32), ((128, di), BF16), ((SPAN, SPAN), BF16),
        ((5, 8, di + sh), F32), ((8, 128), F32), ((dim, 128), F32), ((dim, di), BF16),
    ]
    scratch = [pltpu.VMEM(s, d) for s, d in scratch]
    sems = semaphores(pieces) + semaphores(1) + [pltpu.SemaphoreType.DMA((32,))]
    if gathers:
        near = [
            ((rows, dcol), F32), ((rows, sh + 128), F32), ((rows, dcol), F32), ((rows, dcol), F32), ((8, di), F32)
        ]
        far = []
        scratch += [pltpu.VMEM((8, di), F32)]
        for width, wz in ((di, dcol), (di, dcol), (wa * nt, wa), (128 * nt + sh + 128, sh + 256)):
            scratch += Reduce.scratch(rows, width, nt, wz)
        scratch += SmallSum.scratch((8, di), nt)
        for _ in range(4):
            sems += semaphores(Reduce.MESSAGES)
        sems += semaphores(SmallSum.MESSAGES)
    else:
        far = [((dim, di + sh + 128), BF16), ((dim, di), BF16), ((dim, di), BF16)]
        near = [((8, di), F32)]
    outs = [((tokens, dim), BF16)] * 2 + far + near
    out, ig, *rest = pl.pallas_call(
        functools.partial(backward_kernel, heads, nt, nd, gathers),
        out_shape=[jax.ShapeDtypeStruct(s, d) for s, d in outs],
        in_specs=[pl.BlockSpec(memory_space=k) for k in kinds],
        out_specs=[pl.BlockSpec(memory_space=pl.ANY)] * (2 + len(far)) + [pl.BlockSpec(memory_space=pltpu.VMEM)] * len(near),
        scratch_shapes=scratch + sems,
        compiler_params=pltpu.CompilerParams(vmem_limit_bytes=VMEM_LIMIT, collective_id=1, has_side_effects=True),
        name="backward",
    )(*args)
    if gathers:
        sums = rest
    else:
        sums = reduce_all(nt, nd, *rest, sh)
    finals = [
        ((tokens, dim), BF16), ((tokens, dim), BF16), ((dim,), F32), ((rows, 2, dcol), F32), ((rows, sh), F32),
        ((hloc, rows), F32), ((4, dcol), F32), ((dcol,), F32), ((4, sh), F32), ((sh,), F32), ((hloc,), F32), ((hloc,), F32),
        ((hloc,), F32), ((dcol,), F32), ((rows, dcol), F32),
    ]
    out, ig, *rest = pl.pallas_call(
        functools.partial(finish_kernel, nt, hloc),
        out_shape=[jax.ShapeDtypeStruct(s, d) for s, d in finals],
        in_specs=[pl.BlockSpec(memory_space=pl.ANY)] * 2 + [pl.BlockSpec(memory_space=pltpu.VMEM)] * 5,
        out_specs=[pl.BlockSpec(memory_space=pl.ANY)] * 2 + [pl.BlockSpec(memory_space=pltpu.VMEM)] * 13,
        scratch_shapes=[pltpu.VMEM((tokens, dim), BF16)] * 2 + [pltpu.SemaphoreType.DMA((4,))],
        name="finish",
    )(out, ig, *sums)
    rest[3] = rest[3].T
    rest[-1] = rest[-1].T
    return (out.reshape(block_input.shape), ig.reshape(block_input.shape), *rest)


def solution(mesh):
    placed = (
        P("dp", "tensor", None), P(), P("dp", None, "tensor"), P("dp", None), P("dp", "tensor"), P(None, "tensor"),
        P("tensor"), P(), P(), P("tensor"), P("tensor"), P("tensor"), P("tensor"), P("tensor", "dp"),
        P("dp", "tensor", None),
    )
    return jax.shard_map(
        local,
        mesh=mesh,
        in_specs=placed,
        out_specs=(
            P("dp", "tensor", None), P("dp", "tensor", None), P(), P("dp", None, "tensor"), P("dp", None),
            P("dp", "tensor"), P(None, "tensor"), P("tensor"), P(), P(), P("tensor"), P("tensor"), P("tensor"),
            P("tensor"), P("tensor", "dp"),
        ),
        check_vma=False,
    )
```

```python
import functools

import jax
import jax.numpy as jnp
from jax import lax
from jax.experimental import pallas as pl
from jax.experimental.pallas import tpu as pltpu
from jax.sharding import PartitionSpec as P

P_SIZE = 64
SPAN = 256
HALF = SPAN // 2
EPSILON = 1e-05
LOG2E = 1.4426950408889634
F32 = jnp.float32
BF16 = jnp.bfloat16
VMEM_LIMIT = 65024 * 1024
WIDE = 512
PIECES = 512, 256


def dot(a, b):
    return jnp.dot(a, b, preferred_element_type=F32)


def dot_nt(a, b):
    return lax.dot_general(a, b, (((1,), (1,)), ((), ())), preferred_element_type=F32)


def dot_tn(a, b):
    return lax.dot_general(a, b, (((0,), (0,)), ((), ())), preferred_element_type=F32)


def sigmoid(v):
    return 0.5 * jnp.tanh(0.5 * v) + 0.5


def split2(v):
    hi = v.astype(BF16)
    return hi, (v - hi.astype(F32)).astype(BF16)


def lanes_of(shape):
    return lax.broadcasted_iota(jnp.int32, shape, len(shape) - 1)


def packed(v, heads):
    v = jnp.where(lanes_of(v.shape) < heads, v, 0.0)
    hi = v.astype(BF16).astype(F32)
    low = (v - hi).astype(BF16).astype(F32)
    return (hi + pltpu.roll(low, 32, 1)).astype(BF16)


def spread_heads(pk, sel):
    return dot(pk, sel)


def gather_heads(v, sel):
    hi, low = split2(v)
    return dot_nt(hi, sel) + dot_nt(low, sel)


def cumulate(tri, v, heads):
    v = jnp.where(lanes_of(v.shape) < heads, v, 0.0)
    p0 = v.astype(BF16).astype(F32)
    r = v - p0
    p1 = r.astype(BF16).astype(F32)
    p2 = r - p1
    pk = (p0 + pltpu.roll(p1, 32, 1) + pltpu.roll(p2, 64, 1)).astype(BF16)
    s = dot(tri, pk)
    n = s.shape[1]
    s = s + pltpu.roll(s, n - 32, 1) + pltpu.roll(s, n - 64, 1)
    return jnp.where(lanes_of(v.shape) < heads, s, 0.0)


def lane_tiles(v):
    return sum(v[:, c0 : c0 + 128] for c0 in range(0, v.shape[1], 128))


def row_tiles(v):
    return jnp.sum(v.reshape(v.shape[0] // 8, 8, v.shape[1]), axis=0)


def block_rows(b, size):
    return pl.ds(pl.multiple_of(b * size, size), size)


MESH = pl.DeviceIdType.MESH


class Sends:
    def __init__(self, send, recv):
        self.send, self.recv, self.used, self.started = send, recv, 0, []

    def make(self, src, dst, to):
        k = self.used
        self.used += 1
        return pltpu.make_async_remote_copy(
            src_ref=src, dst_ref=dst, send_sem=self.send.at[k], recv_sem=self.recv.at[k],
            device_id=to, device_id_type=MESH,
        )

    def start(self, src, dst, to):
        copy = self.make(src, dst, to)
        copy.start()
        self.started.append(copy)
        return copy

    def finish(self):
        for copy in self.started:
            copy.wait_send()


def hello(others):
    barrier = pltpu.get_barrier_semaphore()
    for to in others:
        pl.semaphore_signal(barrier, inc=1, device_id=to, device_id_type=MESH)


def greet(others):
    hello(others)
    pl.semaphore_wait(pltpu.get_barrier_semaphore(), len(others))


def place():
    z = lax.axis_index("tensor")
    d = lax.axis_index("dp")
    core = lax.rem(d, 2)
    x = lax.rem(d // 2, 2)
    y = d // 4
    return z, d, core, x, y


def xor_peer(core, x, y, k):
    c1 = 1 - core if k & 1 else core
    x1 = 1 - x if k & 2 else x
    y1 = 1 - y if k & 4 else y
    return y1 * 4 + x1 * 2 + c1


def dp_rows(d, size, part=None):
    if part is None:
        return pl.ds(pl.multiple_of(d * size, 16), size)
    return pl.ds(pl.multiple_of(d * size + part * (size // 2), 16), size // 2)


def columns(t, size):
    return pl.ds(pl.multiple_of(t * size, 128), size)


def cut_at(base, size, by_t, t):
    return pl.ds(pl.multiple_of(base + t * size, 128), size) if by_t else pl.ds(base, size)


class Gather:
    MESSAGES = 13

    def __init__(self, sends, nt, shard, full, here):
        self.sends, self.nt, self.shard, self.full = sends, nt, shard, full
        self.z, self.d, self.core, self.x, self.y = here
        self.rows, self.width = shard.shape

    def to(self, k):
        return {"dp": xor_peer(self.core, self.x, self.y, k)}

    def ref(self, k, part=None):
        return self.full.at[dp_rows(xor_peer(self.core, self.x, self.y, k), self.rows, part), :]

    def begin(self, sem):
        mine = self.full.at[dp_rows(self.d, self.rows), columns(self.z, self.width)]
        self.local = pltpu.make_async_copy(self.shard, mine, sem)
        self.local.start()
        self.zs = []
        for dz in range(1, self.nt):
            to = {"tensor": lax.rem(self.z + dz, self.nt)}
            self.zs.append(self.sends.start(self.shard, mine, to))

    def column(self):
        self.local.wait()
        for copy in self.zs:
            copy.wait_recv()
        own_a, own_b = self.ref(0, 0), self.ref(0, 1)
        self.x0 = self.sends.start(own_a, own_a, self.to(2))
        self.y0 = self.sends.start(own_b, own_b, self.to(4))
        self.c = [self.sends.start(self.ref(0), self.ref(0), self.to(1))]
        self.y1 = self.sends.start(own_a, own_a, self.to(4))
        self.x1 = self.sends.start(own_b, own_b, self.to(2))

    def forward(self):
        self.forward_first()
        self.forward_second()

    def forward_first(self):
        self.x0.wait_recv()
        self.y2 = self.sends.start(self.ref(2, 0), self.ref(2, 0), self.to(4))
        self.y0.wait_recv()
        self.x2 = self.sends.start(self.ref(4, 1), self.ref(4, 1), self.to(2))

    def forward_second(self):
        self.x1.wait_recv()
        self.c.append(self.sends.start(self.ref(2), self.ref(2), self.to(1)))
        self.y1.wait_recv()
        self.c.append(self.sends.start(self.ref(4), self.ref(4), self.to(1)))

    def corner(self):
        self.y2.wait_recv()
        self.x2.wait_recv()
        self.c.append(self.sends.start(self.ref(6), self.ref(6), self.to(1)))

    def finish(self):
        for copy in self.c:
            copy.wait_recv()


class Reduce:
    MESSAGES = 18

    @staticmethod
    def scratch(rows, width, nt, wz):
        half = rows // 2
        shapes = [(4, rows, width), (2, half, width), (2, half, width), (half, width), (half, width), (nt, rows, wz)]
        return [pltpu.VMEM(s, BF16) for s in shapes]

    def __init__(self, sends, nt, g, bufs, cuts, here):
        self.nt, self.g, self.cuts = nt, g, cuts
        self.rc, self.ra, self.rb, self.ta, self.tb, self.rz = bufs
        self.z, self.d, core, x, y = here
        rows = self.rc.shape[1]
        to = lambda k: {"dp": xor_peer(core, x, y, k)}
        at = lambda y, x, core, part=None: dp_rows(4 * y + 2 * x + core, rows, part)
        send = lambda src, dst, to: sends.make(g.at[src, :], dst, to)
        self.core = [send(at(q // 2, q % 2, 1 - core), self.rc.at[q], to(1)) for q in range(4)]
        self.core_rows = [at(q // 2, q % 2, core) for q in range(4)]
        self.a = [send(at(i, 1 - x, core, 0), self.ra.at[i], to(2)) for i in range(2)]
        self.b = [send(at(1 - y, i, core, 1), self.rb.at[i], to(4)) for i in range(2)]
        self.a_rows = [at(i, x, core, 0) for i in range(2)]
        self.b_rows = [at(y, i, core, 1) for i in range(2)]
        self.a2 = send(at(1 - y, x, core, 0), self.ta, to(4))
        self.b2 = send(at(y, 1 - x, core, 1), self.tb, to(2))
        self.halves = [dp_rows(self.d, rows, i) for i in range(2)]
        self.own = dp_rows(self.d, rows)
        self.zs = []
        self.places = []
        first = 0
        for base, size, by_t in cuts:
            dst = self.rz.at[self.z, :, pl.ds(first, size)]
            for dz in range(1, nt):
                t = lax.rem(self.z + dz, nt)
                src = g.at[self.own, cut_at(base, size, by_t, t)]
                self.zs.append(sends.make(src, dst, {"tensor": t}))
            self.places.append((first, size, cut_at(base, size, by_t, self.z)))
            first += size

    def add(self, rows, other):
        self.g[rows, :] = (self.g[rows, :].astype(F32) + other.astype(F32)).astype(BF16)

    def begin(self):
        for copy in self.core:
            copy.start()

    def first(self):
        for q in range(4):
            self.core[q].wait_recv()
            self.add(self.core_rows[q], self.rc[q])
        for copy in self.a + self.b:
            copy.start()

    def second(self):
        for i in range(2):
            self.a[i].wait_recv()
            self.add(self.a_rows[i], self.ra[i])
            self.b[i].wait_recv()
            self.add(self.b_rows[i], self.rb[i])
        self.a2.start()
        self.b2.start()

    def third(self):
        self.a2.wait_recv()
        self.add(self.halves[0], self.ta[...])
        self.b2.wait_recv()
        self.add(self.halves[1], self.tb[...])
        for copy in self.zs:
            copy.start()
        for first, size, cols in self.places:
            self.rz[self.z, :, first : first + size] = self.g[self.own, cols]

    def last(self, *outs):
        for copy in self.zs:
            copy.wait_recv()
        for out, (first, size, _) in zip(outs, self.places):
            total = self.rz[0, :, first : first + size].astype(F32)
            for t in range(1, self.nt):
                total = total + self.rz[t, :, first : first + size].astype(F32)
            out[...] = total

    def finish(self):
        for copy in self.core + self.a + self.b + [self.a2, self.b2] + self.zs:
            copy.wait_send()


class SmallSum:
    MESSAGES = 6

    @staticmethod
    def scratch(shape, nt):
        return [pltpu.VMEM((2,) + shape, F32), pltpu.VMEM((3,) + shape, F32), pltpu.VMEM((nt,) + shape, F32)]

    def __init__(self, sends, nt, v, bufs, here):
        self.nt, self.v = nt, v
        self.own, self.got, self.rz = bufs
        self.z, d, core, x, y = here
        self.copies = [
            sends.make(self.own.at[k - 1] if k else v, self.got.at[k], {"dp": xor_peer(core, x, y, 2**k)}) for k in range(3)
        ]
        part = self.rz.at[self.z]
        self.zs = [sends.make(part, part, {"tensor": lax.rem(self.z + dz, nt)}) for dz in range(1, nt)]

    def begin(self):
        self.copies[0].start()

    def step(self, k):
        self.copies[k - 1].wait_recv()
        total = (self.own[k - 2] if k > 1 else self.v[...]) + self.got[k - 1]
        if k < 3:
            self.own[k - 1] = total
            self.copies[k].start()
        else:
            self.rz[self.z] = total
            for copy in self.zs:
                copy.start()

    def finish(self):
        for copy in self.copies + self.zs:
            copy.wait_send()

    def last(self):
        for copy in self.zs:
            copy.wait_recv()
        total = self.rz[0]
        for t in range(1, self.nt):
            total = total + self.rz[t]
        return total


class Chain:
    def __init__(self, nt, by, mine, whole, got, out, send, recv, piece, slots, near, far):
        self.mine, self.whole, self.got, self.out, self.send, self.recv = mine, whole, got, out, send, recv
        z = lax.axis_index("tensor")
        self.seqs, _, di = got.shape
        self.piece = piece
        self.per = di // piece
        self.pieces = self.seqs * self.per
        self.at = z if by > 0 else nt - 1 - z
        self.has_prev = self.at > 0
        self.has_next = self.at < nt - 1
        self.next = {"tensor": lax.rem(z + by + nt, nt)}
        self.slots = slots
        self.when = [jnp.where(self.at == 1, a, b) for a, b in zip(near, far)]

    def copy(self, k):
        s = k // self.per
        cols = pl.ds(pl.multiple_of((k - s * self.per) * self.piece, self.piece), self.piece)
        return pltpu.make_async_remote_copy(
            src_ref=self.out.at[s, :, cols], dst_ref=self.got.at[s, :, cols], send_sem=self.send.at[k],
            recv_sem=self.recv.at[k], device_id=self.next, device_id_type=MESH,
        )

    def pass_on(self, k, first):
        s = k // self.per
        cols = pl.ds(pl.multiple_of((k - s * self.per) * self.piece, self.piece), self.piece)
        v = self.mine[s, :, cols].astype(F32)
        if not first:
            v = v + self.whole[s, 0:1, cols] * self.got[s, :, cols].astype(F32)
        self.out[s, :, cols] = v.astype(BF16)
        self.copy(k).start()

    def begin(self, s):
        @pl.when(jnp.logical_not(self.has_prev))
        def _():
            self.got[s] = jnp.zeros(self.got.shape[1:], BF16)
            for k in range(self.per * s, self.per * (s + 1)):
                self.pass_on(k, True)

    def step(self, k):
        self.copy(k).wait_recv()

        @pl.when(self.has_next)
        def _():
            self.pass_on(k, False)

    def slot(self, n):
        k, hit = 0, 0
        for at in self.when:
            k = k + jnp.where(at < n, 1, 0)
            hit = hit + jnp.where(at == n, 1, 0)

        @pl.when(self.has_prev & self.has_next & (hit == 1))
        def _():
            self.step(k)

    def rest(self, first, last, now=True):
        for k in range(first, last):

            @pl.when(self.has_prev & self.has_next & (self.when[k] >= self.slots) & now)
            def _(k=k):
                self.step(k)

    def arrive(self, s):
        for i in range(self.per):

            @pl.when(jnp.logical_not(self.has_next))
            def _(i=i):
                self.copy(self.per * s + i).wait_recv()

    def finish(self):
        @pl.when(self.has_next)
        def _():
            for k in range(self.pieces):
                self.copy(k).wait_send()


class Moves:
    def __init__(self, sems):
        self.sems, self.used, self.open = sems, 0, []

    def start(self, src, dst):
        copy = pltpu.make_async_copy(src, dst, self.sems.at[self.used])
        self.used += 1
        copy.start()
        self.open.append(copy)
        return copy

    def finish(self, done=()):
        for copy in self.open:
            if all(copy is not other for other in done):
                copy.wait()


def heads_table(sel_ref, di):
    r = lax.broadcasted_iota(jnp.int32, (128, WIDE), 0)
    c = lax.broadcasted_iota(jnp.int32, (128, WIDE), 1)
    for c0 in range(0, di, WIDE):
        hit = ((r & 31) == ((c + c0) >> 6)) & (r < 64)
        sel_ref[:, c0 : c0 + WIDE] = jnp.where(hit, 1.0, 0.0).astype(BF16)


def ones_below(tri_ref, up):
    r = lax.broadcasted_iota(jnp.int32, (SPAN, SPAN), 0)
    c = lax.broadcasted_iota(jnp.int32, (SPAN, SPAN), 1)
    tri_ref[...] = jnp.where(r <= c if up else r >= c, 1.0, 0.0).astype(BF16)


def forward_kernel(heads, nt, nd, gathers, *refs):
    refs = list(refs)
    take = lambda n: [refs.pop(0) for _ in range(n)]
    x_hbm, c_hbm, norm_gain_ref, conv_shared_ref, shift_shared_ref = take(5)
    if gathers:
        (wgi_ref, wdelta_ref, wo_ref, wsh_ref, conv_inner_ref, shift_inner_ref, gated_gain_ref, decay_ref, bias_ref,
         skip_gain_ref) = take(10)
    else:
        w1_hbm, w2_hbm, w3_hbm, ws_hbm, parf_ref, xhf_ref = take(6)
    (h_hbm, rawi_hbm, raws_hbm, xs_hbm, bc_hbm, w1_out, w2_out, w3_out, ws_out, yn_hbm, dgate_hbm, dy_hbm, draw_hbm,
     acs_hbm, bs_hbm, rr_hbm, fresh_hbm, vv_hbm, mineb_hbm, sin_hbm) = take(20)
    (dec_ref, whole_ref, chan_ref, dpar_ref, skip_ref, gg_ref, sk_ref, ts_ref) = take(8)
    (x_ref, c_ref, h_ref, w1_ref, w2_ref, w3_ref, ws_ref, pf_ref, xh_ref, rawi_ref, raws_ref, xs_ref, bc_ref, y_ref,
     skc_ref, yn_ref, dgate_ref, dy_ref, g_ref, mine_ref, sb_ref, hh_ref, ea_ref, bst_ref,
     sel_ref, tri_ref, pack_ref, par_ref, zd_ref, wss_ref, turn_ref,
     draw_ref, acs_ref, bs_ref, rr_ref, fresh_ref, eaf_ref, vv_ref, mineb_ref, sin_ref, wk_ref) = take(41)
    send, recv, chain_send, chain_recv, local, moves, result_sems = take(7)

    tokens, dim = x_ref.shape
    seqs, ext, di = rawi_ref.shape
    span = ext - 16
    per = span // SPAN
    blocks = seqs * per
    sh = bc_ref.shape[1]
    state = sh // 2
    dcol = di // nt
    wa = dcol - 128
    inner = nt * wa
    z = lax.axis_index("tensor")
    store = Moves(moves)
    load_x = store.start(x_hbm, x_ref)
    load_c = store.start(c_hbm, c_ref)

    sends = Sends(send, recv)
    zpeers = [{"tensor": lax.rem(z + dz, nt)} for dz in range(1, nt)]
    if gathers:
        here = place()
        _, d, core, x, y = here
        others = zpeers + [{"dp": xor_peer(core, x, y, k)} for k in range(1, 8)]
        hello(others)
        rows = wgi_ref.shape[0]
        hloc = heads // nt
        pack_ref[:, :dcol] = wgi_ref[:, 1, :]
        pl.semaphore_wait(pltpu.get_barrier_semaphore(), len(others))
        shards = (
            (pack_ref.at[:, pl.ds(0, wa)], w1_ref.at[:, pl.ds(0, inner)]),
            (pack_ref.at[:, pl.ds(wa, 128)], w1_ref.at[:, pl.ds(inner, 128 * nt)]),
            (pack_ref.at[:, pl.ds(dcol, dcol)], w2_ref),
            (wo_ref, w3_ref),
        )
        secs = [Gather(sends, nt, a, b, here) for a, b in shards]
        secs[1].begin(local.at[1])
        secs[0].begin(local.at[0])
        pack_ref[:, dcol:] = wgi_ref[:, 0, :]
        turn_ref[...] = jnp.zeros_like(turn_ref)
        turn_ref[0:hloc, 0:rows] = wdelta_ref[...].astype(F32)
        zd_ref[z] = turn_ref[...].T[0:rows].astype(BF16)
        wss_ref[:, :sh] = wsh_ref[...]
        par_ref[...] = jnp.zeros_like(par_ref)
        par_ref[0:4, :] = conv_inner_ref[...].astype(F32)
        par_ref[4:5, :] = shift_inner_ref[...].astype(F32).reshape(1, dcol)
        par_ref[5:6, :] = gated_gain_ref[...].reshape(1, dcol)
        for k, ref in enumerate((decay_ref, bias_ref, skip_gain_ref)):
            par_ref[8 + k : 9 + k, 0:hloc] = ref[...].reshape(1, hloc)
        deltas = [sends.start(zd_ref.at[z], zd_ref.at[z], to) for to in zpeers]
        mine = ws_ref.at[dp_rows(d, rows), :]
        own = [pltpu.make_async_copy(wss_ref, mine, local.at[4]), pltpu.make_async_copy(par_ref, pf_ref.at[z], local.at[5])]
        own[1].start()
        got = [sends.start(par_ref, pf_ref.at[z], to) for to in zpeers]
        edges = [
            sends.make(
                x_hbm.at[pl.ds((s + 1) * span - 16, 16), :], xh_ref.at[pl.ds(16 * s, 16), :],
                {"tensor": lax.rem(z + 1, nt)},
            )
            for s in range(seqs)
        ]

        @pl.when(z < nt - 1)
        def _():
            for copy in edges:
                copy.start()

    else:
        greet(({"tensor": lax.rem(z + nt - 1, nt)}, {"tensor": lax.rem(z + 1, nt)}))
        loads = [store.start(a, b) for a, b in ((w1_hbm, w1_ref), (w2_hbm, w2_ref), (w3_hbm, w3_ref), (ws_hbm, ws_ref))]
        pf_ref[...] = parf_ref[...]
        xh_ref[...] = xhf_ref[...]

    heads_table(sel_ref, di)
    ones_below(tri_ref, False)

    gain = norm_gain_ref[...].reshape(1, dim)
    ts_ref[...] = jnp.zeros_like(ts_ref)
    ts_ref[0:4, :] = conv_shared_ref[...].astype(F32)
    ts_ref[4:5, :] = shift_shared_ref[...].astype(F32).reshape(1, sh)

    def norm(v):
        v = v.astype(F32)
        return (v * lax.rsqrt(jnp.mean(v * v, axis=-1, keepdims=True) + EPSILON) * gain).astype(BF16)

    load_x.wait()

    def norm_step(b, c):
        rows = block_rows(b, SPAN)
        h_ref[rows, :] = norm(x_ref[rows, :])
        return c

    lax.fori_loop(0, blocks, norm_step, 0)
    store.start(h_ref, h_hbm)

    if gathers:
        secs[1].column()
        for copy in deltas:
            copy.wait_recv()
        delta = zd_ref[0].astype(F32)
        for t in range(1, nt):
            delta = delta + pltpu.roll(zd_ref[t].astype(F32), hloc * t, 1)
        wss_ref[:, sh:] = delta.astype(BF16)
        own[0].start()
        got += [sends.start(wss_ref, mine, {"dp": xor_peer(core, x, y, k)}) for k in range(1, 8)]
        secs[0].column()
        secs[1].forward()
        secs[2].begin(local.at[2])
        secs[0].forward_first()

        @pl.when(z > 0)
        def _():
            for copy in edges:
                copy.wait_recv()

        @pl.when(z == 0)
        def _():
            xh_ref[...] = jnp.zeros_like(xh_ref)

        for copy in own:
            copy.wait()
        for copy in got:
            copy.wait_recv()

    hh_ref[...] = norm(xh_ref[...])
    head = pf_ref[0, 8:16, 0:128]
    for t in range(nt):
        chan_ref[:, dcol * t : dcol * (t + 1)] = pf_ref[t, 0:8, :]
        if t > 0:
            head = head + pltpu.roll(pf_ref[t, 8:16, 0:128], heads // nt * t, 1)
    ak = -jnp.exp(head[0:1])
    ak = jnp.where(lanes_of(ak.shape) < heads, ak, 0.0)
    dpar_ref[0:1, :] = head[1:2]
    dpar_ref[1:2, :] = ak * LOG2E
    dpar_ref[2:3, :] = ak
    dpar_ref[3:8, :] = jnp.zeros((5, 128), F32)
    sk8 = packed(jnp.broadcast_to(head[2:3], (8, 128)), heads)
    for c0 in range(0, di, WIDE):
        skip_ref[:, c0 : c0 + WIDE] = spread_heads(sk8, sel_ref[:, c0 : c0 + WIDE])

    def conv(raw, par, out, s, cols):
        def step(r, c):
            r0 = pl.multiple_of(r * 128, 128)
            v = raw[s, pl.ds(r0 + 8, 136), cols]
            acc = par[4:5, cols] + par[3:4, cols] * v[8:]
            for k in range(3):
                acc = acc + par[k : k + 1, cols] * v[5 + k : 133 + k]
            out[pl.ds(pl.multiple_of(s * span + r0, 128), 128), cols] = (acc * sigmoid(acc)).astype(BF16)
            return c

        lax.fori_loop(0, span // 128, step, 0)

    if not gathers:
        loads[3].wait()
    for s in range(seqs):
        rows = slice(span * s, span * (s + 1))
        raws_ref[s, 0:16, :] = dot(hh_ref[16 * s : 16 * s + 16, :], ws_ref[:, :sh])
        both = dot(h_ref[rows, :], ws_ref[...])
        raws_ref[s, 16:ext, :] = both[:, :sh]
        draw_ref[rows, :] = both[:, sh:] + dpar_ref[0:1, :]
        for c0 in range(0, sh, 256):
            conv(raws_ref, ts_ref, bc_ref, s, slice(c0, c0 + 256))
    store.start(raws_ref, raws_hbm)
    store.start(bc_ref, bc_hbm)
    store.start(ws_ref, ws_out)

    def first_part(s):
        def step(t, carry):
            cols = pl.ds(pl.multiple_of(dcol * t, 128), wa)
            w = w1_ref[:, pl.ds(pl.multiple_of(wa * t, 128), wa)]
            rawi_ref[s, 0:16, cols] = dot(hh_ref[16 * s : 16 * s + 16, :], w)
            rawi_ref[s, 16:ext, cols] = dot(h_ref[span * s : span * (s + 1), :], w)
            conv(rawi_ref, chan_ref, xs_ref, s, cols)
            return carry

        lax.fori_loop(0, nt, step, 0)

    def second_part(s):
        rows = slice(span * s, span * (s + 1))

        def step(t, carry):
            cols = pl.ds(pl.multiple_of(dcol * t + wa, 128), 128)
            w = w1_ref[:, pl.ds(pl.multiple_of(inner + 128 * t, 128), 128)]
            rawi_ref[s, 0:16, cols] = dot(hh_ref[16 * s : 16 * s + 16, :], w)
            rawi_ref[s, 16:ext, cols] = dot(h_ref[rows, :], w)
            conv(rawi_ref, chan_ref, xs_ref, s, cols)
            return carry

        lax.fori_loop(0, nt, step, 0)

    def block_step(s, j, c):
        b = s * per + j
        rows = block_rows(b, SPAN)
        bt = bc_ref[rows, :state].astype(F32).T.astype(BF16)
        w = spread_heads(wk_ref[rows, :], sel_ref[...])
        fresh = dot(bt, (w * xs_ref[rows, :].astype(F32)).astype(BF16))

        @pl.when(j == 0)
        def _():
            fresh_ref[s] = fresh.astype(BF16)
            mine_ref[s] = fresh

        @pl.when(j > 0)
        def _():
            mine_ref[s] = dec_ref[b, 0:1, :] * mine_ref[s] + fresh

        return c

    def decay_step(b, c):
        rows = block_rows(b, SPAN)
        s = b // per
        j = b - s * per
        x = draw_ref[rows, :]
        dt = jnp.maximum(x, 0.0) + jnp.log1p(jnp.exp(-jnp.abs(x)))
        lg = jnp.where(x < -20.0, x * LOG2E, jnp.log2(jnp.maximum(dt, 1e-30)))
        acs = cumulate(tri_ref[...], dt * dpar_ref[1:2, :], heads)
        bs = acs - lg
        acs_ref[rows, :] = acs
        bs_ref[rows, :] = bs
        bst_ref[b] = bs.T
        end = acs[SPAN - 1 : SPAN, :]
        wk_ref[rows, :] = packed(jnp.exp2(end - bs), heads)
        ea_ref[rows, :] = packed(jnp.exp2(acs), heads)
        de = spread_heads(packed(jnp.broadcast_to(jnp.exp2(end), (8, 128)), heads), sel_ref[...])
        dec_ref[b] = de

        @pl.when(j == 0)
        def _():
            whole_ref[s] = de

        @pl.when(j > 0)
        def _():
            whole_ref[s] = de * whole_ref[s]

        return c

    chain = Chain(
        nt, 1, mine_ref, whole_ref, sin_ref, sb_ref, chain_send, chain_recv, PIECES[0],
        3 * blocks + 2 * seqs, (2, 7, 12, 13, 14, 15), (10, 12, 14, 16, 17, 18),
    )
    if gathers:
        secs[1].corner()
        secs[0].forward_second()
    lax.fori_loop(0, blocks, decay_step, 0)
    for a, b in ((draw_ref, draw_hbm), (acs_ref, acs_hbm), (bs_ref, bs_hbm)):
        store.start(a, b)
    if gathers:
        secs[1].finish()
        secs[0].corner()
        secs[2].column()
        secs[3].begin(local.at[3])
    else:
        loads[0].wait()
    for s in range(seqs):
        second_part(s)
    if gathers:
        secs[0].finish()
        secs[2].forward_first()
    store.start(w1_ref, w1_out)
    for s in range(seqs):
        first_part(s)
        store.start(rawi_ref.at[s], rawi_hbm.at[s])
        store.start(xs_ref.at[pl.ds(span * s, span), :], xs_hbm.at[pl.ds(span * s, span), :])
        lax.fori_loop(0, per, functools.partial(block_step, s), 0)
        chain.begin(s)
        if s == seqs - 1:
            store.start(fresh_ref, fresh_hbm)
        if gathers and s == 0:
            secs[2].forward_second()
            secs[3].column()
            secs[2].corner()
    if gathers:
        secs[3].forward()

    lower = lax.broadcasted_iota(jnp.int32, (HALF, HALF), 0) >= lax.broadcasted_iota(jnp.int32, (HALF, HALF), 1)
    first = lanes_of((HALF, 128)) < P_SIZE
    pairs = di // 128

    def intra_step(b, carry):
        rows = block_rows(b, SPAN)
        bb = bc_ref[rows, :state]
        cc = bc_ref[rows, state:]
        g00 = dot_nt(cc[:HALF], bb[:HALF])
        g10 = dot_nt(cc[HALF:], bb[:HALF])
        g11 = dot_nt(cc[HALF:], bb[HALF:])
        for p in range(pairs):
            cols = slice(128 * p, 128 * p + 128)
            xp = xs_ref[rows, cols]
            y0, y1 = [], []
            for h in (2 * p, 2 * p + 1):
                a0 = acs_ref[block_rows(2 * b, HALF), h : h + 1]
                a1 = acs_ref[block_rows(2 * b + 1, HALF), h : h + 1]
                r0 = bst_ref[b, h : h + 1, :HALF]
                r1 = bst_ref[b, h : h + 1, HALF:]
                m00 = jnp.where(lower, jnp.exp2(a0 - r0) * g00, 0.0).astype(BF16)
                m10 = (jnp.exp2(a1 - r0) * g10).astype(BF16)
                m11 = jnp.where(lower, jnp.exp2(a1 - r1) * g11, 0.0).astype(BF16)
                y0.append(m00)
                y1.append(jnp.concatenate([m10, m11], axis=1))
            y0 = dot(jnp.concatenate(y0, axis=0), xp[:HALF])
            y1 = dot(jnp.concatenate(y1, axis=0), xp)
            y_ref[block_rows(2 * b, HALF), cols] = jnp.where(first, y0[:HALF], y0[HALF:])
            y_ref[block_rows(2 * b + 1, HALF), cols] = jnp.where(first, y1[:HALF], y1[HALF:])
            if (p + 1) % (pairs // 3) == 0:
                chain.slot(3 * b + (p + 1) // (pairs // 3) - 1)
        return carry

    lax.fori_loop(0, blocks, intra_step, 0)
    load_c.wait()
    if gathers:
        secs[3].corner()
        secs[2].finish()
    else:
        loads[1].wait()
        loads[2].wait()
    store.start(w2_ref, w2_out)

    def gate_step(b, carry):
        rows = block_rows(b, span)

        def column_step(i, c):
            cols = columns(i, WIDE)
            dy_ref[rows, cols] = dot(h_ref[rows, :], w2_ref[:, cols]).astype(BF16)
            return c

        lax.fori_loop(0, di // WIDE, column_step, 0)
        chain.slot(3 * blocks + b)
        return carry

    def products_step(b, carry):
        rows = block_rows(b, span)

        def column_step(i, c):
            cols = columns(i, WIDE)
            dgate_ref[rows, cols] = (dot(c_ref[rows, :], w3_ref[:, cols]) * chan_ref[5:6, cols]).astype(BF16)
            return c

        lax.fori_loop(0, di // WIDE, column_step, 0)
        chain.slot(3 * blocks + seqs + b)
        return carry

    lax.fori_loop(0, seqs, gate_step, 0)
    if gathers:
        secs[3].finish()
    store.start(w3_ref, w3_out)
    lax.fori_loop(0, seqs, products_step, 0)
    chain.rest(0, chain.per)

    gg_ref[...] = jnp.zeros_like(gg_ref)
    skc_ref[...] = jnp.zeros_like(skc_ref)
    results = ((yn_ref, yn_hbm), (dgate_ref, dgate_hbm), (dy_ref, dy_hbm), (rr_ref, rr_hbm))

    def result_copy(k, b):
        rows = block_rows(b, SPAN)
        return pltpu.make_async_copy(results[k][0].at[rows, :], results[k][1].at[rows, :], result_sems.at[k, b])

    def sin_copy(s):
        return pltpu.make_async_copy(sin_ref.at[s], sin_hbm.at[s], result_sems.at[len(results), s])

    def mid_step(s, j, carry):
        b = s * per + j
        rows = block_rows(b, SPAN)
        cc = bc_ref[rows, state:]
        ss = jnp.zeros((SPAN, 128), F32)
        for c0 in range(0, di, WIDE):
            cols = slice(c0, c0 + WIDE)
            prev = sin_ref[s, :, cols].astype(F32)
            later = dec_ref[s * per, 0:1, cols] * prev + fresh_ref[s, :, cols].astype(F32)
            s_in = jnp.where(j == 0, prev, later).astype(BF16)
            ea = spread_heads(ea_ref[rows, :], sel_ref[:, cols])
            eaf_ref[:, cols] = ea
            ynos = y_ref[rows, cols] + ea * dot(cc, s_in)
            y_ref[rows, cols] = ynos
            y = ynos + skip_ref[0:1, cols] * xs_ref[rows, cols].astype(F32)
            gate = dy_ref[rows, cols].astype(F32)
            g = y * (gate * sigmoid(gate))
            g_ref[:, cols] = g
            ss = ss + lane_tiles(g * g)
        r2 = lax.rsqrt(jnp.sum(ss, axis=-1, keepdims=True) / di + EPSILON)
        qg = jnp.zeros((SPAN, 128), F32)
        for c0 in range(0, di, WIDE):
            cols = slice(c0, c0 + WIDE)
            g = g_ref[:, cols]
            gain = chan_ref[5:6, cols]
            yn_ref[rows, cols] = (g * r2 * gain).astype(BF16)
            qg_here = dgate_ref[rows, cols].astype(F32) * g
            gg_ref[:, cols] += row_tiles(qg_here * r2)
            qg = qg + lane_tiles(qg_here)
        coef = r2 * r2 * r2 * (jnp.sum(qg, axis=-1, keepdims=True) / di)
        rr = jnp.zeros((SPAN, 128), F32)
        ct = cc.astype(F32).T.astype(BF16)
        for c0 in range(0, di, WIDE):
            cols = slice(c0, c0 + WIDE)
            xf = xs_ref[rows, cols].astype(F32)
            ynos = y_ref[rows, cols]
            y = ynos + skip_ref[0:1, cols] * xf
            gate = dy_ref[rows, cols].astype(F32)
            sg = sigmoid(gate)
            dg = r2 * dgate_ref[rows, cols].astype(F32) - coef * g_ref[:, cols]
            dgate_ref[rows, cols] = (dg * y * (sg * (1.0 + gate * (1.0 - sg)))).astype(BF16)
            dyb = (dg * (gate * sg)).astype(BF16)
            dy_ref[rows, cols] = dyb
            dy = dyb.astype(F32)
            rr = rr + gather_heads(dy * ynos, sel_ref[:, cols])
            skc_ref[:, cols] += row_tiles(dy * xf)
            vv = dot(ct, (eaf_ref[:, cols] * dy).astype(BF16))

            @pl.when(j == 0)
            def _(cols=cols, vv=vv):
                mine_ref[s, :, cols] = vv

            @pl.when(j > 0)
            def _(cols=cols, vv=vv):
                vv_ref[s, :, cols] = vv.astype(BF16)
                mine_ref[s, :, cols] += dec_ref[s * per, 0:1, cols] * vv

        rr_ref[rows, :] = rr
        for k in range(len(results)):
            result_copy(k, b).start()
        chain.rest(chain.per, chain.pieces - 1, (s == 0) & (j == 0))
        chain.rest(chain.pieces - 1, chain.pieces, (s == 0) & (j == per - 1))
        return carry

    def mid_sequence(s, carry):
        chain.arrive(s)
        sin_copy(s).start()
        lax.fori_loop(0, per, functools.partial(mid_step, s), 0)
        return carry

    lax.fori_loop(0, seqs, mid_sequence, 0)
    gg_ref[...] = gg_ref[...] / chan_ref[5:6, :]
    sk_ref[...] = jnp.zeros_like(sk_ref)
    for c0 in range(0, di, WIDE):
        sk_ref[...] += gather_heads(skc_ref[:, c0 : c0 + WIDE], sel_ref[:, c0 : c0 + WIDE])
    mineb_ref[...] = mine_ref[...].astype(BF16)
    chain.finish()
    sends.finish()
    if gathers:

        @pl.when(z < nt - 1)
        def _():
            for copy in edges:
                copy.wait_send()

    for s in range(seqs):
        sin_copy(s).wait()
    store.start(mineb_ref, mineb_hbm)
    store.start(vv_ref, vv_hbm)
    for b in range(blocks):
        for k in range(len(results)):
            result_copy(k, b).wait()
    store.finish((load_x, load_c) if gathers else (load_x, load_c, *loads))


def backward_kernel(heads, nt, nd, reduces, *refs):
    refs = list(refs)
    take = lambda n: [refs.pop(0) for _ in range(n)]
    (x_hbm, c_hbm, h_hbm, rawi_hbm, raws_hbm, xs_hbm, bc_hbm, w1_hbm, w2_hbm, w3_hbm, ws_hbm, yn_hbm, dgate_hbm, dy_hbm,
     draw_hbm, acs_hbm, bs_hbm, rr_hbm, fresh_hbm, vv_hbm, sin_hbm, mineb_hbm) = take(22)
    norm_gain_ref, ts_ref, dec_ref, whole_ref, chan_ref, dpar_ref, skip_ref, gg_ref, sk_ref = take(9)
    out_hbm, ig_hbm = take(2)
    if reduces:
        o1_ref, osd_ref, o2_ref, o3_ref, om_ref = take(5)
    else:
        g1_out, g2_out, g3_out, sm_ref = take(4)
    (c_ref, h_ref, rawi_ref, raws_ref, xs_ref, bc_ref, w1_ref, ws_ref, dgate_ref, dy_ref, draw_ref,
     acs_ref, bs_ref, rr_ref, fresh_ref, vv_ref, sin_ref, ds_ref, sb_ref, din_ref, dx_ref, dbc_ref, g_ref, halo_ref,
     edge_ref, keep_ref, acst_ref, dg_ref, sel_ref, triu_ref, tg_ref, small_ref, ng_ref, w2_ref) = take(34)
    if reduces:
        (sm_ref,) = take(1)
        bufs = [take(6) for _ in range(4)]
        small_bufs = take(3)
    chain_send, chain_recv, halo_send, halo_recv, moves = take(5)
    if reduces:
        sems = [take(2) for _ in range(5)]

    tokens, dim = h_ref.shape
    seqs, ext, di = rawi_ref.shape
    span = ext - 16
    per = span // SPAN
    blocks = seqs * per
    sh = bc_ref.shape[1]
    state = sh // 2
    dcol = di // nt
    wa = dcol - 128
    na = nt * wa
    z = lax.axis_index("tensor")
    move = Moves(moves)
    load = lambda a, b: move.start(a, b)
    yn_ref = din_ref.at[:, pl.ds(0, di)]
    l_mine, l_c, l_yn0 = load(mineb_hbm, sb_ref), load(c_hbm, c_ref), load(yn_hbm, yn_ref)
    x_ref = xs_ref.at[:, pl.ds(0, dim)]
    w3_ref = din_ref.at[pl.ds(0, dim), pl.ds(0, di)]

    if reduces:
        here = place()
        _, d, core, x, y = here
        others = [{"tensor": lax.rem(z + dz, nt)} for dz in range(1, nt)]
        others += [{"dp": xor_peer(core, x, y, k)} for k in (1, 2, 4)]
        hello(others)
        cut = ((0, dcol, True),)
        parts = (
            (g_ref.at[:, pl.ds(di, di)], cut), (g_ref.at[:, pl.ds(0, di)], cut),
            (g_ref.at[:, pl.ds(di, na)], ((0, wa, True),)),
            (g_ref.at[:, pl.ds(di + na, 128 * nt + sh + 128)], ((0, 128, True), (128 * nt, sh + 128, False))),
        )
        r3, r2, ra, rb = (Reduce(Sends(*sems[i]), nt, g, bufs[i], cuts, here) for i, (g, cuts) in enumerate(parts))
        small_sum = SmallSum(Sends(*sems[4]), nt, sm_ref, small_bufs, here)
    else:
        others = [{"tensor": lax.rem(z + nt - 1, nt)}, {"tensor": lax.rem(z + 1, nt)}]
        hello(others)
    heads_table(sel_ref, di)
    ones_below(triu_ref, True)
    small_ref[...] = jnp.zeros_like(small_ref)
    ng_ref[...] = jnp.zeros_like(ng_ref)
    tg_ref[...] = jnp.zeros_like(tg_ref)
    pl.semaphore_wait(pltpu.get_barrier_semaphore(), len(others))

    chain = Chain(
        nt, -1, sb_ref, whole_ref, ds_ref, sb_ref, chain_send, chain_recv, PIECES[1], 2 * (di // WIDE) + 3 * blocks,
        (1, 2, 3, 4, 5, 6, 7, 8, 9, 10, 11, 12), (4, 5, 6, 7, 8, 9, 10, 11, 12, 13, 14, 15),
    )
    l_mine.wait()
    for s in range(seqs):
        chain.begin(s)

    def weight_gradient(dv, w, at):
        g = dot_tn(h_ref[...], dv)
        g_ref[:, pl.ds(pl.multiple_of(at, 128), g.shape[1])] = g.astype(BF16)
        ng_ref[...] += lane_tiles(g * w.astype(F32))

    l_c.wait()
    l_yn0.wait()
    l_h, l_dgate, l_w2 = load(h_hbm, h_ref), load(dgate_hbm, dgate_ref), load(w2_hbm, w2_ref)
    parts = di // WIDE

    def output_gradient(i, carry):
        g_ref[:, columns(parts + i, WIDE)] = dot_tn(c_ref[...], din_ref[:, columns(i, WIDE)]).astype(BF16)
        chain.slot(i)
        return carry

    lax.fori_loop(0, parts, output_gradient, 0)
    if reduces:
        r3.begin()
    else:
        s3 = move.start(g_ref.at[:, pl.ds(di, di)], g3_out)
    l_h.wait()
    l_dgate.wait()
    l_w2.wait()
    l_scan = [
        load(a, b)
        for a, b in (
            (xs_hbm, xs_ref), (dy_hbm, dy_ref), (bc_hbm, bc_ref), (acs_hbm, acs_ref), (bs_hbm, bs_ref),
        )
    ]

    def gate_gradient(i, carry):
        cols = columns(i, WIDE)
        weight_gradient(dgate_ref[:, cols], w2_ref[:, cols], i * WIDE)
        chain.slot(parts + i)
        return carry

    lax.fori_loop(0, parts, gate_gradient, 0)
    slot0 = 2 * parts
    if reduces:
        r2.begin()
    else:
        s2 = move.start(g_ref.at[:, pl.ds(0, di)], g2_out)

    for copy in l_scan:
        copy.wait()
    l_state = [
        load(a, b)
        for a, b in (
            (draw_hbm, draw_ref), (rr_hbm, rr_ref), (fresh_hbm, fresh_ref), (vv_hbm, vv_ref), (sin_hbm, sin_ref),
            (rawi_hbm, rawi_ref), (raws_hbm, raws_ref),
        )
    ]
    l_last = [load(w1_hbm, w1_ref), load(ws_hbm, ws_ref)]
    upper = lax.broadcasted_iota(jnp.int32, (HALF, HALF), 0) <= lax.broadcasted_iota(jnp.int32, (HALF, HALF), 1)
    first = lanes_of((HALF, 128)) < P_SIZE
    first_all = lanes_of((SPAN, 128)) < P_SIZE
    pairs = di // 128

    def intra_step(b, carry):
        rows = block_rows(b, SPAN)
        acst_ref[...] = acs_ref[rows, :].T
        bb = bc_ref[rows, :state]
        cc = bc_ref[rows, state:]
        g00 = dot_nt(bb[:HALF], cc[:HALF])
        g01 = dot_nt(bb[:HALF], cc[HALF:])
        g11 = dot_nt(bb[HALF:], cc[HALF:])
        dg_ref[...] = jnp.zeros_like(dg_ref)
        for p in range(pairs):
            cols = slice(128 * p, 128 * p + 128)
            xp = xs_ref[rows, cols]
            dyp = dy_ref[rows, cols]
            zero = jnp.zeros_like(xp)
            xa, xb = jnp.where(first_all, xp, zero), jnp.where(first_all, zero, xp)
            dm0 = dot_nt(jnp.concatenate([xa[:HALF], xb[:HALF]], axis=0), dyp)
            dm1 = dot_nt(jnp.concatenate([xa[HALF:], xb[HALF:]], axis=0), dyp[HALF:])
            d0, d1, de = [], [], []
            for h in (2 * p, 2 * p + 1):
                b0 = bs_ref[block_rows(2 * b, HALF), h : h + 1]
                b1 = bs_ref[block_rows(2 * b + 1, HALF), h : h + 1]
                r0 = acst_ref[h : h + 1, :HALF]
                r1 = acst_ref[h : h + 1, HALF:]
                e00 = jnp.where(upper, jnp.exp2(r0 - b0), 0.0)
                e01 = jnp.exp2(r1 - b0)
                e11 = jnp.where(upper, jnp.exp2(r1 - b1), 0.0)
                m0 = jnp.concatenate([(e00 * g00).astype(BF16), (e01 * g01).astype(BF16)], axis=1)
                m1 = (e11 * g11).astype(BF16)
                d0.append(m0)
                d1.append(m1)
                de.append((e00, e01, e11))
            d0 = dot(jnp.concatenate(d0, axis=0), dyp)
            d1 = dot(jnp.concatenate(d1, axis=0), dyp[HALF:])
            dg_ref[0] += dm0[:HALF, :HALF] * de[0][0] + dm0[HALF:, :HALF] * de[1][0]
            dg_ref[1] += dm0[:HALF, HALF:] * de[0][1] + dm0[HALF:, HALF:] * de[1][1]
            dg_ref[2] += dm1[:HALF] * de[0][2] + dm1[HALF:] * de[1][2]
            dx_ref[block_rows(2 * b, HALF), cols] = jnp.where(first, d0[:HALF], d0[HALF:])
            dx_ref[block_rows(2 * b + 1, HALF), cols] = jnp.where(first, d1[:HALF], d1[HALF:])
            if reduces and p == pairs // 2:
                pl.when(b == blocks // 4)(r3.first)
            if (p + 1) % (pairs // 3) == 0:
                chain.slot(slot0 + 3 * b + (p + 1) // (pairs // 3) - 1)
        dg00 = dg_ref[0]
        dg01 = dg_ref[1]
        dg11 = dg_ref[2]
        dbc_ref[block_rows(2 * b, HALF), :state] = dot(jnp.concatenate([dg00, dg01], axis=1).astype(BF16), cc)
        dbc_ref[block_rows(2 * b + 1, HALF), :state] = dot(dg11.astype(BF16), cc[HALF:])
        dbc_ref[block_rows(2 * b, HALF), state:] = dot(dg00.T.astype(BF16), bb[:HALF])
        dbc_ref[block_rows(2 * b + 1, HALF), state:] = dot(
            jnp.concatenate([dg01.T, dg11.T], axis=1).astype(BF16), bb
        )
        return carry

    lax.fori_loop(0, blocks, intra_step, 0)
    if reduces:
        r3.second()
        r2.first()
    chain.rest(0, chain.per + 1)
    for copy in l_state:
        copy.wait()

    def state_step(s, j):
        b = s * per + j
        rows = block_rows(b, SPAN)
        acs = acs_ref[rows, :]
        end = acs[SPAN - 1 : SPAN, :]
        eak = packed(jnp.exp2(acs), heads)
        wk = packed(jnp.exp2(end - bs_ref[rows, :]), heads)
        bb = bc_ref[rows, :state]
        db = dbc_ref[rows, :state]
        dc = dbc_ref[rows, state:]
        pp = jnp.zeros((SPAN, 128), F32)
        endsum = jnp.zeros((8, 128), F32)
        for c0 in range(0, di, WIDE):
            cols = slice(c0, c0 + WIDE)
            s_in = sin_ref[s, :, cols]
            ds = ds_ref[s, :, cols]
            if j > 0:
                s_in = dec_ref[s * per, 0:1, cols] * s_in.astype(F32) + fresh_ref[s, :, cols].astype(F32)
                s_in = s_in.astype(BF16)
            if j < per - 1:
                ds = dec_ref[s * per + per - 1, 0:1, cols] * ds.astype(F32) + vv_ref[s, :, cols].astype(F32)
                ds = ds.astype(BF16)
            w = spread_heads(wk, sel_ref[:, cols])
            ea = spread_heads(eak, sel_ref[:, cols])
            xf = xs_ref[rows, cols].astype(F32)
            dyf = dy_ref[rows, cols].astype(F32)
            dxs = w * dot(bb, ds)
            dxn = dx_ref[rows, cols] + dxs
            pp = pp + gather_heads(dxn * xf, sel_ref[:, cols])
            at_end = jnp.sum(ds.astype(F32) * s_in.astype(F32), axis=0, keepdims=True) * dec_ref[b, 0:1, cols]
            first_row = lax.broadcasted_iota(jnp.int32, (8, WIDE), 0) == 0
            at_end = row_tiles(dxs * xf) + jnp.where(first_row, jnp.broadcast_to(at_end, (8, WIDE)), 0.0)
            endsum = endsum + gather_heads(at_end, sel_ref[:, cols])
            dc = dc + dot_nt((ea * dyf).astype(BF16), s_in)
            db = db + dot_nt((w * xf).astype(BF16), ds)
            dx_ref[rows, cols] = dxn + skip_ref[0:1, cols] * dyf
        dbc_ref[rows, :state] = db
        dbc_ref[rows, state:] = dc
        da = cumulate(triu_ref[...], rr_ref[rows, :] - pp, heads)
        da = da + jnp.sum(endsum, axis=0, keepdims=True)
        xx = draw_ref[rows, :]
        sg = 1.0 / (1.0 + jnp.exp(-xx))
        dt = jnp.maximum(xx, 0.0) + jnp.log1p(jnp.exp(-jnp.abs(xx)))
        ratio = jnp.where(xx < -20.0, 1.0, sg / jnp.maximum(dt, 1e-30))
        ak = dpar_ref[2:3, :]
        dd = da * ak * sg + pp * ratio
        din_ref[rows, di + sh :] = dd.astype(BF16)
        small_ref[0:1, :] += jnp.sum(da * dt * ak, axis=0, keepdims=True)
        small_ref[1:2, :] += jnp.sum(dd, axis=0, keepdims=True)

        def conv_back(raw, par, dact, off, cols):
            here_cols = pl.ds(pl.multiple_of(off + cols.start, 128), cols.size)

            def step(r, prev):
                r0 = pl.multiple_of(r * HALF, HALF)
                at = pl.ds(pl.multiple_of(16 + j * SPAN + r0, 16), HALF)
                now = raw[s, at, cols]
                v = jnp.concatenate([prev, now], axis=0)
                sh_v = [v[5 + k : 5 + k + HALF] for k in range(3)] + [now]
                pre = par[4:5, cols] + par[0:1, cols] * sh_v[0]
                for k in range(1, 4):
                    pre = pre + par[k : k + 1, cols] * sh_v[k]
                sg = sigmoid(pre)
                dp = dact[pl.ds(pl.multiple_of(b * SPAN + r0, HALF), HALF), cols] * (sg * (1.0 + pre * (1.0 - sg)))
                raw[s, at, cols] = dp
                for k in range(4):
                    tg_ref[k, :, here_cols] += row_tiles(dp * sh_v[k])
                tg_ref[4, :, here_cols] += row_tiles(dp)
                return now[HALF - 8 :]

            prev = raw[s, 8:16, cols] if j == 0 else keep_ref[s, :, here_cols]
            prev = lax.fori_loop(0, SPAN // HALF, step, prev)
            if j < per - 1:
                keep_ref[s, :, here_cols] = prev

        def inner_step(i, carry):
            conv_back(rawi_ref, chan_ref, dx_ref, 0, pl.ds(pl.multiple_of(256 * i, 256), 256))
            return carry

        lax.fori_loop(0, di // 256, inner_step, 0)
        for c0 in range(0, sh, 256):
            conv_back(raws_ref, ts_ref, dbc_ref, di, pl.ds(c0, 256))

    halo_copy = pltpu.make_async_remote_copy(
        src_ref=edge_ref, dst_ref=halo_ref, send_sem=halo_send.at[0], recv_sem=halo_recv.at[0],
        device_id={"tensor": lax.rem(z + nt - 1, nt)}, device_id_type=MESH,
    )
    for j in range(per):

        def seq_step(s, carry, j=j):
            if j == 0:
                chain.rest(chain.per + 1, chain.pieces, s == 1)
                chain.arrive(s)
            state_step(s, j)
            return carry

        lax.fori_loop(0, seqs, seq_step, 0)
        if j == 0:
            edge_ref[:, :, :di] = rawi_ref[:, 16:24, :]
            edge_ref[:, :, di:] = raws_ref[:, 16:24, :]

            @pl.when(z > 0)
            def _():
                halo_copy.start()

            if reduces:
                r3.third()
    l_last += [load(x_hbm, x_ref)]
    l_yn = load(yn_hbm, dy_ref)
    if reduces:
        r3.last(o3_ref)
        r2.second()

    @pl.when(z < nt - 1)
    def _():
        halo_copy.wait_recv()

    @pl.when(z == nt - 1)
    def _():
        halo_ref[...] = jnp.zeros_like(halo_ref)

    def conv_t(dpre, par, off, c0, to):
        cols = pl.ds(pl.multiple_of(c0, 128), 128)
        halo_cols = pl.ds(pl.multiple_of(off + c0, 128), 128)
        to_cols = pl.ds(pl.multiple_of(to, 128), 128)

        def step(s, carry):
            def rows_step(r, nxt):
                r0 = pl.multiple_of(span - HALF * (r + 1), HALF)
                now = dpre[s, pl.ds(pl.multiple_of(16 + r0, 16), HALF), cols]
                v = jnp.concatenate([now, nxt], axis=0)
                acc = par[3:4, cols] * now
                for k in range(3):
                    acc = acc + par[k : k + 1, cols] * v[3 - k : 3 - k + HALF]
                din_ref[pl.ds(pl.multiple_of(s * span + r0, HALF), HALF), to_cols] = acc.astype(BF16)
                return now[0:8]

            lax.fori_loop(0, span // HALF, rows_step, halo_ref[s, :, halo_cols])
            return carry

        lax.fori_loop(0, seqs, step, 0)

    def inner_first(i, carry):
        t = i // (wa // 128)
        r = 128 * (i - t * (wa // 128))
        conv_t(rawi_ref, chan_ref, 0, dcol * t + r, wa * t + r)
        return carry

    def inner_second(t, carry):
        conv_t(rawi_ref, chan_ref, 0, dcol * t + wa, na + 128 * t)
        return carry

    def shared_part(i, carry):
        conv_t(raws_ref, ts_ref, di, 128 * i, di + 128 * i)
        return carry

    lax.fori_loop(0, na // 128, inner_first, 0)
    if reduces:
        r3.finish()
        r2.third()
    else:
        s3.wait()
    for copy in l_last:
        copy.wait()

    def inner_gradient(i, carry):
        cols = columns(i, WIDE)
        weight_gradient(din_ref[:, cols], w1_ref[:, cols], di + i * WIDE)
        return carry

    lax.fori_loop(0, na // WIDE, inner_gradient, 0)
    if reduces:
        ra.begin()
    lax.fori_loop(0, nt, inner_second, 0)
    lax.fori_loop(0, sh // 128, shared_part, 0)
    lax.fori_loop(na // WIDE, di // WIDE, inner_gradient, 0)
    weight_gradient(din_ref[:, di:], ws_ref[...], 2 * di)
    column = lambda v: jnp.sum(v, axis=0, keepdims=True)
    for k in range(5):
        sm_ref[k : k + 1, :] = column(tg_ref[k, :, :di])
    sm_ref[5:6, :] = column(gg_ref[...])
    gain = norm_gain_ref[...].reshape(1, dim)
    sm_ref[6:7, :dim] = column(ng_ref[...].T) / gain
    flat = [column(tg_ref[k, :, di:]) for k in range(5)] + [small_ref[0:1, :], small_ref[1:2, :], column(sk_ref[...])]
    row, at = 6, dim
    for v in flat:
        width = v.shape[1]
        if at + width > di:
            row, at = row + 1, 0
        sm_ref[row : row + 1, at : at + width] = v
        at += width
    sm_ref[row : row + 1, at:] = jnp.zeros((1, di - at), F32)
    if reduces:
        rb.begin()
        small_sum.begin()
    else:
        move.start(g_ref.at[:, pl.ds(di, g_ref.shape[1] - di)], g1_out)
    def last_step(b, carry):
        if reduces:
            pl.when(b == 0)(ra.first)

            @pl.when(b == blocks // 4)
            def _():
                small_sum.step(1)
                rb.first()

            @pl.when(b == 2 * blocks // 4)
            def _():
                small_sum.step(2)

            @pl.when(b == 3 * blocks // 4)
            def _():
                ra.second()
                small_sum.step(3)

        rows = block_rows(b, SPAN)
        dh = dot_nt(dgate_ref[rows, :], w2_ref[...])
        dh = dh + dot_nt(din_ref[rows, :di], w1_ref[...])
        dh = dh + dot_nt(din_ref[rows, di:], ws_ref[...])
        u = x_ref[rows, :].astype(F32)
        r1 = lax.rsqrt(jnp.mean(u * u, axis=-1, keepdims=True) + EPSILON)
        e = dh * gain
        m = jnp.mean(e * u, axis=-1, keepdims=True)
        c_ref[rows, :] = (c_ref[rows, :].astype(F32) + r1 * e - u * (r1 * r1 * r1 * m)).astype(BF16)
        return carry

    lax.fori_loop(0, blocks, last_step, 0)
    move.start(c_ref, ig_hbm)
    l_w3 = load(w3_hbm, w3_ref)

    def output_step(b, carry):
        rows = block_rows(b, SPAN)
        x_ref[rows, :] = (x_ref[rows, :].astype(F32) + dot_nt(dy_ref[rows, :], w3_ref[...])).astype(BF16)
        return carry

    if reduces:
        rb.second()
        ra.third()
    l_w3.wait()
    l_yn.wait()
    lax.fori_loop(0, blocks // 2, output_step, 0)
    if reduces:
        rb.third()
    lax.fori_loop(blocks // 2, blocks, output_step, 0)
    move.start(x_ref, out_hbm)
    if reduces:
        r2.last(o2_ref)
        om_ref[...] = small_sum.last()
        ra.last(o1_ref.at[:, pl.ds(0, wa)])
        rb.last(o1_ref.at[:, pl.ds(wa, 128)], osd_ref)
        for part in (r2, ra, rb, small_sum):
            part.finish()
    chain.finish()

    @pl.when(z > 0)
    def _():
        halo_copy.wait_send()

    move.finish((l_mine, l_c, l_yn0, l_yn, l_w3, l_h, l_dgate, l_w2, *l_scan, *l_state, *l_last) + (() if reduces else (s3,)))


def finish_kernel(nt, hloc, out_hbm, ig_hbm, o1_ref, osd_ref, o2_ref, o3_ref, om_ref, *refs):
    (out_to, ig_to, ng_ref, gi_ref, gs_ref, delta_ref, ci_ref, si_ref, cs_ref, ss_ref, decay_ref, bias_ref, bypass_ref,
     gg_ref, ow_ref, out_ref, ig_ref, sems) = refs
    half = out_ref.shape[0] // 2
    ways = [
        tuple(ref.at[pl.ds(half * i, half), :] for ref in way)
        for i in range(2)
        for way in ((out_hbm, out_ref, out_to), (ig_hbm, ig_ref, ig_to))
    ]
    into = [pltpu.make_async_copy(a, b, sems.at[k]) for k, (a, b, _) in enumerate(ways)]
    onto = [pltpu.make_async_copy(b, c, sems.at[4 + k]) for k, (_, b, c) in enumerate(ways)]
    for copy in into:
        copy.start()
    z = lax.axis_index("tensor")
    dcol = o1_ref.shape[1]
    sh = gs_ref.shape[1]
    dim = ng_ref.shape[0]
    cols = pl.ds(pl.multiple_of(z * dcol, 128), dcol)
    back = lax.rem(128 - z * hloc, 128)
    ng_ref[...] = om_ref[6, :dim]
    gi_ref[:, 0, :] = o2_ref[...]
    gi_ref[:, 1, :] = o1_ref[...]
    gs_ref[...] = osd_ref[:, :sh]
    delta_ref[...] = pltpu.roll(osd_ref[:, sh:], back, 1).T[:hloc]
    ci_ref[...] = om_ref[0:4, cols]
    si_ref[...] = om_ref[4, cols]
    gg_ref[...] = om_ref[5, cols]
    row, at = 6, dim
    taps = []
    for _ in range(5):
        if at + sh > om_ref.shape[1]:
            row, at = row + 1, 0
        taps.append(om_ref[row : row + 1, at : at + sh])
        at += sh
    for k in range(4):
        cs_ref[k : k + 1, :] = taps[k]
    ss_ref[...] = taps[4][0]
    for ref in (decay_ref, bias_ref, bypass_ref):
        if at + 128 > om_ref.shape[1]:
            row, at = row + 1, 0
        v = jnp.broadcast_to(om_ref[row : row + 1, at : at + 128], (8, 128))
        ref[...] = pltpu.roll(v, back, 1)[0, :hloc]
        at += 128
    for copy, after in zip(into, onto):
        copy.wait()
        after.start()
    ow_ref[...] = o3_ref[...]
    for copy in onto:
        copy.wait()


def semaphores(n):
    return [pltpu.SemaphoreType.DMA((n,)), pltpu.SemaphoreType.DMA((n,))]


def shifted(v, axis, by):
    n = lax.axis_size(axis)
    return lax.ppermute(v, axis, [(i, i + by) for i in range(n) if 0 <= i + by < n])


def gather_all(nt, nd, wgi, wdelta, wo, ws, par, edge):
    both = ("tensor", "dp")
    rows = ws.shape[0]
    dcol = wo.shape[0]
    pack = jnp.concatenate([wgi[:, 1], wgi[:, 0], wo.T], axis=1)
    full = lax.all_gather(pack, both, axis=0).reshape(nt, nd * rows, -1)
    whole = lambda a, b: full[:, :, a:b].transpose(1, 0, 2).reshape(nd * rows, nt * (b - a))
    w1 = jnp.concatenate([whole(0, dcol - 128), whole(dcol - 128, dcol)], axis=1)
    delta = lax.all_gather(wdelta, "tensor", axis=1, tiled=True)
    delta = jnp.pad(delta, ((0, 0), (0, 128 - delta.shape[1])))
    return (
        w1, whole(dcol, 2 * dcol), whole(2 * dcol, 3 * dcol),
        lax.all_gather(jnp.concatenate([ws, delta], axis=1), "dp", axis=0, tiled=True),
        lax.all_gather(par, "tensor", axis=0), shifted(edge, "tensor", 1),
    )


def reduce_all(nt, nd, g1, g2, g3, sm, sh):
    dim = g1.shape[0]
    rows = dim // nd
    dcol = g2.shape[1] // nt
    wa = dcol - 128
    both = ("tensor", "dp")
    parts = [
        g[:, at : at + nt * w].reshape(dim, nt, w).transpose(1, 0, 2)
        for g, at, w in ((g1, 0, wa), (g1, wa * nt, 128), (g2, 0, dcol), (g3, 0, dcol))
    ]
    big = jnp.concatenate(parts, axis=2).reshape(nt * nd, rows, -1)
    big = lax.psum_scatter(big, both, scatter_dimension=0).astype(F32)
    shared = g1[:, nt * dcol :].reshape(nd, rows, sh + 128).astype(F32)
    shared = lax.psum(lax.psum_scatter(shared, "dp", scatter_dimension=0), "tensor")
    return big[:, :dcol], shared, big[:, dcol : 2 * dcol], big[:, 2 * dcol :], lax.psum(sm, both)


def local(
    block_input, norm_gain, input_gate_inner_weight, input_shared_weight, input_delta_weight, conv_inner, shift_inner,
    conv_shared, shift_shared, decay_log, delta_bias, skip_gain, gated_gain, output_projection_weight, cotangent,
):
    nt = lax.axis_size("tensor")
    nd = lax.axis_size("dp")
    me = lax.axis_index("tensor")
    seqs, span, dim = block_input.shape
    tokens = seqs * span
    blocks = tokens // SPAN
    rows, _, dcol = input_gate_inner_weight.shape
    di = dcol * nt
    sh = input_shared_weight.shape[1]
    state = sh // 2
    hloc = input_delta_weight.shape[1]
    heads = hloc * nt

    x = block_input.reshape(tokens, dim)
    c = cotangent.reshape(tokens, dim)
    gathers = nd == 8
    args = [x, c, norm_gain, conv_shared, shift_shared]
    kinds = [pl.ANY, pl.ANY] + [pltpu.VMEM] * 3
    if gathers:
        args += [
            input_gate_inner_weight, input_delta_weight.T, output_projection_weight.T, input_shared_weight, conv_inner,
            shift_inner, gated_gain, decay_log, delta_bias, skip_gain,
        ]
        kinds += [pltpu.VMEM] * 10
    else:
        head = jnp.pad(jnp.stack([decay_log, delta_bias, skip_gain]), ((0, 5), (0, dcol - hloc)))
        par = [conv_inner.astype(F32), shift_inner.astype(F32)[None], gated_gain[None], jnp.zeros((2, dcol), F32), head]
        args += gather_all(
            nt, nd, input_gate_inner_weight, input_delta_weight, output_projection_weight, input_shared_weight,
            jnp.concatenate(par, axis=0), block_input[:, span - 16 :].reshape(seqs * 16, dim),
        )
        kinds += [pl.ANY] * 4 + [pltpu.VMEM] * 2
    scan_state = ((seqs, state, di), BF16)
    f128 = ((tokens, 128), F32)
    far = [
        ((tokens, dim), BF16), ((seqs, span + 16, di), F32), ((seqs, span + 16, sh), F32), ((tokens, di), BF16),
        ((tokens, sh), BF16), ((dim, di), BF16), ((dim, di), BF16), ((dim, di), BF16), ((dim, sh + 128), BF16),
        ((tokens, di), BF16), ((tokens, di), BF16), ((tokens, di), BF16), f128, f128, f128, f128, scan_state,
        scan_state, scan_state, scan_state,
    ]
    near = [
        ((blocks, 8, di), F32), ((seqs, 8, di), F32), ((8, di), F32), ((8, 128), F32), ((8, di), F32), ((8, di), F32),
        ((8, 128), F32), ((8, sh), F32)]
    scratch = [
        ((tokens, dim), BF16), ((tokens, dim), BF16), ((tokens, dim), BF16), ((dim, di), BF16), ((dim, di), BF16),
        ((dim, di), BF16), ((dim, sh + 128), BF16), ((nt, 16, dcol), F32), ((seqs * 16, dim), BF16),
        ((seqs, span + 16, di), F32), ((seqs, span + 16, sh), F32), ((tokens, di), BF16), ((tokens, sh), BF16),
        ((tokens, di), F32), ((8, di), F32), ((tokens, di), BF16), ((tokens, di), BF16), ((tokens, di), BF16),
        ((SPAN, di), F32), ((seqs, state, di), F32), scan_state,
        ((seqs * 16, dim), BF16), ((tokens, 128), BF16), ((blocks, 128, SPAN), F32), ((128, di), BF16),
        ((SPAN, SPAN), BF16), ((rows, 2 * dcol), BF16), ((16, dcol), F32), ((nt, rows, 128), BF16), ((rows, sh + 128), BF16),
        ((128, 128), F32), f128, f128, f128, f128, scan_state, ((SPAN, di), F32), scan_state, scan_state, scan_state,
        ((tokens, 128), BF16),
    ]
    pieces = seqs * di // min(PIECES)
    h, rawi, raws, xs, bc, w1, w2, w3, ws, yn, dgate, dy, draw, acs, bs, rr, fresh, vv, mineb, sin, *rest = pl.pallas_call(
        functools.partial(forward_kernel, heads, nt, nd, gathers),
        out_shape=[jax.ShapeDtypeStruct(s, d) for s, d in far + near],
        in_specs=[pl.BlockSpec(memory_space=k) for k in kinds],
        out_specs=[pl.BlockSpec(memory_space=pl.ANY)] * len(far) + [pl.BlockSpec(memory_space=pltpu.VMEM)] * len(near),
        scratch_shapes=[pltpu.VMEM(s, d) for s, d in scratch]
        + semaphores(4 * Gather.MESSAGES + 5 + 2 * nt + seqs) + semaphores(pieces)
        + [pltpu.SemaphoreType.DMA((6,)), pltpu.SemaphoreType.DMA((24,)), pltpu.SemaphoreType.DMA((5, blocks))],
        compiler_params=pltpu.CompilerParams(vmem_limit_bytes=VMEM_LIMIT, collective_id=0, has_side_effects=True),
        name="forward",
    )(*args)
    dec, whole, chan, dpar, skip, ggg, skg, ts = rest

    args = [x, c, h, rawi, raws, xs, bc, w1, w2, w3, ws, yn, dgate, dy, draw, acs, bs, rr, fresh, vv, sin, mineb]
    kinds = [pl.ANY] * len(args)
    more = [norm_gain, ts, dec, whole, chan, dpar, skip, ggg, skg]
    args += more
    kinds += [pltpu.VMEM] * len(more)
    wa = dcol - 128
    scratch = [
        ((tokens, dim), BF16), ((tokens, dim), BF16), ((seqs, span + 16, di), F32),
        ((seqs, span + 16, sh), F32), ((tokens, di), BF16), ((tokens, sh), BF16), ((dim, di), BF16),
        ((dim, sh + 128), BF16), ((tokens, di), BF16), ((tokens, di), BF16), f128, f128, f128, f128, scan_state, scan_state,
        scan_state, scan_state, scan_state, ((tokens, di + sh + 128), BF16), ((tokens, di), F32), ((tokens, sh), F32),
        ((dim, 2 * di + sh + 128), BF16), ((seqs, 8, di + sh), F32), ((seqs, 8, di + sh), F32), ((seqs, 8, di + sh), F32),
        ((128, SPAN), F32), ((3, HALF, HALF), F32), ((128, di), BF16), ((SPAN, SPAN), BF16),
        ((5, 8, di + sh), F32), ((8, 128), F32), ((dim, 128), F32), ((dim, di), BF16),
    ]
    scratch = [pltpu.VMEM(s, d) for s, d in scratch]
    sems = semaphores(pieces) + semaphores(1) + [pltpu.SemaphoreType.DMA((32,))]
    if gathers:
        near = [
            ((rows, dcol), F32), ((rows, sh + 128), F32), ((rows, dcol), F32), ((rows, dcol), F32), ((8, di), F32)
        ]
        far = []
        scratch += [pltpu.VMEM((8, di), F32)]
        for width, wz in ((di, dcol), (di, dcol), (wa * nt, wa), (128 * nt + sh + 128, sh + 256)):
            scratch += Reduce.scratch(rows, width, nt, wz)
        scratch += SmallSum.scratch((8, di), nt)
        for _ in range(4):
            sems += semaphores(Reduce.MESSAGES)
        sems += semaphores(SmallSum.MESSAGES)
    else:
        far = [((dim, di + sh + 128), BF16), ((dim, di), BF16), ((dim, di), BF16)]
        near = [((8, di), F32)]
    outs = [((tokens, dim), BF16)] * 2 + far + near
    out, ig, *rest = pl.pallas_call(
        functools.partial(backward_kernel, heads, nt, nd, gathers),
        out_shape=[jax.ShapeDtypeStruct(s, d) for s, d in outs],
        in_specs=[pl.BlockSpec(memory_space=k) for k in kinds],
        out_specs=[pl.BlockSpec(memory_space=pl.ANY)] * (2 + len(far)) + [pl.BlockSpec(memory_space=pltpu.VMEM)] * len(near),
        scratch_shapes=scratch + sems,
        compiler_params=pltpu.CompilerParams(vmem_limit_bytes=VMEM_LIMIT, collective_id=1, has_side_effects=True),
        name="backward",
    )(*args)
    if gathers:
        sums = rest
    else:
        sums = reduce_all(nt, nd, *rest, sh)
    finals = [
        ((tokens, dim), BF16), ((tokens, dim), BF16), ((dim,), F32), ((rows, 2, dcol), F32), ((rows, sh), F32),
        ((hloc, rows), F32), ((4, dcol), F32), ((dcol,), F32), ((4, sh), F32), ((sh,), F32), ((hloc,), F32), ((hloc,), F32),
        ((hloc,), F32), ((dcol,), F32), ((rows, dcol), F32),
    ]
    out, ig, *rest = pl.pallas_call(
        functools.partial(finish_kernel, nt, hloc),
        out_shape=[jax.ShapeDtypeStruct(s, d) for s, d in finals],
        in_specs=[pl.BlockSpec(memory_space=pl.ANY)] * 2 + [pl.BlockSpec(memory_space=pltpu.VMEM)] * 5,
        out_specs=[pl.BlockSpec(memory_space=pl.ANY)] * 2 + [pl.BlockSpec(memory_space=pltpu.VMEM)] * 13,
        scratch_shapes=[pltpu.VMEM((tokens, dim), BF16)] * 2 + [pltpu.SemaphoreType.DMA((8,))],
        name="finish",
    )(out, ig, *sums)
    rest[3] = rest[3].T
    rest[-1] = rest[-1].T
    return (out.reshape(block_input.shape), ig.reshape(block_input.shape), *rest)


def solution(mesh):
    placed = (
        P("dp", "tensor", None), P(), P("dp", None, "tensor"), P("dp", None), P("dp", "tensor"), P(None, "tensor"),
        P("tensor"), P(), P(), P("tensor"), P("tensor"), P("tensor"), P("tensor"), P("tensor", "dp"),
        P("dp", "tensor", None),
    )
    return jax.shard_map(
        local,
        mesh=mesh,
        in_specs=placed,
        out_specs=(
            P("dp", "tensor", None), P("dp", "tensor", None), P(), P("dp", None, "tensor"), P("dp", None),
            P("dp", "tensor"), P(None, "tensor"), P("tensor"), P(), P(), P("tensor"), P("tensor"), P("tensor"),
            P("tensor"), P("tensor", "dp"),
        ),
        check_vma=False,
    )
```
